32 devices in a mesh: face: 4 (over z), blk: 8 (over y, x, core).
Axes of the slice: x: 2, y: 2, z: 4, core: 2. Of those that a mesh axis runs over, the one named last changes fastest.
Arguments:
- air_state: float32 [3, 16, 64, 1024], P(None, None, 'face', 'blk'), may hold values from -6 to 6
- air_wind: float32 [2, 16, 64, 1024], P(None, None, 'face', 'blk'), may hold values from -4 to 4
- jacobian: float32 [64, 1024], P('face', 'blk'), may hold values from 0.5 to 2
- land_area: float32 [64, 1024], P('face', 'blk'), may hold values from 0.1 to 1
- xgrid_rows: int32 [32, 8, 128], P(('face', 'blk')), may hold values from 0 to 2047
- tracers: float32 [2, 16, 65536], P(None, None, ('face', 'blk')), may hold values from -6 to 6
- edge_coef: float32 [6, 65536], P(None, ('face', 'blk')), may hold values from 0.02 to 0.14
- neighbours: int32 [6, 65536], P(None, ('face', 'blk')), may hold values from 0 to 2303
- vert_rate: float32 [65536], P(('face', 'blk')), may hold values from 0.05 to 0.2
- ocean_area: float32 [65536], P(('face', 'blk')), may hold values from 0.5 to 2
- send_list: int32 [32, 256], P(('face', 'blk')), may hold values from 0 to 2047
- xgrid_cols: int32 [32, 8, 128], P(('face', 'blk')), may hold values from 0 to 2047
- xgrid_weights: float32 [32, 8, 128], P(('face', 'blk')), may hold values from 0 to 1, as said below
Outputs:
- air_final: float32 [3, 16, 64, 1024], P(None, None, 'face', 'blk')
- ocean_final: float32 [2, 16, 65536], P(None, None, ('face', 'blk'))
The draws below stay inside these ranges and needn't reach their ends.
Inputs may be any that keep to these rules, and one draw needn't show every extreme that they name: `xgrid_weights`: in every block of 128 slots the nonzero weights, each at least 0.1, come first and zeros fill the rest; in every draw some blocks of every device are completely full.
All inputs are finite; a program needn't handle non-finite values.
Results may differ from the reference program's by a relative error of at most 0.00016.
Values sent between devices are 32-bit elements; how exact they have to be, the bound alone decides.
No kernel may reach another device: no remote copies, remote signals or barrier semaphores. Data moves between devices by JAX's collectives and lax.ppermute only.
A program may use at most 64 MiB of HBM per device.

```python
import math
import jax
import jax.numpy as jnp
from jax import lax

GLL = 4
FIELDS = 3
LEVELS = 16
SUBSTEPS = 2
OCN_TRACERS = 2
OCEAN_LEVELS = 16
EDGES = 6
CELLS_DEV = 2048
RIM = 128
SLOTS = 128
PX = 16
PY = 128
GX = 64
GY = 1024
CELLS = 65536
N_FACE = 4
N_BLK = 8
DEVICES = 32


def draw_xgrid_weights(key, part):
    base = jax.random.fold_in(key, 7301)
    key_count, key_busy, key_full, key_value = jax.random.split(base, 4)
    counts = jax.random.randint(key_count, (DEVICES, N_BLK), 0, SLOTS + 1)
    busy = jax.random.randint(key_busy, (DEVICES, 1), 0, 4) == 0
    counts = jnp.where(busy, SLOTS, counts)
    full_peer = jax.random.randint(key_full, (DEVICES, 1), 0, N_BLK)
    counts = jnp.where(jnp.arange(N_BLK)[None, :] == full_peer, SLOTS, counts)
    live = jnp.arange(SLOTS)[None, None, :] < counts[:, :, None]
    values = jnp.exp(jax.random.uniform(key_value, (DEVICES, N_BLK, SLOTS), jnp.float32, jnp.log(0.1), 0.0))
    return jnp.where(live, values, 0.0).astype(jnp.float32)


def with_ends(entries, stream_key, low, top_value):
    index_at = [jax.random.randint(jax.random.fold_in(stream_key, axis), (), 0, length) for axis, length in enumerate(entries.shape)]
    longest = entries.shape.index(max(entries.shape))
    next_to = index_at[:longest] + [(index_at[longest] + 1) % entries.shape[longest]] + index_at[longest + 1:]
    return entries.at[tuple(index_at)].set(low).at[tuple(next_to)].set(top_value)


def shard_levels(rng, extent, shards, smallest, high):
    level = 1.0
    for position, blocks in shards:
        heights = jax.random.uniform(jax.random.fold_in(jax.random.fold_in(rng, 6), position), (blocks,), jnp.float32, smallest / len(shards), high / len(shards))
        level = level * jnp.repeat(jnp.exp(heights), extent[position] // blocks).reshape((-1,) + (1,) * (len(extent) - 1 - position))
    return level


def noise(rng, extent, width, limit, cuts=(), kind=jnp.bfloat16):
    drawn = width * jax.random.normal(rng, extent, jnp.float32)
    if cuts:
        drawn = drawn * shard_levels(rng, extent, cuts, -0.22, 0.18)
    return jnp.clip(drawn, -limit, limit).astype(kind)


def setup_inputs(seed: int = 0) -> dict:
    seeds = jax.random.split(jax.random.key(seed), 14)
    air_state = noise(seeds[0], (FIELDS, LEVELS, GX, GY), 1.0, 6.0, ((2, 4), (3, 8)), jnp.float32)
    air_wind = noise(seeds[1], (2, LEVELS, GX, GY), 1.0, 4.0, ((2, 4), (3, 8)), jnp.float32)
    jacobian = jnp.clip(jnp.exp(math.log(2.0) - 1.3862944 * jax.random.uniform(seeds[2], (GX, GY), jnp.float32) ** shard_levels(seeds[2], (GX, GY), ((0, 4), (1, 8)), -0.2, 0.2)), 0.5, 2.0)
    land_area = jnp.clip(jnp.exp(math.log(1.0) - 2.3025851 * jax.random.uniform(seeds[3], (GX, GY), jnp.float32) ** shard_levels(seeds[3], (GX, GY), ((0, 4), (1, 8)), -0.2, 0.2)), 0.1, 1.0)
    xgrid_rows = with_ends(jax.random.randint(seeds[4], (N_FACE * N_BLK, N_BLK, SLOTS), 0, PX * PY), jax.random.fold_in(seeds[4], 1), 0, (PX * PY) - 1).astype(jnp.int32)
    tracers = noise(seeds[5], (OCN_TRACERS, OCEAN_LEVELS, CELLS), 1.0, 6.0, ((2, 32),), jnp.float32)
    edge_coef = jnp.clip(jnp.exp(math.log(0.14) - 1.9459102 * jax.random.uniform(seeds[6], (EDGES, CELLS), jnp.float32) ** shard_levels(seeds[6], (EDGES, CELLS), ((1, 32),), -0.2, 0.2)), 0.02, 0.14)
    neighbours = with_ends(jax.random.randint(seeds[7], (EDGES, CELLS), 0, CELLS_DEV + 2 * RIM), jax.random.fold_in(seeds[7], 1), 0, (CELLS_DEV + 2 * RIM) - 1).astype(jnp.int32)
    vert_rate = jnp.clip(jnp.exp(math.log(0.2) - 1.3862944 * jax.random.uniform(seeds[8], (CELLS,), jnp.float32) ** shard_levels(seeds[8], (CELLS,), ((0, 32),), -0.2, 0.2)), 0.05, 0.2)
    ocean_area = jnp.clip(jnp.exp(math.log(2.0) - 1.3862944 * jax.random.uniform(seeds[9], (CELLS,), jnp.float32) ** shard_levels(seeds[9], (CELLS,), ((0, 32),), -0.2, 0.2)), 0.5, 2.0)
    send_list = with_ends(jax.random.randint(seeds[10], (N_FACE * N_BLK, 2 * RIM), 0, CELLS_DEV), jax.random.fold_in(seeds[10], 1), 0, CELLS_DEV - 1).astype(jnp.int32)
    xgrid_cols = with_ends(jax.random.randint(seeds[11], (N_FACE * N_BLK, N_BLK, SLOTS), 0, CELLS_DEV), jax.random.fold_in(seeds[11], 1), 0, CELLS_DEV - 1).astype(jnp.int32)
    xgrid_weights = draw_xgrid_weights(jax.random.fold_in(seeds[13], 71), 0)
    return dict(air_state=air_state, air_wind=air_wind, jacobian=jacobian, land_area=land_area, xgrid_rows=xgrid_rows, tracers=tracers, edge_coef=edge_coef, neighbours=neighbours, vert_rate=vert_rate, ocean_area=ocean_area, send_list=send_list, xgrid_cols=xgrid_cols, xgrid_weights=xgrid_weights)


deriv_table = [[-3.0, 4.045084971874737, -1.545084971874737, 0.5], [-0.8090169943749475, 0.0, 1.118033988749895, -0.30901699437494745], [0.30901699437494745, -1.118033988749895, 0.0, 0.8090169943749475], [-0.5, 1.545084971874737, -4.045084971874737, 3.0]]
gll_weights = [1.0 / 6.0, 5.0 / 6.0, 5.0 / 6.0, 1.0 / 6.0]
time_step = 0.05
relax_rate = 0.3
flux_gain = 0.2


def along_first(field):
    table = jnp.array(deriv_table, jnp.float32)
    planes, xsize, ysize = field.shape
    shaped = field.reshape(planes, xsize // GLL, GLL, ysize)
    result = jnp.einsum("ik,aeky->aeiy", table, shaped, precision=lax.Precision.HIGHEST)
    return result.reshape(planes, xsize, ysize)


def along_second(field):
    table = jnp.array(deriv_table, jnp.float32)
    planes, xsize, ysize = field.shape
    shaped = field.reshape(planes, xsize, ysize // GLL, GLL)
    result = jnp.einsum("ik,axek->axei", table, shaped, precision=lax.Precision.HIGHEST)
    return result.reshape(planes, xsize, ysize)


def copy_sum(values):
    xsize, ysize = values.shape[-2], values.shape[-1]
    x_pos = jnp.arange(xsize, dtype=jnp.int32) % GLL
    y_pos = jnp.arange(ysize, dtype=jnp.int32) % GLL
    first_row = (x_pos == 0)[:, None]
    last_row = (x_pos == GLL - 1)[:, None]
    partial_sum = values + jnp.where(first_row, jnp.roll(values, 1, -2), 0.0) + jnp.where(last_row, jnp.roll(values, -1, -2), 0.0)
    first_col = y_pos == 0
    last_col = y_pos == GLL - 1
    return partial_sum + jnp.where(first_col, jnp.roll(partial_sum, 1, -1), 0.0) + jnp.where(last_col, jnp.roll(partial_sum, -1, -1), 0.0)


def reference(air_state, air_wind, jacobian, land_area, xgrid_rows, tracers, edge_coef, neighbours, vert_rate, ocean_area, send_list, xgrid_cols, xgrid_weights):
    field_count, levels, gx_all, gy_all = air_state.shape
    x_points = gx_all // N_FACE
    y_points = gy_all // N_BLK
    block_points = x_points * y_points
    ocn_count, ocn_levels, cell_total = tracers.shape
    cell_count = cell_total // (N_FACE * N_BLK)
    slot_count = xgrid_rows.shape[2]
    rim_width = send_list.shape[1] // 2

    def to_blocks(grid):
        return grid.reshape(N_FACE, x_points, N_BLK, y_points).transpose(0, 2, 1, 3).reshape(N_FACE, N_BLK, block_points)

    def from_blocks(flat):
        return flat.reshape(N_FACE, N_BLK, x_points, y_points).transpose(0, 2, 1, 3).reshape(gx_all, gy_all)

    point_ids = xgrid_rows.reshape(N_FACE, N_BLK, N_BLK, slot_count)
    cell_ids = xgrid_cols.reshape(N_FACE, N_BLK, N_BLK, slot_count)
    weights = xgrid_weights.reshape(N_FACE, N_BLK, N_BLK, slot_count)

    surface = tracers[0, 0].reshape(N_FACE, N_BLK, cell_count)
    surface_at = jnp.take_along_axis(surface, cell_ids.reshape(N_FACE, N_BLK, N_BLK * slot_count), axis=2).reshape(N_FACE, N_BLK, N_BLK, slot_count)
    heat_terms = (weights * surface_at).transpose(0, 2, 1, 3)
    frac_terms = weights.transpose(0, 2, 1, 3)
    point_base = (jnp.arange(N_FACE * N_BLK, dtype=jnp.int32) * block_points).reshape(N_FACE, N_BLK, 1, 1)
    point_targets = (point_base + point_ids).reshape(-1).astype(jnp.int32)
    heat_sum = jax.ops.segment_sum(heat_terms.reshape(-1), point_targets, num_segments=N_FACE * N_BLK * block_points)
    frac_sum = jax.ops.segment_sum(frac_terms.reshape(-1), point_targets, num_segments=N_FACE * N_BLK * block_points)
    heat_map = from_blocks(heat_sum)
    frac_map = from_blocks(frac_sum)
    t_surf = (heat_map + land_area * air_state[0, 0]) / (frac_map + land_area)

    table = jnp.array(gll_weights, jnp.float32)
    x_weight = table[jnp.arange(gx_all, dtype=jnp.int32) % GLL]
    y_weight = table[jnp.arange(gy_all, dtype=jnp.int32) % GLL]
    mass_map = x_weight[:, None] * y_weight[None, :] * jacobian
    mass_sum = copy_sum(mass_map)

    def advance(packed):
        field, flag = packed
        for substep in range(SUBSTEPS):
            tendency = -(air_wind[0] * along_first(field) + air_wind[1] * along_second(field))
            moved = field + time_step * tendency
            moved = moved.at[0].add(flag * relax_rate * (t_surf - field[0]))
            field = copy_sum(mass_map * moved) / mass_sum
        return field

    flags = (jnp.arange(field_count, dtype=jnp.int32) == 0).astype(jnp.float32)
    air_final = lax.map(advance, (air_state, flags))

    sea_flux = to_blocks(air_final[0, 0] - t_surf)
    sent = jnp.take_along_axis(sea_flux, point_ids.reshape(N_FACE, N_BLK, N_BLK * slot_count), axis=2).reshape(N_FACE, N_BLK, N_BLK, slot_count)
    arrived = sent.transpose(0, 2, 1, 3)
    cell_base = (jnp.arange(N_FACE * N_BLK, dtype=jnp.int32) * cell_count).reshape(N_FACE, N_BLK, 1, 1)
    cell_targets = (cell_base + cell_ids).reshape(-1).astype(jnp.int32)
    inflow = jax.ops.segment_sum((weights * arrived).reshape(-1), cell_targets, num_segments=N_FACE * N_BLK * cell_count)

    tracer_blocks = tracers.reshape(ocn_count, ocn_levels, N_FACE, N_BLK, cell_count)
    send_ids = send_list.reshape(N_FACE, N_BLK, 2 * rim_width)
    send_full = jnp.broadcast_to(send_ids[None, None], (ocn_count, ocn_levels, N_FACE, N_BLK, 2 * rim_width))
    outgoing = jnp.take_along_axis(tracer_blocks, send_full, axis=4)
    lower_rim = jnp.roll(outgoing[..., rim_width:], 1, axis=3)
    upper_rim = jnp.roll(outgoing[..., :rim_width], -1, axis=3)
    extended = jnp.concatenate([tracer_blocks, lower_rim, upper_rim], axis=4)
    near_ids = neighbours.reshape(EDGES, N_FACE, N_BLK, cell_count)
    coef_blocks = edge_coef.reshape(EDGES, N_FACE, N_BLK, cell_count)
    lateral = jnp.zeros_like(tracer_blocks)
    for edge in range(EDGES):
        index_full = jnp.broadcast_to(near_ids[edge][None, None], tracer_blocks.shape)
        adjacent = jnp.take_along_axis(extended, index_full, axis=4)
        lateral = lateral + coef_blocks[edge] * (adjacent - tracer_blocks)
    lateral = lateral.reshape(ocn_count, ocn_levels, cell_total)
    upper_level = jnp.concatenate([tracers[:, :1], tracers[:, :-1]], axis=1)
    lower_level = jnp.concatenate([tracers[:, 1:], tracers[:, -1:]], axis=1)
    vertical = vert_rate * ((upper_level - tracers) + (lower_level - tracers))
    ocean_final = tracers + lateral + vertical
    ocean_final = ocean_final.at[0, 0].add(flux_gain * inflow / ocean_area)
    return air_final, ocean_final
```

```python
import functools

import jax
import jax.numpy as jnp
from jax import lax
from jax.experimental import pallas as pl
from jax.experimental.pallas import tpu as pltpu
from jax.sharding import PartitionSpec as P

GLL = 4
ROWS = 8
LANES = 128

deriv_table = [
    [-3.0, 4.045084971874737, -1.545084971874737, 0.5],
    [-0.8090169943749475, 0.0, 1.118033988749895, -0.30901699437494745],
    [0.30901699437494745, -1.118033988749895, 0.0, 0.8090169943749475],
    [-0.5, 1.545084971874737, -4.045084971874737, 3.0],
]
time_step = 0.05
relax_rate = 0.3
flux_gain = 0.2

PAIRS = LANES // 2
HEAD = 8
AVG, MASS_SUM, MASS, COEF_X, COEF_Y, SURF = range(6)
SURF_ARRAYS = 6


def iota(shape, dim):
    return lax.broadcasted_iota(jnp.int32, shape, dim)


def take(values, index, axis):
    return jnp.take_along_axis(values, index, axis=axis, mode="promise_in_bounds")


def by_position(pos, values):
    result = jnp.full(pos.shape, values[-1], jnp.float32)
    for i, value in enumerate(values[:-1]):
        result = jnp.where(pos == i, value, result)
    return result


def spread(row):
    return jnp.broadcast_to(row, (ROWS, LANES))


class Geometry:
    def __init__(self):
        shape = (ROWS, LANES)
        self.row, self.lane = iota(shape, 0), iota(shape, 1)
        x_pos, y_pos = self.row & (GLL - 1), self.lane & (GLL - 1)
        self.x_from = [self.row - x_pos + j for j in range(GLL)]
        self.y_from = [self.lane - y_pos + j for j in range(GLL)]
        columns = [[line[j] for line in deriv_table] for j in range(GLL)]
        self.x_coef = [by_position(x_pos, column) for column in columns]
        self.y_coef = [by_position(y_pos, column) for column in columns]
        self.x_swap = (
            self.row + jnp.where(x_pos == GLL - 1, 1, 0) - jnp.where(x_pos == 0, 1, 0)
        ) & (ROWS - 1)
        self.y_swap = (
            self.lane + jnp.where(y_pos == GLL - 1, 1, 0) - jnp.where(y_pos == 0, 1, 0)
        ) & (LANES - 1)
        self.x_edge = (x_pos == 0) | (x_pos == GLL - 1)
        self.y_edge = (y_pos == 0) | (y_pos == GLL - 1)
        self.first_row, self.last_row = self.row == 0, self.row == ROWS - 1
        self.outer_lane = (self.lane == 0) | (self.lane == LANES - 1)
        self.weight = jnp.where(self.x_edge, 1.0 / 6.0, 5.0 / 6.0) * jnp.where(
            self.y_edge, 1.0 / 6.0, 5.0 / 6.0
        )

    def d_x(self, tile):
        return sum(self.x_coef[j] * take(tile, self.x_from[j], 0) for j in range(GLL))

    def d_y(self, tile):
        return sum(self.y_coef[j] * take(tile, self.y_from[j], 1) for j in range(GLL))

    def sum_x(self, low, high, before, after):
        low_swap, high_swap = take(low, self.x_swap, 0), take(high, self.x_swap, 0)
        low_other = jnp.where(
            self.first_row, before, jnp.where(self.last_row, high_swap, low_swap)
        )
        high_other = jnp.where(
            self.first_row, low_swap, jnp.where(self.last_row, after, high_swap)
        )
        return (
            low + jnp.where(self.x_edge, low_other, 0.0),
            high + jnp.where(self.x_edge, high_other, 0.0),
        )

    def sum_y(self, tile, outer):
        other = jnp.where(self.outer_lane, outer, take(tile, self.y_swap, 1))
        return tile + jnp.where(self.y_edge, other, 0.0)

    def sum_y_pair(self, own, strip):
        own_swap, strip_swap = take(own, self.y_swap, 1), take(strip, self.y_swap, 1)
        own_other = jnp.where(self.outer_lane, strip_swap, own_swap)
        strip_other = jnp.where(self.outer_lane, own_swap, strip_swap)
        return (
            own + jnp.where(self.y_edge, own_other, 0.0),
            strip + jnp.where(self.y_edge, strip_other, 0.0),
        )


def pack_edges(geo, packs, tile, number):
    at = number % PAIRS
    rolled = pltpu.roll(tile, (2 * at + 1) % LANES, 1)
    packs[number // PAIRS] = jnp.where(
        (geo.lane >> 1) == at, rolled, packs[number // PAIRS]
    )


def join_edges(geo, from_left, from_right):
    odd = (geo.lane & 1) == 1
    return jnp.where(
        odd, pltpu.roll(from_left, 1, 1), pltpu.roll(from_right, LANES - 1, 1)
    )


def outer_edges(joined, number):
    at = number % PAIRS
    return pltpu.roll(joined[number // PAIRS], (-(2 * at + 1)) % LANES, 1)


def neighbours_of(blocks):
    here = lax.axis_index("blk")
    return lax.rem(here + blocks - 1, blocks), lax.rem(here + 1, blocks)


def scatter_sum(lines, index, bins, allowed=None):
    count = index.shape[0]
    split = []
    for values in lines:
        for part in range(3):
            short = values.astype(jnp.bfloat16).astype(jnp.float32)
            split.append(short)
            values = values - short
    high, low = index >> 7, index & (LANES - 1)
    bin_at = iota((bins, LANES), 0)
    lane_at = iota((LANES, LANES), 0)
    if allowed is not None:
        lane_at = jnp.where(allowed(lane_at), lane_at, -1)
    left, right = [], []
    for c in range(count):
        hit = bin_at == high[c : c + 1]
        left.append(
            jnp.concatenate(
                [jnp.where(hit, part[c : c + 1], 0.0) for part in split], axis=0
            ).astype(jnp.bfloat16)
        )
        right.append(
            jnp.where(lane_at == low[c : c + 1], 1.0, 0.0).astype(jnp.bfloat16)
        )
    total = lax.dot_general(
        jnp.concatenate(left, axis=1),
        jnp.concatenate(right, axis=1),
        (((1,), (1,)), ((), ())),
        preferred_element_type=jnp.float32,
    )
    sums = []
    for i in range(len(lines)):
        part = total[3 * i * bins : 3 * (i + 1) * bins]
        sums.append(part[:bins] + part[bins : 2 * bins] + part[2 * bins :])
    return sums


def start_kernel(
    planes,
    air_ref,
    wind_ref,
    jac_ref,
    land_ref,
    rows_ref,
    tracers_ref,
    send_ref,
    cols_ref,
    weights_ref,
    slab_ref,
    moved_ref,
):
    geo = Geometry()
    blocks = cols_ref.shape[0]
    left, right = neighbours_of(blocks)
    levels = wind_ref.shape[0] // 32
    chunks = tracers_ref.shape[1] // LANES

    def source(group, chunk):
        return tracers_ref[
            ROWS * group : ROWS * (group + 1), LANES * chunk : LANES * (chunk + 1)
        ]

    for group in range(blocks // ROWS):
        at = slice(ROWS * group, ROWS * (group + 1))
        cells = cols_ref[at, :]
        high, low = cells >> 7, cells & (LANES - 1)
        surface = jnp.zeros((ROWS, LANES), jnp.float32)
        for k in range(chunks):
            line = spread(tracers_ref[0:1, LANES * k : LANES * (k + 1)])
            surface = jnp.where(high == k, take(line, low, 1), surface)
        area = weights_ref[at, :]
        heat = area * surface
        for c in range(ROWS):
            owner = ROWS * group + c
            for place, step in enumerate((1, 0, -1)):
                to = (owner + step) % blocks
                slab_ref[to, 2 * place : 2 * place + 1, :] = heat[c : c + 1]
                slab_ref[to, 2 * place + 1 : 2 * place + 2, :] = area[c : c + 1]

    mass = [geo.weight * jac_ref[ROWS * h : ROWS * (h + 1), :] for h in range(2)]
    packs = [
        jnp.zeros((ROWS, LANES), jnp.float32) for _ in range(-(-2 * planes // PAIRS))
    ]
    for level in range(levels):
        wind = [
            [
                time_step * wind_ref[pl.ds((i * levels + level) * 16 + ROWS * h, ROWS), :]
                for h in range(2)
            ]
            for i in range(2)
        ]
        for plane in range(level, planes, levels):
            for h in range(2):
                at = pl.ds(plane * 16 + ROWS * h, ROWS)
                field = air_ref[at, :]
                moved = mass[h] * (
                    field - (wind[0][h] * geo.d_x(field) + wind[1][h] * geo.d_y(field))
                )
                moved_ref[at, :] = moved
                pack_edges(geo, packs, moved, 2 * plane + h)

    base = HEAD
    edge_rows = ROWS * len(packs)
    for to in (left, right):
        for q, pack in enumerate(packs):
            slab_ref[to, base + ROWS * q : base + ROWS * (q + 1), :] = pack
    base += edge_rows
    for h in range(2):
        half = slice(ROWS * h, ROWS * (h + 1))
        strips = [
            air_ref[half, :],
            wind_ref[half, :],
            wind_ref[levels * 16 + ROWS * h : levels * 16 + ROWS * (h + 1), :],
            jac_ref[half, :],
            land_ref[half, :],
        ]
        pack = jnp.zeros((ROWS, LANES), jnp.float32)
        for i, strip in enumerate(strips):
            pack = jnp.where(
                (geo.lane >> 4) == i, pltpu.roll(strip, 16 * i + 8, 1), pack
            )
        for to in (left, right):
            slab_ref[to, base + ROWS * h : base + ROWS * (h + 1), :] = pack
    base += 2 * ROWS
    ids = rows_ref[...].astype(jnp.float32)
    for to in (left, right):
        slab_ref[to, base : base + blocks, :] = ids
    base += blocks
    for part, to in enumerate((left, right)):
        cells = spread(send_ref[0:1, LANES * part : LANES * (part + 1)])
        high, low = cells >> 7, cells & (LANES - 1)
        for group in range(tracers_ref.shape[0] // ROWS):
            rim = jnp.zeros((ROWS, LANES), jnp.float32)
            for k in range(chunks):
                rim = jnp.where(high == k, take(source(group, k), low, 1), rim)
            slab_ref[to, base + ROWS * group : base + ROWS * (group + 1), :] = rim


def panel_kernel(
    planes,
    moved_ref,
    recv_ref,
    air_ref,
    wind_ref,
    jac_ref,
    land_ref,
    rows_ref,
    avg_ref,
    down_ref,
    up_ref,
    surf_ref,
):
    geo = Geometry()
    blocks = rows_ref.shape[0]
    left, right = neighbours_of(blocks)
    levels = wind_ref.shape[0] // 32
    pack_count = -(-2 * planes // PAIRS)
    base = HEAD + ROWS * pack_count

    ids_at = base + 2 * ROWS
    own_ids = rows_ref[...]
    left_ids = recv_ref[left, ids_at : ids_at + blocks, :].astype(jnp.int32)
    right_ids = recv_ref[right, ids_at : ids_at + blocks, :].astype(jnp.int32)
    head = [
        jnp.concatenate([recv_ref[c, i : i + 1, :] for c in range(blocks)], axis=0)
        for i in range(6)
    ]
    heat, frac = scatter_sum(head[2:4], own_ids, 2 * ROWS)
    from_left = scatter_sum(
        head[0:2], left_ids, 2 * ROWS, lambda lane: lane >= LANES - ROWS
    )
    from_right = scatter_sum(head[4:6], right_ids, 2 * ROWS, lambda lane: lane < ROWS)
    strip_heat = from_left[0] + from_right[0]
    strip_frac = from_left[1] + from_right[1]

    in_strip = (geo.lane < ROWS) | (geo.lane >= LANES - ROWS)
    own, strip = [], []
    for h in range(2):
        half = slice(ROWS * h, ROWS * (h + 1))
        pack = jnp.where(
            ((geo.lane >> 3) & 1) == 1,
            recv_ref[right, base + ROWS * h : base + ROWS * (h + 1), :],
            recv_ref[left, base + ROWS * h : base + ROWS * (h + 1), :],
        )
        strip.append(
            [
                jnp.where(
                    in_strip, pltpu.roll(pack, (-(16 * i + 8)) % LANES, 1), 1.0
                )
                for i in range(5)
            ]
        )
        own.append(
            [
                air_ref[half, :],
                wind_ref[half, :],
                wind_ref[levels * 16 + ROWS * h : levels * 16 + ROWS * (h + 1), :],
                jac_ref[half, :],
                land_ref[half, :],
            ]
        )
    for h in range(2):
        half = slice(ROWS * h, ROWS * (h + 1))
        pair = []
        for tile, ((field, wind_x, wind_y, jac, land), tile_heat, tile_frac) in enumerate(
            ((own[h], heat[half], frac[half]), (strip[h], strip_heat[half], strip_frac[half]))
        ):
            mass = geo.weight * jac
            if tile == 1:
                tile_heat = jnp.where(in_strip, tile_heat, 0.0)
                tile_frac = jnp.where(in_strip, tile_frac, 0.0)
            surf = (tile_heat + land * field) / (tile_frac + land)
            coef_x, coef_y = time_step * mass * wind_x, time_step * mass * wind_y
            moved = (
                mass * (field + relax_rate * (surf - field))
                - coef_x * geo.d_x(field)
                - coef_y * geo.d_y(field)
            )
            pair.append((moved, mass))
            at = 2 * ROWS * tile + ROWS * h
            for number, value in (
                (MASS, mass),
                (COEF_X, coef_x),
                (COEF_Y, coef_y),
                (SURF, surf),
            ):
                surf_ref[4 * ROWS * number + at : 4 * ROWS * number + at + ROWS, :] = value
        for number, i in ((AVG, 0), (MASS_SUM, 1)):
            for tile, value in enumerate(geo.sum_y_pair(pair[0][i], pair[1][i])):
                at = 4 * ROWS * number + 2 * ROWS * tile + ROWS * h
                surf_ref[at : at + ROWS, :] = value

    joined = [
        join_edges(
            geo,
            recv_ref[left, HEAD + ROWS * q : HEAD + ROWS * (q + 1), :],
            recv_ref[right, HEAD + ROWS * q : HEAD + ROWS * (q + 1), :],
        )
        for q in range(pack_count)
    ]
    for plane in range(planes):
        for h in range(2):
            at = pl.ds(plane * 16 + ROWS * h, ROWS)
            avg_ref[at, :] = geo.sum_y(
                moved_ref[at, :], outer_edges(joined, 2 * plane + h)
            )

    def line(r):
        return avg_ref[pl.ds(r, planes, stride=16), :]

    def surf_line(number, r):
        return surf_ref[pl.ds(4 * ROWS * number + r, 2, stride=16), :]

    def first_step(get, mass_at):
        return (
            [
                get(1) / mass_at(1),
                get(2) / mass_at(2),
                (get(3) + get(4)) / (mass_at(3) + mass_at(4)),
            ],
            [
                (get(11) + get(12)) / (mass_at(11) + mass_at(12)),
                get(13) / mass_at(13),
                get(14) / mass_at(14),
            ],
        )

    def own_mass_sum(r):
        return surf_ref[4 * ROWS * MASS_SUM + r : 4 * ROWS * MASS_SUM + r + 1, :]

    low_lines, high_lines = first_step(line, own_mass_sum)
    surf_low, surf_high = first_step(
        functools.partial(surf_line, AVG), functools.partial(surf_line, MASS_SUM)
    )
    for out_ref, r, lines, surf_lines, coefs in (
        (down_ref, 0, low_lines, surf_low, deriv_table[0][1:]),
        (up_ref, 15, high_lines, surf_high, deriv_table[3][:3]),
    ):
        slope = sum(coef * value for coef, value in zip(coefs, lines))
        surf_slope = sum(coef * value for coef, value in zip(coefs, surf_lines))
        mass = surf_ref[4 * ROWS * MASS + r : 4 * ROWS * MASS + r + 1, :]
        wind = time_step * mass * wind_ref[pl.ds(r, 2 * levels, stride=16), :]
        out_ref[0:planes, :] = line(r)
        for first in range(0, planes, levels):
            out_ref[planes + first : planes + first + levels, :] = (
                wind[:levels] * slope[first : first + levels]
            )
        base = 2 * planes
        out_ref[base : base + 2 * levels, :] = wind
        base += 2 * levels
        for number in range(SURF_ARRAYS):
            out_ref[base + 2 * number : base + 2 * number + 2, :] = surf_line(number, r)
        base += 2 * SURF_ARRAYS
        out_ref[base : base + 2, :] = surf_line(COEF_X, r) * surf_slope


def second_kernel(
    planes,
    avg_ref,
    surf_ref,
    low_ref,
    high_ref,
    wind_ref,
    rows_ref,
    slab_ref,
    sums_ref,
    final_ref,
    inverse_ref,
    low_halo,
    high_halo,
):
    geo = Geometry()
    blocks = rows_ref.shape[0]
    left, right = neighbours_of(blocks)
    levels = wind_ref.shape[0] // 32
    base = 2 * planes + 2 * levels

    def surf_tile(number, tile, h):
        at = 4 * ROWS * number + 2 * ROWS * tile + ROWS * h
        return surf_ref[at : at + ROWS, :]

    def beside(ref, number, tile):
        at = base + 2 * number + tile
        return spread(ref[at : at + 1, :])

    ends = []
    inverse = []
    for tile in range(2):
        total = geo.sum_x(
            surf_tile(MASS_SUM, tile, 0),
            surf_tile(MASS_SUM, tile, 1),
            beside(low_ref, MASS_SUM, tile),
            beside(high_ref, MASS_SUM, tile),
        )
        inverse.append([1.0 / value for value in total])
        summed = geo.sum_x(
            surf_tile(AVG, tile, 0),
            surf_tile(AVG, tile, 1),
            beside(low_ref, AVG, tile),
            beside(high_ref, AVG, tile),
        )
        fields = [value * scale for value, scale in zip(summed, inverse[tile])]
        moved = []
        for h in range(2):
            field = fields[h]
            moved.append(
                surf_tile(MASS, tile, h)
                * (field + relax_rate * (surf_tile(SURF, tile, h) - field))
                - surf_tile(COEF_X, tile, h) * geo.d_x(field)
                - surf_tile(COEF_Y, tile, h) * geo.d_y(field)
            )
        halos = []
        for ref, field, own_coef in (
            (low_ref, spread(fields[0][:1]), deriv_table[3][3]),
            (high_ref, spread(fields[1][ROWS - 1 :]), deriv_table[0][0]),
        ):
            halos.append(
                beside(ref, MASS, tile)
                * (field + relax_rate * (beside(ref, SURF, tile) - field))
                - beside(ref, SURF_ARRAYS, tile)
                - beside(ref, COEF_X, tile) * (own_coef * field)
                - beside(ref, COEF_Y, tile) * geo.d_y(field)
            )
        ends.append(geo.sum_x(moved[0], moved[1], halos[0], halos[1]))
    final = []
    for h in range(2):
        summed, _ = geo.sum_y_pair(ends[0][h], ends[1][h])
        final.append(summed * inverse[0][h])
        final_ref[ROWS * h : ROWS * (h + 1), :] = final[h]
        inverse_ref[ROWS * h : ROWS * (h + 1), :] = inverse[0][h]
    flux = [final[h] - surf_tile(SURF, 0, h) for h in range(2)]
    for group in range(blocks // ROWS):
        ids = rows_ref[ROWS * group : ROWS * (group + 1), :]
        high, low = ids >> 7, ids & (LANES - 1)
        picked = jnp.zeros((ROWS, LANES), jnp.float32)
        for x in range(2 * ROWS):
            line = spread(flux[x // ROWS][x % ROWS : x % ROWS + 1])
            picked = jnp.where(high == x, take(line, low, 1), picked)
        for c in range(ROWS):
            slab_ref[ROWS * group + c, 0:1, :] = picked[c : c + 1]

    for ref, halo, r, own_coef, scale in (
        (low_ref, low_halo, 0, deriv_table[3][3], inverse[0][0][:1]),
        (high_ref, high_halo, 15, deriv_table[0][0], inverse[0][1][ROWS - 1 :]),
    ):
        field = (avg_ref[pl.ds(r, planes, stride=16), :] + ref[0:planes, :]) * scale
        mass = beside(ref, MASS, 0)
        for first in range(0, planes, ROWS):
            part = field[first : first + ROWS]
            wind_at = 2 * planes + first % levels
            halo[first : first + ROWS, :] = (
                mass * part
                - ref[planes + first : planes + first + ROWS, :]
                - ref[wind_at : wind_at + ROWS, :] * (own_coef * part)
                - ref[wind_at + levels : wind_at + levels + ROWS, :] * geo.d_y(part)
            )

    mass = [surf_tile(MASS, 0, h) for h in range(2)]
    packs = [
        jnp.zeros((ROWS, LANES), jnp.float32) for _ in range(-(-2 * planes // PAIRS))
    ]
    for level in range(levels):
        wind = [
            [
                time_step * wind_ref[pl.ds((i * levels + level) * 16 + ROWS * h, ROWS), :]
                for h in range(2)
            ]
            for i in range(2)
        ]
        for plane in range(level, planes, levels):
            summed = geo.sum_x(
                avg_ref[pl.ds(plane * 16, ROWS), :],
                avg_ref[pl.ds(plane * 16 + ROWS, ROWS), :],
                spread(low_ref[plane : plane + 1, :]),
                spread(high_ref[plane : plane + 1, :]),
            )
            moved = []
            for h in range(2):
                field = summed[h] * inverse[0][h]
                moved.append(
                    mass[h]
                    * (
                        field
                        - (wind[0][h] * geo.d_x(field) + wind[1][h] * geo.d_y(field))
                    )
                )
            summed = geo.sum_x(
                moved[0],
                moved[1],
                spread(low_halo[plane : plane + 1, :]),
                spread(high_halo[plane : plane + 1, :]),
            )
            for h in range(2):
                sums_ref[pl.ds(plane * 16 + ROWS * h, ROWS), :] = summed[h]
                pack_edges(geo, packs, summed[h], 2 * plane + h)
    for to in (left, right):
        for q, pack in enumerate(packs):
            slab_ref[to, HEAD + ROWS * q : HEAD + ROWS * (q + 1), :] = pack


def end_kernel(
    planes,
    sums_ref,
    recv_ref,
    final_ref,
    inverse_ref,
    cols_ref,
    weights_ref,
    area_ref,
    ocean_ref,
    air_out,
    ocean_out,
):
    geo = Geometry()
    blocks = cols_ref.shape[0]
    left, right = neighbours_of(blocks)
    chunks = area_ref.shape[0]
    arrived = jnp.concatenate([recv_ref[c, 0:1, :] for c in range(blocks)], axis=0)
    (inflow,) = scatter_sum([weights_ref[...] * arrived], cols_ref[...], chunks)
    gain = flux_gain * inflow / area_ref[...]
    ocean_out[...] = ocean_ref[...]
    for k in range(chunks):
        at = slice(LANES * k, LANES * (k + 1))
        ocean_out[0:1, at] = ocean_ref[0:1, at] + gain[k : k + 1]

    joined = [
        join_edges(
            geo,
            recv_ref[left, HEAD + ROWS * q : HEAD + ROWS * (q + 1), :],
            recv_ref[right, HEAD + ROWS * q : HEAD + ROWS * (q + 1), :],
        )
        for q in range(-(-2 * planes // PAIRS))
    ]
    inverse = [inverse_ref[ROWS * h : ROWS * (h + 1), :] for h in range(2)]
    for plane in range(planes):
        for h in range(2):
            at = pl.ds(plane * 16 + ROWS * h, ROWS)
            if plane == 0:
                air_out[at, :] = final_ref[ROWS * h : ROWS * (h + 1), :]
            else:
                air_out[at, :] = inverse[h] * geo.sum_y(
                    sums_ref[at, :], outer_edges(joined, 2 * plane + h)
                )


def gathered(ids, coefs, source, sources, groups, first=0):
    totals = [jnp.zeros((ROWS, LANES), jnp.float32) for _ in range(groups)]
    for edge in range(ids.shape[0]):
        cell = spread(ids[edge : edge + 1])
        coef = spread(coefs[edge : edge + 1])
        high, low = cell >> 7, cell & (LANES - 1)
        for s in range(sources):
            scaled = jnp.where(high == first + s, coef, 0.0)
            for group in range(groups):
                totals[group] += scaled * take(source(group, s), low, 1)
    return totals


def ocean_kernel(levels, tracers_ref, coef_ref, near_ref, rate_ref, out_ref):
    chunks = tracers_ref.shape[1] // LANES
    groups = tracers_ref.shape[0] // ROWS
    row = iota((ROWS, LANES), 0)

    def source(group, s):
        return tracers_ref[
            ROWS * group : ROWS * (group + 1), LANES * s : LANES * (s + 1)
        ]

    def one_chunk(k, carry):
        at = pl.ds(pl.multiple_of(k * LANES, LANES), LANES)
        ids, coefs = near_ref[:, at], coef_ref[:, at]
        totals = gathered(ids, coefs, source, chunks, groups)
        coef_sum = spread(jnp.sum(coefs, axis=0, keepdims=True))
        rate = spread(rate_ref[pl.ds(k, 1), :])
        tiles = [tracers_ref[ROWS * g : ROWS * (g + 1), at] for g in range(groups)]
        for g in range(groups):
            tile = tiles[g]
            above = pltpu.roll(tile, 1, 0)
            below = pltpu.roll(tile, ROWS - 1, 0)
            top = tile
            if (ROWS * g) % levels:
                top = pltpu.roll(tiles[g - 1], 1, 0)
            bottom = tile
            if (ROWS * (g + 1)) % levels:
                bottom = pltpu.roll(tiles[g + 1], ROWS - 1, 0)
            above = jnp.where(row == 0, top, above)
            below = jnp.where(row == ROWS - 1, bottom, below)
            vertical = rate * ((above - tile) + (below - tile))
            out_ref[ROWS * g : ROWS * (g + 1), at] = (
                tile + (totals[g] - coef_sum * tile) + vertical
            )
        return carry

    lax.fori_loop(0, chunks, one_chunk, 0)


def rim_kernel(rim_at, partial_ref, recv_ref, coef_ref, near_ref, out_ref):
    chunks = partial_ref.shape[1] // LANES
    groups = partial_ref.shape[0] // ROWS
    sides = neighbours_of(recv_ref.shape[0])

    def source(group, s):
        return recv_ref[sides[s], rim_at + ROWS * group : rim_at + ROWS * (group + 1), :]

    for k in range(chunks):
        at = slice(LANES * k, LANES * (k + 1))
        totals = gathered(near_ref[:, at], coef_ref[:, at], source, 2, groups, chunks)
        for g in range(groups):
            half = slice(ROWS * g, ROWS * (g + 1))
            out_ref[half, at] = partial_ref[half, at] + totals[g]


def call(kernel, outs, scratch=(), aliases=None):
    return pl.pallas_call(
        kernel,
        out_shape=[jax.ShapeDtypeStruct(shape, jnp.float32) for shape in outs],
        scratch_shapes=[pltpu.VMEM(shape, jnp.float32) for shape in scratch],
        input_output_aliases=aliases or {},
        compiler_params=pltpu.CompilerParams(vmem_limit_bytes=32 * 2**20),
        name=getattr(kernel, "func", kernel).__name__,
    )


def body(
    air_state,
    air_wind,
    jacobian,
    land_area,
    xgrid_rows,
    tracers,
    edge_coef,
    neighbours,
    vert_rate,
    ocean_area,
    send_list,
    xgrid_cols,
    xgrid_weights,
):
    field_count, levels, x_points, y_points = air_state.shape
    planes = field_count * levels
    ocean_levels, cells = tracers.shape[1:]
    ocean_planes = tracers.shape[0] * ocean_levels
    faces, blocks = lax.axis_size("face"), lax.axis_size("blk")
    air = air_state.reshape(planes * x_points, y_points)
    wind = air_wind.reshape(2 * levels * x_points, y_points)
    ocean = tracers.reshape(ocean_planes, cells)
    point_ids, cell_ids, weights = xgrid_rows[0], xgrid_cols[0], xgrid_weights[0]
    rate = vert_rate.reshape(cells // LANES, LANES)
    area = ocean_area.reshape(cells // LANES, LANES)
    edge_rows = ROWS * (-(-2 * planes // PAIRS))
    rim_at = HEAD + edge_rows + 2 * ROWS + blocks

    slab, moved = call(
        functools.partial(start_kernel, planes),
        [(blocks, rim_at + ocean_planes, LANES), air.shape],
    )(
        air,
        wind,
        jacobian,
        land_area,
        point_ids,
        ocean,
        send_list,
        cell_ids,
        weights,
    )
    recv = lax.all_to_all(slab, "blk", split_axis=0, concat_axis=0, tiled=True)
    (partial,) = call(
        functools.partial(ocean_kernel, ocean_levels), [ocean.shape]
    )(ocean, edge_coef, neighbours, rate)

    side_rows = 2 * planes + 2 * levels + 2 * SURF_ARRAYS + 4
    avg, down, up, surf = call(
        functools.partial(panel_kernel, planes),
        [air.shape, (side_rows, LANES), (side_rows, LANES), (4 * ROWS * SURF_ARRAYS, LANES)],
    )(moved, recv, air, wind, jacobian, land_area, point_ids)
    ring = [(i, (i + 1) % faces) for i in range(faces)]
    low = lax.ppermute(up, "face", ring)
    high = lax.ppermute(down, "face", [(target, source) for source, target in ring])
    (partial,) = call(functools.partial(rim_kernel, rim_at), [ocean.shape])(
        partial, recv, edge_coef, neighbours
    )

    slab, sums, final, inverse = call(
        functools.partial(second_kernel, planes),
        [
            (blocks, HEAD + edge_rows, LANES),
            air.shape,
            (x_points, y_points),
            (x_points, y_points),
        ],
        scratch=[(planes, LANES), (planes, LANES)],
    )(avg, surf, low, high, wind, point_ids)
    recv = lax.all_to_all(slab, "blk", split_axis=0, concat_axis=0, tiled=True)
    air_final, ocean_final = call(
        functools.partial(end_kernel, planes), [air.shape, ocean.shape]
    )(sums, recv, final, inverse, cell_ids, weights, area, partial)
    return air_final.reshape(air_state.shape), ocean_final.reshape(tracers.shape)


def solution(mesh):
    return jax.shard_map(
        body,
        mesh=mesh,
        in_specs=(
            P(None, None, "face", "blk"),
            P(None, None, "face", "blk"),
            P("face", "blk"),
            P("face", "blk"),
            P(("face", "blk"), None, None),
            P(None, None, ("face", "blk")),
            P(None, ("face", "blk")),
            P(None, ("face", "blk")),
            P(("face", "blk")),
            P(("face", "blk")),
            P(("face", "blk"), None),
            P(("face", "blk"), None, None),
            P(("face", "blk"), None, None),
        ),
        out_specs=(P(None, None, "face", "blk"), P(None, None, ("face", "blk"))),
        check_vma=False,
    )
```

```python
import functools

import jax
import jax.numpy as jnp
from jax import lax
from jax.experimental import pallas as pl
from jax.experimental.pallas import tpu as pltpu
from jax.sharding import PartitionSpec as P

GLL = 4
ROWS = 8
LANES = 128

deriv_table = [
    [-3.0, 4.045084971874737, -1.545084971874737, 0.5],
    [-0.8090169943749475, 0.0, 1.118033988749895, -0.30901699437494745],
    [0.30901699437494745, -1.118033988749895, 0.0, 0.8090169943749475],
    [-0.5, 1.545084971874737, -4.045084971874737, 3.0],
]
time_step = 0.05
relax_rate = 0.3
flux_gain = 0.2

PAIRS = LANES // 2
HEAD = 8
AVG, MASS_SUM, MASS, COEF_X, COEF_Y, SURF = range(6)
SURF_ARRAYS = 6


def iota(shape, dim):
    return lax.broadcasted_iota(jnp.int32, shape, dim)


def take(values, index, axis):
    return jnp.take_along_axis(values, index, axis=axis, mode="promise_in_bounds")


def by_position(pos, values):
    result = jnp.full(pos.shape, values[-1], jnp.float32)
    for i, value in enumerate(values[:-1]):
        result = jnp.where(pos == i, value, result)
    return result


def spread(row):
    return jnp.broadcast_to(row, (ROWS, LANES))


class Geometry:
    def __init__(self):
        shape = (ROWS, LANES)
        self.row, self.lane = iota(shape, 0), iota(shape, 1)
        x_pos, y_pos = self.row & (GLL - 1), self.lane & (GLL - 1)
        self.y_from = [self.lane - y_pos + j for j in range(GLL)]
        columns = [[line[j] for line in deriv_table] for j in range(GLL)]
        self.x_coef = {
            step: by_position(
                x_pos,
                [
                    deriv_table[i][i + step] if 0 <= i + step < GLL else 0.0
                    for i in range(GLL)
                ],
            )
            for step in range(1 - GLL, GLL)
        }
        self.y_coef = [by_position(y_pos, column) for column in columns]
        self.y_swap = (
            self.lane + jnp.where(y_pos == GLL - 1, 1, 0) - jnp.where(y_pos == 0, 1, 0)
        ) & (LANES - 1)
        self.x_edge = (x_pos == 0) | (x_pos == GLL - 1)
        self.y_edge = (y_pos == 0) | (y_pos == GLL - 1)
        self.first_row, self.last_row = self.row == 0, self.row == ROWS - 1
        self.middle_row = self.row == GLL
        self.outer_lane = (self.lane == 0) | (self.lane == LANES - 1)
        self.weight = jnp.where(self.x_edge, 1.0 / 6.0, 5.0 / 6.0) * jnp.where(
            self.y_edge, 1.0 / 6.0, 5.0 / 6.0
        )

    def d_x(self, tile):
        return sum(
            coef * (pltpu.roll(tile, -step % ROWS, 0) if step else tile)
            for step, coef in self.x_coef.items()
        )

    def d_y(self, *tiles):
        totals = [0.0] * len(tiles)
        for j in range(GLL):
            for i, tile in enumerate(tiles):
                totals[i] += self.y_coef[j] * take(tile, self.y_from[j], 1)
        return totals

    def sum_x(self, low, high, before, after):
        low_down, low_up = pltpu.roll(low, 1, 0), pltpu.roll(low, ROWS - 1, 0)
        high_down, high_up = pltpu.roll(high, 1, 0), pltpu.roll(high, ROWS - 1, 0)
        low_other = jnp.where(
            self.first_row,
            before,
            jnp.where(
                self.middle_row, low_down, jnp.where(self.last_row, high_up, low_up)
            ),
        )
        high_other = jnp.where(
            self.first_row,
            low_down,
            jnp.where(
                self.middle_row, high_down, jnp.where(self.last_row, after, high_up)
            ),
        )
        return (
            low + jnp.where(self.x_edge, low_other, 0.0),
            high + jnp.where(self.x_edge, high_other, 0.0),
        )

    def sum_y(self, tile, outer):
        other = jnp.where(self.outer_lane, outer, take(tile, self.y_swap, 1))
        return tile + jnp.where(self.y_edge, other, 0.0)

    def sum_y_pair(self, own, strip):
        own_swap, strip_swap = take(own, self.y_swap, 1), take(strip, self.y_swap, 1)
        own_other = jnp.where(self.outer_lane, strip_swap, own_swap)
        strip_other = jnp.where(self.outer_lane, own_swap, strip_swap)
        return (
            own + jnp.where(self.y_edge, own_other, 0.0),
            strip + jnp.where(self.y_edge, strip_other, 0.0),
        )


def pack_edges(geo, packs, tile, number):
    at = number % PAIRS
    rolled = pltpu.roll(tile, (2 * at + 1) % LANES, 1)
    packs[number // PAIRS] = jnp.where(
        (geo.lane >> 1) == at, rolled, packs[number // PAIRS]
    )


def join_edges(geo, from_left, from_right):
    odd = (geo.lane & 1) == 1
    return jnp.where(
        odd, pltpu.roll(from_left, 1, 1), pltpu.roll(from_right, LANES - 1, 1)
    )


def outer_edges(joined, number):
    at = number % PAIRS
    return pltpu.roll(joined[number // PAIRS], (-(2 * at + 1)) % LANES, 1)


def neighbours_of(blocks):
    here = lax.axis_index("blk")
    return lax.rem(here + blocks - 1, blocks), lax.rem(here + 1, blocks)


def scatter_sum(lines, index, bins, allowed=None):
    count = index.shape[0]
    split = []
    for values in lines:
        for part in range(3):
            short = values.astype(jnp.bfloat16).astype(jnp.float32)
            split.append(short)
            values = values - short
    high, low = index >> 7, index & (LANES - 1)
    bin_at = iota((bins, LANES), 0)
    lane_at = iota((LANES, LANES), 0)
    if allowed is not None:
        lane_at = jnp.where(allowed(lane_at), lane_at, -1)
    left, right = [], []
    for c in range(count):
        hit = bin_at == high[c : c + 1]
        left.append(
            jnp.concatenate(
                [jnp.where(hit, part[c : c + 1], 0.0) for part in split], axis=0
            ).astype(jnp.bfloat16)
        )
        right.append(
            jnp.where(lane_at == low[c : c + 1], 1.0, 0.0).astype(jnp.bfloat16)
        )
    total = lax.dot_general(
        jnp.concatenate(left, axis=1),
        jnp.concatenate(right, axis=1),
        (((1,), (1,)), ((), ())),
        preferred_element_type=jnp.float32,
    )
    sums = []
    for i in range(len(lines)):
        part = total[3 * i * bins : 3 * (i + 1) * bins]
        sums.append(part[:bins] + part[bins : 2 * bins] + part[2 * bins :])
    return sums


def start_kernel(planes, inputs, *refs):
    sources, (slab_ref, moved_ref), held = (
        refs[:inputs],
        refs[inputs : inputs + 2],
        refs[inputs + 2 : -1],
    )
    copies = [
        pltpu.make_async_copy(source, target, refs[-1].at[i])
        for i, (source, target) in enumerate(zip(sources, held))
    ]
    for copy in copies:
        copy.start()
    (
        cols_ref,
        weights_ref,
        tracers_ref,
        send_ref,
        rows_ref,
        jac_ref,
        land_ref,
        wind_ref,
        air_ref,
    ) = held
    for copy in copies[:4]:
        copy.wait()
    geo = Geometry()
    blocks = cols_ref.shape[0]
    left, right = neighbours_of(blocks)
    levels = wind_ref.shape[0] // 32
    chunks = tracers_ref.shape[1] // LANES

    def source(group, chunk):
        return tracers_ref[
            ROWS * group : ROWS * (group + 1), LANES * chunk : LANES * (chunk + 1)
        ]

    for group in range(blocks // ROWS):
        at = slice(ROWS * group, ROWS * (group + 1))
        cells = cols_ref[at, :]
        high, low = cells >> 7, cells & (LANES - 1)
        surface = jnp.zeros((ROWS, LANES), jnp.float32)
        for k in range(chunks):
            line = spread(tracers_ref[0:1, LANES * k : LANES * (k + 1)])
            surface = jnp.where(high == k, take(line, low, 1), surface)
        area = weights_ref[at, :]
        heat = area * surface
        for c in range(ROWS):
            owner = ROWS * group + c
            for place, step in enumerate((1, 0, -1)):
                to = (owner + step) % blocks
                slab_ref[to, 2 * place : 2 * place + 1, :] = heat[c : c + 1]
                slab_ref[to, 2 * place + 1 : 2 * place + 2, :] = area[c : c + 1]

    base = HEAD + ROWS * (-(-2 * planes // PAIRS)) + 2 * ROWS + blocks
    for part, to in enumerate((left, right)):
        cells = spread(send_ref[0:1, LANES * part : LANES * (part + 1)])
        high, low = cells >> 7, cells & (LANES - 1)
        for group in range(tracers_ref.shape[0] // ROWS):
            rim = jnp.zeros((ROWS, LANES), jnp.float32)
            for k in range(chunks):
                rim = jnp.where(high == k, take(source(group, k), low, 1), rim)
            slab_ref[to, base + ROWS * group : base + ROWS * (group + 1), :] = rim

    for copy in copies[4:]:
        copy.wait()
    mass = [geo.weight * jac_ref[ROWS * h : ROWS * (h + 1), :] for h in range(2)]
    packs = [
        jnp.zeros((ROWS, LANES), jnp.float32) for _ in range(-(-2 * planes // PAIRS))
    ]
    for level in range(levels):
        wind = [
            [
                time_step * wind_ref[pl.ds((i * levels + level) * 16 + ROWS * h, ROWS), :]
                for h in range(2)
            ]
            for i in range(2)
        ]
        places = [
            (plane, h) for plane in range(level, planes, levels) for h in range(2)
        ]
        fields = [air_ref[pl.ds(plane * 16 + ROWS * h, ROWS), :] for plane, h in places]
        for (plane, h), field, slope in zip(places, fields, geo.d_y(*fields)):
            moved = mass[h] * (
                field - (wind[0][h] * geo.d_x(field) + wind[1][h] * slope)
            )
            moved_ref[pl.ds(plane * 16 + ROWS * h, ROWS), :] = moved
            pack_edges(geo, packs, moved, 2 * plane + h)

    base = HEAD
    edge_rows = ROWS * len(packs)
    for to in (left, right):
        for q, pack in enumerate(packs):
            slab_ref[to, base + ROWS * q : base + ROWS * (q + 1), :] = pack
    base += edge_rows
    for h in range(2):
        half = slice(ROWS * h, ROWS * (h + 1))
        strips = [
            air_ref[half, :],
            wind_ref[half, :],
            wind_ref[levels * 16 + ROWS * h : levels * 16 + ROWS * (h + 1), :],
            jac_ref[half, :],
            land_ref[half, :],
        ]
        pack = jnp.zeros((ROWS, LANES), jnp.float32)
        for i, strip in enumerate(strips):
            pack = jnp.where(
                (geo.lane >> 4) == i, pltpu.roll(strip, 16 * i + 8, 1), pack
            )
        for to in (left, right):
            slab_ref[to, base + ROWS * h : base + ROWS * (h + 1), :] = pack
    base += 2 * ROWS
    ids = rows_ref[...].astype(jnp.float32)
    for to in (left, right):
        slab_ref[to, base : base + blocks, :] = ids


def panel_kernel(
    planes,
    moved_ref,
    recv_ref,
    air_ref,
    wind_ref,
    jac_ref,
    land_ref,
    rows_ref,
    after_ref,
    avg_ref,
    down_ref,
    up_ref,
    surf_ref,
):
    geo = Geometry()
    blocks = rows_ref.shape[0]
    left, right = neighbours_of(blocks)
    levels = wind_ref.shape[0] // 32
    pack_count = -(-2 * planes // PAIRS)
    base = HEAD + ROWS * pack_count

    ids_at = base + 2 * ROWS
    own_ids = rows_ref[...]
    left_ids = recv_ref[left, ids_at : ids_at + blocks, :].astype(jnp.int32)
    right_ids = recv_ref[right, ids_at : ids_at + blocks, :].astype(jnp.int32)
    head = [
        jnp.concatenate([recv_ref[c, i : i + 1, :] for c in range(blocks)], axis=0)
        for i in range(6)
    ]
    heat, frac = scatter_sum(head[2:4], own_ids, 2 * ROWS)
    from_left = scatter_sum(
        head[0:2], left_ids, 2 * ROWS, lambda lane: lane >= LANES - ROWS
    )
    from_right = scatter_sum(head[4:6], right_ids, 2 * ROWS, lambda lane: lane < ROWS)
    strip_heat = from_left[0] + from_right[0]
    strip_frac = from_left[1] + from_right[1]

    in_strip = (geo.lane < ROWS) | (geo.lane >= LANES - ROWS)
    own, strip = [], []
    for h in range(2):
        half = slice(ROWS * h, ROWS * (h + 1))
        pack = jnp.where(
            ((geo.lane >> 3) & 1) == 1,
            recv_ref[right, base + ROWS * h : base + ROWS * (h + 1), :],
            recv_ref[left, base + ROWS * h : base + ROWS * (h + 1), :],
        )
        strip.append(
            [
                jnp.where(
                    in_strip, pltpu.roll(pack, (-(16 * i + 8)) % LANES, 1), 1.0
                )
                for i in range(5)
            ]
        )
        own.append(
            [
                air_ref[half, :],
                wind_ref[half, :],
                wind_ref[levels * 16 + ROWS * h : levels * 16 + ROWS * (h + 1), :],
                jac_ref[half, :],
                land_ref[half, :],
            ]
        )
    for h in range(2):
        half = slice(ROWS * h, ROWS * (h + 1))
        pair = []
        for tile, ((field, wind_x, wind_y, jac, land), tile_heat, tile_frac) in enumerate(
            ((own[h], heat[half], frac[half]), (strip[h], strip_heat[half], strip_frac[half]))
        ):
            mass = geo.weight * jac
            if tile == 1:
                tile_heat = jnp.where(in_strip, tile_heat, 0.0)
                tile_frac = jnp.where(in_strip, tile_frac, 0.0)
            surf = (tile_heat + land * field) / (tile_frac + land)
            coef_x, coef_y = time_step * mass * wind_x, time_step * mass * wind_y
            moved = (
                mass * (field + relax_rate * (surf - field))
                - coef_x * geo.d_x(field)
                - coef_y * geo.d_y(field)[0]
            )
            pair.append((moved, mass))
            at = 2 * ROWS * tile + ROWS * h
            for number, value in (
                (MASS, mass),
                (COEF_X, coef_x),
                (COEF_Y, coef_y),
                (SURF, surf),
            ):
                surf_ref[4 * ROWS * number + at : 4 * ROWS * number + at + ROWS, :] = value
        for number, i in ((AVG, 0), (MASS_SUM, 1)):
            for tile, value in enumerate(geo.sum_y_pair(pair[0][i], pair[1][i])):
                at = 4 * ROWS * number + 2 * ROWS * tile + ROWS * h
                surf_ref[at : at + ROWS, :] = value

    joined = [
        join_edges(
            geo,
            recv_ref[left, HEAD + ROWS * q : HEAD + ROWS * (q + 1), :],
            recv_ref[right, HEAD + ROWS * q : HEAD + ROWS * (q + 1), :],
        )
        for q in range(pack_count)
    ]
    for plane in range(planes):
        for h in range(2):
            at = pl.ds(plane * 16 + ROWS * h, ROWS)
            avg_ref[at, :] = geo.sum_y(
                moved_ref[at, :], outer_edges(joined, 2 * plane + h)
            )

    def line(r):
        return avg_ref[pl.ds(r, planes, stride=16), :]

    def surf_line(number, r):
        return surf_ref[pl.ds(4 * ROWS * number + r, 2, stride=16), :]

    def first_step(get, mass_at):
        return (
            [
                get(1) / mass_at(1),
                get(2) / mass_at(2),
                (get(3) + get(4)) / (mass_at(3) + mass_at(4)),
            ],
            [
                (get(11) + get(12)) / (mass_at(11) + mass_at(12)),
                get(13) / mass_at(13),
                get(14) / mass_at(14),
            ],
        )

    def own_mass_sum(r):
        return surf_ref[4 * ROWS * MASS_SUM + r : 4 * ROWS * MASS_SUM + r + 1, :]

    low_lines, high_lines = first_step(line, own_mass_sum)
    surf_low, surf_high = first_step(
        functools.partial(surf_line, AVG), functools.partial(surf_line, MASS_SUM)
    )
    for out_ref, r, lines, surf_lines, coefs in (
        (down_ref, 0, low_lines, surf_low, deriv_table[0][1:]),
        (up_ref, 15, high_lines, surf_high, deriv_table[3][:3]),
    ):
        slope = sum(coef * value for coef, value in zip(coefs, lines))
        surf_slope = sum(coef * value for coef, value in zip(coefs, surf_lines))
        mass = surf_ref[4 * ROWS * MASS + r : 4 * ROWS * MASS + r + 1, :]
        wind = time_step * mass * wind_ref[pl.ds(r, 2 * levels, stride=16), :]
        out_ref[0:planes, :] = line(r)
        for first in range(0, planes, levels):
            out_ref[planes + first : planes + first + levels, :] = (
                wind[:levels] * slope[first : first + levels]
            )
        base = 2 * planes
        out_ref[base : base + 2 * levels, :] = wind
        base += 2 * levels
        for number in range(SURF_ARRAYS):
            out_ref[base + 2 * number : base + 2 * number + 2, :] = surf_line(number, r)
        base += 2 * SURF_ARRAYS
        out_ref[base : base + 2, :] = surf_line(COEF_X, r) * surf_slope


def second_kernel(
    planes,
    avg_ref,
    surf_ref,
    low_ref,
    high_ref,
    wind_ref,
    rows_ref,
    after_ref,
    slab_ref,
    sums_ref,
    final_ref,
    inverse_ref,
    low_halo,
    high_halo,
):
    geo = Geometry()
    blocks = rows_ref.shape[0]
    left, right = neighbours_of(blocks)
    levels = wind_ref.shape[0] // 32
    base = 2 * planes + 2 * levels

    def surf_tile(number, tile, h):
        at = 4 * ROWS * number + 2 * ROWS * tile + ROWS * h
        return surf_ref[at : at + ROWS, :]

    def beside(ref, number, tile):
        at = base + 2 * number + tile
        return spread(ref[at : at + 1, :])

    ends = []
    inverse = []
    for tile in range(2):
        total = geo.sum_x(
            surf_tile(MASS_SUM, tile, 0),
            surf_tile(MASS_SUM, tile, 1),
            beside(low_ref, MASS_SUM, tile),
            beside(high_ref, MASS_SUM, tile),
        )
        inverse.append([1.0 / value for value in total])
        summed = geo.sum_x(
            surf_tile(AVG, tile, 0),
            surf_tile(AVG, tile, 1),
            beside(low_ref, AVG, tile),
            beside(high_ref, AVG, tile),
        )
        fields = [value * scale for value, scale in zip(summed, inverse[tile])]
        moved = []
        for h in range(2):
            field = fields[h]
            moved.append(
                surf_tile(MASS, tile, h)
                * (field + relax_rate * (surf_tile(SURF, tile, h) - field))
                - surf_tile(COEF_X, tile, h) * geo.d_x(field)
                - surf_tile(COEF_Y, tile, h) * geo.d_y(field)[0]
            )
        halos = []
        for ref, field, own_coef in (
            (low_ref, spread(fields[0][:1]), deriv_table[3][3]),
            (high_ref, spread(fields[1][ROWS - 1 :]), deriv_table[0][0]),
        ):
            halos.append(
                beside(ref, MASS, tile)
                * (field + relax_rate * (beside(ref, SURF, tile) - field))
                - beside(ref, SURF_ARRAYS, tile)
                - beside(ref, COEF_X, tile) * (own_coef * field)
                - beside(ref, COEF_Y, tile) * geo.d_y(field)[0]
            )
        ends.append(geo.sum_x(moved[0], moved[1], halos[0], halos[1]))
    final = []
    for h in range(2):
        summed, _ = geo.sum_y_pair(ends[0][h], ends[1][h])
        final.append(summed * inverse[0][h])
        final_ref[ROWS * h : ROWS * (h + 1), :] = final[h]
        inverse_ref[ROWS * h : ROWS * (h + 1), :] = inverse[0][h]
    flux = [final[h] - surf_tile(SURF, 0, h) for h in range(2)]
    for group in range(blocks // ROWS):
        ids = rows_ref[ROWS * group : ROWS * (group + 1), :]
        high, low = ids >> 7, ids & (LANES - 1)
        picked = jnp.zeros((ROWS, LANES), jnp.float32)
        for x in range(2 * ROWS):
            line = spread(flux[x // ROWS][x % ROWS : x % ROWS + 1])
            picked = jnp.where(high == x, take(line, low, 1), picked)
        for c in range(ROWS):
            slab_ref[ROWS * group + c, 0:1, :] = picked[c : c + 1]

    for ref, halo, r, own_coef, scale in (
        (low_ref, low_halo, 0, deriv_table[3][3], inverse[0][0][:1]),
        (high_ref, high_halo, 15, deriv_table[0][0], inverse[0][1][ROWS - 1 :]),
    ):
        field = (avg_ref[pl.ds(r, planes, stride=16), :] + ref[0:planes, :]) * scale
        mass = beside(ref, MASS, 0)
        for first in range(0, planes, ROWS):
            part = field[first : first + ROWS]
            wind_at = 2 * planes + first % levels
            halo[first : first + ROWS, :] = (
                mass * part
                - ref[planes + first : planes + first + ROWS, :]
                - ref[wind_at : wind_at + ROWS, :] * (own_coef * part)
                - ref[wind_at + levels : wind_at + levels + ROWS, :] * geo.d_y(part)[0]
            )

    mass = [surf_tile(MASS, 0, h) for h in range(2)]
    packs = [
        jnp.zeros((ROWS, LANES), jnp.float32) for _ in range(-(-2 * planes // PAIRS))
    ]
    for level in range(levels):
        wind = [
            [
                time_step * wind_ref[pl.ds((i * levels + level) * 16 + ROWS * h, ROWS), :]
                for h in range(2)
            ]
            for i in range(2)
        ]
        group = list(range(level, planes, levels))
        fields = []
        for plane in group:
            summed = geo.sum_x(
                avg_ref[pl.ds(plane * 16, ROWS), :],
                avg_ref[pl.ds(plane * 16 + ROWS, ROWS), :],
                spread(low_ref[plane : plane + 1, :]),
                spread(high_ref[plane : plane + 1, :]),
            )
            fields += [summed[h] * inverse[0][h] for h in range(2)]
        slopes = geo.d_y(*fields)
        for number, plane in enumerate(group):
            moved = []
            for h in range(2):
                field = fields[2 * number + h]
                moved.append(
                    mass[h]
                    * (
                        field
                        - (
                            wind[0][h] * geo.d_x(field)
                            + wind[1][h] * slopes[2 * number + h]
                        )
                    )
                )
            summed = geo.sum_x(
                moved[0],
                moved[1],
                spread(low_halo[plane : plane + 1, :]),
                spread(high_halo[plane : plane + 1, :]),
            )
            for h in range(2):
                sums_ref[pl.ds(plane * 16 + ROWS * h, ROWS), :] = summed[h]
                pack_edges(geo, packs, summed[h], 2 * plane + h)
    for to in (left, right):
        for q, pack in enumerate(packs):
            slab_ref[to, HEAD + ROWS * q : HEAD + ROWS * (q + 1), :] = pack


def end_kernel(
    planes,
    sums_ref,
    recv_ref,
    final_ref,
    inverse_ref,
    cols_ref,
    weights_ref,
    gain_ref,
    ocean_ref,
    air_out,
    ocean_out,
):
    geo = Geometry()
    blocks = cols_ref.shape[0]
    left, right = neighbours_of(blocks)
    chunks = gain_ref.shape[0]
    arrived = jnp.concatenate([recv_ref[c, 0:1, :] for c in range(blocks)], axis=0)
    (inflow,) = scatter_sum([weights_ref[...] * arrived], cols_ref[...], chunks)
    gain = inflow * gain_ref[...]
    ocean_out[...] = ocean_ref[...]
    for k in range(chunks):
        at = slice(LANES * k, LANES * (k + 1))
        ocean_out[0:1, at] = ocean_ref[0:1, at] + gain[k : k + 1]

    joined = [
        join_edges(
            geo,
            recv_ref[left, HEAD + ROWS * q : HEAD + ROWS * (q + 1), :],
            recv_ref[right, HEAD + ROWS * q : HEAD + ROWS * (q + 1), :],
        )
        for q in range(-(-2 * planes // PAIRS))
    ]
    inverse = [inverse_ref[ROWS * h : ROWS * (h + 1), :] for h in range(2)]
    for plane in range(planes):
        for h in range(2):
            at = pl.ds(plane * 16 + ROWS * h, ROWS)
            if plane == 0:
                air_out[at, :] = final_ref[ROWS * h : ROWS * (h + 1), :]
            else:
                air_out[at, :] = inverse[h] * geo.sum_y(
                    sums_ref[at, :], outer_edges(joined, 2 * plane + h)
                )


def gathered(ids, coefs, source, sources, groups, first=0):
    totals = [jnp.zeros((ROWS, LANES), jnp.float32) for _ in range(groups)]
    for edge in range(ids.shape[0]):
        cell = spread(ids[edge : edge + 1])
        coef = spread(coefs[edge : edge + 1])
        high, low = cell >> 7, cell & (LANES - 1)
        for s in range(sources):
            scaled = jnp.where(high == first + s, coef, 0.0)
            for group in range(groups):
                totals[group] += scaled * take(source(group, s), low, 1)
    return totals


def ocean_kernel(levels, number, tracers_ref, coef_ref, near_ref, rate_ref, after_ref, out_ref):
    chunks = tracers_ref.shape[1] // LANES
    groups = levels // ROWS
    base = levels * number
    row = iota((ROWS, LANES), 0)

    def source(group, s):
        return tracers_ref[
            base + ROWS * group : base + ROWS * (group + 1), LANES * s : LANES * (s + 1)
        ]

    def one_chunk(k, carry):
        at = pl.ds(pl.multiple_of(k * LANES, LANES), LANES)
        ids, coefs = near_ref[:, at], coef_ref[:, at]
        totals = gathered(ids, coefs, source, chunks, groups)
        coef_sum = spread(jnp.sum(coefs, axis=0, keepdims=True))
        rate = spread(rate_ref[pl.ds(k, 1), :])
        tiles = [
            tracers_ref[base + ROWS * g : base + ROWS * (g + 1), at]
            for g in range(groups)
        ]
        for g in range(groups):
            tile = tiles[g]
            above = pltpu.roll(tile, 1, 0)
            below = pltpu.roll(tile, ROWS - 1, 0)
            top = pltpu.roll(tiles[g - 1], 1, 0) if g else tile
            bottom = tile
            if g + 1 < groups:
                bottom = pltpu.roll(tiles[g + 1], ROWS - 1, 0)
            above = jnp.where(row == 0, top, above)
            below = jnp.where(row == ROWS - 1, bottom, below)
            vertical = rate * ((above - tile) + (below - tile))
            out_ref[ROWS * g : ROWS * (g + 1), at] = (
                tile + (totals[g] - coef_sum * tile) + vertical
            )
        return carry

    lax.fori_loop(0, chunks, one_chunk, 0)


def rim_kernel(
    rim_at,
    parts,
    recv_ref,
    coef_ref,
    near_ref,
    area_ref,
    after_ref,
    *refs,
):
    partial_refs, (out_ref, gain_ref) = refs[:parts], refs[parts:]
    chunks = coef_ref.shape[1] // LANES
    groups = out_ref.shape[0] // ROWS
    part_groups = groups // parts
    sides = neighbours_of(recv_ref.shape[0])
    gain_ref[...] = flux_gain / area_ref[...]

    def source(group, s):
        return recv_ref[sides[s], rim_at + ROWS * group : rim_at + ROWS * (group + 1), :]

    for k in range(chunks):
        at = slice(LANES * k, LANES * (k + 1))
        totals = gathered(near_ref[:, at], coef_ref[:, at], source, 2, groups, chunks)
        for g in range(groups):
            place = ROWS * (g % part_groups)
            partial = partial_refs[g // part_groups][place : place + ROWS, at]
            out_ref[ROWS * g : ROWS * (g + 1), at] = partial + totals[g]


VMEM_SPEC = pl.BlockSpec(memory_space=pltpu.VMEM)
ANY_SPEC = pl.BlockSpec(memory_space=pl.ANY)
HBM_SPEC = pl.BlockSpec(memory_space=pltpu.HBM)


def call(kernel, outs, specs, scratch=(), cost=0):
    estimate = None
    if cost:
        estimate = pl.CostEstimate(flops=0, bytes_accessed=cost, transcendentals=0)
    return pl.pallas_call(
        kernel,
        out_shape=[jax.ShapeDtypeStruct(shape, jnp.float32) for shape in outs],
        in_specs=specs,
        scratch_shapes=list(scratch),
        cost_estimate=estimate,
        compiler_params=pltpu.CompilerParams(vmem_limit_bytes=32 * 2**20),
        name=getattr(kernel, "func", kernel).__name__,
    )


def body(
    air_state,
    air_wind,
    jacobian,
    land_area,
    xgrid_rows,
    tracers,
    edge_coef,
    neighbours,
    vert_rate,
    ocean_area,
    send_list,
    xgrid_cols,
    xgrid_weights,
):
    field_count, levels, x_points, y_points = air_state.shape
    planes = field_count * levels
    ocean_levels, cells = tracers.shape[1:]
    ocean_planes = tracers.shape[0] * ocean_levels
    faces, blocks = lax.axis_size("face"), lax.axis_size("blk")
    air = air_state.reshape(planes * x_points, y_points)
    wind = air_wind.reshape(2 * levels * x_points, y_points)
    ocean = tracers.reshape(ocean_planes, cells)
    point_ids, cell_ids, weights = xgrid_rows[0], xgrid_cols[0], xgrid_weights[0]
    rate = vert_rate.reshape(cells // LANES, LANES)
    area = ocean_area.reshape(cells // LANES, LANES)
    edge_rows = ROWS * (-(-2 * planes // PAIRS))
    rim_at = HEAD + edge_rows + 2 * ROWS + blocks

    first_inputs = (
        cell_ids,
        weights,
        ocean,
        send_list,
        point_ids,
        jacobian,
        land_area,
        wind,
        air,
    )
    slab, moved = call(
        functools.partial(start_kernel, planes, len(first_inputs)),
        [(blocks, rim_at + ocean_planes, LANES), air.shape],
        [HBM_SPEC] * len(first_inputs),
        [pltpu.VMEM(array.shape, array.dtype) for array in first_inputs]
        + [pltpu.SemaphoreType.DMA((len(first_inputs),))],
    )(*(pltpu.with_memory_space_constraint(array, pltpu.HBM) for array in first_inputs))
    recv = lax.all_to_all(slab, "blk", split_axis=0, concat_axis=0, tiled=True)

    parts = tracers.shape[0]
    tile_reads = edge_coef.shape[0] * (cells // LANES) ** 2 * ocean_levels // ROWS

    def ocean_part(number, after):
        (result,) = call(
            functools.partial(ocean_kernel, ocean_levels, number),
            [(ocean_levels, cells)],
            [VMEM_SPEC] * 4 + [ANY_SPEC],
            cost=tile_reads * ROWS * LANES * 4,
        )(ocean, edge_coef, neighbours, rate, after)
        return result

    first_part = ocean_part(0, moved)
    side_rows = 2 * planes + 2 * levels + 2 * SURF_ARRAYS + 4
    avg, down, up, surf = call(
        functools.partial(panel_kernel, planes),
        [air.shape, (side_rows, LANES), (side_rows, LANES), (4 * ROWS * SURF_ARRAYS, LANES)],
        [VMEM_SPEC] * 7 + [ANY_SPEC],
    )(moved, recv, air, wind, jacobian, land_area, point_ids, first_part)
    ring = [(i, (i + 1) % faces) for i in range(faces)]
    low = lax.ppermute(up, "face", ring)
    high = lax.ppermute(down, "face", [(target, source) for source, target in ring])
    second_part = ocean_part(1, surf)

    slab, sums, final, inverse = call(
        functools.partial(second_kernel, planes),
        [
            (blocks, HEAD + edge_rows, LANES),
            air.shape,
            (x_points, y_points),
            (x_points, y_points),
        ],
        [VMEM_SPEC] * 6 + [ANY_SPEC],
        [pltpu.VMEM((planes, LANES), jnp.float32) for _ in range(2)],
    )(avg, surf, low, high, wind, point_ids, second_part)
    arrived = lax.all_to_all(slab, "blk", split_axis=0, concat_axis=0, tiled=True)
    partial, gain = call(
        functools.partial(rim_kernel, rim_at, parts),
        [ocean.shape, area.shape],
        [VMEM_SPEC] * 4 + [ANY_SPEC] + [VMEM_SPEC] * parts,
        cost=tile_reads * ROWS * LANES,
    )(recv, edge_coef, neighbours, area, final, first_part, second_part)
    air_final, ocean_final = call(
        functools.partial(end_kernel, planes),
        [air.shape, ocean.shape],
        [VMEM_SPEC] * 8,
    )(sums, arrived, final, inverse, cell_ids, weights, gain, partial)
    return air_final.reshape(air_state.shape), ocean_final.reshape(tracers.shape)


def solution(mesh):
    return jax.shard_map(
        body,
        mesh=mesh,
        in_specs=(
            P(None, None, "face", "blk"),
            P(None, None, "face", "blk"),
            P("face", "blk"),
            P("face", "blk"),
            P(("face", "blk"), None, None),
            P(None, None, ("face", "blk")),
            P(None, ("face", "blk")),
            P(None, ("face", "blk")),
            P(("face", "blk")),
            P(("face", "blk")),
            P(("face", "blk"), None),
            P(("face", "blk"), None, None),
            P(("face", "blk"), None, None),
        ),
        out_specs=(P(None, None, "face", "blk"), P(None, None, ("face", "blk"))),
        check_vma=False,
    )
```

```python
import functools

import jax
import jax.numpy as jnp
from jax import lax
from jax.experimental import pallas as pl
from jax.experimental.pallas import tpu as pltpu
from jax.sharding import PartitionSpec as P

GLL = 4
ROWS = 8
LANES = 128

deriv_table = [
    [-3.0, 4.045084971874737, -1.545084971874737, 0.5],
    [-0.8090169943749475, 0.0, 1.118033988749895, -0.30901699437494745],
    [0.30901699437494745, -1.118033988749895, 0.0, 0.8090169943749475],
    [-0.5, 1.545084971874737, -4.045084971874737, 3.0],
]
time_step = 0.05
relax_rate = 0.3
flux_gain = 0.2

PAIRS = LANES // 2
AVG, MASS_SUM, MASS, COEF_X, COEF_Y, SURF = range(6)
SURF_ARRAYS = 6


def iota(shape, dim):
    return lax.broadcasted_iota(jnp.int32, shape, dim)


def take(values, index, axis):
    return jnp.take_along_axis(values, index, axis=axis, mode="promise_in_bounds")


def by_position(pos, values):
    result = jnp.full(pos.shape, values[-1], jnp.float32)
    for i, value in enumerate(values[:-1]):
        result = jnp.where(pos == i, value, result)
    return result


def spread(row):
    return jnp.broadcast_to(row, (ROWS, LANES))


class Geometry:
    def __init__(self):
        shape = (ROWS, LANES)
        self.row, self.lane = iota(shape, 0), iota(shape, 1)
        x_pos, y_pos = self.row & (GLL - 1), self.lane & (GLL - 1)
        self.y_from = [self.lane - y_pos + j for j in range(GLL)]
        columns = [[line[j] for line in deriv_table] for j in range(GLL)]
        self.x_coef = {
            step: by_position(
                x_pos,
                [
                    deriv_table[i][i + step] if 0 <= i + step < GLL else 0.0
                    for i in range(GLL)
                ],
            )
            for step in range(1 - GLL, GLL)
        }
        self.y_coef = [by_position(y_pos, column) for column in columns]
        self.y_swap = (
            self.lane + jnp.where(y_pos == GLL - 1, 1, 0) - jnp.where(y_pos == 0, 1, 0)
        ) & (LANES - 1)
        self.x_edge = (x_pos == 0) | (x_pos == GLL - 1)
        self.y_edge = (y_pos == 0) | (y_pos == GLL - 1)
        self.first_row, self.last_row = self.row == 0, self.row == ROWS - 1
        self.middle_row = self.row == GLL
        self.outer_lane = (self.lane == 0) | (self.lane == LANES - 1)
        self.weight = jnp.where(self.x_edge, 1.0 / 6.0, 5.0 / 6.0) * jnp.where(
            self.y_edge, 1.0 / 6.0, 5.0 / 6.0
        )

    def d_x(self, tile):
        return sum(
            coef * (pltpu.roll(tile, -step % ROWS, 0) if step else tile)
            for step, coef in self.x_coef.items()
        )

    def d_y(self, *tiles):
        totals = [0.0] * len(tiles)
        for j in range(GLL):
            for i, tile in enumerate(tiles):
                totals[i] += self.y_coef[j] * take(tile, self.y_from[j], 1)
        return totals

    def sum_x(self, low, high, before, after):
        low_down, low_up = pltpu.roll(low, 1, 0), pltpu.roll(low, ROWS - 1, 0)
        high_down, high_up = pltpu.roll(high, 1, 0), pltpu.roll(high, ROWS - 1, 0)
        low_other = jnp.where(
            self.first_row,
            before,
            jnp.where(
                self.middle_row, low_down, jnp.where(self.last_row, high_up, low_up)
            ),
        )
        high_other = jnp.where(
            self.first_row,
            low_down,
            jnp.where(
                self.middle_row, high_down, jnp.where(self.last_row, after, high_up)
            ),
        )
        return (
            low + jnp.where(self.x_edge, low_other, 0.0),
            high + jnp.where(self.x_edge, high_other, 0.0),
        )

    def sum_y(self, tile, outer):
        other = jnp.where(self.outer_lane, outer, take(tile, self.y_swap, 1))
        return tile + jnp.where(self.y_edge, other, 0.0)

    def sum_y_pair(self, own, strip):
        own_swap, strip_swap = take(own, self.y_swap, 1), take(strip, self.y_swap, 1)
        own_other = jnp.where(self.outer_lane, strip_swap, own_swap)
        strip_other = jnp.where(self.outer_lane, own_swap, strip_swap)
        return (
            own + jnp.where(self.y_edge, own_other, 0.0),
            strip + jnp.where(self.y_edge, strip_other, 0.0),
        )


def pack_edges(geo, packs, tile, number):
    at = number % PAIRS
    rolled = pltpu.roll(tile, (2 * at + 1) % LANES, 1)
    packs[number // PAIRS] = jnp.where(
        (geo.lane >> 1) == at, rolled, packs[number // PAIRS]
    )


def join_edges(geo, from_left, from_right):
    odd = (geo.lane & 1) == 1
    return jnp.where(
        odd, pltpu.roll(from_left, 1, 1), pltpu.roll(from_right, LANES - 1, 1)
    )


def outer_edges(joined, number):
    at = number % PAIRS
    return pltpu.roll(joined[number // PAIRS], (-(2 * at + 1)) % LANES, 1)


def neighbours_of(blocks):
    here = lax.axis_index("blk")
    return lax.rem(here + blocks - 1, blocks), lax.rem(here + 1, blocks)


def scatter_sum(lines, index, bins, allowed=None):
    count = index.shape[0]
    split = []
    for values in lines:
        for part in range(3):
            short = values.astype(jnp.bfloat16).astype(jnp.float32)
            split.append(short)
            values = values - short
    high, low = index >> 7, index & (LANES - 1)
    bin_at = iota((bins, LANES), 0)
    lane_at = iota((LANES, LANES), 0)
    if allowed is not None:
        lane_at = jnp.where(allowed(lane_at), lane_at, -1)
    left, right = [], []
    for c in range(count):
        hit = bin_at == high[c : c + 1]
        left.append(
            jnp.concatenate(
                [jnp.where(hit, part[c : c + 1], 0.0) for part in split], axis=0
            ).astype(jnp.bfloat16)
        )
        right.append(
            jnp.where(lane_at == low[c : c + 1], 1.0, 0.0).astype(jnp.bfloat16)
        )
    total = lax.dot_general(
        jnp.concatenate(left, axis=1),
        jnp.concatenate(right, axis=1),
        (((1,), (1,)), ((), ())),
        preferred_element_type=jnp.float32,
    )
    sums = []
    for i in range(len(lines)):
        part = total[3 * i * bins : 3 * (i + 1) * bins]
        sums.append(part[:bins] + part[bins : 2 * bins] + part[2 * bins :])
    return sums


def start_kernel(planes, inputs, *refs):
    sources, (slab_ref, moved_ref), held = (
        refs[:inputs],
        refs[inputs : inputs + 2],
        refs[inputs + 2 : -1],
    )
    copies = [
        pltpu.make_async_copy(source, target, refs[-1].at[i])
        for i, (source, target) in enumerate(zip(sources, held))
    ]
    for copy in copies:
        copy.start()
    (
        cols_ref,
        weights_ref,
        tracers_ref,
        send_ref,
        rows_ref,
        jac_ref,
        land_ref,
        wind_ref,
        air_ref,
    ) = held
    for copy in copies[:4]:
        copy.wait()
    geo = Geometry()
    blocks = cols_ref.shape[0]
    levels = wind_ref.shape[0] // 32
    chunks = tracers_ref.shape[1] // LANES

    def source(group, chunk):
        return tracers_ref[
            ROWS * group : ROWS * (group + 1), LANES * chunk : LANES * (chunk + 1)
        ]

    for group in range(blocks // ROWS):
        at = slice(ROWS * group, ROWS * (group + 1))
        cells = cols_ref[at, :]
        high, low = cells >> 7, cells & (LANES - 1)
        surface = jnp.zeros((ROWS, LANES), jnp.float32)
        for k in range(chunks):
            line = spread(tracers_ref[0:1, LANES * k : LANES * (k + 1)])
            surface = jnp.where(high == k, take(line, low, 1), surface)
        area = weights_ref[at, :]
        heat = area * surface
        slab_ref[at, :] = heat
        slab_ref[blocks + ROWS * group : blocks + ROWS * (group + 1), :] = area

    base = 2 * blocks + ROWS * (-(-2 * planes // PAIRS)) + 2 * ROWS + blocks
    for part in range(2):
        cells = spread(send_ref[0:1, LANES * part : LANES * (part + 1)])
        high, low = cells >> 7, cells & (LANES - 1)
        for group in range(tracers_ref.shape[0] // ROWS):
            rim = jnp.zeros((ROWS, LANES), jnp.float32)
            for k in range(chunks):
                rim = jnp.where(high == k, take(source(group, k), low, 1), rim)
            at = base + tracers_ref.shape[0] * part + ROWS * group
            slab_ref[at : at + ROWS, :] = rim

    for copy in copies[4:]:
        copy.wait()
    mass = [geo.weight * jac_ref[ROWS * h : ROWS * (h + 1), :] for h in range(2)]
    packs = [
        jnp.zeros((ROWS, LANES), jnp.float32) for _ in range(-(-2 * planes // PAIRS))
    ]
    for level in range(levels):
        wind = [
            [
                time_step * wind_ref[pl.ds((i * levels + level) * 16 + ROWS * h, ROWS), :]
                for h in range(2)
            ]
            for i in range(2)
        ]
        places = [
            (plane, h) for plane in range(level, planes, levels) for h in range(2)
        ]
        fields = [air_ref[pl.ds(plane * 16 + ROWS * h, ROWS), :] for plane, h in places]
        for (plane, h), field, slope in zip(places, fields, geo.d_y(*fields)):
            moved = mass[h] * (
                field - (wind[0][h] * geo.d_x(field) + wind[1][h] * slope)
            )
            moved_ref[pl.ds(plane * 16 + ROWS * h, ROWS), :] = moved
            pack_edges(geo, packs, moved, 2 * plane + h)

    base = 2 * blocks
    edge_rows = ROWS * len(packs)
    for q, pack in enumerate(packs):
        slab_ref[base + ROWS * q : base + ROWS * (q + 1), :] = pack
    base += edge_rows
    for h in range(2):
        half = slice(ROWS * h, ROWS * (h + 1))
        strips = [
            air_ref[half, :],
            wind_ref[half, :],
            wind_ref[levels * 16 + ROWS * h : levels * 16 + ROWS * (h + 1), :],
            jac_ref[half, :],
            land_ref[half, :],
        ]
        pack = jnp.zeros((ROWS, LANES), jnp.float32)
        for i, strip in enumerate(strips):
            pack = jnp.where(
                (geo.lane >> 4) == i, pltpu.roll(strip, 16 * i + 8, 1), pack
            )
        slab_ref[base + ROWS * h : base + ROWS * (h + 1), :] = pack
    base += 2 * ROWS
    ids = rows_ref[...].astype(jnp.float32)
    slab_ref[base : base + blocks, :] = ids


def panel_kernel(
    planes,
    moved_ref,
    recv_ref,
    air_ref,
    wind_ref,
    jac_ref,
    land_ref,
    rows_ref,
    after_ref,
    avg_ref,
    down_ref,
    up_ref,
    surf_ref,
):
    geo = Geometry()
    blocks = rows_ref.shape[0]
    left, right = neighbours_of(blocks)
    levels = wind_ref.shape[0] // 32
    pack_count = -(-2 * planes // PAIRS)
    base = 2 * blocks + ROWS * pack_count
    here = lax.axis_index("blk")

    ids_at = base + 2 * ROWS
    own_ids = rows_ref[...]
    left_ids = recv_ref[left, ids_at : ids_at + blocks, :].astype(jnp.int32)
    right_ids = recv_ref[right, ids_at : ids_at + blocks, :].astype(jnp.int32)
    head = [
        jnp.concatenate(
            [recv_ref[c, pl.ds(first + owner, 1), :] for c in range(blocks)], axis=0
        )
        for owner in (left, here, right)
        for first in (0, blocks)
    ]
    heat, frac = scatter_sum(head[2:4], own_ids, 2 * ROWS)
    from_left = scatter_sum(
        head[0:2], left_ids, 2 * ROWS, lambda lane: lane >= LANES - ROWS
    )
    from_right = scatter_sum(head[4:6], right_ids, 2 * ROWS, lambda lane: lane < ROWS)
    strip_heat = from_left[0] + from_right[0]
    strip_frac = from_left[1] + from_right[1]

    in_strip = (geo.lane < ROWS) | (geo.lane >= LANES - ROWS)
    own, strip = [], []
    for h in range(2):
        half = slice(ROWS * h, ROWS * (h + 1))
        pack = jnp.where(
            ((geo.lane >> 3) & 1) == 1,
            recv_ref[right, base + ROWS * h : base + ROWS * (h + 1), :],
            recv_ref[left, base + ROWS * h : base + ROWS * (h + 1), :],
        )
        strip.append(
            [
                jnp.where(
                    in_strip, pltpu.roll(pack, (-(16 * i + 8)) % LANES, 1), 1.0
                )
                for i in range(5)
            ]
        )
        own.append(
            [
                air_ref[half, :],
                wind_ref[half, :],
                wind_ref[levels * 16 + ROWS * h : levels * 16 + ROWS * (h + 1), :],
                jac_ref[half, :],
                land_ref[half, :],
            ]
        )
    for h in range(2):
        half = slice(ROWS * h, ROWS * (h + 1))
        pair = []
        for tile, ((field, wind_x, wind_y, jac, land), tile_heat, tile_frac) in enumerate(
            ((own[h], heat[half], frac[half]), (strip[h], strip_heat[half], strip_frac[half]))
        ):
            mass = geo.weight * jac
            if tile == 1:
                tile_heat = jnp.where(in_strip, tile_heat, 0.0)
                tile_frac = jnp.where(in_strip, tile_frac, 0.0)
            surf = (tile_heat + land * field) / (tile_frac + land)
            coef_x, coef_y = time_step * mass * wind_x, time_step * mass * wind_y
            moved = (
                mass * (field + relax_rate * (surf - field))
                - coef_x * geo.d_x(field)
                - coef_y * geo.d_y(field)[0]
            )
            pair.append((moved, mass))
            at = 2 * ROWS * tile + ROWS * h
            for number, value in (
                (MASS, mass),
                (COEF_X, coef_x),
                (COEF_Y, coef_y),
                (SURF, surf),
            ):
                surf_ref[4 * ROWS * number + at : 4 * ROWS * number + at + ROWS, :] = value
        for number, i in ((AVG, 0), (MASS_SUM, 1)):
            for tile, value in enumerate(geo.sum_y_pair(pair[0][i], pair[1][i])):
                at = 4 * ROWS * number + 2 * ROWS * tile + ROWS * h
                surf_ref[at : at + ROWS, :] = value

    joined = [
        join_edges(
            geo,
            recv_ref[left, 2 * blocks + ROWS * q : 2 * blocks + ROWS * (q + 1), :],
            recv_ref[right, 2 * blocks + ROWS * q : 2 * blocks + ROWS * (q + 1), :],
        )
        for q in range(pack_count)
    ]
    for plane in range(planes):
        for h in range(2):
            at = pl.ds(plane * 16 + ROWS * h, ROWS)
            avg_ref[at, :] = geo.sum_y(
                moved_ref[at, :], outer_edges(joined, 2 * plane + h)
            )

    def line(r):
        return avg_ref[pl.ds(r, planes, stride=16), :]

    def surf_line(number, r):
        return surf_ref[pl.ds(4 * ROWS * number + r, 2, stride=16), :]

    def first_step(get, mass_at):
        return (
            [
                get(1) / mass_at(1),
                get(2) / mass_at(2),
                (get(3) + get(4)) / (mass_at(3) + mass_at(4)),
            ],
            [
                (get(11) + get(12)) / (mass_at(11) + mass_at(12)),
                get(13) / mass_at(13),
                get(14) / mass_at(14),
            ],
        )

    def own_mass_sum(r):
        return surf_ref[4 * ROWS * MASS_SUM + r : 4 * ROWS * MASS_SUM + r + 1, :]

    low_lines, high_lines = first_step(line, own_mass_sum)
    surf_low, surf_high = first_step(
        functools.partial(surf_line, AVG), functools.partial(surf_line, MASS_SUM)
    )
    for out_ref, r, lines, surf_lines, coefs in (
        (down_ref, 0, low_lines, surf_low, deriv_table[0][1:]),
        (up_ref, 15, high_lines, surf_high, deriv_table[3][:3]),
    ):
        slope = sum(coef * value for coef, value in zip(coefs, lines))
        surf_slope = sum(coef * value for coef, value in zip(coefs, surf_lines))
        mass = surf_ref[4 * ROWS * MASS + r : 4 * ROWS * MASS + r + 1, :]
        wind = time_step * mass * wind_ref[pl.ds(r, 2 * levels, stride=16), :]
        out_ref[0:planes, :] = line(r)
        for first in range(0, planes, levels):
            out_ref[planes + first : planes + first + levels, :] = (
                wind[:levels] * slope[first : first + levels]
            )
        base = 2 * planes
        out_ref[base : base + 2 * levels, :] = wind
        base += 2 * levels
        for number in range(SURF_ARRAYS):
            out_ref[base + 2 * number : base + 2 * number + 2, :] = surf_line(number, r)
        base += 2 * SURF_ARRAYS
        out_ref[base : base + 2, :] = surf_line(COEF_X, r) * surf_slope


def second_kernel(
    planes,
    avg_ref,
    surf_ref,
    low_ref,
    high_ref,
    wind_ref,
    rows_ref,
    after_ref,
    slab_ref,
    sums_ref,
    final_ref,
    inverse_ref,
    low_halo,
    high_halo,
):
    geo = Geometry()
    blocks = rows_ref.shape[0]
    levels = wind_ref.shape[0] // 32
    base = 2 * planes + 2 * levels

    def surf_tile(number, tile, h):
        at = 4 * ROWS * number + 2 * ROWS * tile + ROWS * h
        return surf_ref[at : at + ROWS, :]

    def beside(ref, number, tile):
        at = base + 2 * number + tile
        return spread(ref[at : at + 1, :])

    ends = []
    inverse = []
    for tile in range(2):
        total = geo.sum_x(
            surf_tile(MASS_SUM, tile, 0),
            surf_tile(MASS_SUM, tile, 1),
            beside(low_ref, MASS_SUM, tile),
            beside(high_ref, MASS_SUM, tile),
        )
        inverse.append([1.0 / value for value in total])
        summed = geo.sum_x(
            surf_tile(AVG, tile, 0),
            surf_tile(AVG, tile, 1),
            beside(low_ref, AVG, tile),
            beside(high_ref, AVG, tile),
        )
        fields = [value * scale for value, scale in zip(summed, inverse[tile])]
        moved = []
        for h in range(2):
            field = fields[h]
            moved.append(
                surf_tile(MASS, tile, h)
                * (field + relax_rate * (surf_tile(SURF, tile, h) - field))
                - surf_tile(COEF_X, tile, h) * geo.d_x(field)
                - surf_tile(COEF_Y, tile, h) * geo.d_y(field)[0]
            )
        halos = []
        for ref, field, own_coef in (
            (low_ref, spread(fields[0][:1]), deriv_table[3][3]),
            (high_ref, spread(fields[1][ROWS - 1 :]), deriv_table[0][0]),
        ):
            halos.append(
                beside(ref, MASS, tile)
                * (field + relax_rate * (beside(ref, SURF, tile) - field))
                - beside(ref, SURF_ARRAYS, tile)
                - beside(ref, COEF_X, tile) * (own_coef * field)
                - beside(ref, COEF_Y, tile) * geo.d_y(field)[0]
            )
        ends.append(geo.sum_x(moved[0], moved[1], halos[0], halos[1]))
    final = []
    for h in range(2):
        summed, _ = geo.sum_y_pair(ends[0][h], ends[1][h])
        final.append(summed * inverse[0][h])
        final_ref[ROWS * h : ROWS * (h + 1), :] = final[h]
        inverse_ref[ROWS * h : ROWS * (h + 1), :] = inverse[0][h]
    flux = [final[h] - surf_tile(SURF, 0, h) for h in range(2)]
    for group in range(blocks // ROWS):
        ids = rows_ref[ROWS * group : ROWS * (group + 1), :]
        high, low = ids >> 7, ids & (LANES - 1)
        picked = jnp.zeros((ROWS, LANES), jnp.float32)
        for x in range(2 * ROWS):
            line = spread(flux[x // ROWS][x % ROWS : x % ROWS + 1])
            picked = jnp.where(high == x, take(line, low, 1), picked)
        slab_ref[ROWS * group : ROWS * (group + 1), :] = picked

    for ref, halo, r, own_coef, scale in (
        (low_ref, low_halo, 0, deriv_table[3][3], inverse[0][0][:1]),
        (high_ref, high_halo, 15, deriv_table[0][0], inverse[0][1][ROWS - 1 :]),
    ):
        field = (avg_ref[pl.ds(r, planes, stride=16), :] + ref[0:planes, :]) * scale
        mass = beside(ref, MASS, 0)
        for first in range(0, planes, ROWS):
            part = field[first : first + ROWS]
            wind_at = 2 * planes + first % levels
            halo[first : first + ROWS, :] = (
                mass * part
                - ref[planes + first : planes + first + ROWS, :]
                - ref[wind_at : wind_at + ROWS, :] * (own_coef * part)
                - ref[wind_at + levels : wind_at + levels + ROWS, :] * geo.d_y(part)[0]
            )

    mass = [surf_tile(MASS, 0, h) for h in range(2)]
    packs = [
        jnp.zeros((ROWS, LANES), jnp.float32) for _ in range(-(-2 * planes // PAIRS))
    ]
    for level in range(levels):
        wind = [
            [
                time_step * wind_ref[pl.ds((i * levels + level) * 16 + ROWS * h, ROWS), :]
                for h in range(2)
            ]
            for i in range(2)
        ]
        group = list(range(level, planes, levels))
        fields = []
        for plane in group:
            summed = geo.sum_x(
                avg_ref[pl.ds(plane * 16, ROWS), :],
                avg_ref[pl.ds(plane * 16 + ROWS, ROWS), :],
                spread(low_ref[plane : plane + 1, :]),
                spread(high_ref[plane : plane + 1, :]),
            )
            fields += [summed[h] * inverse[0][h] for h in range(2)]
        slopes = geo.d_y(*fields)
        for number, plane in enumerate(group):
            moved = []
            for h in range(2):
                field = fields[2 * number + h]
                moved.append(
                    mass[h]
                    * (
                        field
                        - (
                            wind[0][h] * geo.d_x(field)
                            + wind[1][h] * slopes[2 * number + h]
                        )
                    )
                )
            summed = geo.sum_x(
                moved[0],
                moved[1],
                spread(low_halo[plane : plane + 1, :]),
                spread(high_halo[plane : plane + 1, :]),
            )
            for h in range(2):
                sums_ref[pl.ds(plane * 16 + ROWS * h, ROWS), :] = summed[h]
                pack_edges(geo, packs, summed[h], 2 * plane + h)
    for q, pack in enumerate(packs):
        slab_ref[blocks + ROWS * q : blocks + ROWS * (q + 1), :] = pack


def end_kernel(
    planes,
    sums_ref,
    recv_ref,
    final_ref,
    inverse_ref,
    cols_ref,
    weights_ref,
    gain_ref,
    ocean_ref,
    air_out,
    ocean_out,
):
    geo = Geometry()
    blocks = cols_ref.shape[0]
    left, right = neighbours_of(blocks)
    chunks = gain_ref.shape[0]
    here = lax.axis_index("blk")
    arrived = jnp.concatenate(
        [recv_ref[c, pl.ds(here, 1), :] for c in range(blocks)], axis=0
    )
    (inflow,) = scatter_sum([weights_ref[...] * arrived], cols_ref[...], chunks)
    gain = inflow * gain_ref[...]
    ocean_out[...] = ocean_ref[...]
    for k in range(chunks):
        at = slice(LANES * k, LANES * (k + 1))
        ocean_out[0:1, at] = ocean_ref[0:1, at] + gain[k : k + 1]

    joined = [
        join_edges(
            geo,
            recv_ref[left, blocks + ROWS * q : blocks + ROWS * (q + 1), :],
            recv_ref[right, blocks + ROWS * q : blocks + ROWS * (q + 1), :],
        )
        for q in range(-(-2 * planes // PAIRS))
    ]
    inverse = [inverse_ref[ROWS * h : ROWS * (h + 1), :] for h in range(2)]
    for plane in range(planes):
        for h in range(2):
            at = pl.ds(plane * 16 + ROWS * h, ROWS)
            if plane == 0:
                air_out[at, :] = final_ref[ROWS * h : ROWS * (h + 1), :]
            else:
                air_out[at, :] = inverse[h] * geo.sum_y(
                    sums_ref[at, :], outer_edges(joined, 2 * plane + h)
                )


def gathered(ids, coefs, source, sources, groups, first=0):
    totals = [jnp.zeros((ROWS, LANES), jnp.float32) for _ in range(groups)]
    for edge in range(ids.shape[0]):
        cell = spread(ids[edge : edge + 1])
        coef = spread(coefs[edge : edge + 1])
        high, low = cell >> 7, cell & (LANES - 1)
        for s in range(sources):
            scaled = jnp.where(high == first + s, coef, 0.0)
            for group in range(groups):
                totals[group] += scaled * take(source(group, s), low, 1)
    return totals


def ocean_kernel(levels, number, tracers_ref, coef_ref, near_ref, rate_ref, after_ref, out_ref):
    chunks = tracers_ref.shape[1] // LANES
    groups = levels // ROWS
    base = levels * number
    row = iota((ROWS, LANES), 0)

    def source(group, s):
        return tracers_ref[
            base + ROWS * group : base + ROWS * (group + 1), LANES * s : LANES * (s + 1)
        ]

    def one_chunk(k, carry):
        at = pl.ds(pl.multiple_of(k * LANES, LANES), LANES)
        ids, coefs = near_ref[:, at], coef_ref[:, at]
        totals = gathered(ids, coefs, source, chunks, groups)
        coef_sum = spread(jnp.sum(coefs, axis=0, keepdims=True))
        rate = spread(rate_ref[pl.ds(k, 1), :])
        tiles = [
            tracers_ref[base + ROWS * g : base + ROWS * (g + 1), at]
            for g in range(groups)
        ]
        for g in range(groups):
            tile = tiles[g]
            above = pltpu.roll(tile, 1, 0)
            below = pltpu.roll(tile, ROWS - 1, 0)
            top = pltpu.roll(tiles[g - 1], 1, 0) if g else tile
            bottom = tile
            if g + 1 < groups:
                bottom = pltpu.roll(tiles[g + 1], ROWS - 1, 0)
            above = jnp.where(row == 0, top, above)
            below = jnp.where(row == ROWS - 1, bottom, below)
            vertical = rate * ((above - tile) + (below - tile))
            out_ref[ROWS * g : ROWS * (g + 1), at] = (
                tile + (totals[g] - coef_sum * tile) + vertical
            )
        return carry

    lax.fori_loop(0, chunks, one_chunk, 0)


def rim_kernel(
    rim_at,
    parts,
    recv_ref,
    coef_ref,
    near_ref,
    area_ref,
    after_ref,
    *refs,
):
    partial_refs, (out_ref, gain_ref) = refs[:parts], refs[parts:]
    chunks = coef_ref.shape[1] // LANES
    groups = out_ref.shape[0] // ROWS
    part_groups = groups // parts
    sides = neighbours_of(recv_ref.shape[0])
    gain_ref[...] = flux_gain / area_ref[...]

    def source(group, s):
        at = rim_at + ROWS * groups * (1 - s) + ROWS * group
        return recv_ref[sides[s], at : at + ROWS, :]

    for k in range(chunks):
        at = slice(LANES * k, LANES * (k + 1))
        totals = gathered(near_ref[:, at], coef_ref[:, at], source, 2, groups, chunks)
        for g in range(groups):
            place = ROWS * (g % part_groups)
            partial = partial_refs[g // part_groups][place : place + ROWS, at]
            out_ref[ROWS * g : ROWS * (g + 1), at] = partial + totals[g]


VMEM_SPEC = pl.BlockSpec(memory_space=pltpu.VMEM)
ANY_SPEC = pl.BlockSpec(memory_space=pl.ANY)
HBM_SPEC = pl.BlockSpec(memory_space=pltpu.HBM)


def call(kernel, outs, specs, scratch=(), cost=0):
    estimate = None
    if cost:
        estimate = pl.CostEstimate(flops=0, bytes_accessed=cost, transcendentals=0)
    return pl.pallas_call(
        kernel,
        out_shape=[jax.ShapeDtypeStruct(shape, jnp.float32) for shape in outs],
        in_specs=specs,
        scratch_shapes=list(scratch),
        cost_estimate=estimate,
        compiler_params=pltpu.CompilerParams(vmem_limit_bytes=32 * 2**20),
        name=getattr(kernel, "func", kernel).__name__,
    )


def body(
    air_state,
    air_wind,
    jacobian,
    land_area,
    xgrid_rows,
    tracers,
    edge_coef,
    neighbours,
    vert_rate,
    ocean_area,
    send_list,
    xgrid_cols,
    xgrid_weights,
):
    field_count, levels, x_points, y_points = air_state.shape
    planes = field_count * levels
    ocean_levels, cells = tracers.shape[1:]
    ocean_planes = tracers.shape[0] * ocean_levels
    faces, blocks = lax.axis_size("face"), lax.axis_size("blk")
    air = air_state.reshape(planes * x_points, y_points)
    wind = air_wind.reshape(2 * levels * x_points, y_points)
    ocean = tracers.reshape(ocean_planes, cells)
    point_ids, cell_ids, weights = xgrid_rows[0], xgrid_cols[0], xgrid_weights[0]
    rate = vert_rate.reshape(cells // LANES, LANES)
    area = ocean_area.reshape(cells // LANES, LANES)
    edge_rows = ROWS * (-(-2 * planes // PAIRS))
    rim_at = 2 * blocks + edge_rows + 2 * ROWS + blocks

    first_inputs = (
        cell_ids,
        weights,
        ocean,
        send_list,
        point_ids,
        jacobian,
        land_area,
        wind,
        air,
    )
    slab, moved = call(
        functools.partial(start_kernel, planes, len(first_inputs)),
        [(rim_at + 2 * ocean_planes, LANES), air.shape],
        [HBM_SPEC] * len(first_inputs),
        [pltpu.VMEM(array.shape, array.dtype) for array in first_inputs]
        + [pltpu.SemaphoreType.DMA((len(first_inputs),))],
    )(*(pltpu.with_memory_space_constraint(array, pltpu.HBM) for array in first_inputs))
    recv = lax.all_gather(slab, "blk")

    parts = tracers.shape[0]
    tile_reads = edge_coef.shape[0] * (cells // LANES) ** 2 * ocean_levels // ROWS

    def ocean_part(number, after):
        (result,) = call(
            functools.partial(ocean_kernel, ocean_levels, number),
            [(ocean_levels, cells)],
            [VMEM_SPEC] * 4 + [ANY_SPEC],
            cost=tile_reads * ROWS * LANES * 4,
        )(ocean, edge_coef, neighbours, rate, after)
        return result

    first_part = ocean_part(0, moved)
    side_rows = 2 * planes + 2 * levels + 2 * SURF_ARRAYS + 4
    avg, down, up, surf = call(
        functools.partial(panel_kernel, planes),
        [air.shape, (side_rows, LANES), (side_rows, LANES), (4 * ROWS * SURF_ARRAYS, LANES)],
        [VMEM_SPEC] * 7 + [ANY_SPEC],
    )(moved, recv, air, wind, jacobian, land_area, point_ids, first_part)
    ring = [(i, (i + 1) % faces) for i in range(faces)]
    low = lax.ppermute(up, "face", ring)
    high = lax.ppermute(down, "face", [(target, source) for source, target in ring])
    second_part = ocean_part(1, surf)

    slab, sums, final, inverse = call(
        functools.partial(second_kernel, planes),
        [
            (blocks + edge_rows, LANES),
            air.shape,
            (x_points, y_points),
            (x_points, y_points),
        ],
        [VMEM_SPEC] * 6 + [ANY_SPEC],
        [pltpu.VMEM((planes, LANES), jnp.float32) for _ in range(2)],
    )(avg, surf, low, high, wind, point_ids, second_part)
    arrived = lax.all_gather(slab, "blk")
    partial, gain = call(
        functools.partial(rim_kernel, rim_at, parts),
        [ocean.shape, area.shape],
        [VMEM_SPEC] * 4 + [ANY_SPEC] + [VMEM_SPEC] * parts,
        cost=tile_reads * ROWS * LANES,
    )(recv, edge_coef, neighbours, area, final, first_part, second_part)
    air_final, ocean_final = call(
        functools.partial(end_kernel, planes),
        [air.shape, ocean.shape],
        [VMEM_SPEC] * 8,
    )(sums, arrived, final, inverse, cell_ids, weights, gain, partial)
    return air_final.reshape(air_state.shape), ocean_final.reshape(tracers.shape)


def solution(mesh):
    return jax.shard_map(
        body,
        mesh=mesh,
        in_specs=(
            P(None, None, "face", "blk"),
            P(None, None, "face", "blk"),
            P("face", "blk"),
            P("face", "blk"),
            P(("face", "blk"), None, None),
            P(None, None, ("face", "blk")),
            P(None, ("face", "blk")),
            P(None, ("face", "blk")),
            P(("face", "blk")),
            P(("face", "blk")),
            P(("face", "blk"), None),
            P(("face", "blk"), None, None),
            P(("face", "blk"), None, None),
        ),
        out_specs=(P(None, None, "face", "blk"), P(None, None, ("face", "blk"))),
        check_vma=False,
    )
```

```python
import functools

import jax
import jax.numpy as jnp
from jax import lax
from jax.experimental import pallas as pl
from jax.experimental.pallas import tpu as pltpu
from jax.sharding import PartitionSpec as P

GLL = 4
ROWS = 8
LANES = 128

deriv_table = [
    [-3.0, 4.045084971874737, -1.545084971874737, 0.5],
    [-0.8090169943749475, 0.0, 1.118033988749895, -0.30901699437494745],
    [0.30901699437494745, -1.118033988749895, 0.0, 0.8090169943749475],
    [-0.5, 1.545084971874737, -4.045084971874737, 3.0],
]
time_step = 0.05
relax_rate = 0.3
flux_gain = 0.2

HEAD, EDGE_AT, STRIP_AT, IDS_AT = 8, 8, 16, 24
AVG, MASS_SUM, MASS, COEF_X, COEF_Y, SURF = range(6)
SURF_ARRAYS = 6


def iota(shape, dim):
    return lax.broadcasted_iota(jnp.int32, shape, dim)


def take(values, index, axis):
    return jnp.take_along_axis(values, index, axis=axis, mode="promise_in_bounds")


def by_position(pos, values):
    result = jnp.full(pos.shape, values[-1], jnp.float32)
    for i, value in enumerate(values[:-1]):
        result = jnp.where(pos == i, value, result)
    return result


def spread(row):
    return jnp.broadcast_to(row, (ROWS, LANES))


class Geometry:
    def __init__(self):
        shape = (ROWS, LANES)
        self.row, self.lane = iota(shape, 0), iota(shape, 1)
        x_pos, y_pos = self.row & (GLL - 1), self.lane & (GLL - 1)
        self.y_from = [self.lane - y_pos + j for j in range(GLL)]
        columns = [[line[j] for line in deriv_table] for j in range(GLL)]
        self.x_coef = {
            step: by_position(
                x_pos,
                [
                    deriv_table[i][i + step] if 0 <= i + step < GLL else 0.0
                    for i in range(GLL)
                ],
            )
            for step in range(1 - GLL, GLL)
        }
        self.y_coef = [by_position(y_pos, column) for column in columns]
        self.y_swap = (
            self.lane + jnp.where(y_pos == GLL - 1, 1, 0) - jnp.where(y_pos == 0, 1, 0)
        ) & (LANES - 1)
        self.x_edge = (x_pos == 0) | (x_pos == GLL - 1)
        self.y_edge = (y_pos == 0) | (y_pos == GLL - 1)
        self.first_row, self.last_row = self.row == 0, self.row == ROWS - 1
        self.middle_row = self.row == GLL
        self.outer_lane = (self.lane == 0) | (self.lane == LANES - 1)
        self.weight = jnp.where(self.x_edge, 1.0 / 6.0, 5.0 / 6.0) * jnp.where(
            self.y_edge, 1.0 / 6.0, 5.0 / 6.0
        )

    def d_x(self, tile):
        return sum(
            coef * (pltpu.roll(tile, -step % ROWS, 0) if step else tile)
            for step, coef in self.x_coef.items()
        )

    def d_y(self, *tiles):
        totals = [0.0] * len(tiles)
        for j in range(GLL):
            for i, tile in enumerate(tiles):
                totals[i] += self.y_coef[j] * take(tile, self.y_from[j], 1)
        return totals

    def sum_x(self, low, high, before, after):
        low_down, low_up = pltpu.roll(low, 1, 0), pltpu.roll(low, ROWS - 1, 0)
        high_down, high_up = pltpu.roll(high, 1, 0), pltpu.roll(high, ROWS - 1, 0)
        low_other = jnp.where(
            self.first_row,
            before,
            jnp.where(
                self.middle_row, low_down, jnp.where(self.last_row, high_up, low_up)
            ),
        )
        high_other = jnp.where(
            self.first_row,
            low_down,
            jnp.where(
                self.middle_row, high_down, jnp.where(self.last_row, after, high_up)
            ),
        )
        return (
            low + jnp.where(self.x_edge, low_other, 0.0),
            high + jnp.where(self.x_edge, high_other, 0.0),
        )

    def sum_y(self, tile, outer):
        other = jnp.where(self.outer_lane, outer, take(tile, self.y_swap, 1))
        return tile + jnp.where(self.y_edge, other, 0.0)

    def sum_y_pair(self, own, strip):
        own_swap, strip_swap = take(own, self.y_swap, 1), take(strip, self.y_swap, 1)
        own_other = jnp.where(self.outer_lane, strip_swap, own_swap)
        strip_other = jnp.where(self.outer_lane, own_swap, strip_swap)
        return (
            own + jnp.where(self.y_edge, own_other, 0.0),
            strip + jnp.where(self.y_edge, strip_other, 0.0),
        )


def edge_place(x, group):
    return x // ROWS, LANES // 2 * (x % 2) + ROWS * group + 2 * (x % ROWS // 2)


def pack_edges(geo, packs, tile, x, group):
    q, at = edge_place(x, group)
    rolled = pltpu.roll(tile, (at + 1) % LANES, 1)
    packs[q] = jnp.where((geo.lane >> 1) == at // 2, rolled, packs[q])


def outer_edges(joined, x, group):
    q, at = edge_place(x, group)
    return pltpu.roll(joined[q], (-(at + 1)) % LANES, 1)


def split_sides(geo, first, second, unit):
    odd = (geo.lane & unit) != 0
    return (
        jnp.where(odd, pltpu.roll(second, unit, 1), first),
        jnp.where(odd, second, pltpu.roll(first, LANES - unit, 1)),
    )


def join_sides(geo, before, after, unit):
    odd = (geo.lane & unit) != 0
    return (
        jnp.where(odd, pltpu.roll(after, unit, 1), before),
        jnp.where(odd, after, pltpu.roll(before, LANES - unit, 1)),
    )


def join_edges(geo, before, after):
    odd = (geo.lane & 1) != 0
    return (
        jnp.where(odd, pltpu.roll(before, 1, 1), after),
        jnp.where(odd, before, pltpu.roll(after, LANES - 1, 1)),
    )


def neighbours_of(blocks):
    here = lax.axis_index("blk")
    return lax.rem(here + blocks - 1, blocks), lax.rem(here + 1, blocks)


def scatter_sum(lines, index, bins, allowed=None):
    count = index.shape[0]
    split = []
    for values in lines:
        for part in range(3):
            short = values.astype(jnp.bfloat16).astype(jnp.float32)
            split.append(short)
            values = values - short
    high, low = index >> 7, index & (LANES - 1)
    bin_at = iota((bins, LANES), 0)
    lane_at = iota((LANES, LANES), 0)
    if allowed is not None:
        lane_at = jnp.where(allowed(lane_at), lane_at, -1)
    left, right = [], []
    for c in range(count):
        hit = bin_at == high[c : c + 1]
        left.append(
            jnp.concatenate(
                [jnp.where(hit, part[c : c + 1], 0.0) for part in split], axis=0
            ).astype(jnp.bfloat16)
        )
        right.append(
            jnp.where(lane_at == low[c : c + 1], 1.0, 0.0).astype(jnp.bfloat16)
        )
    total = lax.dot_general(
        jnp.concatenate(left, axis=1),
        jnp.concatenate(right, axis=1),
        (((1,), (1,)), ((), ())),
        preferred_element_type=jnp.float32,
    )
    sums = []
    for i in range(len(lines)):
        part = total[3 * i * bins : 3 * (i + 1) * bins]
        sums.append(part[:bins] + part[bins : 2 * bins] + part[2 * bins :])
    return sums


def start_kernel(planes, inputs, *refs):
    sources, slab_ref, held = refs[:inputs], refs[inputs], refs[inputs + 1 : -1]
    copies = [
        pltpu.make_async_copy(source, target, refs[-1].at[i])
        for i, (source, target) in enumerate(zip(sources, held))
    ]
    for copy in copies:
        copy.start()
    (
        cols_ref,
        weights_ref,
        tracers_ref,
        send_ref,
        rows_ref,
        jac_ref,
        land_ref,
        wind_ref,
        air_ref,
    ) = held
    geo = Geometry()
    blocks = cols_ref.shape[0]
    x_points = jac_ref.shape[0]
    left, right = neighbours_of(blocks)
    levels = wind_ref.shape[0] // (2 * x_points)
    chunks = tracers_ref.shape[1] // LANES
    for copy in copies[:5]:
        copy.wait()

    def source(group, chunk):
        return tracers_ref[
            ROWS * group : ROWS * (group + 1), LANES * chunk : LANES * (chunk + 1)
        ]

    for group in range(blocks // ROWS):
        at = slice(ROWS * group, ROWS * (group + 1))
        cells = cols_ref[at, :]
        high, low = cells >> 7, cells & (LANES - 1)
        surface = jnp.zeros((ROWS, LANES), jnp.float32)
        for k in range(chunks):
            line = spread(tracers_ref[0:1, LANES * k : LANES * (k + 1)])
            surface = jnp.where(high == k, take(line, low, 1), surface)
        area = weights_ref[at, :]
        heat = area * surface
        for c in range(ROWS):
            owner = ROWS * group + c
            for place, step in enumerate((1, 0, -1)):
                to = (owner + step) % blocks
                slab_ref[to, 2 * place : 2 * place + 1, :] = heat[c : c + 1]
                slab_ref[to, 2 * place + 1 : 2 * place + 2, :] = area[c : c + 1]

    ids = rows_ref[...].astype(jnp.float32)
    for to in (left, right):
        slab_ref[to, IDS_AT : IDS_AT + blocks, :] = ids
    for part, to in enumerate((left, right)):
        cells = spread(send_ref[0:1, LANES * part : LANES * (part + 1)])
        high, low = cells >> 7, cells & (LANES - 1)
        for group in range(tracers_ref.shape[0] // ROWS):
            rim = jnp.zeros((ROWS, LANES), jnp.float32)
            for k in range(chunks):
                rim = jnp.where(high == k, take(source(group, k), low, 1), rim)
            at = IDS_AT + blocks + ROWS * group
            slab_ref[to, at : at + ROWS, :] = rim

    for copy in copies[5:]:
        copy.wait()
    strips = []
    for h in range(2):
        half = slice(ROWS * h, ROWS * (h + 1))
        second = levels * x_points
        pack = jnp.zeros((ROWS, LANES), jnp.float32)
        for i, strip in enumerate(
            (
                air_ref[half, :],
                wind_ref[half, :],
                wind_ref[second + ROWS * h : second + ROWS * (h + 1), :],
                jac_ref[half, :],
                land_ref[half, :],
            )
        ):
            pack = jnp.where(
                (geo.lane >> 4) == i, pltpu.roll(strip, 16 * i + 8, 1), pack
            )
        strips.append(pack)
    to_right, to_left = split_sides(geo, strips[0], strips[1], ROWS)
    slab_ref[right, STRIP_AT : STRIP_AT + ROWS, :] = to_right
    slab_ref[left, STRIP_AT : STRIP_AT + ROWS, :] = to_left

    level_groups = levels // ROWS
    eight = geo.lane >> 3

    def edge_tile(get, groups, repeat):
        pack = pltpu.roll(get(0), GLL, 1)
        for group in range(1, groups):
            pack = jnp.where(
                eight == group, pltpu.roll(get(group), ROWS * group + GLL, 1), pack
            )
        return take(pack, geo.lane & (ROWS * groups - 1), 1) if repeat else pack

    y_weight = jnp.where(geo.y_edge, 1.0 / 6.0, 5.0 / 6.0)
    packs = [jnp.zeros((ROWS, LANES), jnp.float32) for _ in range(2)]
    for element in range(x_points // GLL):
        lines = [GLL * element + i for i in range(GLL)]
        fields = [
            edge_tile(
                lambda g: air_ref[pl.ds(ROWS * g * x_points + x, ROWS, stride=x_points), :],
                planes // ROWS,
                False,
            )
            for x in lines
        ]
        slopes = geo.d_y(*fields)
        for i, x in enumerate(lines):
            wind = [
                edge_tile(
                    lambda g: wind_ref[
                        pl.ds(
                            (levels * part + ROWS * g) * x_points + x,
                            ROWS,
                            stride=x_points,
                        ),
                        :,
                    ],
                    level_groups,
                    True,
                )
                for part in range(2)
            ]
            jac = edge_tile(lambda g: spread(jac_ref[x : x + 1, :]), 1, True)
            x_weight = 1.0 / 6.0 if i in (0, GLL - 1) else 5.0 / 6.0
            slope = sum(deriv_table[i][j] * fields[j] for j in range(GLL))
            moved = (x_weight * y_weight * jac) * (
                fields[i] - time_step * (wind[0] * slope + wind[1] * slopes[i])
            )
            q, at = edge_place(x, 0)
            mine = ((geo.lane & (ROWS - 1)) >> 1 == at % ROWS // 2) & (
                (geo.lane >> 6) == at // (LANES // 2)
            )
            packs[q] = jnp.where(mine, pltpu.roll(moved, (at - GLL + 1) % LANES, 1), packs[q])
    to_right, to_left = split_sides(geo, packs[0], packs[1], 1)
    slab_ref[right, EDGE_AT : EDGE_AT + ROWS, :] = to_right
    slab_ref[left, EDGE_AT : EDGE_AT + ROWS, :] = to_left


def moved_kernel(planes, air_ref, wind_ref, jac_ref, after_ref, moved_ref):
    geo = Geometry()
    x_points = jac_ref.shape[0]
    levels = wind_ref.shape[0] // (2 * x_points)
    y_weight = jnp.where(geo.y_edge, 1.0 / 6.0, 5.0 / 6.0)
    for element in range(x_points // GLL):
        lines = [GLL * element + i for i in range(GLL)]
        mass = [
            (1.0 / 6.0 if i in (0, GLL - 1) else 5.0 / 6.0)
            * y_weight
            * spread(jac_ref[x : x + 1, :])
            for i, x in enumerate(lines)
        ]
        for level in range(0, levels, ROWS):
            wind = [
                [
                    time_step
                    * wind_ref[
                        pl.ds((levels * part + level) * x_points + x, ROWS, stride=x_points), :
                    ]
                    for x in lines
                ]
                for part in range(2)
            ]
            for plane in range(level, planes, levels):
                fields = [
                    air_ref[pl.ds(plane * x_points + x, ROWS, stride=x_points), :]
                    for x in lines
                ]
                slopes = geo.d_y(*fields)
                for i, x in enumerate(lines):
                    slope = sum(deriv_table[i][j] * fields[j] for j in range(GLL))
                    moved_ref[planes * x + plane : planes * x + plane + ROWS, :] = mass[
                        i
                    ] * (fields[i] - (wind[0][i] * slope + wind[1][i] * slopes[i]))


def panel_kernel(
    planes,
    moved_ref,
    recv_ref,
    air_ref,
    wind_ref,
    jac_ref,
    land_ref,
    rows_ref,
    after_ref,
    avg_ref,
    down_ref,
    up_ref,
    surf_ref,
):
    geo = Geometry()
    blocks = rows_ref.shape[0]
    left, right = neighbours_of(blocks)
    x_points = jac_ref.shape[0]
    levels = wind_ref.shape[0] // (2 * x_points)

    own_ids = rows_ref[...]
    left_ids = recv_ref[left, IDS_AT : IDS_AT + blocks, :].astype(jnp.int32)
    right_ids = recv_ref[right, IDS_AT : IDS_AT + blocks, :].astype(jnp.int32)
    head = [
        jnp.concatenate([recv_ref[c, i : i + 1, :] for c in range(blocks)], axis=0)
        for i in range(6)
    ]
    heat, frac = scatter_sum(head[2:4], own_ids, 2 * ROWS)
    from_left = scatter_sum(
        head[0:2], left_ids, 2 * ROWS, lambda lane: lane >= LANES - ROWS
    )
    from_right = scatter_sum(head[4:6], right_ids, 2 * ROWS, lambda lane: lane < ROWS)
    strip_heat = from_left[0] + from_right[0]
    strip_frac = from_left[1] + from_right[1]

    in_strip = (geo.lane < ROWS) | (geo.lane >= LANES - ROWS)
    packs = join_sides(
        geo,
        recv_ref[left, STRIP_AT : STRIP_AT + ROWS, :],
        recv_ref[right, STRIP_AT : STRIP_AT + ROWS, :],
        ROWS,
    )
    own, strip = [], []
    for h, pack in enumerate(packs):
        half = slice(ROWS * h, ROWS * (h + 1))
        strip.append(
            [
                jnp.where(
                    in_strip, pltpu.roll(pack, (-(16 * i + 8)) % LANES, 1), 1.0
                )
                for i in range(5)
            ]
        )
        own.append(
            [
                air_ref[half, :],
                wind_ref[half, :],
                wind_ref[
                    levels * x_points + ROWS * h : levels * x_points + ROWS * (h + 1), :
                ],
                jac_ref[half, :],
                land_ref[half, :],
            ]
        )
    for h in range(2):
        half = slice(ROWS * h, ROWS * (h + 1))
        pair = []
        for tile, ((field, wind_x, wind_y, jac, land), tile_heat, tile_frac) in enumerate(
            ((own[h], heat[half], frac[half]), (strip[h], strip_heat[half], strip_frac[half]))
        ):
            mass = geo.weight * jac
            if tile == 1:
                tile_heat = jnp.where(in_strip, tile_heat, 0.0)
                tile_frac = jnp.where(in_strip, tile_frac, 0.0)
            surf = (tile_heat + land * field) / (tile_frac + land)
            coef_x, coef_y = time_step * mass * wind_x, time_step * mass * wind_y
            moved = (
                mass * (field + relax_rate * (surf - field))
                - coef_x * geo.d_x(field)
                - coef_y * geo.d_y(field)[0]
            )
            pair.append((moved, mass))
            at = 2 * ROWS * tile + ROWS * h
            for number, value in (
                (MASS, mass),
                (COEF_X, coef_x),
                (COEF_Y, coef_y),
                (SURF, surf),
            ):
                surf_ref[4 * ROWS * number + at : 4 * ROWS * number + at + ROWS, :] = value
        for number, i in ((AVG, 0), (MASS_SUM, 1)):
            for tile, value in enumerate(geo.sum_y_pair(pair[0][i], pair[1][i])):
                at = 4 * ROWS * number + 2 * ROWS * tile + ROWS * h
                surf_ref[at : at + ROWS, :] = value

    joined = join_edges(
        geo,
        recv_ref[left, EDGE_AT : EDGE_AT + ROWS, :],
        recv_ref[right, EDGE_AT : EDGE_AT + ROWS, :],
    )
    for x in range(x_points):
        for group in range(planes // ROWS):
            at = slice(planes * x + ROWS * group, planes * x + ROWS * (group + 1))
            avg_ref[at, :] = geo.sum_y(moved_ref[at, :], outer_edges(joined, x, group))

    def line(r):
        return avg_ref[planes * r : planes * (r + 1), :]

    def surf_line(number, r):
        return surf_ref[pl.ds(4 * ROWS * number + r, 2, stride=x_points), :]

    def first_step(get, mass_at):
        return (
            [
                get(1) / mass_at(1),
                get(2) / mass_at(2),
                (get(3) + get(4)) / (mass_at(3) + mass_at(4)),
            ],
            [
                (get(11) + get(12)) / (mass_at(11) + mass_at(12)),
                get(13) / mass_at(13),
                get(14) / mass_at(14),
            ],
        )

    def own_mass_sum(r):
        return surf_ref[4 * ROWS * MASS_SUM + r : 4 * ROWS * MASS_SUM + r + 1, :]

    low_lines, high_lines = first_step(line, own_mass_sum)
    surf_low, surf_high = first_step(
        functools.partial(surf_line, AVG), functools.partial(surf_line, MASS_SUM)
    )
    for out_ref, r, lines, surf_lines, coefs in (
        (down_ref, 0, low_lines, surf_low, deriv_table[0][1:]),
        (up_ref, 15, high_lines, surf_high, deriv_table[3][:3]),
    ):
        slope = sum(coef * value for coef, value in zip(coefs, lines))
        surf_slope = sum(coef * value for coef, value in zip(coefs, surf_lines))
        mass = surf_ref[4 * ROWS * MASS + r : 4 * ROWS * MASS + r + 1, :]
        wind = time_step * mass * wind_ref[pl.ds(r, 2 * levels, stride=x_points), :]
        out_ref[0:planes, :] = line(r)
        for first in range(0, planes, levels):
            out_ref[planes + first : planes + first + levels, :] = (
                wind[:levels] * slope[first : first + levels]
            )
        base = 2 * planes
        out_ref[base : base + 2 * levels, :] = wind
        base += 2 * levels
        for number in range(SURF_ARRAYS):
            out_ref[base + 2 * number : base + 2 * number + 2, :] = surf_line(number, r)
        base += 2 * SURF_ARRAYS
        out_ref[base : base + 2, :] = surf_line(COEF_X, r) * surf_slope


def surface_kernel(
    surf_ref, low_ref, high_ref, rows_ref, after_ref, slab_ref, final_ref, inverse_ref
):
    geo = Geometry()
    blocks = rows_ref.shape[0]
    base = low_ref.shape[0] - 2 * SURF_ARRAYS - 4

    def surf_tile(number, tile, h):
        at = 4 * ROWS * number + 2 * ROWS * tile + ROWS * h
        return surf_ref[at : at + ROWS, :]

    def beside(ref, number, tile):
        at = base + 2 * number + tile
        return spread(ref[at : at + 1, :])

    ends = []
    inverse = []
    for tile in range(2):
        total = geo.sum_x(
            surf_tile(MASS_SUM, tile, 0),
            surf_tile(MASS_SUM, tile, 1),
            beside(low_ref, MASS_SUM, tile),
            beside(high_ref, MASS_SUM, tile),
        )
        inverse.append([1.0 / value for value in total])
        summed = geo.sum_x(
            surf_tile(AVG, tile, 0),
            surf_tile(AVG, tile, 1),
            beside(low_ref, AVG, tile),
            beside(high_ref, AVG, tile),
        )
        fields = [value * scale for value, scale in zip(summed, inverse[tile])]
        moved = []
        for h in range(2):
            field = fields[h]
            moved.append(
                surf_tile(MASS, tile, h)
                * (field + relax_rate * (surf_tile(SURF, tile, h) - field))
                - surf_tile(COEF_X, tile, h) * geo.d_x(field)
                - surf_tile(COEF_Y, tile, h) * geo.d_y(field)[0]
            )
        halos = []
        for ref, field, own_coef in (
            (low_ref, spread(fields[0][:1]), deriv_table[3][3]),
            (high_ref, spread(fields[1][ROWS - 1 :]), deriv_table[0][0]),
        ):
            halos.append(
                beside(ref, MASS, tile)
                * (field + relax_rate * (beside(ref, SURF, tile) - field))
                - beside(ref, SURF_ARRAYS, tile)
                - beside(ref, COEF_X, tile) * (own_coef * field)
                - beside(ref, COEF_Y, tile) * geo.d_y(field)[0]
            )
        ends.append(geo.sum_x(moved[0], moved[1], halos[0], halos[1]))
    final = []
    for h in range(2):
        summed, _ = geo.sum_y_pair(ends[0][h], ends[1][h])
        final.append(summed * inverse[0][h])
        final_ref[ROWS * h : ROWS * (h + 1), :] = final[h]
        inverse_ref[ROWS * h : ROWS * (h + 1), :] = inverse[0][h]
    flux = [final[h] - surf_tile(SURF, 0, h) for h in range(2)]
    for group in range(blocks // ROWS):
        ids = rows_ref[ROWS * group : ROWS * (group + 1), :]
        high, low = ids >> 7, ids & (LANES - 1)
        picked = jnp.zeros((ROWS, LANES), jnp.float32)
        for x in range(2 * ROWS):
            line = spread(flux[x // ROWS][x % ROWS : x % ROWS + 1])
            picked = jnp.where(high == x, take(line, low, 1), picked)
        for c in range(ROWS):
            slab_ref[ROWS * group + c, 0:1, :] = picked[c : c + 1]


def second_kernel(
    planes,
    avg_ref,
    surf_ref,
    inverse_ref,
    low_ref,
    high_ref,
    wind_ref,
    sums_ref,
    edges_ref,
):
    geo = Geometry()
    x_points = inverse_ref.shape[0]
    levels = wind_ref.shape[0] // (2 * x_points)
    surf_base = low_ref.shape[0] - 2 * SURF_ARRAYS - 4
    packs = [jnp.zeros((ROWS, LANES), jnp.float32) for _ in range(2)]

    def put(x, plane, value):
        sums_ref[planes * x + plane : planes * x + plane + ROWS, :] = value
        pack_edges(geo, packs, value, x, plane // ROWS)

    def beyond(ref, plane, field, slope, own_coef):
        mass_at = surf_base + 2 * MASS
        wind_at = 2 * planes + plane % levels
        return (
            spread(ref[mass_at : mass_at + 1, :]) * field
            - ref[planes + plane : planes + plane + ROWS, :]
            - ref[wind_at : wind_at + ROWS, :] * (own_coef * field)
            - ref[wind_at + levels : wind_at + levels + ROWS, :] * slope
        )

    for plane in range(0, planes, ROWS):
        here = slice(plane, plane + ROWS)
        held = None
        for element in range(x_points // GLL):
            lines = [GLL * element + i for i in range(GLL)]
            fields = []
            for i, x in enumerate(lines):
                total = avg_ref[planes * x + plane : planes * x + plane + ROWS, :]
                other = x - 1 if i == 0 else x + 1
                if other < 0:
                    total = total + low_ref[here, :]
                elif other == x_points:
                    total = total + high_ref[here, :]
                elif i in (0, GLL - 1):
                    at = planes * other + plane
                    total = total + avg_ref[at : at + ROWS, :]
                fields.append(total * spread(inverse_ref[x : x + 1, :]))
            slopes = geo.d_y(*fields)
            moved = []
            for i, x in enumerate(lines):
                wind = [
                    time_step
                    * wind_ref[
                        pl.ds(
                            (levels * part + plane % levels) * x_points + x,
                            ROWS,
                            stride=x_points,
                        ),
                        :,
                    ]
                    for part in range(2)
                ]
                slope = sum(deriv_table[i][j] * fields[j] for j in range(GLL))
                mass_at = 4 * ROWS * MASS + x
                moved.append(
                    spread(surf_ref[mass_at : mass_at + 1, :])
                    * (fields[i] - (wind[0] * slope + wind[1] * slopes[i]))
                )
            first, last = lines[0], lines[-1]
            if first == 0:
                before = beyond(low_ref, plane, fields[0], slopes[0], deriv_table[3][3])
                put(first, plane, before + moved[0])
            else:
                shared = held + moved[0]
                put(first - 1, plane, shared)
                put(first, plane, shared)
            for i in range(1, GLL - 1):
                put(lines[i], plane, moved[i])
            held = moved[-1]
            if last == x_points - 1:
                after = beyond(high_ref, plane, fields[-1], slopes[-1], deriv_table[0][0])
                put(last, plane, held + after)
    for q, pack in enumerate(packs):
        edges_ref[ROWS * q : ROWS * (q + 1), :] = pack


def end_kernel(
    planes,
    sums_ref,
    before_ref,
    after_ref,
    recv_ref,
    final_ref,
    inverse_ref,
    cols_ref,
    weights_ref,
    gain_ref,
    ocean_ref,
    air_out,
    ocean_out,
):
    geo = Geometry()
    blocks = cols_ref.shape[0]
    chunks = gain_ref.shape[0]
    arrived = jnp.concatenate([recv_ref[c, 0:1, :] for c in range(blocks)], axis=0)
    (inflow,) = scatter_sum([weights_ref[...] * arrived], cols_ref[...], chunks)
    gain = inflow * gain_ref[...]
    ocean_out[...] = ocean_ref[...]
    for k in range(chunks):
        at = slice(LANES * k, LANES * (k + 1))
        ocean_out[0:1, at] = ocean_ref[0:1, at] + gain[k : k + 1]

    x_points = inverse_ref.shape[0]
    odd = (geo.lane & 1) != 0
    joined = [
        jnp.where(
            odd,
            pltpu.roll(before_ref[ROWS * q : ROWS * (q + 1), :], 1, 1),
            pltpu.roll(after_ref[ROWS * q : ROWS * (q + 1), :], LANES - 1, 1),
        )
        for q in range(2)
    ]
    for x in range(x_points):
        inverse = spread(inverse_ref[x : x + 1, :])
        for group in range(planes // ROWS):
            at = planes * x + ROWS * group
            air_out[pl.ds(ROWS * group * x_points + x, ROWS, stride=x_points), :] = (
                inverse
                * geo.sum_y(sums_ref[at : at + ROWS, :], outer_edges(joined, x, group))
            )
    air_out[0:x_points, :] = final_ref[...]


def gathered(ids, coefs, source, sources, groups, first=0):
    totals = [jnp.zeros((ROWS, LANES), jnp.float32) for _ in range(groups)]
    for edge in range(ids.shape[0]):
        cell = spread(ids[edge : edge + 1])
        coef = spread(coefs[edge : edge + 1])
        high, low = cell >> 7, cell & (LANES - 1)
        for s in range(sources):
            scaled = jnp.where(high == first + s, coef, 0.0)
            for group in range(groups):
                totals[group] += scaled * take(source(group, s), low, 1)
    return totals


def ocean_kernel(
    levels, start, tracers_ref, coef_ref, near_ref, rate_ref, after_ref, out_ref
):
    chunks = tracers_ref.shape[1] // LANES
    groups = tracers_ref.shape[0] // ROWS
    row = iota((ROWS, LANES), 0)

    def source(group, s):
        return tracers_ref[
            ROWS * group : ROWS * (group + 1), LANES * s : LANES * (s + 1)
        ]

    def one_chunk(number, carry):
        k = number + start
        at = pl.ds(pl.multiple_of(k * LANES, LANES), LANES)
        out_at = pl.ds(pl.multiple_of(number * LANES, LANES), LANES)
        ids, coefs = near_ref[:, at], coef_ref[:, at]
        totals = gathered(ids, coefs, source, chunks, groups)
        coef_sum = spread(jnp.sum(coefs, axis=0, keepdims=True))
        rate = spread(rate_ref[pl.ds(k, 1), :])
        tiles = [tracers_ref[ROWS * g : ROWS * (g + 1), at] for g in range(groups)]
        for g in range(groups):
            tile = tiles[g]
            top = bottom = tile
            if (ROWS * g) % levels:
                top = pltpu.roll(tiles[g - 1], 1, 0)
            if (ROWS * (g + 1)) % levels:
                bottom = pltpu.roll(tiles[g + 1], ROWS - 1, 0)
            above = jnp.where(row == 0, top, pltpu.roll(tile, 1, 0))
            below = jnp.where(row == ROWS - 1, bottom, pltpu.roll(tile, ROWS - 1, 0))
            vertical = rate * ((above - tile) + (below - tile))
            out_ref[ROWS * g : ROWS * (g + 1), out_at] = (
                tile + (totals[g] - coef_sum * tile) + vertical
            )
        return carry

    lax.fori_loop(0, out_ref.shape[1] // LANES, one_chunk, 0)


def rim_kernel(
    starts,
    recv_ref,
    coef_ref,
    near_ref,
    area_ref,
    after_ref,
    *refs,
):
    partial_refs, (out_ref, gain_ref) = refs[: len(starts)], refs[len(starts) :]
    chunks = coef_ref.shape[1] // LANES
    groups = out_ref.shape[0] // ROWS
    blocks = recv_ref.shape[0]
    sides = neighbours_of(blocks)
    gain_ref[...] = flux_gain / area_ref[...]

    def source(group, s):
        at = IDS_AT + blocks + ROWS * group
        return recv_ref[sides[s], at : at + ROWS, :]

    for k in range(chunks):
        at = slice(LANES * k, LANES * (k + 1))
        totals = gathered(near_ref[:, at], coef_ref[:, at], source, 2, groups, chunks)
        part = max(i for i, start in enumerate(starts) if start <= k)
        place = slice(LANES * (k - starts[part]), LANES * (k - starts[part] + 1))
        for g in range(groups):
            half = slice(ROWS * g, ROWS * (g + 1))
            out_ref[half, at] = partial_refs[part][half, place] + totals[g]


VMEM_SPEC = pl.BlockSpec(memory_space=pltpu.VMEM)
ANY_SPEC = pl.BlockSpec(memory_space=pl.ANY)
HBM_SPEC = pl.BlockSpec(memory_space=pltpu.HBM)


def call(kernel, outs, specs, scratch=(), cost=0):
    estimate = None
    if cost:
        estimate = pl.CostEstimate(flops=0, bytes_accessed=cost, transcendentals=0)
    return pl.pallas_call(
        kernel,
        out_shape=[jax.ShapeDtypeStruct(shape, jnp.float32) for shape in outs],
        in_specs=specs,
        scratch_shapes=list(scratch),
        cost_estimate=estimate,
        compiler_params=pltpu.CompilerParams(vmem_limit_bytes=32 * 2**20),
        name=getattr(kernel, "func", kernel).__name__,
    )


def body(
    air_state,
    air_wind,
    jacobian,
    land_area,
    xgrid_rows,
    tracers,
    edge_coef,
    neighbours,
    vert_rate,
    ocean_area,
    send_list,
    xgrid_cols,
    xgrid_weights,
):
    field_count, levels, x_points, y_points = air_state.shape
    planes = field_count * levels
    ocean_levels, cells = tracers.shape[1:]
    ocean_planes = tracers.shape[0] * ocean_levels
    faces, blocks = lax.axis_size("face"), lax.axis_size("blk")
    air = air_state.reshape(planes * x_points, y_points)
    wind = air_wind.reshape(2 * levels * x_points, y_points)
    ocean = tracers.reshape(ocean_planes, cells)
    point_ids, cell_ids, weights = xgrid_rows[0], xgrid_cols[0], xgrid_weights[0]
    rate = vert_rate.reshape(cells // LANES, LANES)
    area = ocean_area.reshape(cells // LANES, LANES)
    first_inputs = (
        cell_ids,
        weights,
        ocean,
        send_list,
        point_ids,
        jacobian,
        land_area,
        wind,
        air,
    )
    (slab,) = call(
        functools.partial(start_kernel, planes, len(first_inputs)),
        [(blocks, IDS_AT + blocks + ocean_planes, LANES)],
        [HBM_SPEC] * len(first_inputs),
        [pltpu.VMEM(array.shape, array.dtype) for array in first_inputs]
        + [pltpu.SemaphoreType.DMA((len(first_inputs),))],
    )(*(pltpu.with_memory_space_constraint(array, pltpu.HBM) for array in first_inputs))
    recv = lax.all_to_all(slab, "blk", split_axis=0, concat_axis=0, tiled=True)

    chunks = cells // LANES
    reads_per_chunk = edge_coef.shape[0] * chunks * (ocean_planes // ROWS)
    starts = (0, chunks * 5 // 8)

    def ocean_part(start, end, after):
        (result,) = call(
            functools.partial(ocean_kernel, ocean_levels, start),
            [(ocean_planes, (end - start) * LANES)],
            [VMEM_SPEC] * 4 + [ANY_SPEC],
            cost=(end - start) * reads_per_chunk * ROWS * LANES * 4,
        )(ocean, edge_coef, neighbours, rate, after)
        return result

    (moved,) = call(
        functools.partial(moved_kernel, planes),
        [air.shape],
        [VMEM_SPEC] * 3 + [ANY_SPEC],
        cost=4 * air.size * 4,
    )(air, wind, jacobian, slab)
    first_part = ocean_part(starts[0], starts[1], slab)
    side_rows = 2 * planes + 2 * levels + 2 * SURF_ARRAYS + 4
    avg, down, up, surf = call(
        functools.partial(panel_kernel, planes),
        [air.shape, (side_rows, LANES), (side_rows, LANES), (4 * ROWS * SURF_ARRAYS, LANES)],
        [VMEM_SPEC] * 7 + [ANY_SPEC],
    )(moved, recv, air, wind, jacobian, land_area, point_ids, first_part)
    after_me = [(i, (i + 1) % faces) for i in range(faces)]
    low = lax.ppermute(up, "face", after_me)
    high = lax.ppermute(down, "face", [(to, source) for source, to in after_me])
    second_part = ocean_part(starts[1], chunks, surf)

    slab, final, inverse = call(
        surface_kernel,
        [(blocks, ROWS, LANES), (x_points, y_points), (x_points, y_points)],
        [VMEM_SPEC] * 4 + [ANY_SPEC],
    )(surf, low, high, point_ids, second_part)
    arrived = lax.all_to_all(slab, "blk", split_axis=0, concat_axis=0, tiled=True)
    sums, edges = call(
        functools.partial(second_kernel, planes),
        [air.shape, (2 * ROWS, LANES)],
        [VMEM_SPEC] * 6,
        cost=4 * air.size * 4,
    )(avg, surf, inverse, low, high, wind)
    after_me = [(i, (i + 1) % blocks) for i in range(blocks)]
    before = lax.ppermute(edges, "blk", after_me)
    after = lax.ppermute(edges, "blk", [(to, source) for source, to in after_me])
    partial, gain = call(
        functools.partial(rim_kernel, starts),
        [ocean.shape, area.shape],
        [VMEM_SPEC] * 4 + [ANY_SPEC] + [VMEM_SPEC] * len(starts),
        cost=chunks * reads_per_chunk // 8 * ROWS * LANES * 4,
    )(recv, edge_coef, neighbours, area, edges, first_part, second_part)
    air_final, ocean_final = call(
        functools.partial(end_kernel, planes),
        [air.shape, ocean.shape],
        [VMEM_SPEC] * 10,
    )(sums, before, after, arrived, final, inverse, cell_ids, weights, gain, partial)
    return air_final.reshape(air_state.shape), ocean_final.reshape(tracers.shape)


def solution(mesh):
    return jax.shard_map(
        body,
        mesh=mesh,
        in_specs=(
            P(None, None, "face", "blk"),
            P(None, None, "face", "blk"),
            P("face", "blk"),
            P("face", "blk"),
            P(("face", "blk"), None, None),
            P(None, None, ("face", "blk")),
            P(None, ("face", "blk")),
            P(None, ("face", "blk")),
            P(("face", "blk")),
            P(("face", "blk")),
            P(("face", "blk"), None),
            P(("face", "blk"), None, None),
            P(("face", "blk"), None, None),
        ),
        out_specs=(P(None, None, "face", "blk"), P(None, None, ("face", "blk"))),
        check_vma=False,
    )
```

```python
import functools

import jax
import jax.numpy as jnp
from jax import lax
from jax.experimental import pallas as pl
from jax.experimental.pallas import tpu as pltpu
from jax.sharding import PartitionSpec as P

GLL = 4
ROWS = 8
LANES = 128

deriv_table = [
    [-3.0, 4.045084971874737, -1.545084971874737, 0.5],
    [-0.8090169943749475, 0.0, 1.118033988749895, -0.30901699437494745],
    [0.30901699437494745, -1.118033988749895, 0.0, 0.8090169943749475],
    [-0.5, 1.545084971874737, -4.045084971874737, 3.0],
]
time_step = 0.05
relax_rate = 0.3
flux_gain = 0.2

HEAD, EDGE_AT, STRIP_AT, IDS_AT = 8, 8, 16, 24
AVG, MASS_SUM, MASS, COEF_X, COEF_Y, SURF = range(6)
SURF_ARRAYS = 6


def iota(shape, dim):
    return lax.broadcasted_iota(jnp.int32, shape, dim)


def take(values, index, axis):
    return jnp.take_along_axis(values, index, axis=axis, mode="promise_in_bounds")


def by_position(pos, values):
    result = jnp.full(pos.shape, values[-1], jnp.float32)
    for i, value in enumerate(values[:-1]):
        result = jnp.where(pos == i, value, result)
    return result


def spread(row):
    return jnp.broadcast_to(row, (ROWS, LANES))


class Geometry:
    def __init__(self):
        shape = (ROWS, LANES)
        self.row, self.lane = iota(shape, 0), iota(shape, 1)
        x_pos, y_pos = self.row & (GLL - 1), self.lane & (GLL - 1)
        self.y_from = [self.lane - y_pos + j for j in range(GLL)]
        columns = [[line[j] for line in deriv_table] for j in range(GLL)]
        self.x_coef = {
            step: by_position(
                x_pos,
                [
                    deriv_table[i][i + step] if 0 <= i + step < GLL else 0.0
                    for i in range(GLL)
                ],
            )
            for step in range(1 - GLL, GLL)
        }
        self.y_coef = [by_position(y_pos, column) for column in columns]
        self.y_swap = (
            self.lane + jnp.where(y_pos == GLL - 1, 1, 0) - jnp.where(y_pos == 0, 1, 0)
        ) & (LANES - 1)
        self.x_edge = (x_pos == 0) | (x_pos == GLL - 1)
        self.y_edge = (y_pos == 0) | (y_pos == GLL - 1)
        self.first_row, self.last_row = self.row == 0, self.row == ROWS - 1
        self.middle_row = self.row == GLL
        self.outer_lane = (self.lane == 0) | (self.lane == LANES - 1)
        self.weight = jnp.where(self.x_edge, 1.0 / 6.0, 5.0 / 6.0) * jnp.where(
            self.y_edge, 1.0 / 6.0, 5.0 / 6.0
        )

    def d_x(self, tile):
        return sum(
            coef * (pltpu.roll(tile, -step % ROWS, 0) if step else tile)
            for step, coef in self.x_coef.items()
        )

    def d_y(self, *tiles):
        totals = [0.0] * len(tiles)
        for j in range(GLL):
            for i, tile in enumerate(tiles):
                totals[i] += self.y_coef[j] * take(tile, self.y_from[j], 1)
        return totals

    def sum_x(self, low, high, before, after):
        low_down, low_up = pltpu.roll(low, 1, 0), pltpu.roll(low, ROWS - 1, 0)
        high_down, high_up = pltpu.roll(high, 1, 0), pltpu.roll(high, ROWS - 1, 0)
        low_other = jnp.where(
            self.first_row,
            before,
            jnp.where(
                self.middle_row, low_down, jnp.where(self.last_row, high_up, low_up)
            ),
        )
        high_other = jnp.where(
            self.first_row,
            low_down,
            jnp.where(
                self.middle_row, high_down, jnp.where(self.last_row, after, high_up)
            ),
        )
        return (
            low + jnp.where(self.x_edge, low_other, 0.0),
            high + jnp.where(self.x_edge, high_other, 0.0),
        )

    def sum_y(self, tile, outer):
        other = jnp.where(self.outer_lane, outer, take(tile, self.y_swap, 1))
        return tile + jnp.where(self.y_edge, other, 0.0)

    def sum_y_pair(self, own, strip):
        own_swap, strip_swap = take(own, self.y_swap, 1), take(strip, self.y_swap, 1)
        own_other = jnp.where(self.outer_lane, strip_swap, own_swap)
        strip_other = jnp.where(self.outer_lane, own_swap, strip_swap)
        return (
            own + jnp.where(self.y_edge, own_other, 0.0),
            strip + jnp.where(self.y_edge, strip_other, 0.0),
        )


def edge_place(x, group):
    return x // ROWS, LANES // 2 * (x % 2) + ROWS * group + 2 * (x % ROWS // 2)


def pack_edges(geo, packs, tile, x, group):
    q, at = edge_place(x, group)
    rolled = pltpu.roll(tile, (at + 1) % LANES, 1)
    packs[q] = jnp.where((geo.lane >> 1) == at // 2, rolled, packs[q])


def outer_edges(joined, x, group):
    q, at = edge_place(x, group)
    return pltpu.roll(joined[q], (-(at + 1)) % LANES, 1)


def split_sides(geo, first, second, unit):
    odd = (geo.lane & unit) != 0
    return (
        jnp.where(odd, pltpu.roll(second, unit, 1), first),
        jnp.where(odd, second, pltpu.roll(first, LANES - unit, 1)),
    )


def join_sides(geo, before, after, unit):
    odd = (geo.lane & unit) != 0
    return (
        jnp.where(odd, pltpu.roll(after, unit, 1), before),
        jnp.where(odd, after, pltpu.roll(before, LANES - unit, 1)),
    )


def join_edges(geo, before, after):
    odd = (geo.lane & 1) != 0
    return (
        jnp.where(odd, pltpu.roll(before, 1, 1), after),
        jnp.where(odd, before, pltpu.roll(after, LANES - 1, 1)),
    )


def neighbours_of(blocks):
    here = lax.axis_index("blk")
    return lax.rem(here + blocks - 1, blocks), lax.rem(here + 1, blocks)


def scatter_sum(lines, index, bins, allowed=None):
    count = index.shape[0]
    split = []
    for values in lines:
        for part in range(3):
            short = values.astype(jnp.bfloat16).astype(jnp.float32)
            split.append(short)
            values = values - short
    high, low = index >> 7, index & (LANES - 1)
    bin_at = iota((bins, LANES), 0)
    lane_at = iota((LANES, LANES), 0)
    if allowed is not None:
        lane_at = jnp.where(allowed(lane_at), lane_at, -1)
    left, right = [], []
    for c in range(count):
        hit = bin_at == high[c : c + 1]
        left.append(
            jnp.concatenate(
                [jnp.where(hit, part[c : c + 1], 0.0) for part in split], axis=0
            ).astype(jnp.bfloat16)
        )
        right.append(
            jnp.where(lane_at == low[c : c + 1], 1.0, 0.0).astype(jnp.bfloat16)
        )
    total = lax.dot_general(
        jnp.concatenate(left, axis=1),
        jnp.concatenate(right, axis=1),
        (((1,), (1,)), ((), ())),
        preferred_element_type=jnp.float32,
    )
    sums = []
    for i in range(len(lines)):
        part = total[3 * i * bins : 3 * (i + 1) * bins]
        sums.append(part[:bins] + part[bins : 2 * bins] + part[2 * bins :])
    return sums


def wind_tiles(wind_ref, x_points, level, lines):
    levels = wind_ref.shape[0] // (2 * x_points)
    return [
        [
            time_step
            * wind_ref[
                pl.ds((levels * part + level) * x_points + x, ROWS, stride=x_points), :
            ]
            for x in lines
        ]
        for part in range(2)
    ]


def start_kernel(planes, inputs, *refs):
    sources, (slab_ref, moved_ref), held = (
        refs[:inputs],
        refs[inputs : inputs + 2],
        refs[inputs + 2 : -1],
    )
    copies = [
        pltpu.make_async_copy(source, target, refs[-1].at[i])
        for i, (source, target) in enumerate(zip(sources, held))
    ]
    for copy in copies:
        copy.start()
    (
        cols_ref,
        weights_ref,
        tracers_ref,
        send_ref,
        rows_ref,
        jac_ref,
        land_ref,
        wind_ref,
        air_ref,
    ) = held
    geo = Geometry()
    blocks = cols_ref.shape[0]
    x_points = jac_ref.shape[0]
    left, right = neighbours_of(blocks)
    levels = wind_ref.shape[0] // (2 * x_points)
    chunks = tracers_ref.shape[1] // LANES
    for copy in copies[:5]:
        copy.wait()

    def source(group, chunk):
        return tracers_ref[
            ROWS * group : ROWS * (group + 1), LANES * chunk : LANES * (chunk + 1)
        ]

    for group in range(blocks // ROWS):
        at = slice(ROWS * group, ROWS * (group + 1))
        cells = cols_ref[at, :]
        high, low = cells >> 7, cells & (LANES - 1)
        surface = jnp.zeros((ROWS, LANES), jnp.float32)
        for k in range(chunks):
            line = spread(tracers_ref[0:1, LANES * k : LANES * (k + 1)])
            surface = jnp.where(high == k, take(line, low, 1), surface)
        area = weights_ref[at, :]
        heat = area * surface
        for c in range(ROWS):
            owner = ROWS * group + c
            for place, step in enumerate((1, 0, -1)):
                to = (owner + step) % blocks
                slab_ref[to, 2 * place : 2 * place + 1, :] = heat[c : c + 1]
                slab_ref[to, 2 * place + 1 : 2 * place + 2, :] = area[c : c + 1]

    ids = rows_ref[...].astype(jnp.float32)
    for to in (left, right):
        slab_ref[to, IDS_AT : IDS_AT + blocks, :] = ids
    for part, to in enumerate((left, right)):
        cells = spread(send_ref[0:1, LANES * part : LANES * (part + 1)])
        high, low = cells >> 7, cells & (LANES - 1)
        for group in range(tracers_ref.shape[0] // ROWS):
            rim = jnp.zeros((ROWS, LANES), jnp.float32)
            for k in range(chunks):
                rim = jnp.where(high == k, take(source(group, k), low, 1), rim)
            at = IDS_AT + blocks + ROWS * group
            slab_ref[to, at : at + ROWS, :] = rim

    for copy in copies[5:]:
        copy.wait()
    strips = []
    for h in range(2):
        half = slice(ROWS * h, ROWS * (h + 1))
        second = levels * x_points
        pack = jnp.zeros((ROWS, LANES), jnp.float32)
        for i, strip in enumerate(
            (
                air_ref[half, :],
                wind_ref[half, :],
                wind_ref[second + ROWS * h : second + ROWS * (h + 1), :],
                jac_ref[half, :],
                land_ref[half, :],
            )
        ):
            pack = jnp.where(
                (geo.lane >> 4) == i, pltpu.roll(strip, 16 * i + 8, 1), pack
            )
        strips.append(pack)
    to_right, to_left = split_sides(geo, strips[0], strips[1], ROWS)
    slab_ref[right, STRIP_AT : STRIP_AT + ROWS, :] = to_right
    slab_ref[left, STRIP_AT : STRIP_AT + ROWS, :] = to_left

    y_weight = jnp.where(geo.y_edge, 1.0 / 6.0, 5.0 / 6.0)
    packs = [jnp.zeros((ROWS, LANES), jnp.float32) for _ in range(2)]
    for element in range(x_points // GLL):
        lines = [GLL * element + i for i in range(GLL)]
        mass = [
            (1.0 / 6.0 if i in (0, GLL - 1) else 5.0 / 6.0)
            * y_weight
            * spread(jac_ref[x : x + 1, :])
            for i, x in enumerate(lines)
        ]
        for level in range(0, levels, ROWS):
            wind = wind_tiles(wind_ref, x_points, level, lines)
            for plane in range(level, planes, levels):
                fields = [
                    air_ref[pl.ds(plane * x_points + x, ROWS, stride=x_points), :]
                    for x in lines
                ]
                slopes = geo.d_y(*fields)
                for i, x in enumerate(lines):
                    slope = sum(deriv_table[i][j] * fields[j] for j in range(GLL))
                    moved = mass[i] * (
                        fields[i] - (wind[0][i] * slope + wind[1][i] * slopes[i])
                    )
                    moved_ref[planes * x + plane : planes * x + plane + ROWS, :] = moved
                    pack_edges(geo, packs, moved, x, plane // ROWS)
    to_right, to_left = split_sides(geo, packs[0], packs[1], 1)
    slab_ref[right, EDGE_AT : EDGE_AT + ROWS, :] = to_right
    slab_ref[left, EDGE_AT : EDGE_AT + ROWS, :] = to_left


def panel_kernel(
    planes,
    moved_ref,
    recv_ref,
    air_ref,
    wind_ref,
    jac_ref,
    land_ref,
    rows_ref,
    after_ref,
    avg_ref,
    down_ref,
    up_ref,
    surf_ref,
):
    geo = Geometry()
    blocks = rows_ref.shape[0]
    left, right = neighbours_of(blocks)
    x_points = jac_ref.shape[0]
    levels = wind_ref.shape[0] // (2 * x_points)

    own_ids = rows_ref[...]
    left_ids = recv_ref[left, IDS_AT : IDS_AT + blocks, :].astype(jnp.int32)
    right_ids = recv_ref[right, IDS_AT : IDS_AT + blocks, :].astype(jnp.int32)
    head = [
        jnp.concatenate([recv_ref[c, i : i + 1, :] for c in range(blocks)], axis=0)
        for i in range(6)
    ]
    heat, frac = scatter_sum(head[2:4], own_ids, 2 * ROWS)
    from_left = scatter_sum(
        head[0:2], left_ids, 2 * ROWS, lambda lane: lane >= LANES - ROWS
    )
    from_right = scatter_sum(head[4:6], right_ids, 2 * ROWS, lambda lane: lane < ROWS)
    strip_heat = from_left[0] + from_right[0]
    strip_frac = from_left[1] + from_right[1]

    in_strip = (geo.lane < ROWS) | (geo.lane >= LANES - ROWS)
    packs = join_sides(
        geo,
        recv_ref[left, STRIP_AT : STRIP_AT + ROWS, :],
        recv_ref[right, STRIP_AT : STRIP_AT + ROWS, :],
        ROWS,
    )
    own, strip = [], []
    for h, pack in enumerate(packs):
        half = slice(ROWS * h, ROWS * (h + 1))
        strip.append(
            [
                jnp.where(
                    in_strip, pltpu.roll(pack, (-(16 * i + 8)) % LANES, 1), 1.0
                )
                for i in range(5)
            ]
        )
        own.append(
            [
                air_ref[half, :],
                wind_ref[half, :],
                wind_ref[
                    levels * x_points + ROWS * h : levels * x_points + ROWS * (h + 1), :
                ],
                jac_ref[half, :],
                land_ref[half, :],
            ]
        )
    for h in range(2):
        half = slice(ROWS * h, ROWS * (h + 1))
        pair = []
        for tile, ((field, wind_x, wind_y, jac, land), tile_heat, tile_frac) in enumerate(
            ((own[h], heat[half], frac[half]), (strip[h], strip_heat[half], strip_frac[half]))
        ):
            mass = geo.weight * jac
            if tile == 1:
                tile_heat = jnp.where(in_strip, tile_heat, 0.0)
                tile_frac = jnp.where(in_strip, tile_frac, 0.0)
            surf = (tile_heat + land * field) / (tile_frac + land)
            coef_x, coef_y = time_step * mass * wind_x, time_step * mass * wind_y
            moved = (
                mass * (field + relax_rate * (surf - field))
                - coef_x * geo.d_x(field)
                - coef_y * geo.d_y(field)[0]
            )
            pair.append((moved, mass))
            at = 2 * ROWS * tile + ROWS * h
            for number, value in (
                (MASS, mass),
                (COEF_X, coef_x),
                (COEF_Y, coef_y),
                (SURF, surf),
            ):
                surf_ref[4 * ROWS * number + at : 4 * ROWS * number + at + ROWS, :] = value
        for number, i in ((AVG, 0), (MASS_SUM, 1)):
            for tile, value in enumerate(geo.sum_y_pair(pair[0][i], pair[1][i])):
                at = 4 * ROWS * number + 2 * ROWS * tile + ROWS * h
                surf_ref[at : at + ROWS, :] = value

    joined = join_edges(
        geo,
        recv_ref[left, EDGE_AT : EDGE_AT + ROWS, :],
        recv_ref[right, EDGE_AT : EDGE_AT + ROWS, :],
    )
    for x in range(x_points):
        for group in range(planes // ROWS):
            at = slice(planes * x + ROWS * group, planes * x + ROWS * (group + 1))
            avg_ref[at, :] = geo.sum_y(moved_ref[at, :], outer_edges(joined, x, group))

    def line(r):
        return avg_ref[planes * r : planes * (r + 1), :]

    def surf_line(number, r):
        return surf_ref[pl.ds(4 * ROWS * number + r, 2, stride=x_points), :]

    def first_step(get, mass_at):
        return (
            [
                get(1) / mass_at(1),
                get(2) / mass_at(2),
                (get(3) + get(4)) / (mass_at(3) + mass_at(4)),
            ],
            [
                (get(11) + get(12)) / (mass_at(11) + mass_at(12)),
                get(13) / mass_at(13),
                get(14) / mass_at(14),
            ],
        )

    def own_mass_sum(r):
        return surf_ref[4 * ROWS * MASS_SUM + r : 4 * ROWS * MASS_SUM + r + 1, :]

    low_lines, high_lines = first_step(line, own_mass_sum)
    surf_low, surf_high = first_step(
        functools.partial(surf_line, AVG), functools.partial(surf_line, MASS_SUM)
    )
    for out_ref, r, lines, surf_lines, coefs in (
        (down_ref, 0, low_lines, surf_low, deriv_table[0][1:]),
        (up_ref, 15, high_lines, surf_high, deriv_table[3][:3]),
    ):
        slope = sum(coef * value for coef, value in zip(coefs, lines))
        surf_slope = sum(coef * value for coef, value in zip(coefs, surf_lines))
        mass = surf_ref[4 * ROWS * MASS + r : 4 * ROWS * MASS + r + 1, :]
        wind = time_step * mass * wind_ref[pl.ds(r, 2 * levels, stride=x_points), :]
        out_ref[0:planes, :] = line(r)
        for first in range(0, planes, levels):
            out_ref[planes + first : planes + first + levels, :] = (
                wind[:levels] * slope[first : first + levels]
            )
        base = 2 * planes
        out_ref[base : base + 2 * levels, :] = wind
        base += 2 * levels
        for number in range(SURF_ARRAYS):
            out_ref[base + 2 * number : base + 2 * number + 2, :] = surf_line(number, r)
        base += 2 * SURF_ARRAYS
        out_ref[base : base + 2, :] = surf_line(COEF_X, r) * surf_slope


def second_kernel(
    planes,
    avg_ref,
    surf_ref,
    low_ref,
    high_ref,
    wind_ref,
    rows_ref,
    after_ref,
    slab_ref,
    sums_ref,
    final_ref,
    inverse_ref,
):
    geo = Geometry()
    blocks = rows_ref.shape[0]
    left, right = neighbours_of(blocks)
    x_points = final_ref.shape[0]
    levels = wind_ref.shape[0] // (2 * x_points)
    base = low_ref.shape[0] - 2 * SURF_ARRAYS - 4

    def surf_tile(number, tile, h):
        at = 4 * ROWS * number + 2 * ROWS * tile + ROWS * h
        return surf_ref[at : at + ROWS, :]

    def beside(ref, number, tile):
        at = base + 2 * number + tile
        return spread(ref[at : at + 1, :])

    ends = []
    inverse = []
    for tile in range(2):
        total = geo.sum_x(
            surf_tile(MASS_SUM, tile, 0),
            surf_tile(MASS_SUM, tile, 1),
            beside(low_ref, MASS_SUM, tile),
            beside(high_ref, MASS_SUM, tile),
        )
        inverse.append([1.0 / value for value in total])
        summed = geo.sum_x(
            surf_tile(AVG, tile, 0),
            surf_tile(AVG, tile, 1),
            beside(low_ref, AVG, tile),
            beside(high_ref, AVG, tile),
        )
        fields = [value * scale for value, scale in zip(summed, inverse[tile])]
        moved = []
        for h in range(2):
            field = fields[h]
            moved.append(
                surf_tile(MASS, tile, h)
                * (field + relax_rate * (surf_tile(SURF, tile, h) - field))
                - surf_tile(COEF_X, tile, h) * geo.d_x(field)
                - surf_tile(COEF_Y, tile, h) * geo.d_y(field)[0]
            )
        halos = []
        for ref, field, own_coef in (
            (low_ref, spread(fields[0][:1]), deriv_table[3][3]),
            (high_ref, spread(fields[1][ROWS - 1 :]), deriv_table[0][0]),
        ):
            halos.append(
                beside(ref, MASS, tile)
                * (field + relax_rate * (beside(ref, SURF, tile) - field))
                - beside(ref, SURF_ARRAYS, tile)
                - beside(ref, COEF_X, tile) * (own_coef * field)
                - beside(ref, COEF_Y, tile) * geo.d_y(field)[0]
            )
        ends.append(geo.sum_x(moved[0], moved[1], halos[0], halos[1]))
    final = []
    for h in range(2):
        summed, _ = geo.sum_y_pair(ends[0][h], ends[1][h])
        final.append(summed * inverse[0][h])
        final_ref[ROWS * h : ROWS * (h + 1), :] = final[h]
        inverse_ref[ROWS * h : ROWS * (h + 1), :] = inverse[0][h]
    flux = [final[h] - surf_tile(SURF, 0, h) for h in range(2)]
    for group in range(blocks // ROWS):
        ids = rows_ref[ROWS * group : ROWS * (group + 1), :]
        high, low = ids >> 7, ids & (LANES - 1)
        picked = jnp.zeros((ROWS, LANES), jnp.float32)
        for x in range(2 * ROWS):
            line = spread(flux[x // ROWS][x % ROWS : x % ROWS + 1])
            picked = jnp.where(high == x, take(line, low, 1), picked)
        for c in range(ROWS):
            slab_ref[ROWS * group + c, 0:1, :] = picked[c : c + 1]

    packs = [jnp.zeros((ROWS, LANES), jnp.float32) for _ in range(2)]

    def put(x, plane, value):
        sums_ref[planes * x + plane : planes * x + plane + ROWS, :] = value
        pack_edges(geo, packs, value, x, plane // ROWS)

    def beyond(ref, plane, field, slope, own_coef):
        wind_at = 2 * planes + plane % levels
        return (
            beside(ref, MASS, 0) * field
            - ref[planes + plane : planes + plane + ROWS, :]
            - ref[wind_at : wind_at + ROWS, :] * (own_coef * field)
            - ref[wind_at + levels : wind_at + levels + ROWS, :] * slope
        )

    def row_of(tiles, x):
        return spread(tiles[x // ROWS][x % ROWS : x % ROWS + 1])

    masses = [surf_tile(MASS, 0, h) for h in range(2)]
    held = {}
    for element in range(x_points // GLL):
        lines = [GLL * element + i for i in range(GLL)]
        first, last = lines[0], lines[-1]
        scale = [row_of(inverse[0], x) for x in lines]
        mass = [row_of(masses, x) for x in lines]
        for level in range(0, levels, ROWS):
            wind = wind_tiles(wind_ref, x_points, level, lines)
            for plane in range(level, planes, levels):
                here = slice(plane, plane + ROWS)
                fields = []
                for i, x in enumerate(lines):
                    total = avg_ref[planes * x + plane : planes * x + plane + ROWS, :]
                    other = x - 1 if i == 0 else x + 1
                    if other < 0:
                        total = total + low_ref[here, :]
                    elif other == x_points:
                        total = total + high_ref[here, :]
                    elif i in (0, GLL - 1):
                        at = planes * other + plane
                        total = total + avg_ref[at : at + ROWS, :]
                    fields.append(total * scale[i])
                slopes = geo.d_y(*fields)
                moved = []
                for i, x in enumerate(lines):
                    slope = sum(deriv_table[i][j] * fields[j] for j in range(GLL))
                    moved.append(
                        mass[i] * (fields[i] - (wind[0][i] * slope + wind[1][i] * slopes[i]))
                    )
                if first == 0:
                    before = beyond(low_ref, plane, fields[0], slopes[0], deriv_table[3][3])
                    put(first, plane, before + moved[0])
                else:
                    shared = held[plane] + moved[0]
                    put(first - 1, plane, shared)
                    put(first, plane, shared)
                for i in range(1, GLL - 1):
                    put(lines[i], plane, moved[i])
                held[plane] = moved[-1]
                if last == x_points - 1:
                    after = beyond(
                        high_ref, plane, fields[-1], slopes[-1], deriv_table[0][0]
                    )
                    put(last, plane, held[plane] + after)
    to_right, to_left = split_sides(geo, packs[0], packs[1], 1)
    slab_ref[right, EDGE_AT : EDGE_AT + ROWS, :] = to_right
    slab_ref[left, EDGE_AT : EDGE_AT + ROWS, :] = to_left


def end_kernel(
    planes,
    sums_ref,
    recv_ref,
    final_ref,
    inverse_ref,
    cols_ref,
    weights_ref,
    gain_ref,
    ocean_ref,
    air_out,
    ocean_out,
):
    geo = Geometry()
    blocks = cols_ref.shape[0]
    left, right = neighbours_of(blocks)
    chunks = gain_ref.shape[0]
    arrived = jnp.concatenate([recv_ref[c, 0:1, :] for c in range(blocks)], axis=0)
    (inflow,) = scatter_sum([weights_ref[...] * arrived], cols_ref[...], chunks)
    gain = inflow * gain_ref[...]
    ocean_out[...] = ocean_ref[...]
    for k in range(chunks):
        at = slice(LANES * k, LANES * (k + 1))
        ocean_out[0:1, at] = ocean_ref[0:1, at] + gain[k : k + 1]

    x_points = inverse_ref.shape[0]
    joined = join_edges(
        geo,
        recv_ref[left, EDGE_AT : EDGE_AT + ROWS, :],
        recv_ref[right, EDGE_AT : EDGE_AT + ROWS, :],
    )
    for x in range(x_points):
        inverse = spread(inverse_ref[x : x + 1, :])
        for group in range(planes // ROWS):
            at = planes * x + ROWS * group
            air_out[pl.ds(ROWS * group * x_points + x, ROWS, stride=x_points), :] = (
                inverse
                * geo.sum_y(sums_ref[at : at + ROWS, :], outer_edges(joined, x, group))
            )
    air_out[0:x_points, :] = final_ref[...]


def gathered(ids, coefs, source, sources, groups, first=0):
    totals = [jnp.zeros((ROWS, LANES), jnp.float32) for _ in range(groups)]
    for edge in range(ids.shape[0]):
        cell = spread(ids[edge : edge + 1])
        coef = spread(coefs[edge : edge + 1])
        high, low = cell >> 7, cell & (LANES - 1)
        for s in range(sources):
            scaled = jnp.where(high == first + s, coef, 0.0)
            for group in range(groups):
                totals[group] += scaled * take(source(group, s), low, 1)
    return totals


def ocean_kernel(
    levels, start, tracers_ref, coef_ref, near_ref, rate_ref, after_ref, out_ref
):
    chunks = tracers_ref.shape[1] // LANES
    groups = tracers_ref.shape[0] // ROWS
    row = iota((ROWS, LANES), 0)

    def source(group, s):
        return tracers_ref[
            ROWS * group : ROWS * (group + 1), LANES * s : LANES * (s + 1)
        ]

    def one_chunk(number, carry):
        k = number + start
        at = pl.ds(pl.multiple_of(k * LANES, LANES), LANES)
        out_at = pl.ds(pl.multiple_of(number * LANES, LANES), LANES)
        ids, coefs = near_ref[:, at], coef_ref[:, at]
        totals = gathered(ids, coefs, source, chunks, groups)
        coef_sum = spread(jnp.sum(coefs, axis=0, keepdims=True))
        rate = spread(rate_ref[pl.ds(k, 1), :])
        tiles = [tracers_ref[ROWS * g : ROWS * (g + 1), at] for g in range(groups)]
        for g in range(groups):
            tile = tiles[g]
            top = bottom = tile
            if (ROWS * g) % levels:
                top = pltpu.roll(tiles[g - 1], 1, 0)
            if (ROWS * (g + 1)) % levels:
                bottom = pltpu.roll(tiles[g + 1], ROWS - 1, 0)
            above = jnp.where(row == 0, top, pltpu.roll(tile, 1, 0))
            below = jnp.where(row == ROWS - 1, bottom, pltpu.roll(tile, ROWS - 1, 0))
            vertical = rate * ((above - tile) + (below - tile))
            out_ref[ROWS * g : ROWS * (g + 1), out_at] = (
                tile + (totals[g] - coef_sum * tile) + vertical
            )
        return carry

    lax.fori_loop(0, out_ref.shape[1] // LANES, one_chunk, 0)


def rim_kernel(
    starts,
    recv_ref,
    coef_ref,
    near_ref,
    area_ref,
    after_ref,
    *refs,
):
    partial_refs, (out_ref, gain_ref) = refs[: len(starts)], refs[len(starts) :]
    chunks = coef_ref.shape[1] // LANES
    groups = out_ref.shape[0] // ROWS
    blocks = recv_ref.shape[0]
    sides = neighbours_of(blocks)
    gain_ref[...] = flux_gain / area_ref[...]

    def source(group, s):
        at = IDS_AT + blocks + ROWS * group
        return recv_ref[sides[s], at : at + ROWS, :]

    for k in range(chunks):
        at = slice(LANES * k, LANES * (k + 1))
        totals = gathered(near_ref[:, at], coef_ref[:, at], source, 2, groups, chunks)
        part = max(i for i, start in enumerate(starts) if start <= k)
        place = slice(LANES * (k - starts[part]), LANES * (k - starts[part] + 1))
        for g in range(groups):
            half = slice(ROWS * g, ROWS * (g + 1))
            out_ref[half, at] = partial_refs[part][half, place] + totals[g]


VMEM_SPEC = pl.BlockSpec(memory_space=pltpu.VMEM)
ANY_SPEC = pl.BlockSpec(memory_space=pl.ANY)
HBM_SPEC = pl.BlockSpec(memory_space=pltpu.HBM)


def call(kernel, outs, specs, scratch=(), cost=0, in_vmem=()):
    estimate = None
    if cost:
        estimate = pl.CostEstimate(flops=0, bytes_accessed=cost, transcendentals=0)
    return pl.pallas_call(
        kernel,
        out_shape=[
            pltpu.VMEM(shape, jnp.float32)
            if number in in_vmem
            else jax.ShapeDtypeStruct(shape, jnp.float32)
            for number, shape in enumerate(outs)
        ],
        in_specs=specs,
        scratch_shapes=list(scratch),
        cost_estimate=estimate,
        compiler_params=pltpu.CompilerParams(vmem_limit_bytes=32 * 2**20),
        name=getattr(kernel, "func", kernel).__name__,
    )


def body(
    air_state,
    air_wind,
    jacobian,
    land_area,
    xgrid_rows,
    tracers,
    edge_coef,
    neighbours,
    vert_rate,
    ocean_area,
    send_list,
    xgrid_cols,
    xgrid_weights,
):
    field_count, levels, x_points, y_points = air_state.shape
    planes = field_count * levels
    ocean_levels, cells = tracers.shape[1:]
    ocean_planes = tracers.shape[0] * ocean_levels
    faces, blocks = lax.axis_size("face"), lax.axis_size("blk")
    air = air_state.reshape(planes * x_points, y_points)
    wind = air_wind.reshape(2 * levels * x_points, y_points)
    ocean = tracers.reshape(ocean_planes, cells)
    point_ids, cell_ids, weights = xgrid_rows[0], xgrid_cols[0], xgrid_weights[0]
    rate = vert_rate.reshape(cells // LANES, LANES)
    area = ocean_area.reshape(cells // LANES, LANES)
    first_inputs = (
        cell_ids,
        weights,
        ocean,
        send_list,
        point_ids,
        jacobian,
        land_area,
        wind,
        air,
    )
    slab, moved = call(
        functools.partial(start_kernel, planes, len(first_inputs)),
        [(blocks, IDS_AT + blocks + ocean_planes, LANES), air.shape],
        [HBM_SPEC] * len(first_inputs),
        [pltpu.VMEM(array.shape, array.dtype) for array in first_inputs]
        + [pltpu.SemaphoreType.DMA((len(first_inputs),))],
        in_vmem=(0,),
    )(*(pltpu.with_memory_space_constraint(array, pltpu.HBM) for array in first_inputs))
    recv = lax.all_to_all(slab, "blk", split_axis=0, concat_axis=0, tiled=True)

    chunks = cells // LANES
    reads_per_chunk = edge_coef.shape[0] * chunks * (ocean_planes // ROWS)
    starts = (0, chunks * 11 // 16)

    def ocean_part(start, end, after):
        (result,) = call(
            functools.partial(ocean_kernel, ocean_levels, start),
            [(ocean_planes, (end - start) * LANES)],
            [VMEM_SPEC] * 4 + [ANY_SPEC],
            cost=(end - start) * reads_per_chunk * ROWS * LANES * 4,
        )(ocean, edge_coef, neighbours, rate, after)
        return result

    first_part = ocean_part(starts[0], starts[1], moved)
    side_rows = 2 * planes + 2 * levels + 2 * SURF_ARRAYS + 4
    avg, down, up, surf = call(
        functools.partial(panel_kernel, planes),
        [air.shape, (side_rows, LANES), (side_rows, LANES), (4 * ROWS * SURF_ARRAYS, LANES)],
        [VMEM_SPEC] * 7 + [ANY_SPEC],
    )(moved, recv, air, wind, jacobian, land_area, point_ids, first_part)
    after_me = [(i, (i + 1) % faces) for i in range(faces)]
    low = lax.ppermute(up, "face", after_me)
    high = lax.ppermute(down, "face", [(to, source) for source, to in after_me])
    second_part = ocean_part(starts[1], chunks, surf)

    slab, sums, final, inverse = call(
        functools.partial(second_kernel, planes),
        [
            (blocks, EDGE_AT + ROWS, LANES),
            air.shape,
            (x_points, y_points),
            (x_points, y_points),
        ],
        [VMEM_SPEC] * 6 + [ANY_SPEC],
        in_vmem=(0,),
    )(avg, surf, low, high, wind, point_ids, second_part)
    arrived = lax.all_to_all(slab, "blk", split_axis=0, concat_axis=0, tiled=True)
    partial, gain = call(
        functools.partial(rim_kernel, starts),
        [ocean.shape, area.shape],
        [VMEM_SPEC] * 4 + [ANY_SPEC] + [VMEM_SPEC] * len(starts),
        cost=chunks * reads_per_chunk // 8 * ROWS * LANES * 4,
    )(recv, edge_coef, neighbours, area, final, first_part, second_part)
    air_final, ocean_final = call(
        functools.partial(end_kernel, planes),
        [air.shape, ocean.shape],
        [VMEM_SPEC] * 8,
    )(sums, arrived, final, inverse, cell_ids, weights, gain, partial)
    return air_final.reshape(air_state.shape), ocean_final.reshape(tracers.shape)


def solution(mesh):
    return jax.shard_map(
        body,
        mesh=mesh,
        in_specs=(
            P(None, None, "face", "blk"),
            P(None, None, "face", "blk"),
            P("face", "blk"),
            P("face", "blk"),
            P(("face", "blk"), None, None),
            P(None, None, ("face", "blk")),
            P(None, ("face", "blk")),
            P(None, ("face", "blk")),
            P(("face", "blk")),
            P(("face", "blk")),
            P(("face", "blk"), None),
            P(("face", "blk"), None, None),
            P(("face", "blk"), None, None),
        ),
        out_specs=(P(None, None, "face", "blk"), P(None, None, ("face", "blk"))),
        check_vma=False,
    )
```

```python
import functools

import jax
import jax.numpy as jnp
from jax import lax
from jax.experimental import pallas as pl
from jax.experimental.pallas import tpu as pltpu
from jax.sharding import PartitionSpec as P

GLL = 4
ROWS = 8
LANES = 128

deriv_table = [
    [-3.0, 4.045084971874737, -1.545084971874737, 0.5],
    [-0.8090169943749475, 0.0, 1.118033988749895, -0.30901699437494745],
    [0.30901699437494745, -1.118033988749895, 0.0, 0.8090169943749475],
    [-0.5, 1.545084971874737, -4.045084971874737, 3.0],
]
time_step = 0.05
relax_rate = 0.3
flux_gain = 0.2

HEAD, EDGE_AT, STRIP_AT, IDS_AT = 8, 8, 16, 24
AVG, MASS_SUM, MASS, COEF_X, COEF_Y, SURF = range(6)
SURF_ARRAYS = 6


def iota(shape, dim):
    return lax.broadcasted_iota(jnp.int32, shape, dim)


def take(values, index, axis):
    return jnp.take_along_axis(values, index, axis=axis, mode="promise_in_bounds")


def by_position(pos, values):
    result = jnp.full(pos.shape, values[-1], jnp.float32)
    for i, value in enumerate(values[:-1]):
        result = jnp.where(pos == i, value, result)
    return result


def spread(row):
    return jnp.broadcast_to(row, (ROWS, LANES))


class Geometry:
    def __init__(self):
        shape = (ROWS, LANES)
        self.row, self.lane = iota(shape, 0), iota(shape, 1)
        x_pos, y_pos = self.row & (GLL - 1), self.lane & (GLL - 1)
        self.y_from = [self.lane - y_pos + j for j in range(GLL)]
        columns = [[line[j] for line in deriv_table] for j in range(GLL)]
        self.x_coef = {
            step: by_position(
                x_pos,
                [
                    deriv_table[i][i + step] if 0 <= i + step < GLL else 0.0
                    for i in range(GLL)
                ],
            )
            for step in range(1 - GLL, GLL)
        }
        self.y_coef = [by_position(y_pos, column) for column in columns]
        self.y_swap = (
            self.lane + jnp.where(y_pos == GLL - 1, 1, 0) - jnp.where(y_pos == 0, 1, 0)
        ) & (LANES - 1)
        self.x_edge = (x_pos == 0) | (x_pos == GLL - 1)
        self.y_edge = (y_pos == 0) | (y_pos == GLL - 1)
        self.first_row, self.last_row = self.row == 0, self.row == ROWS - 1
        self.middle_row = self.row == GLL
        self.outer_lane = (self.lane == 0) | (self.lane == LANES - 1)
        self.weight = jnp.where(self.x_edge, 1.0 / 6.0, 5.0 / 6.0) * jnp.where(
            self.y_edge, 1.0 / 6.0, 5.0 / 6.0
        )

    def d_x(self, tile):
        return sum(
            coef * (pltpu.roll(tile, -step % ROWS, 0) if step else tile)
            for step, coef in self.x_coef.items()
        )

    def d_y(self, *tiles):
        totals = [0.0] * len(tiles)
        for j in range(GLL):
            for i, tile in enumerate(tiles):
                totals[i] += self.y_coef[j] * take(tile, self.y_from[j], 1)
        return totals

    def sum_x(self, low, high, before, after):
        low_down, low_up = pltpu.roll(low, 1, 0), pltpu.roll(low, ROWS - 1, 0)
        high_down, high_up = pltpu.roll(high, 1, 0), pltpu.roll(high, ROWS - 1, 0)
        low_other = jnp.where(
            self.first_row,
            before,
            jnp.where(
                self.middle_row, low_down, jnp.where(self.last_row, high_up, low_up)
            ),
        )
        high_other = jnp.where(
            self.first_row,
            low_down,
            jnp.where(
                self.middle_row, high_down, jnp.where(self.last_row, after, high_up)
            ),
        )
        return (
            low + jnp.where(self.x_edge, low_other, 0.0),
            high + jnp.where(self.x_edge, high_other, 0.0),
        )

    def sum_y(self, tile, outer):
        other = jnp.where(self.outer_lane, outer, take(tile, self.y_swap, 1))
        return tile + jnp.where(self.y_edge, other, 0.0)

    def sum_y_pair(self, own, strip):
        own_swap, strip_swap = take(own, self.y_swap, 1), take(strip, self.y_swap, 1)
        own_other = jnp.where(self.outer_lane, strip_swap, own_swap)
        strip_other = jnp.where(self.outer_lane, own_swap, strip_swap)
        return (
            own + jnp.where(self.y_edge, own_other, 0.0),
            strip + jnp.where(self.y_edge, strip_other, 0.0),
        )


def edge_place(x, group):
    return x // ROWS, LANES // 2 * (x % 2) + ROWS * group + 2 * (x % ROWS // 2)


def all_edges(geo, ref, planes, x_points):
    packs = [jnp.zeros((ROWS, LANES), jnp.float32) for _ in range(2)]
    for x in range(x_points):
        for group in range(planes // ROWS):
            q, at = edge_place(x, group)
            tile = ref[planes * x + ROWS * group : planes * x + ROWS * (group + 1), :]
            rolled = pltpu.roll(tile, (at + 1) % LANES, 1)
            packs[q] = jnp.where((geo.lane >> 1) == at // 2, rolled, packs[q])
    return packs


def outer_edges(joined, x, group):
    q, at = edge_place(x, group)
    return pltpu.roll(joined[q], (-(at + 1)) % LANES, 1)


def split_sides(geo, first, second, unit):
    odd = (geo.lane & unit) != 0
    return (
        jnp.where(odd, pltpu.roll(second, unit, 1), first),
        jnp.where(odd, second, pltpu.roll(first, LANES - unit, 1)),
    )


def join_sides(geo, before, after, unit):
    odd = (geo.lane & unit) != 0
    return (
        jnp.where(odd, pltpu.roll(after, unit, 1), before),
        jnp.where(odd, after, pltpu.roll(before, LANES - unit, 1)),
    )


def join_edges(geo, before, after):
    odd = (geo.lane & 1) != 0
    return (
        jnp.where(odd, pltpu.roll(before, 1, 1), after),
        jnp.where(odd, before, pltpu.roll(after, LANES - 1, 1)),
    )


def neighbours_of(blocks):
    here = lax.axis_index("blk")
    return lax.rem(here + blocks - 1, blocks), lax.rem(here + 1, blocks)


def scatter_sum(lines, index, bins, allowed=None):
    count = index.shape[0]
    split = []
    for values in lines:
        for part in range(3):
            short = values.astype(jnp.bfloat16).astype(jnp.float32)
            split.append(short)
            values = values - short
    high, low = index >> 7, index & (LANES - 1)
    bin_at = iota((bins, LANES), 0)
    lane_at = iota((LANES, LANES), 0)
    if allowed is not None:
        lane_at = jnp.where(allowed(lane_at), lane_at, -1)
    left, right = [], []
    for c in range(count):
        hit = bin_at == high[c : c + 1]
        left.append(
            jnp.concatenate(
                [jnp.where(hit, part[c : c + 1], 0.0) for part in split], axis=0
            ).astype(jnp.bfloat16)
        )
        right.append(
            jnp.where(lane_at == low[c : c + 1], 1.0, 0.0).astype(jnp.bfloat16)
        )
    total = lax.dot_general(
        jnp.concatenate(left, axis=1),
        jnp.concatenate(right, axis=1),
        (((1,), (1,)), ((), ())),
        preferred_element_type=jnp.float32,
    )
    sums = []
    for i in range(len(lines)):
        part = total[3 * i * bins : 3 * (i + 1) * bins]
        sums.append(part[:bins] + part[bins : 2 * bins] + part[2 * bins :])
    return sums


def wind_tiles(wind_ref, x_points, level, lines):
    levels = wind_ref.shape[0] // (2 * x_points)
    return [
        [
            time_step
            * wind_ref[
                pl.ds((levels * part + level) * x_points + x, ROWS, stride=x_points), :
            ]
            for x in lines
        ]
        for part in range(2)
    ]


def start_kernel(planes, inputs, *refs):
    sources, (slab_ref, moved_ref), held = (
        refs[:inputs],
        refs[inputs : inputs + 2],
        refs[inputs + 2 : -1],
    )
    copies = [
        pltpu.make_async_copy(source.at[: target.shape[0]], target, refs[-1].at[i])
        for i, (source, target) in enumerate(zip(sources, held))
    ]
    for copy in copies:
        copy.start()
    (
        cols_ref,
        weights_ref,
        tracers_ref,
        rows_ref,
        jac_ref,
        land_ref,
        wind_ref,
        air_ref,
    ) = held
    geo = Geometry()
    blocks = cols_ref.shape[0]
    x_points = jac_ref.shape[0]
    left, right = neighbours_of(blocks)
    levels = wind_ref.shape[0] // (2 * x_points)
    chunks = tracers_ref.shape[1] // LANES
    for copy in copies[:4]:
        copy.wait()

    for group in range(blocks // ROWS):
        at = slice(ROWS * group, ROWS * (group + 1))
        cells = cols_ref[at, :]
        high, low = cells >> 7, cells & (LANES - 1)
        surface = jnp.zeros((ROWS, LANES), jnp.float32)
        for k in range(chunks):
            line = spread(tracers_ref[0:1, LANES * k : LANES * (k + 1)])
            surface = jnp.where(high == k, take(line, low, 1), surface)
        area = weights_ref[at, :]
        heat = area * surface
        for c in range(ROWS):
            owner = ROWS * group + c
            for place, step in enumerate((1, 0, -1)):
                to = (owner + step) % blocks
                slab_ref[to, 2 * place : 2 * place + 1, :] = heat[c : c + 1]
                slab_ref[to, 2 * place + 1 : 2 * place + 2, :] = area[c : c + 1]

    ids = rows_ref[...].astype(jnp.float32)
    for to in (left, right):
        slab_ref[to, IDS_AT : IDS_AT + blocks, :] = ids
    for copy in copies[4:]:
        copy.wait()
    strips = []
    for h in range(2):
        half = slice(ROWS * h, ROWS * (h + 1))
        second = levels * x_points
        pack = jnp.zeros((ROWS, LANES), jnp.float32)
        for i, strip in enumerate(
            (
                air_ref[half, :],
                wind_ref[half, :],
                wind_ref[second + ROWS * h : second + ROWS * (h + 1), :],
                jac_ref[half, :],
                land_ref[half, :],
            )
        ):
            pack = jnp.where(
                (geo.lane >> 4) == i, pltpu.roll(strip, 16 * i + 8, 1), pack
            )
        strips.append(pack)
    to_right, to_left = split_sides(geo, strips[0], strips[1], ROWS)
    slab_ref[right, STRIP_AT : STRIP_AT + ROWS, :] = to_right
    slab_ref[left, STRIP_AT : STRIP_AT + ROWS, :] = to_left

    y_weight = jnp.where(geo.y_edge, 1.0 / 6.0, 5.0 / 6.0)
    for element in range(x_points // GLL):
        lines = [GLL * element + i for i in range(GLL)]
        mass = [
            (1.0 / 6.0 if i in (0, GLL - 1) else 5.0 / 6.0)
            * y_weight
            * spread(jac_ref[x : x + 1, :])
            for i, x in enumerate(lines)
        ]
        for level in range(0, levels, ROWS):
            wind = wind_tiles(wind_ref, x_points, level, lines)
            for plane in range(level, planes, levels):
                fields = [
                    air_ref[pl.ds(plane * x_points + x, ROWS, stride=x_points), :]
                    for x in lines
                ]
                slopes = geo.d_y(*fields)
                for i, x in enumerate(lines):
                    slope = sum(deriv_table[i][j] * fields[j] for j in range(GLL))
                    moved = mass[i] * (
                        fields[i] - (wind[0][i] * slope + wind[1][i] * slopes[i])
                    )
                    moved_ref[planes * x + plane : planes * x + plane + ROWS, :] = moved
    packs = all_edges(geo, moved_ref, planes, x_points)
    to_right, to_left = split_sides(geo, packs[0], packs[1], 1)
    slab_ref[right, EDGE_AT : EDGE_AT + ROWS, :] = to_right
    slab_ref[left, EDGE_AT : EDGE_AT + ROWS, :] = to_left


def panel_kernel(
    planes,
    moved_ref,
    recv_ref,
    air_ref,
    wind_ref,
    jac_ref,
    land_ref,
    rows_ref,
    after_ref,
    rim_before_ref,
    rim_after_ref,
    avg_ref,
    down_ref,
    up_ref,
    surf_ref,
):
    geo = Geometry()
    blocks = rows_ref.shape[0]
    left, right = neighbours_of(blocks)
    x_points = jac_ref.shape[0]
    levels = wind_ref.shape[0] // (2 * x_points)

    own_ids = rows_ref[...]
    left_ids = recv_ref[left, IDS_AT : IDS_AT + blocks, :].astype(jnp.int32)
    right_ids = recv_ref[right, IDS_AT : IDS_AT + blocks, :].astype(jnp.int32)
    head = [
        jnp.concatenate([recv_ref[c, i : i + 1, :] for c in range(blocks)], axis=0)
        for i in range(6)
    ]
    heat, frac = scatter_sum(head[2:4], own_ids, 2 * ROWS)
    from_left = scatter_sum(
        head[0:2], left_ids, 2 * ROWS, lambda lane: lane >= LANES - ROWS
    )
    from_right = scatter_sum(head[4:6], right_ids, 2 * ROWS, lambda lane: lane < ROWS)
    strip_heat = from_left[0] + from_right[0]
    strip_frac = from_left[1] + from_right[1]

    in_strip = (geo.lane < ROWS) | (geo.lane >= LANES - ROWS)
    packs = join_sides(
        geo,
        recv_ref[left, STRIP_AT : STRIP_AT + ROWS, :],
        recv_ref[right, STRIP_AT : STRIP_AT + ROWS, :],
        ROWS,
    )
    own, strip = [], []
    for h, pack in enumerate(packs):
        half = slice(ROWS * h, ROWS * (h + 1))
        strip.append(
            [
                jnp.where(
                    in_strip, pltpu.roll(pack, (-(16 * i + 8)) % LANES, 1), 1.0
                )
                for i in range(5)
            ]
        )
        own.append(
            [
                air_ref[half, :],
                wind_ref[half, :],
                wind_ref[
                    levels * x_points + ROWS * h : levels * x_points + ROWS * (h + 1), :
                ],
                jac_ref[half, :],
                land_ref[half, :],
            ]
        )
    for h in range(2):
        half = slice(ROWS * h, ROWS * (h + 1))
        pair = []
        for tile, ((field, wind_x, wind_y, jac, land), tile_heat, tile_frac) in enumerate(
            ((own[h], heat[half], frac[half]), (strip[h], strip_heat[half], strip_frac[half]))
        ):
            mass = geo.weight * jac
            if tile == 1:
                tile_heat = jnp.where(in_strip, tile_heat, 0.0)
                tile_frac = jnp.where(in_strip, tile_frac, 0.0)
            surf = (tile_heat + land * field) / (tile_frac + land)
            coef_x, coef_y = time_step * mass * wind_x, time_step * mass * wind_y
            moved = (
                mass * (field + relax_rate * (surf - field))
                - coef_x * geo.d_x(field)
                - coef_y * geo.d_y(field)[0]
            )
            pair.append((moved, mass))
            at = 2 * ROWS * tile + ROWS * h
            for number, value in (
                (MASS, mass),
                (COEF_X, coef_x),
                (COEF_Y, coef_y),
                (SURF, surf),
            ):
                surf_ref[4 * ROWS * number + at : 4 * ROWS * number + at + ROWS, :] = value
        for number, i in ((AVG, 0), (MASS_SUM, 1)):
            for tile, value in enumerate(geo.sum_y_pair(pair[0][i], pair[1][i])):
                at = 4 * ROWS * number + 2 * ROWS * tile + ROWS * h
                surf_ref[at : at + ROWS, :] = value

    joined = join_edges(
        geo,
        recv_ref[left, EDGE_AT : EDGE_AT + ROWS, :],
        recv_ref[right, EDGE_AT : EDGE_AT + ROWS, :],
    )
    for x in range(x_points):
        for group in range(planes // ROWS):
            at = slice(planes * x + ROWS * group, planes * x + ROWS * (group + 1))
            avg_ref[at, :] = geo.sum_y(moved_ref[at, :], outer_edges(joined, x, group))

    def line(r):
        return avg_ref[planes * r : planes * (r + 1), :]

    def surf_line(number, r):
        return surf_ref[pl.ds(4 * ROWS * number + r, 2, stride=x_points), :]

    def first_step(get, mass_at):
        return (
            [
                get(1) / mass_at(1),
                get(2) / mass_at(2),
                (get(3) + get(4)) / (mass_at(3) + mass_at(4)),
            ],
            [
                (get(11) + get(12)) / (mass_at(11) + mass_at(12)),
                get(13) / mass_at(13),
                get(14) / mass_at(14),
            ],
        )

    def own_mass_sum(r):
        return surf_ref[4 * ROWS * MASS_SUM + r : 4 * ROWS * MASS_SUM + r + 1, :]

    low_lines, high_lines = first_step(line, own_mass_sum)
    surf_low, surf_high = first_step(
        functools.partial(surf_line, AVG), functools.partial(surf_line, MASS_SUM)
    )
    for out_ref, r, lines, surf_lines, coefs in (
        (down_ref, 0, low_lines, surf_low, deriv_table[0][1:]),
        (up_ref, 15, high_lines, surf_high, deriv_table[3][:3]),
    ):
        slope = sum(coef * value for coef, value in zip(coefs, lines))
        surf_slope = sum(coef * value for coef, value in zip(coefs, surf_lines))
        mass = surf_ref[4 * ROWS * MASS + r : 4 * ROWS * MASS + r + 1, :]
        wind = time_step * mass * wind_ref[pl.ds(r, 2 * levels, stride=x_points), :]
        out_ref[0:planes, :] = line(r)
        for first in range(0, planes, levels):
            out_ref[planes + first : planes + first + levels, :] = (
                wind[:levels] * slope[first : first + levels]
            )
        base = 2 * planes
        out_ref[base : base + 2 * levels, :] = wind
        base += 2 * levels
        for number in range(SURF_ARRAYS):
            out_ref[base + 2 * number : base + 2 * number + 2, :] = surf_line(number, r)
        base += 2 * SURF_ARRAYS
        out_ref[base : base + 2, :] = surf_line(COEF_X, r) * surf_slope


def second_kernel(
    planes,
    avg_ref,
    surf_ref,
    low_ref,
    high_ref,
    wind_ref,
    rows_ref,
    after_ref,
    slab_ref,
    sums_ref,
    final_ref,
    inverse_ref,
):
    geo = Geometry()
    blocks = rows_ref.shape[0]
    left, right = neighbours_of(blocks)
    x_points = final_ref.shape[0]
    levels = wind_ref.shape[0] // (2 * x_points)
    base = low_ref.shape[0] - 2 * SURF_ARRAYS - 4

    def surf_tile(number, tile, h):
        at = 4 * ROWS * number + 2 * ROWS * tile + ROWS * h
        return surf_ref[at : at + ROWS, :]

    def beside(ref, number, tile):
        at = base + 2 * number + tile
        return spread(ref[at : at + 1, :])

    ends = []
    inverse = []
    for tile in range(2):
        total = geo.sum_x(
            surf_tile(MASS_SUM, tile, 0),
            surf_tile(MASS_SUM, tile, 1),
            beside(low_ref, MASS_SUM, tile),
            beside(high_ref, MASS_SUM, tile),
        )
        inverse.append([1.0 / value for value in total])
        summed = geo.sum_x(
            surf_tile(AVG, tile, 0),
            surf_tile(AVG, tile, 1),
            beside(low_ref, AVG, tile),
            beside(high_ref, AVG, tile),
        )
        fields = [value * scale for value, scale in zip(summed, inverse[tile])]
        moved = []
        for h in range(2):
            field = fields[h]
            moved.append(
                surf_tile(MASS, tile, h)
                * (field + relax_rate * (surf_tile(SURF, tile, h) - field))
                - surf_tile(COEF_X, tile, h) * geo.d_x(field)
                - surf_tile(COEF_Y, tile, h) * geo.d_y(field)[0]
            )
        halos = []
        for ref, field, own_coef in (
            (low_ref, spread(fields[0][:1]), deriv_table[3][3]),
            (high_ref, spread(fields[1][ROWS - 1 :]), deriv_table[0][0]),
        ):
            halos.append(
                beside(ref, MASS, tile)
                * (field + relax_rate * (beside(ref, SURF, tile) - field))
                - beside(ref, SURF_ARRAYS, tile)
                - beside(ref, COEF_X, tile) * (own_coef * field)
                - beside(ref, COEF_Y, tile) * geo.d_y(field)[0]
            )
        ends.append(geo.sum_x(moved[0], moved[1], halos[0], halos[1]))
    final = []
    for h in range(2):
        summed, _ = geo.sum_y_pair(ends[0][h], ends[1][h])
        final.append(summed * inverse[0][h])
        final_ref[ROWS * h : ROWS * (h + 1), :] = final[h]
        inverse_ref[ROWS * h : ROWS * (h + 1), :] = inverse[0][h]
    flux = [final[h] - surf_tile(SURF, 0, h) for h in range(2)]
    for group in range(blocks // ROWS):
        ids = rows_ref[ROWS * group : ROWS * (group + 1), :]
        high, low = ids >> 7, ids & (LANES - 1)
        picked = jnp.zeros((ROWS, LANES), jnp.float32)
        for x in range(2 * ROWS):
            line = spread(flux[x // ROWS][x % ROWS : x % ROWS + 1])
            picked = jnp.where(high == x, take(line, low, 1), picked)
        for c in range(ROWS):
            slab_ref[ROWS * group + c, 0:1, :] = picked[c : c + 1]

    def put(x, plane, value):
        sums_ref[planes * x + plane : planes * x + plane + ROWS, :] = value

    def beyond(ref, plane, field, slope, own_coef):
        wind_at = 2 * planes + plane % levels
        return (
            beside(ref, MASS, 0) * field
            - ref[planes + plane : planes + plane + ROWS, :]
            - ref[wind_at : wind_at + ROWS, :] * (own_coef * field)
            - ref[wind_at + levels : wind_at + levels + ROWS, :] * slope
        )

    def row_of(tiles, x):
        return spread(tiles[x // ROWS][x % ROWS : x % ROWS + 1])

    masses = [surf_tile(MASS, 0, h) for h in range(2)]
    held = {}
    for element in range(x_points // GLL):
        lines = [GLL * element + i for i in range(GLL)]
        first, last = lines[0], lines[-1]
        scale = [row_of(inverse[0], x) for x in lines]
        mass = [row_of(masses, x) for x in lines]
        for level in range(0, levels, ROWS):
            wind = wind_tiles(wind_ref, x_points, level, lines)
            for plane in range(level, planes, levels):
                here = slice(plane, plane + ROWS)
                fields = []
                for i, x in enumerate(lines):
                    total = avg_ref[planes * x + plane : planes * x + plane + ROWS, :]
                    other = x - 1 if i == 0 else x + 1
                    if other < 0:
                        total = total + low_ref[here, :]
                    elif other == x_points:
                        total = total + high_ref[here, :]
                    elif i in (0, GLL - 1):
                        at = planes * other + plane
                        total = total + avg_ref[at : at + ROWS, :]
                    fields.append(total * scale[i])
                slopes = geo.d_y(*fields)
                moved = []
                for i, x in enumerate(lines):
                    slope = sum(deriv_table[i][j] * fields[j] for j in range(GLL))
                    moved.append(
                        mass[i] * (fields[i] - (wind[0][i] * slope + wind[1][i] * slopes[i]))
                    )
                if first == 0:
                    before = beyond(low_ref, plane, fields[0], slopes[0], deriv_table[3][3])
                    put(first, plane, before + moved[0])
                else:
                    shared = held[plane] + moved[0]
                    put(first - 1, plane, shared)
                    put(first, plane, shared)
                for i in range(1, GLL - 1):
                    put(lines[i], plane, moved[i])
                held[plane] = moved[-1]
                if last == x_points - 1:
                    after = beyond(
                        high_ref, plane, fields[-1], slopes[-1], deriv_table[0][0]
                    )
                    put(last, plane, held[plane] + after)
    packs = all_edges(geo, sums_ref, planes, x_points)
    to_right, to_left = split_sides(geo, packs[0], packs[1], 1)
    slab_ref[right, EDGE_AT : EDGE_AT + ROWS, :] = to_right
    slab_ref[left, EDGE_AT : EDGE_AT + ROWS, :] = to_left


def end_kernel(
    planes,
    sums_ref,
    recv_ref,
    final_ref,
    inverse_ref,
    cols_ref,
    weights_ref,
    gain_ref,
    ocean_ref,
    air_out,
    ocean_out,
):
    geo = Geometry()
    blocks = cols_ref.shape[0]
    left, right = neighbours_of(blocks)
    chunks = gain_ref.shape[0]
    arrived = jnp.concatenate([recv_ref[c, 0:1, :] for c in range(blocks)], axis=0)
    (inflow,) = scatter_sum([weights_ref[...] * arrived], cols_ref[...], chunks)
    gain = inflow * gain_ref[...]
    ocean_out[...] = ocean_ref[...]
    for k in range(chunks):
        at = slice(LANES * k, LANES * (k + 1))
        ocean_out[0:1, at] = ocean_ref[0:1, at] + gain[k : k + 1]

    x_points = inverse_ref.shape[0]
    joined = join_edges(
        geo,
        recv_ref[left, EDGE_AT : EDGE_AT + ROWS, :],
        recv_ref[right, EDGE_AT : EDGE_AT + ROWS, :],
    )
    for x in range(x_points):
        inverse = spread(inverse_ref[x : x + 1, :])
        for group in range(planes // ROWS):
            at = planes * x + ROWS * group
            air_out[pl.ds(ROWS * group * x_points + x, ROWS, stride=x_points), :] = (
                inverse
                * geo.sum_y(sums_ref[at : at + ROWS, :], outer_edges(joined, x, group))
            )
    air_out[0:x_points, :] = final_ref[...]


def gathered(ids, coefs, source, sources, groups, first=0):
    totals = [jnp.zeros((ROWS, LANES), jnp.float32) for _ in range(groups)]
    for edge in range(ids.shape[0]):
        cell = spread(ids[edge : edge + 1])
        coef = spread(coefs[edge : edge + 1])
        high, low = cell >> 7, cell & (LANES - 1)
        for s in range(sources):
            scaled = jnp.where(high == first + s, coef, 0.0)
            for group in range(groups):
                totals[group] += scaled * take(source(group, s), low, 1)
    return totals


def ocean_kernel(
    levels, start, tracers_ref, coef_ref, near_ref, rate_ref, after_ref, out_ref
):
    chunks = tracers_ref.shape[1] // LANES
    groups = tracers_ref.shape[0] // ROWS
    row = iota((ROWS, LANES), 0)

    def source(group, s):
        return tracers_ref[
            ROWS * group : ROWS * (group + 1), LANES * s : LANES * (s + 1)
        ]

    def one_chunk(number, carry):
        k = number + start
        at = pl.ds(pl.multiple_of(k * LANES, LANES), LANES)
        out_at = pl.ds(pl.multiple_of(number * LANES, LANES), LANES)
        ids, coefs = near_ref[:, at], coef_ref[:, at]
        totals = gathered(ids, coefs, source, chunks, groups)
        coef_sum = spread(jnp.sum(coefs, axis=0, keepdims=True))
        rate = spread(rate_ref[pl.ds(k, 1), :])
        tiles = [tracers_ref[ROWS * g : ROWS * (g + 1), at] for g in range(groups)]
        for g in range(groups):
            tile = tiles[g]
            top = bottom = tile
            if (ROWS * g) % levels:
                top = pltpu.roll(tiles[g - 1], 1, 0)
            if (ROWS * (g + 1)) % levels:
                bottom = pltpu.roll(tiles[g + 1], ROWS - 1, 0)
            above = jnp.where(row == 0, top, pltpu.roll(tile, 1, 0))
            below = jnp.where(row == ROWS - 1, bottom, pltpu.roll(tile, ROWS - 1, 0))
            vertical = rate * ((above - tile) + (below - tile))
            out_ref[ROWS * g : ROWS * (g + 1), out_at] = (
                tile + (totals[g] - coef_sum * tile) + vertical
            )
        return carry

    lax.fori_loop(0, out_ref.shape[1] // LANES, one_chunk, 0)


def send_kernel(tracers_ref, send_ref, after_ref, *rim_refs):
    chunks = tracers_ref.shape[1] // LANES
    for part, rim_ref in enumerate(rim_refs):
        cells = spread(send_ref[0:1, LANES * part : LANES * (part + 1)])
        high, low = cells >> 7, cells & (LANES - 1)
        for group in range(tracers_ref.shape[0] // ROWS):
            half = slice(ROWS * group, ROWS * (group + 1))
            rim = jnp.zeros((ROWS, LANES), jnp.float32)
            for k in range(chunks):
                tile = tracers_ref[half, LANES * k : LANES * (k + 1)]
                rim = jnp.where(high == k, take(tile, low, 1), rim)
            rim_ref[half, :] = rim


def rim_kernel(
    starts,
    before_ref,
    after_ref,
    coef_ref,
    near_ref,
    area_ref,
    *refs,
):
    partial_refs, (out_ref, gain_ref) = refs[: len(starts)], refs[len(starts) :]
    chunks = coef_ref.shape[1] // LANES
    groups = out_ref.shape[0] // ROWS
    sides = before_ref, after_ref
    gain_ref[...] = flux_gain / area_ref[...]

    def source(group, s):
        return sides[s][ROWS * group : ROWS * (group + 1), :]

    for k in range(chunks):
        at = slice(LANES * k, LANES * (k + 1))
        totals = gathered(near_ref[:, at], coef_ref[:, at], source, 2, groups, chunks)
        part = max(i for i, start in enumerate(starts) if start <= k)
        place = slice(LANES * (k - starts[part]), LANES * (k - starts[part] + 1))
        for g in range(groups):
            half = slice(ROWS * g, ROWS * (g + 1))
            out_ref[half, at] = partial_refs[part][half, place] + totals[g]


VMEM_SPEC = pl.BlockSpec(memory_space=pltpu.VMEM)
ANY_SPEC = pl.BlockSpec(memory_space=pl.ANY)
HBM_SPEC = pl.BlockSpec(memory_space=pltpu.HBM)


def call(kernel, outs, specs, scratch=(), cost=0):
    estimate = None
    if cost:
        estimate = pl.CostEstimate(flops=0, bytes_accessed=cost, transcendentals=0)
    return pl.pallas_call(
        kernel,
        out_shape=[jax.ShapeDtypeStruct(shape, jnp.float32) for shape in outs],
        in_specs=specs,
        scratch_shapes=list(scratch),
        cost_estimate=estimate,
        compiler_params=pltpu.CompilerParams(vmem_limit_bytes=32 * 2**20),
        name=getattr(kernel, "func", kernel).__name__,
    )


def body(
    air_state,
    air_wind,
    jacobian,
    land_area,
    xgrid_rows,
    tracers,
    edge_coef,
    neighbours,
    vert_rate,
    ocean_area,
    send_list,
    xgrid_cols,
    xgrid_weights,
):
    field_count, levels, x_points, y_points = air_state.shape
    planes = field_count * levels
    ocean_levels, cells = tracers.shape[1:]
    ocean_planes = tracers.shape[0] * ocean_levels
    faces, blocks = lax.axis_size("face"), lax.axis_size("blk")
    air = air_state.reshape(planes * x_points, y_points)
    wind = air_wind.reshape(2 * levels * x_points, y_points)
    ocean = tracers.reshape(ocean_planes, cells)
    point_ids, cell_ids, weights = xgrid_rows[0], xgrid_cols[0], xgrid_weights[0]
    rate = vert_rate.reshape(cells // LANES, LANES)
    area = ocean_area.reshape(cells // LANES, LANES)
    first_inputs = (
        cell_ids,
        weights,
        ocean,
        point_ids,
        jacobian,
        land_area,
        wind,
        air,
    )
    slab, moved = call(
        functools.partial(start_kernel, planes, len(first_inputs)),
        [(blocks, IDS_AT + blocks, LANES), air.shape],
        [HBM_SPEC] * len(first_inputs),
        [
            pltpu.VMEM((ROWS, cells) if array is ocean else array.shape, array.dtype)
            for array in first_inputs
        ]
        + [pltpu.SemaphoreType.DMA((len(first_inputs),))],
    )(*(pltpu.with_memory_space_constraint(array, pltpu.HBM) for array in first_inputs))
    recv = lax.all_to_all(slab, "blk", split_axis=0, concat_axis=0, tiled=True)

    chunks = cells // LANES
    reads_per_chunk = edge_coef.shape[0] * chunks * (ocean_planes // ROWS)
    starts = (0, chunks * 5 // 16, chunks * 11 // 16)

    def ocean_part(start, end, after):
        (result,) = call(
            functools.partial(ocean_kernel, ocean_levels, start),
            [(ocean_planes, (end - start) * LANES)],
            [VMEM_SPEC] * 4 + [ANY_SPEC],
            cost=(end - start) * reads_per_chunk * ROWS * LANES * 4,
        )(ocean, edge_coef, neighbours, rate, after)
        return result

    to_before, to_after = call(
        send_kernel,
        [(ocean_planes, LANES)] * 2,
        [VMEM_SPEC] * 2 + [ANY_SPEC],
        cost=reads_per_chunk * ROWS * LANES,
    )(ocean, send_list, moved)
    onward = [(i, (i + 1) % blocks) for i in range(blocks)]
    rim_before = lax.ppermute(to_after, "blk", onward)
    rim_after = lax.ppermute(to_before, "blk", [(to, source) for source, to in onward])
    first_part = ocean_part(starts[0], starts[1], to_before)
    side_rows = 2 * planes + 2 * levels + 2 * SURF_ARRAYS + 4
    avg, down, up, surf = call(
        functools.partial(panel_kernel, planes),
        [air.shape, (side_rows, LANES), (side_rows, LANES), (4 * ROWS * SURF_ARRAYS, LANES)],
        [VMEM_SPEC] * 7 + [ANY_SPEC] * 3,
    )(
        moved,
        recv,
        air,
        wind,
        jacobian,
        land_area,
        point_ids,
        first_part,
        rim_before,
        rim_after,
    )
    after_me = [(i, (i + 1) % faces) for i in range(faces)]
    low = lax.ppermute(up, "face", after_me)
    high = lax.ppermute(down, "face", [(to, source) for source, to in after_me])
    second_part = ocean_part(starts[1], starts[2], surf)

    slab, sums, final, inverse = call(
        functools.partial(second_kernel, planes),
        [
            (blocks, EDGE_AT + ROWS, LANES),
            air.shape,
            (x_points, y_points),
            (x_points, y_points),
        ],
        [VMEM_SPEC] * 6 + [ANY_SPEC],
    )(avg, surf, low, high, wind, point_ids, second_part)
    arrived = lax.all_to_all(slab, "blk", split_axis=0, concat_axis=0, tiled=True)
    third_part = ocean_part(starts[2], chunks, final)
    partial, gain = call(
        functools.partial(rim_kernel, starts),
        [ocean.shape, area.shape],
        [VMEM_SPEC] * (5 + len(starts)),
        cost=chunks * reads_per_chunk // 8 * ROWS * LANES * 4,
    )(rim_before, rim_after, edge_coef, neighbours, area, first_part, second_part, third_part)
    air_final, ocean_final = call(
        functools.partial(end_kernel, planes),
        [air.shape, ocean.shape],
        [VMEM_SPEC] * 8,
    )(sums, arrived, final, inverse, cell_ids, weights, gain, partial)
    return air_final.reshape(air_state.shape), ocean_final.reshape(tracers.shape)


def solution(mesh):
    return jax.shard_map(
        body,
        mesh=mesh,
        in_specs=(
            P(None, None, "face", "blk"),
            P(None, None, "face", "blk"),
            P("face", "blk"),
            P("face", "blk"),
            P(("face", "blk"), None, None),
            P(None, None, ("face", "blk")),
            P(None, ("face", "blk")),
            P(None, ("face", "blk")),
            P(("face", "blk")),
            P(("face", "blk")),
            P(("face", "blk"), None),
            P(("face", "blk"), None, None),
            P(("face", "blk"), None, None),
        ),
        out_specs=(P(None, None, "face", "blk"), P(None, None, ("face", "blk"))),
        check_vma=False,
    )
```

```python
import functools

import jax
import jax.numpy as jnp
from jax import lax
from jax.experimental import pallas as pl
from jax.experimental.pallas import tpu as pltpu
from jax.sharding import PartitionSpec as P

GLL = 4
ROWS = 8
LANES = 128

deriv_table = [
    [-3.0, 4.045084971874737, -1.545084971874737, 0.5],
    [-0.8090169943749475, 0.0, 1.118033988749895, -0.30901699437494745],
    [0.30901699437494745, -1.118033988749895, 0.0, 0.8090169943749475],
    [-0.5, 1.545084971874737, -4.045084971874737, 3.0],
]
time_step = 0.05
relax_rate = 0.3
flux_gain = 0.2

HEAD, EDGE_AT = 8, 8
SIDE_EDGE, SIDE_STRIP, SIDE_IDS = 0, 8, 16
AVG, MASS_SUM, MASS, COEF_X, COEF_Y, SURF = range(6)
SURF_ARRAYS = 6


def iota(shape, dim):
    return lax.broadcasted_iota(jnp.int32, shape, dim)


def take(values, index, axis):
    return jnp.take_along_axis(values, index, axis=axis, mode="promise_in_bounds")


def by_position(pos, values):
    result = jnp.full(pos.shape, values[-1], jnp.float32)
    for i, value in enumerate(values[:-1]):
        result = jnp.where(pos == i, value, result)
    return result


def spread(row):
    return jnp.broadcast_to(row, (ROWS, LANES))


class Geometry:
    def __init__(self):
        shape = (ROWS, LANES)
        self.row, self.lane = iota(shape, 0), iota(shape, 1)
        x_pos, y_pos = self.row & (GLL - 1), self.lane & (GLL - 1)
        self.y_from = [self.lane - y_pos + j for j in range(GLL)]
        columns = [[line[j] for line in deriv_table] for j in range(GLL)]
        self.x_coef = {
            step: by_position(
                x_pos,
                [
                    deriv_table[i][i + step] if 0 <= i + step < GLL else 0.0
                    for i in range(GLL)
                ],
            )
            for step in range(1 - GLL, GLL)
        }
        self.y_coef = [by_position(y_pos, column) for column in columns]
        self.y_swap = (
            self.lane + jnp.where(y_pos == GLL - 1, 1, 0) - jnp.where(y_pos == 0, 1, 0)
        ) & (LANES - 1)
        self.x_edge = (x_pos == 0) | (x_pos == GLL - 1)
        self.y_edge = (y_pos == 0) | (y_pos == GLL - 1)
        self.first_row, self.last_row = self.row == 0, self.row == ROWS - 1
        self.middle_row = self.row == GLL
        self.outer_lane = (self.lane == 0) | (self.lane == LANES - 1)
        self.weight = jnp.where(self.x_edge, 1.0 / 6.0, 5.0 / 6.0) * jnp.where(
            self.y_edge, 1.0 / 6.0, 5.0 / 6.0
        )

    def d_x(self, tile):
        return sum(
            coef * (pltpu.roll(tile, -step % ROWS, 0) if step else tile)
            for step, coef in self.x_coef.items()
        )

    def d_y(self, *tiles):
        totals = [0.0] * len(tiles)
        for j in range(GLL):
            for i, tile in enumerate(tiles):
                totals[i] += self.y_coef[j] * take(tile, self.y_from[j], 1)
        return totals

    def sum_x(self, low, high, before, after):
        low_down, low_up = pltpu.roll(low, 1, 0), pltpu.roll(low, ROWS - 1, 0)
        high_down, high_up = pltpu.roll(high, 1, 0), pltpu.roll(high, ROWS - 1, 0)
        low_other = jnp.where(
            self.first_row,
            before,
            jnp.where(
                self.middle_row, low_down, jnp.where(self.last_row, high_up, low_up)
            ),
        )
        high_other = jnp.where(
            self.first_row,
            low_down,
            jnp.where(
                self.middle_row, high_down, jnp.where(self.last_row, after, high_up)
            ),
        )
        return (
            low + jnp.where(self.x_edge, low_other, 0.0),
            high + jnp.where(self.x_edge, high_other, 0.0),
        )

    def sum_y(self, tile, outer):
        other = jnp.where(self.outer_lane, outer, take(tile, self.y_swap, 1))
        return tile + jnp.where(self.y_edge, other, 0.0)

    def sum_y_pair(self, own, strip):
        own_swap, strip_swap = take(own, self.y_swap, 1), take(strip, self.y_swap, 1)
        own_other = jnp.where(self.outer_lane, strip_swap, own_swap)
        strip_other = jnp.where(self.outer_lane, own_swap, strip_swap)
        return (
            own + jnp.where(self.y_edge, own_other, 0.0),
            strip + jnp.where(self.y_edge, strip_other, 0.0),
        )


def edge_place(x, group):
    return x // ROWS, LANES // 2 * (x % 2) + ROWS * group + 2 * (x % ROWS // 2)


def all_edges(geo, ref, planes, x_points):
    packs = [jnp.zeros((ROWS, LANES), jnp.float32) for _ in range(2)]
    for x in range(x_points):
        for group in range(planes // ROWS):
            q, at = edge_place(x, group)
            tile = ref[planes * x + ROWS * group : planes * x + ROWS * (group + 1), :]
            rolled = pltpu.roll(tile, (at + 1) % LANES, 1)
            packs[q] = jnp.where((geo.lane >> 1) == at // 2, rolled, packs[q])
    return packs


def outer_edges(joined, x, group):
    q, at = edge_place(x, group)
    return pltpu.roll(joined[q], (-(at + 1)) % LANES, 1)


def split_sides(geo, first, second, unit):
    odd = (geo.lane & unit) != 0
    return (
        jnp.where(odd, pltpu.roll(second, unit, 1), first),
        jnp.where(odd, second, pltpu.roll(first, LANES - unit, 1)),
    )


def join_sides(geo, before, after, unit):
    odd = (geo.lane & unit) != 0
    return (
        jnp.where(odd, pltpu.roll(after, unit, 1), before),
        jnp.where(odd, after, pltpu.roll(before, LANES - unit, 1)),
    )


def join_edges(geo, before, after):
    odd = (geo.lane & 1) != 0
    return (
        jnp.where(odd, pltpu.roll(before, 1, 1), after),
        jnp.where(odd, before, pltpu.roll(after, LANES - 1, 1)),
    )


def neighbours_of(blocks):
    here = lax.axis_index("blk")
    return lax.rem(here + blocks - 1, blocks), lax.rem(here + 1, blocks)


def scatter_sum(lines, index, bins, allowed=None):
    count = index.shape[0]
    split = []
    for values in lines:
        for part in range(3):
            short = values.astype(jnp.bfloat16).astype(jnp.float32)
            split.append(short)
            values = values - short
    high, low = index >> 7, index & (LANES - 1)
    bin_at = iota((bins, LANES), 0)
    lane_at = iota((LANES, LANES), 0)
    if allowed is not None:
        lane_at = jnp.where(allowed(lane_at), lane_at, -1)
    left, right = [], []
    for c in range(count):
        hit = bin_at == high[c : c + 1]
        left.append(
            jnp.concatenate(
                [jnp.where(hit, part[c : c + 1], 0.0) for part in split], axis=0
            ).astype(jnp.bfloat16)
        )
        right.append(
            jnp.where(lane_at == low[c : c + 1], 1.0, 0.0).astype(jnp.bfloat16)
        )
    total = lax.dot_general(
        jnp.concatenate(left, axis=1),
        jnp.concatenate(right, axis=1),
        (((1,), (1,)), ((), ())),
        preferred_element_type=jnp.float32,
    )
    sums = []
    for i in range(len(lines)):
        part = total[3 * i * bins : 3 * (i + 1) * bins]
        sums.append(part[:bins] + part[bins : 2 * bins] + part[2 * bins :])
    return sums


def wind_tiles(wind_ref, x_points, level, lines):
    levels = wind_ref.shape[0] // (2 * x_points)
    return [
        [
            time_step
            * wind_ref[
                pl.ds((levels * part + level) * x_points + x, ROWS, stride=x_points), :
            ]
            for x in lines
        ]
        for part in range(2)
    ]


def start_kernel(
    planes,
    cols_in,
    weights_in,
    tracers_in,
    rows_in,
    jac_in,
    land_in,
    wind_in,
    air_in,
    send_in,
    slab_out,
    moved_ref,
    before_ref,
    after_ref,
    cols_ref,
    weights_ref,
    rows_ref,
    send_ref,
    slab_ref,
    tracers_ref,
    jac_ref,
    land_ref,
    wind_ref,
    air_ref,
    semaphores,
):
    copies = [
        pltpu.make_async_copy(source, target, semaphores.at[i])
        for i, (source, target) in enumerate(
            (
                (cols_in, cols_ref),
                (tracers_in.at[:ROWS], tracers_ref),
                (weights_in, weights_ref),
                (rows_in, rows_ref),
                (air_in, air_ref),
                (wind_in, wind_ref),
                (jac_in, jac_ref),
                (land_in, land_ref),
                (send_in, send_ref),
            )
        )
    ]
    for copy in copies:
        copy.start()
    geo = Geometry()
    blocks = cols_ref.shape[0]
    x_points = jac_ref.shape[0]
    levels = wind_ref.shape[0] // (2 * x_points)
    chunks = tracers_ref.shape[1] // LANES
    for copy in copies[:4]:
        copy.wait()

    for group in range(blocks // ROWS):
        at = slice(ROWS * group, ROWS * (group + 1))
        cells = cols_ref[at, :]
        high, low = cells >> 7, cells & (LANES - 1)
        surface = jnp.zeros((ROWS, LANES), jnp.float32)
        for k in range(chunks):
            line = spread(tracers_ref[0:1, LANES * k : LANES * (k + 1)])
            surface = jnp.where(high == k, take(line, low, 1), surface)
        area = weights_ref[at, :]
        heat = area * surface
        for c in range(ROWS):
            owner = ROWS * group + c
            for place, step in enumerate((1, 0, -1)):
                to = (owner + step) % blocks
                slab_ref[to, 2 * place : 2 * place + 1, :] = heat[c : c + 1]
                slab_ref[to, 2 * place + 1 : 2 * place + 2, :] = area[c : c + 1]

    out = pltpu.make_async_copy(slab_ref, slab_out, semaphores.at[len(copies)])
    out.start()
    ids = rows_ref[...].astype(jnp.float32)
    for side_ref in (before_ref, after_ref):
        side_ref[SIDE_IDS : SIDE_IDS + blocks, :] = ids

    for copy in copies[4:]:
        copy.wait()
    strips = []
    for h in range(2):
        half = slice(ROWS * h, ROWS * (h + 1))
        second = levels * x_points
        pack = jnp.zeros((ROWS, LANES), jnp.float32)
        for i, strip in enumerate(
            (
                air_ref[half, :],
                wind_ref[half, :],
                wind_ref[second + ROWS * h : second + ROWS * (h + 1), :],
                jac_ref[half, :],
                land_ref[half, :],
            )
        ):
            pack = jnp.where(
                (geo.lane >> 4) == i, pltpu.roll(strip, 16 * i + 8, 1), pack
            )
        strips.append(pack)
    to_right, to_left = split_sides(geo, strips[0], strips[1], ROWS)
    after_ref[SIDE_STRIP : SIDE_STRIP + ROWS, :] = to_right
    before_ref[SIDE_STRIP : SIDE_STRIP + ROWS, :] = to_left

    y_weight = jnp.where(geo.y_edge, 1.0 / 6.0, 5.0 / 6.0)
    for element in range(x_points // GLL):
        lines = [GLL * element + i for i in range(GLL)]
        mass = [
            (1.0 / 6.0 if i in (0, GLL - 1) else 5.0 / 6.0)
            * y_weight
            * spread(jac_ref[x : x + 1, :])
            for i, x in enumerate(lines)
        ]
        for level in range(0, levels, ROWS):
            wind = wind_tiles(wind_ref, x_points, level, lines)
            for plane in range(level, planes, levels):
                fields = [
                    air_ref[pl.ds(plane * x_points + x, ROWS, stride=x_points), :]
                    for x in lines
                ]
                slopes = geo.d_y(*fields)
                for i, x in enumerate(lines):
                    slope = sum(deriv_table[i][j] * fields[j] for j in range(GLL))
                    moved = mass[i] * (
                        fields[i] - (wind[0][i] * slope + wind[1][i] * slopes[i])
                    )
                    moved_ref[planes * x + plane : planes * x + plane + ROWS, :] = moved
    packs = all_edges(geo, moved_ref, planes, x_points)
    to_right, to_left = split_sides(geo, packs[0], packs[1], 1)
    after_ref[SIDE_EDGE : SIDE_EDGE + ROWS, :] = to_right
    before_ref[SIDE_EDGE : SIDE_EDGE + ROWS, :] = to_left
    out.wait()


def panel_kernel(
    planes,
    moved_ref,
    recv_ref,
    before_ref,
    after_ref,
    air_ref,
    wind_ref,
    jac_ref,
    land_ref,
    rows_ref,
    ocean_ref,
    avg_ref,
    down_ref,
    up_ref,
    surf_ref,
):
    geo = Geometry()
    blocks = rows_ref.shape[0]
    x_points = jac_ref.shape[0]
    levels = wind_ref.shape[0] // (2 * x_points)

    own_ids = rows_ref[...]
    left_ids = before_ref[SIDE_IDS : SIDE_IDS + blocks, :].astype(jnp.int32)
    right_ids = after_ref[SIDE_IDS : SIDE_IDS + blocks, :].astype(jnp.int32)
    head = [
        jnp.concatenate([recv_ref[c, i : i + 1, :] for c in range(blocks)], axis=0)
        for i in range(6)
    ]
    heat, frac = scatter_sum(head[2:4], own_ids, 2 * ROWS)
    from_left = scatter_sum(
        head[0:2], left_ids, 2 * ROWS, lambda lane: lane >= LANES - ROWS
    )
    from_right = scatter_sum(head[4:6], right_ids, 2 * ROWS, lambda lane: lane < ROWS)
    strip_heat = from_left[0] + from_right[0]
    strip_frac = from_left[1] + from_right[1]

    in_strip = (geo.lane < ROWS) | (geo.lane >= LANES - ROWS)
    packs = join_sides(
        geo,
        before_ref[SIDE_STRIP : SIDE_STRIP + ROWS, :],
        after_ref[SIDE_STRIP : SIDE_STRIP + ROWS, :],
        ROWS,
    )
    own, strip = [], []
    for h, pack in enumerate(packs):
        half = slice(ROWS * h, ROWS * (h + 1))
        strip.append(
            [
                jnp.where(
                    in_strip, pltpu.roll(pack, (-(16 * i + 8)) % LANES, 1), 1.0
                )
                for i in range(5)
            ]
        )
        own.append(
            [
                air_ref[half, :],
                wind_ref[half, :],
                wind_ref[
                    levels * x_points + ROWS * h : levels * x_points + ROWS * (h + 1), :
                ],
                jac_ref[half, :],
                land_ref[half, :],
            ]
        )
    for h in range(2):
        half = slice(ROWS * h, ROWS * (h + 1))
        pair = []
        for tile, ((field, wind_x, wind_y, jac, land), tile_heat, tile_frac) in enumerate(
            ((own[h], heat[half], frac[half]), (strip[h], strip_heat[half], strip_frac[half]))
        ):
            mass = geo.weight * jac
            if tile == 1:
                tile_heat = jnp.where(in_strip, tile_heat, 0.0)
                tile_frac = jnp.where(in_strip, tile_frac, 0.0)
            surf = (tile_heat + land * field) / (tile_frac + land)
            coef_x, coef_y = time_step * mass * wind_x, time_step * mass * wind_y
            moved = (
                mass * (field + relax_rate * (surf - field))
                - coef_x * geo.d_x(field)
                - coef_y * geo.d_y(field)[0]
            )
            pair.append((moved, mass))
            at = 2 * ROWS * tile + ROWS * h
            for number, value in (
                (MASS, mass),
                (COEF_X, coef_x),
                (COEF_Y, coef_y),
                (SURF, surf),
            ):
                surf_ref[4 * ROWS * number + at : 4 * ROWS * number + at + ROWS, :] = value
        for number, i in ((AVG, 0), (MASS_SUM, 1)):
            for tile, value in enumerate(geo.sum_y_pair(pair[0][i], pair[1][i])):
                at = 4 * ROWS * number + 2 * ROWS * tile + ROWS * h
                surf_ref[at : at + ROWS, :] = value

    joined = join_edges(
        geo,
        before_ref[SIDE_EDGE : SIDE_EDGE + ROWS, :],
        after_ref[SIDE_EDGE : SIDE_EDGE + ROWS, :],
    )
    for x in range(x_points):
        for group in range(planes // ROWS):
            at = slice(planes * x + ROWS * group, planes * x + ROWS * (group + 1))
            avg_ref[at, :] = geo.sum_y(moved_ref[at, :], outer_edges(joined, x, group))

    def line(r):
        return avg_ref[planes * r : planes * (r + 1), :]

    def surf_line(number, r):
        return surf_ref[pl.ds(4 * ROWS * number + r, 2, stride=x_points), :]

    def first_step(get, mass_at):
        return (
            [
                get(1) / mass_at(1),
                get(2) / mass_at(2),
                (get(3) + get(4)) / (mass_at(3) + mass_at(4)),
            ],
            [
                (get(11) + get(12)) / (mass_at(11) + mass_at(12)),
                get(13) / mass_at(13),
                get(14) / mass_at(14),
            ],
        )

    def own_mass_sum(r):
        return surf_ref[4 * ROWS * MASS_SUM + r : 4 * ROWS * MASS_SUM + r + 1, :]

    low_lines, high_lines = first_step(line, own_mass_sum)
    surf_low, surf_high = first_step(
        functools.partial(surf_line, AVG), functools.partial(surf_line, MASS_SUM)
    )
    for out_ref, r, lines, surf_lines, coefs in (
        (down_ref, 0, low_lines, surf_low, deriv_table[0][1:]),
        (up_ref, 15, high_lines, surf_high, deriv_table[3][:3]),
    ):
        slope = sum(coef * value for coef, value in zip(coefs, lines))
        surf_slope = sum(coef * value for coef, value in zip(coefs, surf_lines))
        mass = surf_ref[4 * ROWS * MASS + r : 4 * ROWS * MASS + r + 1, :]
        wind = time_step * mass * wind_ref[pl.ds(r, 2 * levels, stride=x_points), :]
        out_ref[0:planes, :] = line(r)
        for first in range(0, planes, levels):
            out_ref[planes + first : planes + first + levels, :] = (
                wind[:levels] * slope[first : first + levels]
            )
        base = 2 * planes
        out_ref[base : base + 2 * levels, :] = wind
        base += 2 * levels
        for number in range(SURF_ARRAYS):
            out_ref[base + 2 * number : base + 2 * number + 2, :] = surf_line(number, r)
        base += 2 * SURF_ARRAYS
        out_ref[base : base + 2, :] = surf_line(COEF_X, r) * surf_slope


def second_kernel(
    planes,
    avg_ref,
    surf_ref,
    low_ref,
    high_ref,
    wind_ref,
    rows_ref,
    ocean_ref,
    slab_out,
    sums_ref,
    final_ref,
    inverse_ref,
    flux_ref,
    edges_ref,
    semaphores,
):
    geo = Geometry()
    blocks = rows_ref.shape[0]
    left, right = neighbours_of(blocks)
    x_points = final_ref.shape[0]
    levels = wind_ref.shape[0] // (2 * x_points)
    base = low_ref.shape[0] - 2 * SURF_ARRAYS - 4

    def surf_tile(number, tile, h):
        at = 4 * ROWS * number + 2 * ROWS * tile + ROWS * h
        return surf_ref[at : at + ROWS, :]

    def beside(ref, number, tile):
        at = base + 2 * number + tile
        return spread(ref[at : at + 1, :])

    ends = []
    inverse = []
    for tile in range(2):
        total = geo.sum_x(
            surf_tile(MASS_SUM, tile, 0),
            surf_tile(MASS_SUM, tile, 1),
            beside(low_ref, MASS_SUM, tile),
            beside(high_ref, MASS_SUM, tile),
        )
        inverse.append([1.0 / value for value in total])
        summed = geo.sum_x(
            surf_tile(AVG, tile, 0),
            surf_tile(AVG, tile, 1),
            beside(low_ref, AVG, tile),
            beside(high_ref, AVG, tile),
        )
        fields = [value * scale for value, scale in zip(summed, inverse[tile])]
        moved = []
        for h in range(2):
            field = fields[h]
            moved.append(
                surf_tile(MASS, tile, h)
                * (field + relax_rate * (surf_tile(SURF, tile, h) - field))
                - surf_tile(COEF_X, tile, h) * geo.d_x(field)
                - surf_tile(COEF_Y, tile, h) * geo.d_y(field)[0]
            )
        halos = []
        for ref, field, own_coef in (
            (low_ref, spread(fields[0][:1]), deriv_table[3][3]),
            (high_ref, spread(fields[1][ROWS - 1 :]), deriv_table[0][0]),
        ):
            halos.append(
                beside(ref, MASS, tile)
                * (field + relax_rate * (beside(ref, SURF, tile) - field))
                - beside(ref, SURF_ARRAYS, tile)
                - beside(ref, COEF_X, tile) * (own_coef * field)
                - beside(ref, COEF_Y, tile) * geo.d_y(field)[0]
            )
        ends.append(geo.sum_x(moved[0], moved[1], halos[0], halos[1]))
    final = []
    for h in range(2):
        summed, _ = geo.sum_y_pair(ends[0][h], ends[1][h])
        final.append(summed * inverse[0][h])
        final_ref[ROWS * h : ROWS * (h + 1), :] = final[h]
        inverse_ref[ROWS * h : ROWS * (h + 1), :] = inverse[0][h]
    flux = [final[h] - surf_tile(SURF, 0, h) for h in range(2)]
    for group in range(blocks // ROWS):
        ids = rows_ref[ROWS * group : ROWS * (group + 1), :]
        high, low = ids >> 7, ids & (LANES - 1)
        picked = jnp.zeros((ROWS, LANES), jnp.float32)
        for x in range(2 * ROWS):
            line = spread(flux[x // ROWS][x % ROWS : x % ROWS + 1])
            picked = jnp.where(high == x, take(line, low, 1), picked)
        for c in range(ROWS):
            flux_ref[ROWS * group + c, 0:1, :] = picked[c : c + 1]

    copies = [
        pltpu.make_async_copy(flux_ref, slab_out.at[:, :HEAD], semaphores.at[0])
    ]
    copies[0].start()

    def put(x, plane, value):
        sums_ref[planes * x + plane : planes * x + plane + ROWS, :] = value

    def beyond(ref, plane, field, slope, own_coef):
        wind_at = 2 * planes + plane % levels
        return (
            beside(ref, MASS, 0) * field
            - ref[planes + plane : planes + plane + ROWS, :]
            - ref[wind_at : wind_at + ROWS, :] * (own_coef * field)
            - ref[wind_at + levels : wind_at + levels + ROWS, :] * slope
        )

    def row_of(tiles, x):
        return spread(tiles[x // ROWS][x % ROWS : x % ROWS + 1])

    masses = [surf_tile(MASS, 0, h) for h in range(2)]
    held = {}
    for element in range(x_points // GLL):
        lines = [GLL * element + i for i in range(GLL)]
        first, last = lines[0], lines[-1]
        scale = [row_of(inverse[0], x) for x in lines]
        mass = [row_of(masses, x) for x in lines]
        for level in range(0, levels, ROWS):
            wind = wind_tiles(wind_ref, x_points, level, lines)
            for plane in range(level, planes, levels):
                here = slice(plane, plane + ROWS)
                fields = []
                for i, x in enumerate(lines):
                    total = avg_ref[planes * x + plane : planes * x + plane + ROWS, :]
                    other = x - 1 if i == 0 else x + 1
                    if other < 0:
                        total = total + low_ref[here, :]
                    elif other == x_points:
                        total = total + high_ref[here, :]
                    elif i in (0, GLL - 1):
                        at = planes * other + plane
                        total = total + avg_ref[at : at + ROWS, :]
                    fields.append(total * scale[i])
                slopes = geo.d_y(*fields)
                moved = []
                for i, x in enumerate(lines):
                    slope = sum(deriv_table[i][j] * fields[j] for j in range(GLL))
                    moved.append(
                        mass[i] * (fields[i] - (wind[0][i] * slope + wind[1][i] * slopes[i]))
                    )
                if first == 0:
                    before = beyond(low_ref, plane, fields[0], slopes[0], deriv_table[3][3])
                    put(first, plane, before + moved[0])
                else:
                    shared = held[plane] + moved[0]
                    put(first - 1, plane, shared)
                    put(first, plane, shared)
                for i in range(1, GLL - 1):
                    put(lines[i], plane, moved[i])
                held[plane] = moved[-1]
                if last == x_points - 1:
                    after = beyond(
                        high_ref, plane, fields[-1], slopes[-1], deriv_table[0][0]
                    )
                    put(last, plane, held[plane] + after)
    packs = all_edges(geo, sums_ref, planes, x_points)
    to_right, to_left = split_sides(geo, packs[0], packs[1], 1)
    for i, (to, edges) in enumerate(((right, to_right), (left, to_left))):
        edges_ref[i] = edges
        copies.append(
            pltpu.make_async_copy(
                edges_ref.at[i],
                slab_out.at[to, EDGE_AT : EDGE_AT + ROWS],
                semaphores.at[1 + i],
            )
        )
        copies[-1].start()
    for copy in copies:
        copy.wait()


def end_kernel(
    planes,
    sums_ref,
    recv_ref,
    final_ref,
    inverse_ref,
    cols_ref,
    weights_ref,
    gain_ref,
    ocean_ref,
    air_out,
    ocean_out,
):
    geo = Geometry()
    blocks = cols_ref.shape[0]
    left, right = neighbours_of(blocks)
    chunks = gain_ref.shape[0]
    arrived = jnp.concatenate([recv_ref[c, 0:1, :] for c in range(blocks)], axis=0)
    (inflow,) = scatter_sum([weights_ref[...] * arrived], cols_ref[...], chunks)
    gain = inflow * gain_ref[...]
    ocean_out[...] = ocean_ref[...]
    for k in range(chunks):
        at = slice(LANES * k, LANES * (k + 1))
        ocean_out[0:1, at] = ocean_ref[0:1, at] + gain[k : k + 1]

    x_points = inverse_ref.shape[0]
    joined = join_edges(
        geo,
        recv_ref[left, EDGE_AT : EDGE_AT + ROWS, :],
        recv_ref[right, EDGE_AT : EDGE_AT + ROWS, :],
    )
    for x in range(x_points):
        inverse = spread(inverse_ref[x : x + 1, :])
        for group in range(planes // ROWS):
            at = planes * x + ROWS * group
            air_out[pl.ds(ROWS * group * x_points + x, ROWS, stride=x_points), :] = (
                inverse
                * geo.sum_y(sums_ref[at : at + ROWS, :], outer_edges(joined, x, group))
            )
    air_out[0:x_points, :] = final_ref[...]


def gathered(ids, coefs, source, sources, groups, first=0):
    totals = [jnp.zeros((ROWS, LANES), jnp.float32) for _ in range(groups)]
    for edge in range(ids.shape[0]):
        cell = spread(ids[edge : edge + 1])
        coef = spread(coefs[edge : edge + 1])
        high, low = cell >> 7, cell & (LANES - 1)
        for s in range(sources):
            scaled = jnp.where(high == first + s, coef, 0.0)
            for group in range(groups):
                totals[group] += scaled * take(source(group, s), low, 1)
    return totals


def ocean_kernel(
    levels, start, tracers_ref, coef_ref, near_ref, rate_ref, after_ref, out_ref
):
    chunks = tracers_ref.shape[1] // LANES
    groups = tracers_ref.shape[0] // ROWS
    row = iota((ROWS, LANES), 0)

    def source(group, s):
        return tracers_ref[
            ROWS * group : ROWS * (group + 1), LANES * s : LANES * (s + 1)
        ]

    def one_chunk(number, carry):
        k = number + start
        at = pl.ds(pl.multiple_of(k * LANES, LANES), LANES)
        out_at = pl.ds(pl.multiple_of(number * LANES, LANES), LANES)
        ids, coefs = near_ref[:, at], coef_ref[:, at]
        totals = gathered(ids, coefs, source, chunks, groups)
        coef_sum = spread(jnp.sum(coefs, axis=0, keepdims=True))
        rate = spread(rate_ref[pl.ds(k, 1), :])
        tiles = [tracers_ref[ROWS * g : ROWS * (g + 1), at] for g in range(groups)]
        for g in range(groups):
            tile = tiles[g]
            top = bottom = tile
            if (ROWS * g) % levels:
                top = pltpu.roll(tiles[g - 1], 1, 0)
            if (ROWS * (g + 1)) % levels:
                bottom = pltpu.roll(tiles[g + 1], ROWS - 1, 0)
            above = jnp.where(row == 0, top, pltpu.roll(tile, 1, 0))
            below = jnp.where(row == ROWS - 1, bottom, pltpu.roll(tile, ROWS - 1, 0))
            vertical = rate * ((above - tile) + (below - tile))
            out_ref[ROWS * g : ROWS * (g + 1), out_at] = (
                tile + (totals[g] - coef_sum * tile) + vertical
            )
        return carry

    lax.fori_loop(0, out_ref.shape[1] // LANES, one_chunk, 0)


def send_kernel(tracers_ref, send_ref, before_ref, after_ref, *out_refs):
    chunks = tracers_ref.shape[1] // LANES
    for part, (side_ref, out_ref) in enumerate(zip((before_ref, after_ref), out_refs)):
        base = side_ref.shape[0]
        out_ref[:base, :] = side_ref[...]
        cells = spread(send_ref[0:1, LANES * part : LANES * (part + 1)])
        high, low = cells >> 7, cells & (LANES - 1)
        for group in range(tracers_ref.shape[0] // ROWS):
            half = slice(ROWS * group, ROWS * (group + 1))
            rim = jnp.zeros((ROWS, LANES), jnp.float32)
            for k in range(chunks):
                tile = tracers_ref[half, LANES * k : LANES * (k + 1)]
                rim = jnp.where(high == k, take(tile, low, 1), rim)
            out_ref[base + ROWS * group : base + ROWS * (group + 1), :] = rim


def rim_kernel(
    starts,
    before_ref,
    after_ref,
    coef_ref,
    near_ref,
    area_ref,
    *refs,
):
    partial_refs, (out_ref, gain_ref) = refs[: len(starts)], refs[len(starts) :]
    chunks = coef_ref.shape[1] // LANES
    groups = out_ref.shape[0] // ROWS
    rim_at = before_ref.shape[0] - out_ref.shape[0]
    sides = before_ref, after_ref
    gain_ref[...] = flux_gain / area_ref[...]

    def source(group, s):
        at = rim_at + ROWS * group
        return sides[s][at : at + ROWS, :]

    for k in range(chunks):
        at = slice(LANES * k, LANES * (k + 1))
        totals = gathered(near_ref[:, at], coef_ref[:, at], source, 2, groups, chunks)
        part = max(i for i, start in enumerate(starts) if start <= k)
        place = slice(LANES * (k - starts[part]), LANES * (k - starts[part] + 1))
        for g in range(groups):
            half = slice(ROWS * g, ROWS * (g + 1))
            out_ref[half, at] = partial_refs[part][half, place] + totals[g]


VMEM_SPEC = pl.BlockSpec(memory_space=pltpu.VMEM)
ANY_SPEC = pl.BlockSpec(memory_space=pl.ANY)
HBM_SPEC = pl.BlockSpec(memory_space=pltpu.HBM)


def call(kernel, outs, specs, scratch=(), cost=0, hbm_out=False):
    estimate = None
    if cost:
        estimate = pl.CostEstimate(flops=0, bytes_accessed=cost, transcendentals=0)
    outs = [
        out if isinstance(out, jax.ShapeDtypeStruct) else jax.ShapeDtypeStruct(out, jnp.float32)
        for out in outs
    ]
    out_specs = [VMEM_SPEC] * len(outs)
    if hbm_out:
        out_specs[0] = HBM_SPEC
    return pl.pallas_call(
        kernel,
        out_shape=outs,
        in_specs=specs,
        out_specs=out_specs,
        scratch_shapes=list(scratch),
        cost_estimate=estimate,
        compiler_params=pltpu.CompilerParams(vmem_limit_bytes=32 * 2**20),
        name=getattr(kernel, "func", kernel).__name__,
    )


def body(
    air_state,
    air_wind,
    jacobian,
    land_area,
    xgrid_rows,
    tracers,
    edge_coef,
    neighbours,
    vert_rate,
    ocean_area,
    send_list,
    xgrid_cols,
    xgrid_weights,
):
    field_count, levels, x_points, y_points = air_state.shape
    planes = field_count * levels
    ocean_levels, cells = tracers.shape[1:]
    ocean_planes = tracers.shape[0] * ocean_levels
    faces, blocks = lax.axis_size("face"), lax.axis_size("blk")
    air = air_state.reshape(planes * x_points, y_points)
    wind = air_wind.reshape(2 * levels * x_points, y_points)
    ocean = tracers.reshape(ocean_planes, cells)
    point_ids, cell_ids, weights = xgrid_rows[0], xgrid_cols[0], xgrid_weights[0]
    rate = vert_rate.reshape(cells // LANES, LANES)
    area = ocean_area.reshape(cells // LANES, LANES)
    first_inputs = (
        cell_ids,
        weights,
        ocean,
        point_ids,
        jacobian,
        land_area,
        wind,
        air,
        send_list,
    )
    kept = (cell_ids, weights, point_ids, send_list)
    slab, moved, to_before, to_after, cell_ids, weights, point_ids, send_list = call(
        functools.partial(start_kernel, planes),
        [(blocks, HEAD, LANES), air.shape]
        + [(SIDE_IDS + blocks, LANES)] * 2
        + [jax.ShapeDtypeStruct(array.shape, array.dtype) for array in kept],
        [HBM_SPEC] * len(first_inputs),
        [
            pltpu.VMEM(shape, jnp.float32)
            for shape in (
                (blocks, HEAD, LANES),
                (ROWS, cells),
                jacobian.shape,
                land_area.shape,
                wind.shape,
                air.shape,
            )
        ]
        + [pltpu.SemaphoreType.DMA((len(first_inputs) + 1,))],
        hbm_out=True,
    )(*(pltpu.with_memory_space_constraint(array, pltpu.HBM) for array in first_inputs))
    recv = lax.all_to_all(slab, "blk", split_axis=0, concat_axis=0, tiled=True)

    chunks = cells // LANES
    reads_per_chunk = edge_coef.shape[0] * chunks * (ocean_planes // ROWS)
    starts = (0, chunks * 3 // 16, chunks * 10 // 16)

    def ocean_part(start, end, after):
        (result,) = call(
            functools.partial(ocean_kernel, ocean_levels, start),
            [(ocean_planes, (end - start) * LANES)],
            [VMEM_SPEC] * 4 + [ANY_SPEC],
            cost=(end - start) * reads_per_chunk * ROWS * LANES * 4,
        )(ocean, edge_coef, neighbours, rate, after)
        return result

    to_before, to_after = call(
        send_kernel,
        [(SIDE_IDS + blocks + ocean_planes, LANES)] * 2,
        [VMEM_SPEC] * 4,
        cost=reads_per_chunk * ROWS * LANES,
    )(ocean, send_list, to_before, to_after)
    onward = [(i, (i + 1) % blocks) for i in range(blocks)]
    before = lax.ppermute(to_after, "blk", onward)
    after = lax.ppermute(to_before, "blk", [(to, source) for source, to in onward])
    first_part = ocean_part(starts[0], starts[1], to_before)
    side_rows = 2 * planes + 2 * levels + 2 * SURF_ARRAYS + 4
    avg, down, up, surf = call(
        functools.partial(panel_kernel, planes),
        [air.shape, (side_rows, LANES), (side_rows, LANES), (4 * ROWS * SURF_ARRAYS, LANES)],
        [VMEM_SPEC] * 9 + [ANY_SPEC],
    )(
        moved,
        recv,
        before,
        after,
        air,
        wind,
        jacobian,
        land_area,
        point_ids,
        first_part,
    )
    after_me = [(i, (i + 1) % faces) for i in range(faces)]
    low = lax.ppermute(up, "face", after_me)
    high = lax.ppermute(down, "face", [(to, source) for source, to in after_me])
    second_part = ocean_part(starts[1], starts[2], surf)

    slab, sums, final, inverse = call(
        functools.partial(second_kernel, planes),
        [
            (blocks, EDGE_AT + ROWS, LANES),
            air.shape,
            (x_points, y_points),
            (x_points, y_points),
        ],
        [VMEM_SPEC] * 6 + [ANY_SPEC],
        [
            pltpu.VMEM((blocks, HEAD, LANES), jnp.float32),
            pltpu.VMEM((2, ROWS, LANES), jnp.float32),
            pltpu.SemaphoreType.DMA((3,)),
        ],
        hbm_out=True,
    )(avg, surf, low, high, wind, point_ids, second_part)
    arrived = lax.all_to_all(slab, "blk", split_axis=0, concat_axis=0, tiled=True)
    third_part = ocean_part(starts[2], chunks, final)
    partial, gain = call(
        functools.partial(rim_kernel, starts),
        [ocean.shape, area.shape],
        [VMEM_SPEC] * (5 + len(starts)),
        cost=chunks * reads_per_chunk // 8 * ROWS * LANES * 4,
    )(before, after, edge_coef, neighbours, area, first_part, second_part, third_part)
    air_final, ocean_final = call(
        functools.partial(end_kernel, planes),
        [air.shape, ocean.shape],
        [VMEM_SPEC] * 8,
    )(sums, arrived, final, inverse, cell_ids, weights, gain, partial)
    return air_final.reshape(air_state.shape), ocean_final.reshape(tracers.shape)


def solution(mesh):
    return jax.shard_map(
        body,
        mesh=mesh,
        in_specs=(
            P(None, None, "face", "blk"),
            P(None, None, "face", "blk"),
            P("face", "blk"),
            P("face", "blk"),
            P(("face", "blk"), None, None),
            P(None, None, ("face", "blk")),
            P(None, ("face", "blk")),
            P(None, ("face", "blk")),
            P(("face", "blk")),
            P(("face", "blk")),
            P(("face", "blk"), None),
            P(("face", "blk"), None, None),
            P(("face", "blk"), None, None),
        ),
        out_specs=(P(None, None, "face", "blk"), P(None, None, ("face", "blk"))),
        check_vma=False,
    )
```

```python
import functools

import jax
import jax.numpy as jnp
from jax import lax
from jax.experimental import pallas as pl
from jax.experimental.pallas import tpu as pltpu
from jax.sharding import PartitionSpec as P

GLL = 4
ROWS = 8
LANES = 128

deriv_table = [
    [-3.0, 4.045084971874737, -1.545084971874737, 0.5],
    [-0.8090169943749475, 0.0, 1.118033988749895, -0.30901699437494745],
    [0.30901699437494745, -1.118033988749895, 0.0, 0.8090169943749475],
    [-0.5, 1.545084971874737, -4.045084971874737, 3.0],
]
time_step = 0.05
relax_rate = 0.3
flux_gain = 0.2

HEAD, EDGE_AT = 8, 8
SIDE_EDGE, SIDE_STRIP, SIDE_IDS = 0, 8, 16
AVG, MASS_SUM, MASS, COEF_X, COEF_Y, SURF = range(6)
SURF_ARRAYS = 6


def iota(shape, dim):
    return lax.broadcasted_iota(jnp.int32, shape, dim)


def take(values, index, axis):
    return jnp.take_along_axis(values, index, axis=axis, mode="promise_in_bounds")


def by_position(pos, values):
    result = jnp.full(pos.shape, values[-1], jnp.float32)
    for i, value in enumerate(values[:-1]):
        result = jnp.where(pos == i, value, result)
    return result


def spread(row):
    return jnp.broadcast_to(row, (ROWS, LANES))


class Geometry:
    def __init__(self):
        shape = (ROWS, LANES)
        self.row, self.lane = iota(shape, 0), iota(shape, 1)
        x_pos, y_pos = self.row & (GLL - 1), self.lane & (GLL - 1)
        self.y_from = [self.lane - y_pos + j for j in range(GLL)]
        columns = [[line[j] for line in deriv_table] for j in range(GLL)]
        self.x_coef = {
            step: by_position(
                x_pos,
                [
                    deriv_table[i][i + step] if 0 <= i + step < GLL else 0.0
                    for i in range(GLL)
                ],
            )
            for step in range(1 - GLL, GLL)
        }
        self.y_coef = [by_position(y_pos, column) for column in columns]
        self.y_swap = (
            self.lane + jnp.where(y_pos == GLL - 1, 1, 0) - jnp.where(y_pos == 0, 1, 0)
        ) & (LANES - 1)
        self.x_edge = (x_pos == 0) | (x_pos == GLL - 1)
        self.y_edge = (y_pos == 0) | (y_pos == GLL - 1)
        self.first_row, self.last_row = self.row == 0, self.row == ROWS - 1
        self.middle_row = self.row == GLL
        self.outer_lane = (self.lane == 0) | (self.lane == LANES - 1)
        self.weight = jnp.where(self.x_edge, 1.0 / 6.0, 5.0 / 6.0) * jnp.where(
            self.y_edge, 1.0 / 6.0, 5.0 / 6.0
        )

    def d_x(self, tile):
        return sum(
            coef * (pltpu.roll(tile, -step % ROWS, 0) if step else tile)
            for step, coef in self.x_coef.items()
        )

    def d_y(self, *tiles):
        totals = [0.0] * len(tiles)
        for j in range(GLL):
            for i, tile in enumerate(tiles):
                totals[i] += self.y_coef[j] * take(tile, self.y_from[j], 1)
        return totals

    def sum_x(self, low, high, before, after):
        low_down, low_up = pltpu.roll(low, 1, 0), pltpu.roll(low, ROWS - 1, 0)
        high_down, high_up = pltpu.roll(high, 1, 0), pltpu.roll(high, ROWS - 1, 0)
        low_other = jnp.where(
            self.first_row,
            before,
            jnp.where(
                self.middle_row, low_down, jnp.where(self.last_row, high_up, low_up)
            ),
        )
        high_other = jnp.where(
            self.first_row,
            low_down,
            jnp.where(
                self.middle_row, high_down, jnp.where(self.last_row, after, high_up)
            ),
        )
        return (
            low + jnp.where(self.x_edge, low_other, 0.0),
            high + jnp.where(self.x_edge, high_other, 0.0),
        )

    def sum_y(self, tile, outer):
        other = jnp.where(self.outer_lane, outer, take(tile, self.y_swap, 1))
        return tile + jnp.where(self.y_edge, other, 0.0)

    def sum_y_pair(self, own, strip):
        own_swap, strip_swap = take(own, self.y_swap, 1), take(strip, self.y_swap, 1)
        own_other = jnp.where(self.outer_lane, strip_swap, own_swap)
        strip_other = jnp.where(self.outer_lane, own_swap, strip_swap)
        return (
            own + jnp.where(self.y_edge, own_other, 0.0),
            strip + jnp.where(self.y_edge, strip_other, 0.0),
        )


def edge_place(x, group):
    return x // ROWS, LANES // 2 * (x % 2) + ROWS * group + 2 * (x % ROWS // 2)


def all_edges(geo, ref, planes, x_points, ends_ref=None):
    packs = [jnp.zeros((ROWS, LANES), jnp.float32) for _ in range(2)]
    for x in range(x_points):
        rows, first = ref, planes * x
        if ends_ref is not None and x in (0, x_points - 1):
            rows, first = ends_ref, planes * (x // (x_points - 1))
        for group in range(planes // ROWS):
            q, at = edge_place(x, group)
            tile = rows[first + ROWS * group : first + ROWS * (group + 1), :]
            rolled = pltpu.roll(tile, (at + 1) % LANES, 1)
            packs[q] = jnp.where((geo.lane >> 1) == at // 2, rolled, packs[q])
    return packs


def outer_edges(joined, x, group):
    q, at = edge_place(x, group)
    return pltpu.roll(joined[q], (-(at + 1)) % LANES, 1)


def split_sides(geo, first, second, unit):
    odd = (geo.lane & unit) != 0
    return (
        jnp.where(odd, pltpu.roll(second, unit, 1), first),
        jnp.where(odd, second, pltpu.roll(first, LANES - unit, 1)),
    )


def join_sides(geo, before, after, unit):
    odd = (geo.lane & unit) != 0
    return (
        jnp.where(odd, pltpu.roll(after, unit, 1), before),
        jnp.where(odd, after, pltpu.roll(before, LANES - unit, 1)),
    )


def join_edges(geo, before, after):
    odd = (geo.lane & 1) != 0
    return (
        jnp.where(odd, pltpu.roll(before, 1, 1), after),
        jnp.where(odd, before, pltpu.roll(after, LANES - 1, 1)),
    )


def neighbours_of(blocks):
    here = lax.axis_index("blk")
    return lax.rem(here + blocks - 1, blocks), lax.rem(here + 1, blocks)


def scatter_sum(lines, index, bins, allowed=None):
    count = index.shape[0]
    split = []
    for values in lines:
        for part in range(3):
            short = values.astype(jnp.bfloat16).astype(jnp.float32)
            split.append(short)
            values = values - short
    high, low = index >> 7, index & (LANES - 1)
    bin_at = iota((bins, LANES), 0)
    lane_at = iota((LANES, LANES), 0)
    if allowed is not None:
        lane_at = jnp.where(allowed(lane_at), lane_at, -1)
    left, right = [], []
    for c in range(count):
        hit = bin_at == high[c : c + 1]
        left.append(
            jnp.concatenate(
                [jnp.where(hit, part[c : c + 1], 0.0) for part in split], axis=0
            ).astype(jnp.bfloat16)
        )
        right.append(
            jnp.where(lane_at == low[c : c + 1], 1.0, 0.0).astype(jnp.bfloat16)
        )
    total = lax.dot_general(
        jnp.concatenate(left, axis=1),
        jnp.concatenate(right, axis=1),
        (((1,), (1,)), ((), ())),
        preferred_element_type=jnp.float32,
    )
    sums = []
    for i in range(len(lines)):
        part = total[3 * i * bins : 3 * (i + 1) * bins]
        sums.append(part[:bins] + part[bins : 2 * bins] + part[2 * bins :])
    return sums


def wind_tiles(wind_ref, x_points, level, lines):
    levels = wind_ref.shape[0] // (2 * x_points)
    return [
        [
            time_step
            * wind_ref[
                pl.ds((levels * part + level) * x_points + x, ROWS, stride=x_points), :
            ]
            for x in lines
        ]
        for part in range(2)
    ]


def start_kernel(
    planes,
    cols_in,
    weights_in,
    tracers_in,
    rows_in,
    jac_in,
    land_in,
    wind_in,
    air_in,
    send_in,
    slab_out,
    moved_ref,
    before_ref,
    after_ref,
    cols_ref,
    weights_ref,
    rows_ref,
    send_ref,
    slab_ref,
    tracers_ref,
    jac_ref,
    land_ref,
    wind_ref,
    air_ref,
    semaphores,
):
    copies = [
        pltpu.make_async_copy(source, target, semaphores.at[i])
        for i, (source, target) in enumerate(
            (
                (cols_in, cols_ref),
                (tracers_in.at[:ROWS], tracers_ref),
                (weights_in, weights_ref),
                (rows_in, rows_ref),
                (air_in, air_ref),
                (wind_in, wind_ref),
                (jac_in, jac_ref),
                (land_in, land_ref),
                (send_in, send_ref),
            )
        )
    ]
    for copy in copies:
        copy.start()
    geo = Geometry()
    blocks = cols_ref.shape[0]
    x_points = jac_ref.shape[0]
    levels = wind_ref.shape[0] // (2 * x_points)
    chunks = tracers_ref.shape[1] // LANES
    for copy in copies[:4]:
        copy.wait()

    for group in range(blocks // ROWS):
        at = slice(ROWS * group, ROWS * (group + 1))
        cells = cols_ref[at, :]
        high, low = cells >> 7, cells & (LANES - 1)
        surface = jnp.zeros((ROWS, LANES), jnp.float32)
        for k in range(chunks):
            line = spread(tracers_ref[0:1, LANES * k : LANES * (k + 1)])
            surface = jnp.where(high == k, take(line, low, 1), surface)
        area = weights_ref[at, :]
        heat = area * surface
        for c in range(ROWS):
            owner = ROWS * group + c
            for place, step in enumerate((1, 0, -1)):
                to = (owner + step) % blocks
                slab_ref[to, 2 * place : 2 * place + 1, :] = heat[c : c + 1]
                slab_ref[to, 2 * place + 1 : 2 * place + 2, :] = area[c : c + 1]

    out = pltpu.make_async_copy(slab_ref, slab_out, semaphores.at[len(copies)])
    out.start()
    ids = rows_ref[...].astype(jnp.float32)
    for side_ref in (before_ref, after_ref):
        side_ref[SIDE_IDS : SIDE_IDS + blocks, :] = ids

    for copy in copies[4:]:
        copy.wait()
    strips = []
    for h in range(2):
        half = slice(ROWS * h, ROWS * (h + 1))
        second = levels * x_points
        pack = jnp.zeros((ROWS, LANES), jnp.float32)
        for i, strip in enumerate(
            (
                air_ref[half, :],
                wind_ref[half, :],
                wind_ref[second + ROWS * h : second + ROWS * (h + 1), :],
                jac_ref[half, :],
                land_ref[half, :],
            )
        ):
            pack = jnp.where(
                (geo.lane >> 4) == i, pltpu.roll(strip, 16 * i + 8, 1), pack
            )
        strips.append(pack)
    to_right, to_left = split_sides(geo, strips[0], strips[1], ROWS)
    after_ref[SIDE_STRIP : SIDE_STRIP + ROWS, :] = to_right
    before_ref[SIDE_STRIP : SIDE_STRIP + ROWS, :] = to_left

    y_weight = jnp.where(geo.y_edge, 1.0 / 6.0, 5.0 / 6.0)
    for element in range(x_points // GLL):
        lines = [GLL * element + i for i in range(GLL)]
        mass = [
            (1.0 / 6.0 if i in (0, GLL - 1) else 5.0 / 6.0)
            * y_weight
            * spread(jac_ref[x : x + 1, :])
            for i, x in enumerate(lines)
        ]
        for level in range(0, levels, ROWS):
            wind = wind_tiles(wind_ref, x_points, level, lines)
            for plane in range(level, planes, levels):
                fields = [
                    air_ref[pl.ds(plane * x_points + x, ROWS, stride=x_points), :]
                    for x in lines
                ]
                slopes = geo.d_y(*fields)
                for i, x in enumerate(lines):
                    slope = sum(deriv_table[i][j] * fields[j] for j in range(GLL))
                    moved = mass[i] * (
                        fields[i] - (wind[0][i] * slope + wind[1][i] * slopes[i])
                    )
                    moved_ref[planes * x + plane : planes * x + plane + ROWS, :] = moved
    packs = all_edges(geo, moved_ref, planes, x_points)
    to_right, to_left = split_sides(geo, packs[0], packs[1], 1)
    after_ref[SIDE_EDGE : SIDE_EDGE + ROWS, :] = to_right
    before_ref[SIDE_EDGE : SIDE_EDGE + ROWS, :] = to_left
    out.wait()


def panel_kernel(
    planes,
    moved_ref,
    recv_ref,
    before_ref,
    after_ref,
    air_ref,
    wind_ref,
    jac_ref,
    land_ref,
    rows_ref,
    ocean_ref,
    avg_ref,
    down_ref,
    up_ref,
    surf_ref,
):
    geo = Geometry()
    blocks = rows_ref.shape[0]
    x_points = jac_ref.shape[0]
    levels = wind_ref.shape[0] // (2 * x_points)

    own_ids = rows_ref[...]
    left_ids = before_ref[SIDE_IDS : SIDE_IDS + blocks, :].astype(jnp.int32)
    right_ids = after_ref[SIDE_IDS : SIDE_IDS + blocks, :].astype(jnp.int32)
    head = [
        jnp.concatenate([recv_ref[c, i : i + 1, :] for c in range(blocks)], axis=0)
        for i in range(6)
    ]
    heat, frac = scatter_sum(head[2:4], own_ids, 2 * ROWS)
    from_left = scatter_sum(
        head[0:2], left_ids, 2 * ROWS, lambda lane: lane >= LANES - ROWS
    )
    from_right = scatter_sum(head[4:6], right_ids, 2 * ROWS, lambda lane: lane < ROWS)
    strip_heat = from_left[0] + from_right[0]
    strip_frac = from_left[1] + from_right[1]

    in_strip = (geo.lane < ROWS) | (geo.lane >= LANES - ROWS)
    packs = join_sides(
        geo,
        before_ref[SIDE_STRIP : SIDE_STRIP + ROWS, :],
        after_ref[SIDE_STRIP : SIDE_STRIP + ROWS, :],
        ROWS,
    )
    own, strip = [], []
    for h, pack in enumerate(packs):
        half = slice(ROWS * h, ROWS * (h + 1))
        strip.append(
            [
                jnp.where(
                    in_strip, pltpu.roll(pack, (-(16 * i + 8)) % LANES, 1), 1.0
                )
                for i in range(5)
            ]
        )
        own.append(
            [
                air_ref[half, :],
                wind_ref[half, :],
                wind_ref[
                    levels * x_points + ROWS * h : levels * x_points + ROWS * (h + 1), :
                ],
                jac_ref[half, :],
                land_ref[half, :],
            ]
        )
    for h in range(2):
        half = slice(ROWS * h, ROWS * (h + 1))
        pair = []
        for tile, ((field, wind_x, wind_y, jac, land), tile_heat, tile_frac) in enumerate(
            ((own[h], heat[half], frac[half]), (strip[h], strip_heat[half], strip_frac[half]))
        ):
            mass = geo.weight * jac
            if tile == 1:
                tile_heat = jnp.where(in_strip, tile_heat, 0.0)
                tile_frac = jnp.where(in_strip, tile_frac, 0.0)
            surf = (tile_heat + land * field) / (tile_frac + land)
            coef_x, coef_y = time_step * mass * wind_x, time_step * mass * wind_y
            moved = (
                mass * (field + relax_rate * (surf - field))
                - coef_x * geo.d_x(field)
                - coef_y * geo.d_y(field)[0]
            )
            pair.append((moved, mass))
            at = 2 * ROWS * tile + ROWS * h
            for number, value in (
                (MASS, mass),
                (COEF_X, coef_x),
                (COEF_Y, coef_y),
                (SURF, surf),
            ):
                surf_ref[4 * ROWS * number + at : 4 * ROWS * number + at + ROWS, :] = value
        for number, i in ((AVG, 0), (MASS_SUM, 1)):
            for tile, value in enumerate(geo.sum_y_pair(pair[0][i], pair[1][i])):
                at = 4 * ROWS * number + 2 * ROWS * tile + ROWS * h
                surf_ref[at : at + ROWS, :] = value

    joined = join_edges(
        geo,
        before_ref[SIDE_EDGE : SIDE_EDGE + ROWS, :],
        after_ref[SIDE_EDGE : SIDE_EDGE + ROWS, :],
    )
    for x in range(x_points):
        for group in range(planes // ROWS):
            at = slice(planes * x + ROWS * group, planes * x + ROWS * (group + 1))
            avg_ref[at, :] = geo.sum_y(moved_ref[at, :], outer_edges(joined, x, group))

    def line(r):
        return avg_ref[planes * r : planes * (r + 1), :]

    def surf_line(number, r):
        return surf_ref[pl.ds(4 * ROWS * number + r, 2, stride=x_points), :]

    def first_step(get, mass_at):
        return (
            [
                get(1) / mass_at(1),
                get(2) / mass_at(2),
                (get(3) + get(4)) / (mass_at(3) + mass_at(4)),
            ],
            [
                (get(11) + get(12)) / (mass_at(11) + mass_at(12)),
                get(13) / mass_at(13),
                get(14) / mass_at(14),
            ],
        )

    def own_mass_sum(r):
        return surf_ref[4 * ROWS * MASS_SUM + r : 4 * ROWS * MASS_SUM + r + 1, :]

    low_lines, high_lines = first_step(line, own_mass_sum)
    surf_low, surf_high = first_step(
        functools.partial(surf_line, AVG), functools.partial(surf_line, MASS_SUM)
    )
    for out_ref, r, lines, surf_lines, coefs in (
        (down_ref, 0, low_lines, surf_low, deriv_table[0][1:]),
        (up_ref, 15, high_lines, surf_high, deriv_table[3][:3]),
    ):
        slope = sum(coef * value for coef, value in zip(coefs, lines))
        surf_slope = sum(coef * value for coef, value in zip(coefs, surf_lines))
        mass = surf_ref[4 * ROWS * MASS + r : 4 * ROWS * MASS + r + 1, :]
        wind = time_step * mass * wind_ref[pl.ds(r, 2 * levels, stride=x_points), :]
        out_ref[0:planes, :] = line(r)
        columns = [
            wind[plane % levels : plane % levels + ROWS] * slope[plane : plane + ROWS]
            for plane in range(0, planes, ROWS)
        ] + [wind[level : level + ROWS] for level in range(0, 2 * levels, ROWS)]
        pack = jnp.zeros((ROWS, LANES), jnp.float32)
        for i, tile in enumerate(columns):
            pack = jnp.where((geo.lane >> 1) == i, pltpu.roll(tile, 2 * i + 1, 1), pack)
        out_ref[planes : planes + ROWS, :] = pack
        base = planes + ROWS
        for number in range(SURF_ARRAYS):
            out_ref[base + 2 * number : base + 2 * number + 2, :] = surf_line(number, r)
        base += 2 * SURF_ARRAYS
        out_ref[base : base + 2, :] = surf_line(COEF_X, r) * surf_slope


def second_kernel(
    planes,
    avg_ref,
    surf_ref,
    low_ref,
    high_ref,
    wind_ref,
    rows_ref,
    ocean_ref,
    slab_out,
    sums_ref,
    final_ref,
    inverse_ref,
    flux_ref,
    edges_ref,
    ends_ref,
    semaphores,
):
    geo = Geometry()
    blocks = rows_ref.shape[0]
    left, right = neighbours_of(blocks)
    x_points = final_ref.shape[0]
    levels = wind_ref.shape[0] // (2 * x_points)
    base = planes + ROWS

    def surf_tile(number, tile, h):
        at = 4 * ROWS * number + 2 * ROWS * tile + ROWS * h
        return surf_ref[at : at + ROWS, :]

    def beside(ref, number, tile):
        at = base + 2 * number + tile
        return spread(ref[at : at + 1, :])

    ends = []
    inverse = []
    for tile in range(2):
        total = geo.sum_x(
            surf_tile(MASS_SUM, tile, 0),
            surf_tile(MASS_SUM, tile, 1),
            beside(low_ref, MASS_SUM, tile),
            beside(high_ref, MASS_SUM, tile),
        )
        inverse.append([1.0 / value for value in total])
        summed = geo.sum_x(
            surf_tile(AVG, tile, 0),
            surf_tile(AVG, tile, 1),
            beside(low_ref, AVG, tile),
            beside(high_ref, AVG, tile),
        )
        fields = [value * scale for value, scale in zip(summed, inverse[tile])]
        moved = []
        for h in range(2):
            field = fields[h]
            moved.append(
                surf_tile(MASS, tile, h)
                * (field + relax_rate * (surf_tile(SURF, tile, h) - field))
                - surf_tile(COEF_X, tile, h) * geo.d_x(field)
                - surf_tile(COEF_Y, tile, h) * geo.d_y(field)[0]
            )
        halos = []
        for ref, field, own_coef in (
            (low_ref, spread(fields[0][:1]), deriv_table[3][3]),
            (high_ref, spread(fields[1][ROWS - 1 :]), deriv_table[0][0]),
        ):
            halos.append(
                beside(ref, MASS, tile)
                * (field + relax_rate * (beside(ref, SURF, tile) - field))
                - beside(ref, SURF_ARRAYS, tile)
                - beside(ref, COEF_X, tile) * (own_coef * field)
                - beside(ref, COEF_Y, tile) * geo.d_y(field)[0]
            )
        ends.append(geo.sum_x(moved[0], moved[1], halos[0], halos[1]))
    final = []
    for h in range(2):
        summed, _ = geo.sum_y_pair(ends[0][h], ends[1][h])
        final.append(summed * inverse[0][h])
        final_ref[ROWS * h : ROWS * (h + 1), :] = final[h]
        inverse_ref[ROWS * h : ROWS * (h + 1), :] = inverse[0][h]
    flux = [final[h] - surf_tile(SURF, 0, h) for h in range(2)]
    for group in range(blocks // ROWS):
        ids = rows_ref[ROWS * group : ROWS * (group + 1), :]
        high, low = ids >> 7, ids & (LANES - 1)
        picked = jnp.zeros((ROWS, LANES), jnp.float32)
        for x in range(2 * ROWS):
            line = spread(flux[x // ROWS][x % ROWS : x % ROWS + 1])
            picked = jnp.where(high == x, take(line, low, 1), picked)
        for c in range(ROWS):
            flux_ref[ROWS * group + c, 0:1, :] = picked[c : c + 1]

    copies = [
        pltpu.make_async_copy(flux_ref, slab_out.at[:, :HEAD], semaphores.at[0])
    ]
    copies[0].start()

    def put(x, plane, value):
        sums_ref[planes * x + plane : planes * x + plane + ROWS, :] = value

    def column(ref, number):
        return pltpu.roll(ref[planes : planes + ROWS, :], (-(2 * number + 1)) % LANES, 1)

    def beyond(ref, plane, field, slope, own_coef):
        wind_at = (planes + plane % levels) // ROWS
        return (
            beside(ref, MASS, 0) * field
            - column(ref, plane // ROWS)
            - column(ref, wind_at) * (own_coef * field)
            - column(ref, wind_at + levels // ROWS) * slope
        )

    def row_of(tiles, x):
        return spread(tiles[x // ROWS][x % ROWS : x % ROWS + 1])

    masses = [surf_tile(MASS, 0, h) for h in range(2)]
    held = {}
    for element in range(x_points // GLL):
        lines = [GLL * element + i for i in range(GLL)]
        first, last = lines[0], lines[-1]
        scale = [row_of(inverse[0], x) for x in lines]
        mass = [row_of(masses, x) for x in lines]
        for level in range(0, levels, ROWS):
            wind = wind_tiles(wind_ref, x_points, level, lines)
            for plane in range(level, planes, levels):
                here = slice(plane, plane + ROWS)
                fields = []
                for i, x in enumerate(lines):
                    total = avg_ref[planes * x + plane : planes * x + plane + ROWS, :]
                    other = x - 1 if i == 0 else x + 1
                    if other < 0:
                        total = total + low_ref[here, :]
                    elif other == x_points:
                        total = total + high_ref[here, :]
                    elif i in (0, GLL - 1):
                        at = planes * other + plane
                        total = total + avg_ref[at : at + ROWS, :]
                    fields.append(total * scale[i])
                slopes = geo.d_y(*fields)
                moved = []
                for i, x in enumerate(lines):
                    slope = sum(deriv_table[i][j] * fields[j] for j in range(GLL))
                    moved.append(
                        mass[i] * (fields[i] - (wind[0][i] * slope + wind[1][i] * slopes[i]))
                    )
                if first == 0:
                    put(first, plane, moved[0])
                    ends_ref[plane : plane + ROWS, :] = moved[0] + beyond(
                        low_ref, plane, fields[0], slopes[0], deriv_table[3][3]
                    )
                else:
                    shared = held[plane] + moved[0]
                    put(first - 1, plane, shared)
                    put(first, plane, shared)
                for i in range(1, GLL - 1):
                    put(lines[i], plane, moved[i])
                held[plane] = moved[-1]
                if last == x_points - 1:
                    put(last, plane, moved[-1])
                    at = planes + plane
                    ends_ref[at : at + ROWS, :] = moved[-1] + beyond(
                        high_ref, plane, fields[-1], slopes[-1], deriv_table[0][0]
                    )
    packs = all_edges(geo, sums_ref, planes, x_points, ends_ref)
    to_right, to_left = split_sides(geo, packs[0], packs[1], 1)
    for i, (to, edges) in enumerate(((right, to_right), (left, to_left))):
        edges_ref[i] = edges
        copies.append(
            pltpu.make_async_copy(
                edges_ref.at[i],
                slab_out.at[to, EDGE_AT : EDGE_AT + ROWS],
                semaphores.at[1 + i],
            )
        )
        copies[-1].start()
    for copy in copies:
        copy.wait()


def rows_kernel(sums_ref, down_ref, up_ref):
    planes = down_ref.shape[0]
    down_ref[...] = sums_ref[:planes, :]
    up_ref[...] = sums_ref[sums_ref.shape[0] - planes :, :]


def end_kernel(
    planes,
    sums_ref,
    low_ref,
    high_ref,
    recv_ref,
    final_ref,
    inverse_ref,
    cols_ref,
    weights_ref,
    gain_ref,
    ocean_ref,
    air_out,
    ocean_out,
):
    geo = Geometry()
    blocks = cols_ref.shape[0]
    left, right = neighbours_of(blocks)
    chunks = gain_ref.shape[0]
    arrived = jnp.concatenate([recv_ref[c, 0:1, :] for c in range(blocks)], axis=0)
    (inflow,) = scatter_sum([weights_ref[...] * arrived], cols_ref[...], chunks)
    gain = inflow * gain_ref[...]
    ocean_out[...] = ocean_ref[...]
    for k in range(chunks):
        at = slice(LANES * k, LANES * (k + 1))
        ocean_out[0:1, at] = ocean_ref[0:1, at] + gain[k : k + 1]

    x_points = inverse_ref.shape[0]
    joined = join_edges(
        geo,
        recv_ref[left, EDGE_AT : EDGE_AT + ROWS, :],
        recv_ref[right, EDGE_AT : EDGE_AT + ROWS, :],
    )
    for x in range(x_points):
        inverse = spread(inverse_ref[x : x + 1, :])
        for group in range(planes // ROWS):
            at = planes * x + ROWS * group
            half = slice(ROWS * group, ROWS * (group + 1))
            total = sums_ref[at : at + ROWS, :]
            if x == 0:
                total = total + low_ref[half, :]
            elif x == x_points - 1:
                total = total + high_ref[half, :]
            air_out[pl.ds(ROWS * group * x_points + x, ROWS, stride=x_points), :] = (
                inverse * geo.sum_y(total, outer_edges(joined, x, group))
            )
    air_out[0:x_points, :] = final_ref[...]


def gathered(ids, coefs, source, sources, groups, first=0):
    totals = [jnp.zeros((ROWS, LANES), jnp.float32) for _ in range(groups)]
    for edge in range(ids.shape[0]):
        cell = spread(ids[edge : edge + 1])
        coef = spread(coefs[edge : edge + 1])
        high, low = cell >> 7, cell & (LANES - 1)
        for s in range(sources):
            scaled = jnp.where(high == first + s, coef, 0.0)
            for group in range(groups):
                totals[group] += scaled * take(source(group, s), low, 1)
    return totals


def multiplied(ids, coefs, halves_ref, sources, groups):
    lane_at = iota((LANES, LANES), 0)
    hot = jnp.concatenate(
        [
            jnp.where(lane_at == (ids[edge : edge + 1] & (LANES - 1)), 1.0, 0.0).astype(
                jnp.bfloat16
            )
            for edge in range(2)
        ],
        axis=1,
    )
    picked = jnp.dot(
        halves_ref[...],
        jnp.concatenate([hot, hot], axis=0),
        preferred_element_type=jnp.float32,
    )
    totals = [jnp.zeros((ROWS, LANES), jnp.float32) for _ in range(groups)]
    for edge in range(2):
        high = spread(ids[edge : edge + 1]) >> 7
        coef = spread(coefs[edge : edge + 1])
        side = slice(LANES * edge, LANES * (edge + 1))
        for s in range(sources):
            scaled = jnp.where(high == s, coef, 0.0)
            for group in range(groups):
                at = ROWS * (groups * s + group)
                totals[group] += scaled * picked[at : at + ROWS, side]
    return totals


def ocean_kernel(
    levels, start, tracers_ref, coef_ref, near_ref, rate_ref, after_ref, out_ref, halves_ref
):
    chunks = tracers_ref.shape[1] // LANES
    groups = tracers_ref.shape[0] // ROWS
    row = iota((ROWS, LANES), 0)

    def source(group, s):
        return tracers_ref[
            ROWS * group : ROWS * (group + 1), LANES * s : LANES * (s + 1)
        ]

    planes = tracers_ref.shape[0]
    for s in range(chunks):
        values = tracers_ref[:, LANES * s : LANES * (s + 1)]
        upper = values.astype(jnp.bfloat16)
        at = slice(planes * s, planes * (s + 1))
        halves_ref[at, :LANES] = upper
        halves_ref[at, LANES:] = (values - upper.astype(jnp.float32)).astype(jnp.bfloat16)
    edges = near_ref.shape[0]

    def one_chunk(number, carry):
        k = number + start
        at = pl.ds(pl.multiple_of(k * LANES, LANES), LANES)
        out_at = pl.ds(pl.multiple_of(number * LANES, LANES), LANES)
        ids, coefs = near_ref[:, at], coef_ref[:, at]
        by_gather = edges - edges // 3 * 2
        totals = gathered(ids[:by_gather], coefs[:by_gather], source, chunks, groups)
        for edge in range(by_gather, edges, 2):
            more = multiplied(
                ids[edge : edge + 2], coefs[edge : edge + 2], halves_ref, chunks, groups
            )
            totals = [total + part for total, part in zip(totals, more)]
        coef_sum = spread(jnp.sum(coefs, axis=0, keepdims=True))
        rate = spread(rate_ref[pl.ds(k, 1), :])
        tiles = [tracers_ref[ROWS * g : ROWS * (g + 1), at] for g in range(groups)]
        for g in range(groups):
            tile = tiles[g]
            top = bottom = tile
            if (ROWS * g) % levels:
                top = pltpu.roll(tiles[g - 1], 1, 0)
            if (ROWS * (g + 1)) % levels:
                bottom = pltpu.roll(tiles[g + 1], ROWS - 1, 0)
            above = jnp.where(row == 0, top, pltpu.roll(tile, 1, 0))
            below = jnp.where(row == ROWS - 1, bottom, pltpu.roll(tile, ROWS - 1, 0))
            vertical = rate * ((above - tile) + (below - tile))
            out_ref[ROWS * g : ROWS * (g + 1), out_at] = (
                tile + (totals[g] - coef_sum * tile) + vertical
            )
        return carry

    lax.fori_loop(0, out_ref.shape[1] // LANES, one_chunk, 0)


def send_kernel(tracers_ref, send_ref, before_ref, after_ref, *out_refs):
    chunks = tracers_ref.shape[1] // LANES
    for part, (side_ref, out_ref) in enumerate(zip((before_ref, after_ref), out_refs)):
        base = side_ref.shape[0]
        out_ref[:base, :] = side_ref[...]
        cells = spread(send_ref[0:1, LANES * part : LANES * (part + 1)])
        high, low = cells >> 7, cells & (LANES - 1)
        for group in range(tracers_ref.shape[0] // ROWS):
            half = slice(ROWS * group, ROWS * (group + 1))
            rim = jnp.zeros((ROWS, LANES), jnp.float32)
            for k in range(chunks):
                tile = tracers_ref[half, LANES * k : LANES * (k + 1)]
                rim = jnp.where(high == k, take(tile, low, 1), rim)
            out_ref[base + ROWS * group : base + ROWS * (group + 1), :] = rim


def rim_kernel(
    starts,
    before_ref,
    after_ref,
    coef_ref,
    near_ref,
    area_ref,
    *refs,
):
    partial_refs, (out_ref, gain_ref) = refs[: len(starts)], refs[len(starts) :]
    chunks = coef_ref.shape[1] // LANES
    groups = out_ref.shape[0] // ROWS
    rim_at = before_ref.shape[0] - out_ref.shape[0]
    sides = before_ref, after_ref
    gain_ref[...] = flux_gain / area_ref[...]

    def source(group, s):
        at = rim_at + ROWS * group
        return sides[s][at : at + ROWS, :]

    for k in range(chunks):
        at = slice(LANES * k, LANES * (k + 1))
        totals = gathered(near_ref[:, at], coef_ref[:, at], source, 2, groups, chunks)
        part = max(i for i, start in enumerate(starts) if start <= k)
        place = slice(LANES * (k - starts[part]), LANES * (k - starts[part] + 1))
        for g in range(groups):
            half = slice(ROWS * g, ROWS * (g + 1))
            out_ref[half, at] = partial_refs[part][half, place] + totals[g]


VMEM_SPEC = pl.BlockSpec(memory_space=pltpu.VMEM)
ANY_SPEC = pl.BlockSpec(memory_space=pl.ANY)
HBM_SPEC = pl.BlockSpec(memory_space=pltpu.HBM)


def call(kernel, outs, specs, scratch=(), cost=0, hbm_out=False):
    estimate = None
    if cost:
        estimate = pl.CostEstimate(flops=0, bytes_accessed=cost, transcendentals=0)
    outs = [
        out if isinstance(out, jax.ShapeDtypeStruct) else jax.ShapeDtypeStruct(out, jnp.float32)
        for out in outs
    ]
    out_specs = [VMEM_SPEC] * len(outs)
    if hbm_out:
        out_specs[0] = HBM_SPEC
    return pl.pallas_call(
        kernel,
        out_shape=outs,
        in_specs=specs,
        out_specs=out_specs,
        scratch_shapes=list(scratch),
        cost_estimate=estimate,
        compiler_params=pltpu.CompilerParams(vmem_limit_bytes=32 * 2**20),
        name=getattr(kernel, "func", kernel).__name__,
    )


def body(
    air_state,
    air_wind,
    jacobian,
    land_area,
    xgrid_rows,
    tracers,
    edge_coef,
    neighbours,
    vert_rate,
    ocean_area,
    send_list,
    xgrid_cols,
    xgrid_weights,
):
    field_count, levels, x_points, y_points = air_state.shape
    planes = field_count * levels
    ocean_levels, cells = tracers.shape[1:]
    ocean_planes = tracers.shape[0] * ocean_levels
    faces, blocks = lax.axis_size("face"), lax.axis_size("blk")
    air = air_state.reshape(planes * x_points, y_points)
    wind = air_wind.reshape(2 * levels * x_points, y_points)
    ocean = tracers.reshape(ocean_planes, cells)
    point_ids, cell_ids, weights = xgrid_rows[0], xgrid_cols[0], xgrid_weights[0]
    rate = vert_rate.reshape(cells // LANES, LANES)
    area = ocean_area.reshape(cells // LANES, LANES)
    first_inputs = (
        cell_ids,
        weights,
        ocean,
        point_ids,
        jacobian,
        land_area,
        wind,
        air,
        send_list,
    )
    kept = (cell_ids, weights, point_ids, send_list)
    slab, moved, to_before, to_after, cell_ids, weights, point_ids, send_list = call(
        functools.partial(start_kernel, planes),
        [(blocks, HEAD, LANES), air.shape]
        + [(SIDE_IDS + blocks, LANES)] * 2
        + [jax.ShapeDtypeStruct(array.shape, array.dtype) for array in kept],
        [HBM_SPEC] * len(first_inputs),
        [
            pltpu.VMEM(shape, jnp.float32)
            for shape in (
                (blocks, HEAD, LANES),
                (ROWS, cells),
                jacobian.shape,
                land_area.shape,
                wind.shape,
                air.shape,
            )
        ]
        + [pltpu.SemaphoreType.DMA((len(first_inputs) + 1,))],
        hbm_out=True,
    )(*(pltpu.with_memory_space_constraint(array, pltpu.HBM) for array in first_inputs))
    recv = lax.all_to_all(slab, "blk", split_axis=0, concat_axis=0, tiled=True)

    chunks = cells // LANES
    reads_per_chunk = edge_coef.shape[0] * chunks * (ocean_planes // ROWS)
    starts = (0, chunks * 3 // 16, chunks * 11 // 16)

    def ocean_part(start, end, after):
        (result,) = call(
            functools.partial(ocean_kernel, ocean_levels, start),
            [(ocean_planes, (end - start) * LANES)],
            [VMEM_SPEC] * 4 + [ANY_SPEC],
            [pltpu.VMEM((chunks * ocean_planes, 2 * LANES), jnp.bfloat16)],
            cost=(end - start) * reads_per_chunk * ROWS * LANES * 2,
        )(ocean, edge_coef, neighbours, rate, after)
        return result

    to_before, to_after = call(
        send_kernel,
        [(SIDE_IDS + blocks + ocean_planes, LANES)] * 2,
        [VMEM_SPEC] * 4,
        cost=reads_per_chunk * ROWS * LANES,
    )(ocean, send_list, to_before, to_after)
    onward = [(i, (i + 1) % blocks) for i in range(blocks)]
    before = lax.ppermute(to_after, "blk", onward)
    after = lax.ppermute(to_before, "blk", [(to, source) for source, to in onward])
    first_part = ocean_part(starts[0], starts[1], to_before)
    side_rows = planes + ROWS + 2 * SURF_ARRAYS + 4
    avg, down, up, surf = call(
        functools.partial(panel_kernel, planes),
        [air.shape, (side_rows, LANES), (side_rows, LANES), (4 * ROWS * SURF_ARRAYS, LANES)],
        [VMEM_SPEC] * 9 + [ANY_SPEC],
    )(
        moved,
        recv,
        before,
        after,
        air,
        wind,
        jacobian,
        land_area,
        point_ids,
        first_part,
    )
    after_me = [(i, (i + 1) % faces) for i in range(faces)]
    low = lax.ppermute(up, "face", after_me)
    high = lax.ppermute(down, "face", [(to, source) for source, to in after_me])
    second_part = ocean_part(starts[1], starts[2], surf)

    slab, sums, final, inverse = call(
        functools.partial(second_kernel, planes),
        [
            (blocks, EDGE_AT + ROWS, LANES),
            air.shape,
            (x_points, y_points),
            (x_points, y_points),
        ],
        [VMEM_SPEC] * 6 + [ANY_SPEC],
        [
            pltpu.VMEM((blocks, HEAD, LANES), jnp.float32),
            pltpu.VMEM((2, ROWS, LANES), jnp.float32),
            pltpu.VMEM((2 * planes, LANES), jnp.float32),
            pltpu.SemaphoreType.DMA((3,)),
        ],
        hbm_out=True,
    )(avg, surf, low, high, wind, point_ids, second_part)
    arrived = lax.all_to_all(slab, "blk", split_axis=0, concat_axis=0, tiled=True)
    down, up = call(rows_kernel, [(planes, LANES)] * 2, [VMEM_SPEC])(sums)
    low = lax.ppermute(up, "face", after_me)
    high = lax.ppermute(down, "face", [(to, source) for source, to in after_me])
    third_part = ocean_part(starts[2], chunks, down)
    partial, gain = call(
        functools.partial(rim_kernel, starts),
        [ocean.shape, area.shape],
        [VMEM_SPEC] * (5 + len(starts)),
        cost=chunks * reads_per_chunk // 8 * ROWS * LANES * 4,
    )(before, after, edge_coef, neighbours, area, first_part, second_part, third_part)
    air_final, ocean_final = call(
        functools.partial(end_kernel, planes),
        [air.shape, ocean.shape],
        [VMEM_SPEC] * 10,
    )(sums, low, high, arrived, final, inverse, cell_ids, weights, gain, partial)
    return air_final.reshape(air_state.shape), ocean_final.reshape(tracers.shape)


def solution(mesh):
    return jax.shard_map(
        body,
        mesh=mesh,
        in_specs=(
            P(None, None, "face", "blk"),
            P(None, None, "face", "blk"),
            P("face", "blk"),
            P("face", "blk"),
            P(("face", "blk"), None, None),
            P(None, None, ("face", "blk")),
            P(None, ("face", "blk")),
            P(None, ("face", "blk")),
            P(("face", "blk")),
            P(("face", "blk")),
            P(("face", "blk"), None),
            P(("face", "blk"), None, None),
            P(("face", "blk"), None, None),
        ),
        out_specs=(P(None, None, "face", "blk"), P(None, None, ("face", "blk"))),
        check_vma=False,
    )
```

```python
import functools

import jax
import jax.numpy as jnp
from jax import lax
from jax.experimental import pallas as pl
from jax.experimental.pallas import tpu as pltpu
from jax.sharding import PartitionSpec as P

GLL = 4
ROWS = 8
LANES = 128

deriv_table = [
    [-3.0, 4.045084971874737, -1.545084971874737, 0.5],
    [-0.8090169943749475, 0.0, 1.118033988749895, -0.30901699437494745],
    [0.30901699437494745, -1.118033988749895, 0.0, 0.8090169943749475],
    [-0.5, 1.545084971874737, -4.045084971874737, 3.0],
]
time_step = 0.05
relax_rate = 0.3
flux_gain = 0.2

HEAD, EDGE_AT = 8, 8
SIDE_EDGE, SIDE_STRIP, SIDE_IDS = 0, 8, 16
AVG, MASS_SUM, MASS, COEF_X, COEF_Y, SURF = range(6)
SURF_ARRAYS = 6


def iota(shape, dim):
    return lax.broadcasted_iota(jnp.int32, shape, dim)


def take(values, index, axis):
    return jnp.take_along_axis(values, index, axis=axis, mode="promise_in_bounds")


def by_position(pos, values):
    result = jnp.full(pos.shape, values[-1], jnp.float32)
    for i, value in enumerate(values[:-1]):
        result = jnp.where(pos == i, value, result)
    return result


def spread(row):
    return jnp.broadcast_to(row, (ROWS, LANES))


class Geometry:
    def __init__(self):
        shape = (ROWS, LANES)
        self.row, self.lane = iota(shape, 0), iota(shape, 1)
        x_pos, y_pos = self.row & (GLL - 1), self.lane & (GLL - 1)
        self.y_from = [self.lane - y_pos + j for j in range(GLL)]
        columns = [[line[j] for line in deriv_table] for j in range(GLL)]
        self.x_coef = {
            step: by_position(
                x_pos,
                [
                    deriv_table[i][i + step] if 0 <= i + step < GLL else 0.0
                    for i in range(GLL)
                ],
            )
            for step in range(1 - GLL, GLL)
        }
        self.y_coef = [by_position(y_pos, column) for column in columns]
        self.y_swap = (
            self.lane + jnp.where(y_pos == GLL - 1, 1, 0) - jnp.where(y_pos == 0, 1, 0)
        ) & (LANES - 1)
        self.x_edge = (x_pos == 0) | (x_pos == GLL - 1)
        self.y_edge = (y_pos == 0) | (y_pos == GLL - 1)
        self.first_row, self.last_row = self.row == 0, self.row == ROWS - 1
        self.middle_row = self.row == GLL
        self.outer_lane = (self.lane == 0) | (self.lane == LANES - 1)
        self.weight = jnp.where(self.x_edge, 1.0 / 6.0, 5.0 / 6.0) * jnp.where(
            self.y_edge, 1.0 / 6.0, 5.0 / 6.0
        )

    def d_x(self, tile):
        return sum(
            coef * (pltpu.roll(tile, -step % ROWS, 0) if step else tile)
            for step, coef in self.x_coef.items()
        )

    def d_y(self, *tiles):
        totals = [0.0] * len(tiles)
        for j in range(GLL):
            for i, tile in enumerate(tiles):
                totals[i] += self.y_coef[j] * take(tile, self.y_from[j], 1)
        return totals

    def sum_x(self, low, high, before, after):
        low_down, low_up = pltpu.roll(low, 1, 0), pltpu.roll(low, ROWS - 1, 0)
        high_down, high_up = pltpu.roll(high, 1, 0), pltpu.roll(high, ROWS - 1, 0)
        low_other = jnp.where(
            self.first_row,
            before,
            jnp.where(
                self.middle_row, low_down, jnp.where(self.last_row, high_up, low_up)
            ),
        )
        high_other = jnp.where(
            self.first_row,
            low_down,
            jnp.where(
                self.middle_row, high_down, jnp.where(self.last_row, after, high_up)
            ),
        )
        return (
            low + jnp.where(self.x_edge, low_other, 0.0),
            high + jnp.where(self.x_edge, high_other, 0.0),
        )

    def sum_y(self, tile, outer):
        other = jnp.where(self.outer_lane, outer, take(tile, self.y_swap, 1))
        return tile + jnp.where(self.y_edge, other, 0.0)

    def sum_y_pair(self, own, strip):
        own_swap, strip_swap = take(own, self.y_swap, 1), take(strip, self.y_swap, 1)
        own_other = jnp.where(self.outer_lane, strip_swap, own_swap)
        strip_other = jnp.where(self.outer_lane, own_swap, strip_swap)
        return (
            own + jnp.where(self.y_edge, own_other, 0.0),
            strip + jnp.where(self.y_edge, strip_other, 0.0),
        )


def edge_place(x, group):
    return x // ROWS, LANES // 2 * (x % 2) + ROWS * group + 2 * (x % ROWS // 2)


def all_edges(geo, ref, planes, x_points, ends_ref=None):
    packs = [jnp.zeros((ROWS, LANES), jnp.float32) for _ in range(2)]
    for x in range(x_points):
        rows, first = ref, planes * x
        if ends_ref is not None and x in (0, x_points - 1):
            rows, first = ends_ref, planes * (x // (x_points - 1))
        for group in range(planes // ROWS):
            q, at = edge_place(x, group)
            tile = rows[first + ROWS * group : first + ROWS * (group + 1), :]
            rolled = pltpu.roll(tile, (at + 1) % LANES, 1)
            packs[q] = jnp.where((geo.lane >> 1) == at // 2, rolled, packs[q])
    return packs


def outer_edges(joined, x, group):
    q, at = edge_place(x, group)
    return pltpu.roll(joined[q], (-(at + 1)) % LANES, 1)


def split_sides(geo, first, second, unit):
    odd = (geo.lane & unit) != 0
    return (
        jnp.where(odd, pltpu.roll(second, unit, 1), first),
        jnp.where(odd, second, pltpu.roll(first, LANES - unit, 1)),
    )


def join_sides(geo, before, after, unit):
    odd = (geo.lane & unit) != 0
    return (
        jnp.where(odd, pltpu.roll(after, unit, 1), before),
        jnp.where(odd, after, pltpu.roll(before, LANES - unit, 1)),
    )


def join_edges(geo, before, after):
    odd = (geo.lane & 1) != 0
    return (
        jnp.where(odd, pltpu.roll(before, 1, 1), after),
        jnp.where(odd, before, pltpu.roll(after, LANES - 1, 1)),
    )


def neighbours_of(blocks):
    here = lax.axis_index("blk")
    return lax.rem(here + blocks - 1, blocks), lax.rem(here + 1, blocks)


def scatter_sum(lines, index, bins, allowed=None):
    count = index.shape[0]
    split = []
    for values in lines:
        for part in range(3):
            short = values.astype(jnp.bfloat16).astype(jnp.float32)
            split.append(short)
            values = values - short
    high, low = index >> 7, index & (LANES - 1)
    bin_at = iota((bins, LANES), 0)
    lane_at = iota((LANES, LANES), 0)
    if allowed is not None:
        lane_at = jnp.where(allowed(lane_at), lane_at, -1)
    left, right = [], []
    for c in range(count):
        hit = bin_at == high[c : c + 1]
        left.append(
            jnp.concatenate(
                [jnp.where(hit, part[c : c + 1], 0.0) for part in split], axis=0
            ).astype(jnp.bfloat16)
        )
        right.append(
            jnp.where(lane_at == low[c : c + 1], 1.0, 0.0).astype(jnp.bfloat16)
        )
    total = lax.dot_general(
        jnp.concatenate(left, axis=1),
        jnp.concatenate(right, axis=1),
        (((1,), (1,)), ((), ())),
        preferred_element_type=jnp.float32,
    )
    sums = []
    for i in range(len(lines)):
        part = total[3 * i * bins : 3 * (i + 1) * bins]
        sums.append(part[:bins] + part[bins : 2 * bins] + part[2 * bins :])
    return sums


def wind_tiles(wind_ref, x_points, level, lines):
    levels = wind_ref.shape[0] // (2 * x_points)
    return [
        [
            time_step
            * wind_ref[
                pl.ds((levels * part + level) * x_points + x, ROWS, stride=x_points), :
            ]
            for x in lines
        ]
        for part in range(2)
    ]


def start_kernel(
    planes,
    cols_in,
    weights_in,
    tracers_in,
    rows_in,
    jac_in,
    land_in,
    wind_in,
    air_in,
    send_in,
    slab_out,
    moved_ref,
    before_ref,
    after_ref,
    cols_ref,
    weights_ref,
    rows_ref,
    send_ref,
    slab_ref,
    tracers_ref,
    jac_ref,
    land_ref,
    wind_ref,
    air_ref,
    semaphores,
):
    x_points = jac_ref.shape[0]
    field_rows = wind_ref.shape[0] // 2
    field_count = air_ref.shape[0] // field_rows
    fields_at = [
        slice(field_rows * field, field_rows * (field + 1)) for field in range(field_count)
    ]
    copies = [
        pltpu.make_async_copy(source, target, semaphores.at[i])
        for i, (source, target) in enumerate(
            [
                (cols_in, cols_ref),
                (tracers_in.at[:ROWS], tracers_ref),
                (weights_in, weights_ref),
                (rows_in, rows_ref),
                (jac_in, jac_ref),
                (wind_in, wind_ref),
                (land_in, land_ref),
            ]
            + [(air_in.at[at], air_ref.at[at]) for at in fields_at]
            + [(send_in, send_ref)]
        )
    ]
    for copy in copies:
        copy.start()
    geo = Geometry()
    blocks = cols_ref.shape[0]
    levels = wind_ref.shape[0] // (2 * x_points)
    chunks = tracers_ref.shape[1] // LANES
    for copy in copies[:4]:
        copy.wait()

    for group in range(blocks // ROWS):
        at = slice(ROWS * group, ROWS * (group + 1))
        cells = cols_ref[at, :]
        high, low = cells >> 7, cells & (LANES - 1)
        surface = jnp.zeros((ROWS, LANES), jnp.float32)
        for k in range(chunks):
            line = spread(tracers_ref[0:1, LANES * k : LANES * (k + 1)])
            surface = jnp.where(high == k, take(line, low, 1), surface)
        area = weights_ref[at, :]
        heat = area * surface
        for c in range(ROWS):
            owner = ROWS * group + c
            for place, step in enumerate((1, 0, -1)):
                to = (owner + step) % blocks
                slab_ref[to, 2 * place : 2 * place + 1, :] = heat[c : c + 1]
                slab_ref[to, 2 * place + 1 : 2 * place + 2, :] = area[c : c + 1]

    out = pltpu.make_async_copy(slab_ref, slab_out, semaphores.at[len(copies)])
    out.start()
    ids = rows_ref[...].astype(jnp.float32)
    for side_ref in (before_ref, after_ref):
        side_ref[SIDE_IDS : SIDE_IDS + blocks, :] = ids

    for copy in copies[4:8]:
        copy.wait()
    strips = []
    for h in range(2):
        half = slice(ROWS * h, ROWS * (h + 1))
        second = levels * x_points
        pack = jnp.zeros((ROWS, LANES), jnp.float32)
        for i, strip in enumerate(
            (
                air_ref[half, :],
                wind_ref[half, :],
                wind_ref[second + ROWS * h : second + ROWS * (h + 1), :],
                jac_ref[half, :],
                land_ref[half, :],
            )
        ):
            pack = jnp.where(
                (geo.lane >> 4) == i, pltpu.roll(strip, 16 * i + 8, 1), pack
            )
        strips.append(pack)
    to_right, to_left = split_sides(geo, strips[0], strips[1], ROWS)
    after_ref[SIDE_STRIP : SIDE_STRIP + ROWS, :] = to_right
    before_ref[SIDE_STRIP : SIDE_STRIP + ROWS, :] = to_left

    y_weight = jnp.where(geo.y_edge, 1.0 / 6.0, 5.0 / 6.0)
    for field in range(field_count):
        if field:
            copies[7 + field].wait()
        for element in range(x_points // GLL):
            lines = [GLL * element + i for i in range(GLL)]
            mass = [
                (1.0 / 6.0 if i in (0, GLL - 1) else 5.0 / 6.0)
                * y_weight
                * spread(jac_ref[x : x + 1, :])
                for i, x in enumerate(lines)
            ]
            for level in range(0, levels, ROWS):
                plane = levels * field + level
                wind = wind_tiles(wind_ref, x_points, level, lines)
                values = [
                    air_ref[pl.ds(plane * x_points + x, ROWS, stride=x_points), :]
                    for x in lines
                ]
                slopes = geo.d_y(*values)
                for i, x in enumerate(lines):
                    slope = sum(deriv_table[i][j] * values[j] for j in range(GLL))
                    moved_ref[planes * x + plane : planes * x + plane + ROWS, :] = mass[
                        i
                    ] * (values[i] - (wind[0][i] * slope + wind[1][i] * slopes[i]))
    copies[-1].wait()
    packs = all_edges(geo, moved_ref, planes, x_points)
    to_right, to_left = split_sides(geo, packs[0], packs[1], 1)
    after_ref[SIDE_EDGE : SIDE_EDGE + ROWS, :] = to_right
    before_ref[SIDE_EDGE : SIDE_EDGE + ROWS, :] = to_left
    out.wait()


def panel_kernel(
    planes,
    moved_ref,
    recv_ref,
    before_ref,
    after_ref,
    air_ref,
    wind_ref,
    jac_ref,
    land_ref,
    rows_ref,
    ocean_ref,
    avg_ref,
    down_ref,
    up_ref,
    surf_ref,
):
    geo = Geometry()
    blocks = rows_ref.shape[0]
    x_points = jac_ref.shape[0]
    levels = wind_ref.shape[0] // (2 * x_points)

    own_ids = rows_ref[...]
    left_ids = before_ref[SIDE_IDS : SIDE_IDS + blocks, :].astype(jnp.int32)
    right_ids = after_ref[SIDE_IDS : SIDE_IDS + blocks, :].astype(jnp.int32)
    head = [
        jnp.concatenate([recv_ref[c, i : i + 1, :] for c in range(blocks)], axis=0)
        for i in range(6)
    ]
    heat, frac = scatter_sum(head[2:4], own_ids, 2 * ROWS)
    from_left = scatter_sum(
        head[0:2], left_ids, 2 * ROWS, lambda lane: lane >= LANES - ROWS
    )
    from_right = scatter_sum(head[4:6], right_ids, 2 * ROWS, lambda lane: lane < ROWS)
    strip_heat = from_left[0] + from_right[0]
    strip_frac = from_left[1] + from_right[1]

    in_strip = (geo.lane < ROWS) | (geo.lane >= LANES - ROWS)
    packs = join_sides(
        geo,
        before_ref[SIDE_STRIP : SIDE_STRIP + ROWS, :],
        after_ref[SIDE_STRIP : SIDE_STRIP + ROWS, :],
        ROWS,
    )
    own, strip = [], []
    for h, pack in enumerate(packs):
        half = slice(ROWS * h, ROWS * (h + 1))
        strip.append(
            [
                jnp.where(
                    in_strip, pltpu.roll(pack, (-(16 * i + 8)) % LANES, 1), 1.0
                )
                for i in range(5)
            ]
        )
        own.append(
            [
                air_ref[half, :],
                wind_ref[half, :],
                wind_ref[
                    levels * x_points + ROWS * h : levels * x_points + ROWS * (h + 1), :
                ],
                jac_ref[half, :],
                land_ref[half, :],
            ]
        )
    for h in range(2):
        half = slice(ROWS * h, ROWS * (h + 1))
        pair = []
        for tile, ((field, wind_x, wind_y, jac, land), tile_heat, tile_frac) in enumerate(
            ((own[h], heat[half], frac[half]), (strip[h], strip_heat[half], strip_frac[half]))
        ):
            mass = geo.weight * jac
            if tile == 1:
                tile_heat = jnp.where(in_strip, tile_heat, 0.0)
                tile_frac = jnp.where(in_strip, tile_frac, 0.0)
            surf = (tile_heat + land * field) / (tile_frac + land)
            coef_x, coef_y = time_step * mass * wind_x, time_step * mass * wind_y
            moved = (
                mass * (field + relax_rate * (surf - field))
                - coef_x * geo.d_x(field)
                - coef_y * geo.d_y(field)[0]
            )
            pair.append((moved, mass))
            at = 2 * ROWS * tile + ROWS * h
            for number, value in (
                (MASS, mass),
                (COEF_X, coef_x),
                (COEF_Y, coef_y),
                (SURF, surf),
            ):
                surf_ref[4 * ROWS * number + at : 4 * ROWS * number + at + ROWS, :] = value
        for number, i in ((AVG, 0), (MASS_SUM, 1)):
            for tile, value in enumerate(geo.sum_y_pair(pair[0][i], pair[1][i])):
                at = 4 * ROWS * number + 2 * ROWS * tile + ROWS * h
                surf_ref[at : at + ROWS, :] = value

    joined = join_edges(
        geo,
        before_ref[SIDE_EDGE : SIDE_EDGE + ROWS, :],
        after_ref[SIDE_EDGE : SIDE_EDGE + ROWS, :],
    )
    for x in range(x_points):
        for group in range(planes // ROWS):
            at = slice(planes * x + ROWS * group, planes * x + ROWS * (group + 1))
            avg_ref[at, :] = geo.sum_y(moved_ref[at, :], outer_edges(joined, x, group))

    def line(r):
        return avg_ref[planes * r : planes * (r + 1), :]

    def surf_line(number, r):
        return surf_ref[pl.ds(4 * ROWS * number + r, 2, stride=x_points), :]

    def first_step(get, mass_at):
        return (
            [
                get(1) / mass_at(1),
                get(2) / mass_at(2),
                (get(3) + get(4)) / (mass_at(3) + mass_at(4)),
            ],
            [
                (get(11) + get(12)) / (mass_at(11) + mass_at(12)),
                get(13) / mass_at(13),
                get(14) / mass_at(14),
            ],
        )

    def own_mass_sum(r):
        return surf_ref[4 * ROWS * MASS_SUM + r : 4 * ROWS * MASS_SUM + r + 1, :]

    low_lines, high_lines = first_step(line, own_mass_sum)
    surf_low, surf_high = first_step(
        functools.partial(surf_line, AVG), functools.partial(surf_line, MASS_SUM)
    )
    for out_ref, r, lines, surf_lines, coefs in (
        (down_ref, 0, low_lines, surf_low, deriv_table[0][1:]),
        (up_ref, 15, high_lines, surf_high, deriv_table[3][:3]),
    ):
        slope = sum(coef * value for coef, value in zip(coefs, lines))
        surf_slope = sum(coef * value for coef, value in zip(coefs, surf_lines))
        mass = surf_ref[4 * ROWS * MASS + r : 4 * ROWS * MASS + r + 1, :]
        wind = time_step * mass * wind_ref[pl.ds(r, 2 * levels, stride=x_points), :]
        out_ref[0:planes, :] = line(r)
        columns = [
            wind[plane % levels : plane % levels + ROWS] * slope[plane : plane + ROWS]
            for plane in range(0, planes, ROWS)
        ] + [wind[level : level + ROWS] for level in range(0, 2 * levels, ROWS)]
        pack = jnp.zeros((ROWS, LANES), jnp.float32)
        for i, tile in enumerate(columns):
            pack = jnp.where((geo.lane >> 1) == i, pltpu.roll(tile, 2 * i + 1, 1), pack)
        out_ref[planes : planes + ROWS, :] = pack
        base = planes + ROWS
        for number in range(SURF_ARRAYS):
            out_ref[base + 2 * number : base + 2 * number + 2, :] = surf_line(number, r)
        base += 2 * SURF_ARRAYS
        out_ref[base : base + 2, :] = surf_line(COEF_X, r) * surf_slope


def second_kernel(
    planes,
    avg_ref,
    surf_ref,
    low_ref,
    high_ref,
    wind_ref,
    rows_ref,
    ocean_ref,
    slab_out,
    sums_ref,
    final_ref,
    inverse_ref,
    flux_ref,
    edges_ref,
    ends_ref,
    semaphores,
):
    geo = Geometry()
    blocks = rows_ref.shape[0]
    left, right = neighbours_of(blocks)
    x_points = final_ref.shape[0]
    levels = wind_ref.shape[0] // (2 * x_points)
    base = planes + ROWS

    def surf_tile(number, tile, h):
        at = 4 * ROWS * number + 2 * ROWS * tile + ROWS * h
        return surf_ref[at : at + ROWS, :]

    def beside(ref, number, tile):
        at = base + 2 * number + tile
        return spread(ref[at : at + 1, :])

    ends = []
    inverse = []
    for tile in range(2):
        total = geo.sum_x(
            surf_tile(MASS_SUM, tile, 0),
            surf_tile(MASS_SUM, tile, 1),
            beside(low_ref, MASS_SUM, tile),
            beside(high_ref, MASS_SUM, tile),
        )
        inverse.append([1.0 / value for value in total])
        summed = geo.sum_x(
            surf_tile(AVG, tile, 0),
            surf_tile(AVG, tile, 1),
            beside(low_ref, AVG, tile),
            beside(high_ref, AVG, tile),
        )
        fields = [value * scale for value, scale in zip(summed, inverse[tile])]
        moved = []
        for h in range(2):
            field = fields[h]
            moved.append(
                surf_tile(MASS, tile, h)
                * (field + relax_rate * (surf_tile(SURF, tile, h) - field))
                - surf_tile(COEF_X, tile, h) * geo.d_x(field)
                - surf_tile(COEF_Y, tile, h) * geo.d_y(field)[0]
            )
        halos = []
        for ref, field, own_coef in (
            (low_ref, spread(fields[0][:1]), deriv_table[3][3]),
            (high_ref, spread(fields[1][ROWS - 1 :]), deriv_table[0][0]),
        ):
            halos.append(
                beside(ref, MASS, tile)
                * (field + relax_rate * (beside(ref, SURF, tile) - field))
                - beside(ref, SURF_ARRAYS, tile)
                - beside(ref, COEF_X, tile) * (own_coef * field)
                - beside(ref, COEF_Y, tile) * geo.d_y(field)[0]
            )
        ends.append(geo.sum_x(moved[0], moved[1], halos[0], halos[1]))
    final = []
    for h in range(2):
        summed, _ = geo.sum_y_pair(ends[0][h], ends[1][h])
        final.append(summed * inverse[0][h])
        final_ref[ROWS * h : ROWS * (h + 1), :] = final[h]
        inverse_ref[ROWS * h : ROWS * (h + 1), :] = inverse[0][h]
    flux = [final[h] - surf_tile(SURF, 0, h) for h in range(2)]
    for group in range(blocks // ROWS):
        ids = rows_ref[ROWS * group : ROWS * (group + 1), :]
        high, low = ids >> 7, ids & (LANES - 1)
        picked = jnp.zeros((ROWS, LANES), jnp.float32)
        for x in range(2 * ROWS):
            line = spread(flux[x // ROWS][x % ROWS : x % ROWS + 1])
            picked = jnp.where(high == x, take(line, low, 1), picked)
        for c in range(ROWS):
            flux_ref[ROWS * group + c, 0:1, :] = picked[c : c + 1]

    copies = [
        pltpu.make_async_copy(flux_ref, slab_out.at[:, :HEAD], semaphores.at[0])
    ]
    copies[0].start()

    def put(x, plane, value):
        sums_ref[planes * x + plane : planes * x + plane + ROWS, :] = value

    def column(ref, number):
        return pltpu.roll(ref[planes : planes + ROWS, :], (-(2 * number + 1)) % LANES, 1)

    def beyond(ref, plane, field, slope, own_coef):
        wind_at = (planes + plane % levels) // ROWS
        return (
            beside(ref, MASS, 0) * field
            - column(ref, plane // ROWS)
            - column(ref, wind_at) * (own_coef * field)
            - column(ref, wind_at + levels // ROWS) * slope
        )

    def row_of(tiles, x):
        return spread(tiles[x // ROWS][x % ROWS : x % ROWS + 1])

    masses = [surf_tile(MASS, 0, h) for h in range(2)]
    held = {}
    for element in range(x_points // GLL):
        lines = [GLL * element + i for i in range(GLL)]
        first, last = lines[0], lines[-1]
        scale = [row_of(inverse[0], x) for x in lines]
        mass = [row_of(masses, x) for x in lines]
        for level in range(0, levels, ROWS):
            wind = wind_tiles(wind_ref, x_points, level, lines)
            for plane in range(level, planes, levels):
                here = slice(plane, plane + ROWS)
                fields = []
                for i, x in enumerate(lines):
                    total = avg_ref[planes * x + plane : planes * x + plane + ROWS, :]
                    other = x - 1 if i == 0 else x + 1
                    if other < 0:
                        total = total + low_ref[here, :]
                    elif other == x_points:
                        total = total + high_ref[here, :]
                    elif i in (0, GLL - 1):
                        at = planes * other + plane
                        total = total + avg_ref[at : at + ROWS, :]
                    fields.append(total * scale[i])
                slopes = geo.d_y(*fields)
                moved = []
                for i, x in enumerate(lines):
                    slope = sum(deriv_table[i][j] * fields[j] for j in range(GLL))
                    moved.append(
                        mass[i] * (fields[i] - (wind[0][i] * slope + wind[1][i] * slopes[i]))
                    )
                if first == 0:
                    put(first, plane, moved[0])
                    ends_ref[plane : plane + ROWS, :] = moved[0] + beyond(
                        low_ref, plane, fields[0], slopes[0], deriv_table[3][3]
                    )
                else:
                    shared = held[plane] + moved[0]
                    put(first - 1, plane, shared)
                    put(first, plane, shared)
                for i in range(1, GLL - 1):
                    put(lines[i], plane, moved[i])
                held[plane] = moved[-1]
                if last == x_points - 1:
                    put(last, plane, moved[-1])
                    at = planes + plane
                    ends_ref[at : at + ROWS, :] = moved[-1] + beyond(
                        high_ref, plane, fields[-1], slopes[-1], deriv_table[0][0]
                    )
    packs = all_edges(geo, sums_ref, planes, x_points, ends_ref)
    to_right, to_left = split_sides(geo, packs[0], packs[1], 1)
    for i, (to, edges) in enumerate(((right, to_right), (left, to_left))):
        edges_ref[i] = edges
        copies.append(
            pltpu.make_async_copy(
                edges_ref.at[i],
                slab_out.at[to, EDGE_AT : EDGE_AT + ROWS],
                semaphores.at[1 + i],
            )
        )
        copies[-1].start()
    for copy in copies:
        copy.wait()


def rows_kernel(sums_ref, ocean_ref, down_ref, up_ref):
    planes = down_ref.shape[0]
    down_ref[...] = sums_ref[:planes, :]
    up_ref[...] = sums_ref[sums_ref.shape[0] - planes :, :]


def end_kernel(
    planes,
    sums_ref,
    low_ref,
    high_ref,
    recv_ref,
    final_ref,
    inverse_ref,
    cols_ref,
    weights_ref,
    gain_ref,
    ocean_ref,
    air_out,
    ocean_out,
    air_ref,
    first_ref,
    semaphores,
):
    geo = Geometry()
    blocks = cols_ref.shape[0]
    left, right = neighbours_of(blocks)
    chunks = gain_ref.shape[0]
    x_points = inverse_ref.shape[0]
    copies = []

    def send(source, target):
        copies.append(
            pltpu.make_async_copy(source, target, semaphores.at[len(copies)])
        )
        copies[-1].start()

    send(ocean_ref.at[ROWS:], ocean_out.at[ROWS:])
    arrived = jnp.concatenate([recv_ref[c, 0:1, :] for c in range(blocks)], axis=0)
    (inflow,) = scatter_sum([weights_ref[...] * arrived], cols_ref[...], chunks)
    gain = inflow * gain_ref[...]
    first_ref[...] = ocean_ref[:ROWS, :]
    for k in range(chunks):
        at = slice(LANES * k, LANES * (k + 1))
        first_ref[0:1, at] = ocean_ref[0:1, at] + gain[k : k + 1]
    send(first_ref, ocean_out.at[:ROWS])

    joined = join_edges(
        geo,
        recv_ref[left, EDGE_AT : EDGE_AT + ROWS, :],
        recv_ref[right, EDGE_AT : EDGE_AT + ROWS, :],
    )
    for group in range(planes // ROWS):
        half = slice(ROWS * group, ROWS * (group + 1))
        for x in range(x_points):
            at = planes * x + ROWS * group
            total = sums_ref[at : at + ROWS, :]
            if x == 0:
                total = total + low_ref[half, :]
            elif x == x_points - 1:
                total = total + high_ref[half, :]
            air_ref[pl.ds(ROWS * group * x_points + x, ROWS, stride=x_points), :] = spread(
                inverse_ref[x : x + 1, :]
            ) * geo.sum_y(total, outer_edges(joined, x, group))
        if group == 0:
            air_ref[0:x_points, :] = final_ref[...]
        rows = slice(ROWS * group * x_points, ROWS * (group + 1) * x_points)
        send(air_ref.at[rows], air_out.at[rows])
    for copy in copies:
        copy.wait()


def gathered(ids, coefs, source, sources, groups, first=0):
    totals = [jnp.zeros((ROWS, LANES), jnp.float32) for _ in range(groups)]
    for edge in range(ids.shape[0]):
        cell = spread(ids[edge : edge + 1])
        coef = spread(coefs[edge : edge + 1])
        high, low = cell >> 7, cell & (LANES - 1)
        for s in range(sources):
            scaled = jnp.where(high == first + s, coef, 0.0)
            for group in range(groups):
                totals[group] += scaled * take(source(group, s), low, 1)
    return totals


def multiplied(ids, coefs, halves_ref, sources, groups):
    lane_at = iota((LANES, LANES), 0)
    hot = jnp.concatenate(
        [
            jnp.where(lane_at == (ids[edge : edge + 1] & (LANES - 1)), 1.0, 0.0).astype(
                jnp.bfloat16
            )
            for edge in range(2)
        ],
        axis=1,
    )
    picked = jnp.dot(
        halves_ref[...],
        jnp.concatenate([hot, hot], axis=0),
        preferred_element_type=jnp.float32,
    )
    totals = [jnp.zeros((ROWS, LANES), jnp.float32) for _ in range(groups)]
    for edge in range(2):
        high = spread(ids[edge : edge + 1]) >> 7
        coef = spread(coefs[edge : edge + 1])
        side = slice(LANES * edge, LANES * (edge + 1))
        for s in range(sources):
            scaled = jnp.where(high == s, coef, 0.0)
            for group in range(groups):
                at = ROWS * (groups * s + group)
                totals[group] += scaled * picked[at : at + ROWS, side]
    return totals


def ocean_kernel(
    levels, start, tracers_ref, coef_ref, near_ref, rate_ref, after_ref, out_ref, halves_ref
):
    chunks = tracers_ref.shape[1] // LANES
    groups = tracers_ref.shape[0] // ROWS
    row = iota((ROWS, LANES), 0)

    def source(group, s):
        return tracers_ref[
            ROWS * group : ROWS * (group + 1), LANES * s : LANES * (s + 1)
        ]

    planes = tracers_ref.shape[0]
    for s in range(chunks):
        values = tracers_ref[:, LANES * s : LANES * (s + 1)]
        upper = values.astype(jnp.bfloat16)
        at = slice(planes * s, planes * (s + 1))
        halves_ref[at, :LANES] = upper
        halves_ref[at, LANES:] = (values - upper.astype(jnp.float32)).astype(jnp.bfloat16)
    edges = near_ref.shape[0]

    def one_chunk(number, carry):
        k = number + start
        at = pl.ds(pl.multiple_of(k * LANES, LANES), LANES)
        out_at = pl.ds(pl.multiple_of(number * LANES, LANES), LANES)
        ids, coefs = near_ref[:, at], coef_ref[:, at]
        by_gather = edges - edges // 3 * 2
        totals = gathered(ids[:by_gather], coefs[:by_gather], source, chunks, groups)
        for edge in range(by_gather, edges, 2):
            more = multiplied(
                ids[edge : edge + 2], coefs[edge : edge + 2], halves_ref, chunks, groups
            )
            totals = [total + part for total, part in zip(totals, more)]
        coef_sum = spread(jnp.sum(coefs, axis=0, keepdims=True))
        rate = spread(rate_ref[pl.ds(k, 1), :])
        tiles = [tracers_ref[ROWS * g : ROWS * (g + 1), at] for g in range(groups)]
        for g in range(groups):
            tile = tiles[g]
            top = bottom = tile
            if (ROWS * g) % levels:
                top = pltpu.roll(tiles[g - 1], 1, 0)
            if (ROWS * (g + 1)) % levels:
                bottom = pltpu.roll(tiles[g + 1], ROWS - 1, 0)
            above = jnp.where(row == 0, top, pltpu.roll(tile, 1, 0))
            below = jnp.where(row == ROWS - 1, bottom, pltpu.roll(tile, ROWS - 1, 0))
            vertical = rate * ((above - tile) + (below - tile))
            out_ref[ROWS * g : ROWS * (g + 1), out_at] = (
                tile + (totals[g] - coef_sum * tile) + vertical
            )
        return carry

    count = out_ref.shape[1] // LANES
    step = 2 if count % 2 == 0 else 1

    def some_chunks(number, carry):
        for i in range(step):
            one_chunk(step * number + i, carry)
        return carry

    lax.fori_loop(0, count // step, some_chunks, 0)


def send_kernel(tracers_ref, send_ref, before_ref, after_ref, *out_refs):
    chunks = tracers_ref.shape[1] // LANES
    for part, (side_ref, out_ref) in enumerate(zip((before_ref, after_ref), out_refs)):
        base = side_ref.shape[0]
        out_ref[:base, :] = side_ref[...]
        cells = spread(send_ref[0:1, LANES * part : LANES * (part + 1)])
        high, low = cells >> 7, cells & (LANES - 1)
        for group in range(tracers_ref.shape[0] // ROWS):
            half = slice(ROWS * group, ROWS * (group + 1))
            rim = jnp.zeros((ROWS, LANES), jnp.float32)
            for k in range(chunks):
                tile = tracers_ref[half, LANES * k : LANES * (k + 1)]
                rim = jnp.where(high == k, take(tile, low, 1), rim)
            out_ref[base + ROWS * group : base + ROWS * (group + 1), :] = rim


def rim_kernel(
    starts,
    before_ref,
    after_ref,
    coef_ref,
    near_ref,
    area_ref,
    rows_ref,
    *refs,
):
    partial_refs, (out_ref, gain_ref) = refs[: len(starts)], refs[len(starts) :]
    chunks = coef_ref.shape[1] // LANES
    groups = out_ref.shape[0] // ROWS
    rim_at = before_ref.shape[0] - out_ref.shape[0]
    sides = before_ref, after_ref
    gain_ref[...] = flux_gain / area_ref[...]

    def source(group, s):
        at = rim_at + ROWS * group
        return sides[s][at : at + ROWS, :]

    for k in range(chunks):
        at = slice(LANES * k, LANES * (k + 1))
        totals = gathered(near_ref[:, at], coef_ref[:, at], source, 2, groups, chunks)
        part = max(i for i, start in enumerate(starts) if start <= k)
        place = slice(LANES * (k - starts[part]), LANES * (k - starts[part] + 1))
        for g in range(groups):
            half = slice(ROWS * g, ROWS * (g + 1))
            out_ref[half, at] = partial_refs[part][half, place] + totals[g]


VMEM_SPEC = pl.BlockSpec(memory_space=pltpu.VMEM)
ANY_SPEC = pl.BlockSpec(memory_space=pl.ANY)
HBM_SPEC = pl.BlockSpec(memory_space=pltpu.HBM)


def call(kernel, outs, specs, scratch=(), cost=0, hbm_outs=0):
    estimate = None
    if cost:
        estimate = pl.CostEstimate(flops=0, bytes_accessed=cost, transcendentals=0)
    outs = [
        out if isinstance(out, jax.ShapeDtypeStruct) else jax.ShapeDtypeStruct(out, jnp.float32)
        for out in outs
    ]
    out_specs = [VMEM_SPEC] * len(outs)
    out_specs[:hbm_outs] = [HBM_SPEC] * hbm_outs
    return pl.pallas_call(
        kernel,
        out_shape=outs,
        in_specs=specs,
        out_specs=out_specs,
        scratch_shapes=list(scratch),
        cost_estimate=estimate,
        compiler_params=pltpu.CompilerParams(vmem_limit_bytes=32 * 2**20),
        name=getattr(kernel, "func", kernel).__name__,
    )


def body(
    air_state,
    air_wind,
    jacobian,
    land_area,
    xgrid_rows,
    tracers,
    edge_coef,
    neighbours,
    vert_rate,
    ocean_area,
    send_list,
    xgrid_cols,
    xgrid_weights,
):
    field_count, levels, x_points, y_points = air_state.shape
    planes = field_count * levels
    ocean_levels, cells = tracers.shape[1:]
    ocean_planes = tracers.shape[0] * ocean_levels
    faces, blocks = lax.axis_size("face"), lax.axis_size("blk")
    air = air_state.reshape(planes * x_points, y_points)
    wind = air_wind.reshape(2 * levels * x_points, y_points)
    ocean = tracers.reshape(ocean_planes, cells)
    point_ids, cell_ids, weights = xgrid_rows[0], xgrid_cols[0], xgrid_weights[0]
    rate = vert_rate.reshape(cells // LANES, LANES)
    area = ocean_area.reshape(cells // LANES, LANES)
    first_inputs = (
        cell_ids,
        weights,
        ocean,
        point_ids,
        jacobian,
        land_area,
        wind,
        air,
        send_list,
    )
    kept = (cell_ids, weights, point_ids, send_list)
    slab, moved, to_before, to_after, cell_ids, weights, point_ids, send_list = call(
        functools.partial(start_kernel, planes),
        [(blocks, HEAD, LANES), air.shape]
        + [(SIDE_IDS + blocks, LANES)] * 2
        + [jax.ShapeDtypeStruct(array.shape, array.dtype) for array in kept],
        [HBM_SPEC] * len(first_inputs),
        [
            pltpu.VMEM(shape, jnp.float32)
            for shape in (
                (blocks, HEAD, LANES),
                (ROWS, cells),
                jacobian.shape,
                land_area.shape,
                wind.shape,
                air.shape,
            )
        ]
        + [pltpu.SemaphoreType.DMA((len(first_inputs) + field_count,))],
        hbm_outs=1,
    )(*(pltpu.with_memory_space_constraint(array, pltpu.HBM) for array in first_inputs))
    recv = lax.all_to_all(slab, "blk", split_axis=0, concat_axis=0, tiled=True)

    chunks = cells // LANES
    reads_per_chunk = edge_coef.shape[0] * chunks * (ocean_planes // ROWS)
    starts = (0, chunks // 4, chunks * 3 // 4)

    def ocean_part(start, end, after):
        (result,) = call(
            functools.partial(ocean_kernel, ocean_levels, start),
            [(ocean_planes, (end - start) * LANES)],
            [VMEM_SPEC] * 4 + [ANY_SPEC],
            [pltpu.VMEM((chunks * ocean_planes, 2 * LANES), jnp.bfloat16)],
            cost=(end - start) * reads_per_chunk * ROWS * LANES * 2,
        )(ocean, edge_coef, neighbours, rate, after)
        return result

    to_before, to_after = call(
        send_kernel,
        [(SIDE_IDS + blocks + ocean_planes, LANES)] * 2,
        [VMEM_SPEC] * 4,
        cost=reads_per_chunk * ROWS * LANES,
    )(ocean, send_list, to_before, to_after)
    onward = [(i, (i + 1) % blocks) for i in range(blocks)]
    before = lax.ppermute(to_after, "blk", onward)
    after = lax.ppermute(to_before, "blk", [(to, source) for source, to in onward])
    first_part = ocean_part(starts[0], starts[1], to_before)
    side_rows = planes + ROWS + 2 * SURF_ARRAYS + 4
    avg, down, up, surf = call(
        functools.partial(panel_kernel, planes),
        [air.shape, (side_rows, LANES), (side_rows, LANES), (4 * ROWS * SURF_ARRAYS, LANES)],
        [VMEM_SPEC] * 9 + [ANY_SPEC],
    )(
        moved,
        recv,
        before,
        after,
        air,
        wind,
        jacobian,
        land_area,
        point_ids,
        first_part,
    )
    after_me = [(i, (i + 1) % faces) for i in range(faces)]
    low = lax.ppermute(up, "face", after_me)
    high = lax.ppermute(down, "face", [(to, source) for source, to in after_me])
    second_part = ocean_part(starts[1], starts[2], surf)

    slab, sums, final, inverse = call(
        functools.partial(second_kernel, planes),
        [
            (blocks, EDGE_AT + ROWS, LANES),
            air.shape,
            (x_points, y_points),
            (x_points, y_points),
        ],
        [VMEM_SPEC] * 6 + [ANY_SPEC],
        [
            pltpu.VMEM((blocks, HEAD, LANES), jnp.float32),
            pltpu.VMEM((2, ROWS, LANES), jnp.float32),
            pltpu.VMEM((2 * planes, LANES), jnp.float32),
            pltpu.SemaphoreType.DMA((3,)),
        ],
        hbm_outs=1,
    )(avg, surf, low, high, wind, point_ids, second_part)
    arrived = lax.all_to_all(slab, "blk", split_axis=0, concat_axis=0, tiled=True)
    third_part = ocean_part(starts[2], chunks, final)
    down, up = call(rows_kernel, [(planes, LANES)] * 2, [VMEM_SPEC, ANY_SPEC])(
        sums, third_part
    )
    low = lax.ppermute(up, "face", after_me)
    high = lax.ppermute(down, "face", [(to, source) for source, to in after_me])
    partial, gain = call(
        functools.partial(rim_kernel, starts),
        [ocean.shape, area.shape],
        [VMEM_SPEC] * 5 + [ANY_SPEC] + [VMEM_SPEC] * len(starts),
        cost=chunks * reads_per_chunk // 8 * ROWS * LANES * 4,
    )(
        before,
        after,
        edge_coef,
        neighbours,
        area,
        down,
        first_part,
        second_part,
        third_part,
    )
    air_final, ocean_final = call(
        functools.partial(end_kernel, planes),
        [air.shape, ocean.shape],
        [VMEM_SPEC] * 10,
        [
            pltpu.VMEM(air.shape, jnp.float32),
            pltpu.VMEM((ROWS, cells), jnp.float32),
            pltpu.SemaphoreType.DMA((2 + planes // ROWS,)),
        ],
        hbm_outs=2,
    )(sums, low, high, arrived, final, inverse, cell_ids, weights, gain, partial)
    return air_final.reshape(air_state.shape), ocean_final.reshape(tracers.shape)


def solution(mesh):
    return jax.shard_map(
        body,
        mesh=mesh,
        in_specs=(
            P(None, None, "face", "blk"),
            P(None, None, "face", "blk"),
            P("face", "blk"),
            P("face", "blk"),
            P(("face", "blk"), None, None),
            P(None, None, ("face", "blk")),
            P(None, ("face", "blk")),
            P(None, ("face", "blk")),
            P(("face", "blk")),
            P(("face", "blk")),
            P(("face", "blk"), None),
            P(("face", "blk"), None, None),
            P(("face", "blk"), None, None),
        ),
        out_specs=(P(None, None, "face", "blk"), P(None, None, ("face", "blk"))),
        check_vma=False,
    )
```

```python
import functools

import jax
import jax.numpy as jnp
from jax import lax
from jax.experimental import pallas as pl
from jax.experimental.pallas import tpu as pltpu
from jax.sharding import PartitionSpec as P

GLL = 4
ROWS = 8
LANES = 128

deriv_table = [
    [-3.0, 4.045084971874737, -1.545084971874737, 0.5],
    [-0.8090169943749475, 0.0, 1.118033988749895, -0.30901699437494745],
    [0.30901699437494745, -1.118033988749895, 0.0, 0.8090169943749475],
    [-0.5, 1.545084971874737, -4.045084971874737, 3.0],
]
time_step = 0.05
relax_rate = 0.3
flux_gain = 0.2

HEAD, EDGE_AT = 8, 8
SIDE_EDGE, SIDE_STRIP, SIDE_IDS = 0, 8, 16
AVG, MASS_SUM, MASS, COEF_X, COEF_Y, SURF = range(6)
SURF_ARRAYS = 6


def iota(shape, dim):
    return lax.broadcasted_iota(jnp.int32, shape, dim)


def take(values, index, axis):
    return jnp.take_along_axis(values, index, axis=axis, mode="promise_in_bounds")


def by_position(pos, values):
    result = jnp.full(pos.shape, values[-1], jnp.float32)
    for i, value in enumerate(values[:-1]):
        result = jnp.where(pos == i, value, result)
    return result


def spread(row):
    return jnp.broadcast_to(row, (ROWS, LANES))


class Geometry:
    def __init__(self):
        shape = (ROWS, LANES)
        self.row, self.lane = iota(shape, 0), iota(shape, 1)
        x_pos, y_pos = self.row & (GLL - 1), self.lane & (GLL - 1)
        self.y_from = [self.lane - y_pos + j for j in range(GLL)]
        columns = [[line[j] for line in deriv_table] for j in range(GLL)]
        self.x_coef = {
            step: by_position(
                x_pos,
                [
                    deriv_table[i][i + step] if 0 <= i + step < GLL else 0.0
                    for i in range(GLL)
                ],
            )
            for step in range(1 - GLL, GLL)
        }
        self.y_coef = [by_position(y_pos, column) for column in columns]
        self.y_swap = (
            self.lane + jnp.where(y_pos == GLL - 1, 1, 0) - jnp.where(y_pos == 0, 1, 0)
        ) & (LANES - 1)
        self.x_edge = (x_pos == 0) | (x_pos == GLL - 1)
        self.y_edge = (y_pos == 0) | (y_pos == GLL - 1)
        self.first_row, self.last_row = self.row == 0, self.row == ROWS - 1
        self.middle_row = self.row == GLL
        self.outer_lane = (self.lane == 0) | (self.lane == LANES - 1)
        self.weight = jnp.where(self.x_edge, 1.0 / 6.0, 5.0 / 6.0) * jnp.where(
            self.y_edge, 1.0 / 6.0, 5.0 / 6.0
        )

    def d_x(self, tile):
        return sum(
            coef * (pltpu.roll(tile, -step % ROWS, 0) if step else tile)
            for step, coef in self.x_coef.items()
        )

    def d_y(self, *tiles):
        totals = [0.0] * len(tiles)
        for j in range(GLL):
            for i, tile in enumerate(tiles):
                totals[i] += self.y_coef[j] * take(tile, self.y_from[j], 1)
        return totals

    def sum_x(self, low, high, before, after):
        low_down, low_up = pltpu.roll(low, 1, 0), pltpu.roll(low, ROWS - 1, 0)
        high_down, high_up = pltpu.roll(high, 1, 0), pltpu.roll(high, ROWS - 1, 0)
        low_other = jnp.where(
            self.first_row,
            before,
            jnp.where(
                self.middle_row, low_down, jnp.where(self.last_row, high_up, low_up)
            ),
        )
        high_other = jnp.where(
            self.first_row,
            low_down,
            jnp.where(
                self.middle_row, high_down, jnp.where(self.last_row, after, high_up)
            ),
        )
        return (
            low + jnp.where(self.x_edge, low_other, 0.0),
            high + jnp.where(self.x_edge, high_other, 0.0),
        )

    def sum_y(self, tile, outer):
        other = jnp.where(self.outer_lane, outer, take(tile, self.y_swap, 1))
        return tile + jnp.where(self.y_edge, other, 0.0)

    def sum_y_pair(self, own, strip):
        own_swap, strip_swap = take(own, self.y_swap, 1), take(strip, self.y_swap, 1)
        own_other = jnp.where(self.outer_lane, strip_swap, own_swap)
        strip_other = jnp.where(self.outer_lane, own_swap, strip_swap)
        return (
            own + jnp.where(self.y_edge, own_other, 0.0),
            strip + jnp.where(self.y_edge, strip_other, 0.0),
        )


def edge_place(x, group):
    return x // ROWS, LANES // 2 * (x % 2) + ROWS * group + 2 * (x % ROWS // 2)


def edges_of(geo, packs, ref, planes, lines, first=None):
    packs = list(packs)
    for number, x in enumerate(lines):
        base = planes * (number if first is None else x - first)
        for group in range(planes // ROWS):
            q, at = edge_place(x, group)
            tile = ref[base + ROWS * group : base + ROWS * (group + 1), :]
            rolled = pltpu.roll(tile, (at + 1) % LANES, 1)
            packs[q] = jnp.where((geo.lane >> 1) == at // 2, rolled, packs[q])
    return packs


def outer_edges(joined, x, group):
    q, at = edge_place(x, group)
    return pltpu.roll(joined[q], (-(at + 1)) % LANES, 1)


def split_sides(geo, first, second, unit):
    odd = (geo.lane & unit) != 0
    return (
        jnp.where(odd, pltpu.roll(second, unit, 1), first),
        jnp.where(odd, second, pltpu.roll(first, LANES - unit, 1)),
    )


def join_sides(geo, before, after, unit):
    odd = (geo.lane & unit) != 0
    return (
        jnp.where(odd, pltpu.roll(after, unit, 1), before),
        jnp.where(odd, after, pltpu.roll(before, LANES - unit, 1)),
    )


def join_edges(geo, before, after):
    odd = (geo.lane & 1) != 0
    return (
        jnp.where(odd, pltpu.roll(before, 1, 1), after),
        jnp.where(odd, before, pltpu.roll(after, LANES - 1, 1)),
    )


def neighbours_of(blocks):
    here = lax.axis_index("blk")
    return lax.rem(here + blocks - 1, blocks), lax.rem(here + 1, blocks)


def scatter_sum(lines, index, bins, allowed=None):
    count = index.shape[0]
    split = []
    for values in lines:
        for part in range(3):
            short = values.astype(jnp.bfloat16).astype(jnp.float32)
            split.append(short)
            values = values - short
    high, low = index >> 7, index & (LANES - 1)
    bin_at = iota((bins, LANES), 0)
    lane_at = iota((LANES, LANES), 0)
    if allowed is not None:
        lane_at = jnp.where(allowed(lane_at), lane_at, -1)
    left, right = [], []
    for c in range(count):
        hit = bin_at == high[c : c + 1]
        left.append(
            jnp.concatenate(
                [jnp.where(hit, part[c : c + 1], 0.0) for part in split], axis=0
            ).astype(jnp.bfloat16)
        )
        right.append(
            jnp.where(lane_at == low[c : c + 1], 1.0, 0.0).astype(jnp.bfloat16)
        )
    total = lax.dot_general(
        jnp.concatenate(left, axis=1),
        jnp.concatenate(right, axis=1),
        (((1,), (1,)), ((), ())),
        preferred_element_type=jnp.float32,
    )
    sums = []
    for i in range(len(lines)):
        part = total[3 * i * bins : 3 * (i + 1) * bins]
        sums.append(part[:bins] + part[bins : 2 * bins] + part[2 * bins :])
    return sums


def wind_tiles(wind_ref, x_points, level, lines):
    levels = wind_ref.shape[0] // (2 * x_points)
    return [
        [
            time_step
            * wind_ref[
                pl.ds((levels * part + level) * x_points + x, ROWS, stride=x_points), :
            ]
            for x in lines
        ]
        for part in range(2)
    ]


def start_kernel(
    planes,
    cols_in,
    weights_in,
    tracers_in,
    rows_in,
    jac_in,
    land_in,
    wind_in,
    air_in,
    send_in,
    slab_out,
    moved_ref,
    before_ref,
    after_ref,
    cols_ref,
    weights_ref,
    rows_ref,
    send_ref,
    slab_ref,
    tracers_ref,
    jac_ref,
    land_ref,
    wind_ref,
    air_ref,
    semaphores,
):
    copies = [
        pltpu.make_async_copy(source, target, semaphores.at[i])
        for i, (source, target) in enumerate(
            (
                (cols_in, cols_ref),
                (tracers_in.at[:ROWS], tracers_ref),
                (weights_in, weights_ref),
                (rows_in, rows_ref),
                (air_in, air_ref),
                (wind_in, wind_ref),
                (jac_in, jac_ref),
                (land_in, land_ref),
                (send_in, send_ref),
            )
        )
    ]
    for copy in copies:
        copy.start()
    geo = Geometry()
    blocks = cols_ref.shape[0]
    x_points = jac_ref.shape[0]
    levels = wind_ref.shape[0] // (2 * x_points)
    chunks = tracers_ref.shape[1] // LANES
    for copy in copies[:4]:
        copy.wait()

    for group in range(blocks // ROWS):
        at = slice(ROWS * group, ROWS * (group + 1))
        cells = cols_ref[at, :]
        high, low = cells >> 7, cells & (LANES - 1)
        surface = jnp.zeros((ROWS, LANES), jnp.float32)
        for k in range(chunks):
            line = spread(tracers_ref[0:1, LANES * k : LANES * (k + 1)])
            surface = jnp.where(high == k, take(line, low, 1), surface)
        area = weights_ref[at, :]
        heat = area * surface
        for c in range(ROWS):
            owner = ROWS * group + c
            for place, step in enumerate((1, 0, -1)):
                to = (owner + step) % blocks
                slab_ref[to, 2 * place : 2 * place + 1, :] = heat[c : c + 1]
                slab_ref[to, 2 * place + 1 : 2 * place + 2, :] = area[c : c + 1]

    out = pltpu.make_async_copy(slab_ref, slab_out, semaphores.at[len(copies)])
    out.start()
    ids = rows_ref[...].astype(jnp.float32)
    for side_ref in (before_ref, after_ref):
        side_ref[SIDE_IDS : SIDE_IDS + blocks, :] = ids

    for copy in copies[4:]:
        copy.wait()
    strips = []
    for h in range(2):
        half = slice(ROWS * h, ROWS * (h + 1))
        second = levels * x_points
        pack = jnp.zeros((ROWS, LANES), jnp.float32)
        for i, strip in enumerate(
            (
                air_ref[half, :],
                wind_ref[half, :],
                wind_ref[second + ROWS * h : second + ROWS * (h + 1), :],
                jac_ref[half, :],
                land_ref[half, :],
            )
        ):
            pack = jnp.where(
                (geo.lane >> 4) == i, pltpu.roll(strip, 16 * i + 8, 1), pack
            )
        strips.append(pack)
    to_right, to_left = split_sides(geo, strips[0], strips[1], ROWS)
    after_ref[SIDE_STRIP : SIDE_STRIP + ROWS, :] = to_right
    before_ref[SIDE_STRIP : SIDE_STRIP + ROWS, :] = to_left

    y_weight = jnp.where(geo.y_edge, 1.0 / 6.0, 5.0 / 6.0)
    for element in range(x_points // GLL):
        lines = [GLL * element + i for i in range(GLL)]
        mass = [
            (1.0 / 6.0 if i in (0, GLL - 1) else 5.0 / 6.0)
            * y_weight
            * spread(jac_ref[x : x + 1, :])
            for i, x in enumerate(lines)
        ]
        for level in range(0, levels, ROWS):
            wind = wind_tiles(wind_ref, x_points, level, lines)
            for plane in range(level, planes, levels):
                fields = [
                    air_ref[pl.ds(plane * x_points + x, ROWS, stride=x_points), :]
                    for x in lines
                ]
                slopes = geo.d_y(*fields)
                for i, x in enumerate(lines):
                    slope = sum(deriv_table[i][j] * fields[j] for j in range(GLL))
                    moved = mass[i] * (
                        fields[i] - (wind[0][i] * slope + wind[1][i] * slopes[i])
                    )
                    moved_ref[planes * x + plane : planes * x + plane + ROWS, :] = moved
    packs = [jnp.zeros((ROWS, LANES), jnp.float32) for _ in range(2)]
    packs = edges_of(geo, packs, moved_ref, planes, range(x_points))
    to_right, to_left = split_sides(geo, packs[0], packs[1], 1)
    after_ref[SIDE_EDGE : SIDE_EDGE + ROWS, :] = to_right
    before_ref[SIDE_EDGE : SIDE_EDGE + ROWS, :] = to_left
    out.wait()


def panel_kernel(
    planes,
    moved_ref,
    recv_ref,
    before_ref,
    after_ref,
    air_ref,
    wind_ref,
    jac_ref,
    land_ref,
    rows_ref,
    ocean_ref,
    avg_ref,
    down_ref,
    up_ref,
    surf_ref,
):
    geo = Geometry()
    blocks = rows_ref.shape[0]
    x_points = jac_ref.shape[0]
    levels = wind_ref.shape[0] // (2 * x_points)

    own_ids = rows_ref[...]
    left_ids = before_ref[SIDE_IDS : SIDE_IDS + blocks, :].astype(jnp.int32)
    right_ids = after_ref[SIDE_IDS : SIDE_IDS + blocks, :].astype(jnp.int32)
    head = [
        jnp.concatenate([recv_ref[c, i : i + 1, :] for c in range(blocks)], axis=0)
        for i in range(6)
    ]
    heat, frac = scatter_sum(head[2:4], own_ids, 2 * ROWS)
    from_left = scatter_sum(
        head[0:2], left_ids, 2 * ROWS, lambda lane: lane >= LANES - ROWS
    )
    from_right = scatter_sum(head[4:6], right_ids, 2 * ROWS, lambda lane: lane < ROWS)
    strip_heat = from_left[0] + from_right[0]
    strip_frac = from_left[1] + from_right[1]

    in_strip = (geo.lane < ROWS) | (geo.lane >= LANES - ROWS)
    packs = join_sides(
        geo,
        before_ref[SIDE_STRIP : SIDE_STRIP + ROWS, :],
        after_ref[SIDE_STRIP : SIDE_STRIP + ROWS, :],
        ROWS,
    )
    own, strip = [], []
    for h, pack in enumerate(packs):
        half = slice(ROWS * h, ROWS * (h + 1))
        strip.append(
            [
                jnp.where(
                    in_strip, pltpu.roll(pack, (-(16 * i + 8)) % LANES, 1), 1.0
                )
                for i in range(5)
            ]
        )
        own.append(
            [
                air_ref[half, :],
                wind_ref[half, :],
                wind_ref[
                    levels * x_points + ROWS * h : levels * x_points + ROWS * (h + 1), :
                ],
                jac_ref[half, :],
                land_ref[half, :],
            ]
        )
    for h in range(2):
        half = slice(ROWS * h, ROWS * (h + 1))
        pair = []
        for tile, ((field, wind_x, wind_y, jac, land), tile_heat, tile_frac) in enumerate(
            ((own[h], heat[half], frac[half]), (strip[h], strip_heat[half], strip_frac[half]))
        ):
            mass = geo.weight * jac
            if tile == 1:
                tile_heat = jnp.where(in_strip, tile_heat, 0.0)
                tile_frac = jnp.where(in_strip, tile_frac, 0.0)
            surf = (tile_heat + land * field) / (tile_frac + land)
            coef_x, coef_y = time_step * mass * wind_x, time_step * mass * wind_y
            moved = (
                mass * (field + relax_rate * (surf - field))
                - coef_x * geo.d_x(field)
                - coef_y * geo.d_y(field)[0]
            )
            pair.append((moved, mass))
            at = 2 * ROWS * tile + ROWS * h
            for number, value in (
                (MASS, mass),
                (COEF_X, coef_x),
                (COEF_Y, coef_y),
                (SURF, surf),
            ):
                surf_ref[4 * ROWS * number + at : 4 * ROWS * number + at + ROWS, :] = value
        for number, i in ((AVG, 0), (MASS_SUM, 1)):
            for tile, value in enumerate(geo.sum_y_pair(pair[0][i], pair[1][i])):
                at = 4 * ROWS * number + 2 * ROWS * tile + ROWS * h
                surf_ref[at : at + ROWS, :] = value

    joined = join_edges(
        geo,
        before_ref[SIDE_EDGE : SIDE_EDGE + ROWS, :],
        after_ref[SIDE_EDGE : SIDE_EDGE + ROWS, :],
    )
    for x in outer_rows(x_points):
        for group in range(planes // ROWS):
            at = slice(planes * x + ROWS * group, planes * x + ROWS * (group + 1))
            avg_ref[at, :] = geo.sum_y(moved_ref[at, :], outer_edges(joined, x, group))

    def line(r):
        return avg_ref[planes * r : planes * (r + 1), :]

    def surf_line(number, r):
        return surf_ref[pl.ds(4 * ROWS * number + r, 2, stride=x_points), :]

    def first_step(get, mass_at):
        return (
            [
                get(1) / mass_at(1),
                get(2) / mass_at(2),
                (get(3) + get(4)) / (mass_at(3) + mass_at(4)),
            ],
            [
                (get(11) + get(12)) / (mass_at(11) + mass_at(12)),
                get(13) / mass_at(13),
                get(14) / mass_at(14),
            ],
        )

    def own_mass_sum(r):
        return surf_ref[4 * ROWS * MASS_SUM + r : 4 * ROWS * MASS_SUM + r + 1, :]

    low_lines, high_lines = first_step(line, own_mass_sum)
    surf_low, surf_high = first_step(
        functools.partial(surf_line, AVG), functools.partial(surf_line, MASS_SUM)
    )
    for out_ref, r, lines, surf_lines, coefs in (
        (down_ref, 0, low_lines, surf_low, deriv_table[0][1:]),
        (up_ref, 15, high_lines, surf_high, deriv_table[3][:3]),
    ):
        slope = sum(coef * value for coef, value in zip(coefs, lines))
        surf_slope = sum(coef * value for coef, value in zip(coefs, surf_lines))
        mass = surf_ref[4 * ROWS * MASS + r : 4 * ROWS * MASS + r + 1, :]
        wind = time_step * mass * wind_ref[pl.ds(r, 2 * levels, stride=x_points), :]
        out_ref[0:planes, :] = line(r)
        for first in range(0, planes, levels):
            out_ref[planes + first : planes + first + levels, :] = (
                wind[:levels] * slope[first : first + levels]
            )
        base = 2 * planes
        out_ref[base : base + 2 * levels, :] = wind
        base += 2 * levels
        for number in range(SURF_ARRAYS):
            out_ref[base + 2 * number : base + 2 * number + 2, :] = surf_line(number, r)
        base += 2 * SURF_ARRAYS
        out_ref[base : base + 2, :] = surf_line(COEF_X, r) * surf_slope


def outer_rows(x_points):
    return [x for x in range(x_points) if x <= GLL or x >= x_points - GLL - 1]


def advance(geo, fields, wind, mass):
    slopes = geo.d_y(*fields)
    moved = []
    for i in range(GLL):
        slope = sum(deriv_table[i][j] * fields[j] for j in range(GLL))
        moved.append(mass[i] * (fields[i] - (wind[0][i] * slope + wind[1][i] * slopes[i])))
    return moved, slopes


def inner_kernel(
    planes, avg_ref, moved_ref, before_ref, after_ref, surf_ref, wind_ref, out_ref, packs_ref
):
    geo = Geometry()
    x_points = avg_ref.shape[0] // planes
    levels = wind_ref.shape[0] // (2 * x_points)
    joined = join_edges(
        geo,
        before_ref[SIDE_EDGE : SIDE_EDGE + ROWS, :],
        after_ref[SIDE_EDGE : SIDE_EDGE + ROWS, :],
    )
    outer = outer_rows(x_points)

    def average(x, plane):
        at = slice(planes * x + plane, planes * x + plane + ROWS)
        if x in outer:
            return avg_ref[at, :]
        return geo.sum_y(moved_ref[at, :], outer_edges(joined, x, plane // ROWS))

    def surf_row(number, x):
        at = 4 * ROWS * number + x
        return spread(surf_ref[at : at + 1, :])

    def put(x, plane, value):
        at = planes * (x - GLL) + plane
        out_ref[at : at + ROWS, :] = value

    held = {}
    carried = {}
    for element in range(1, x_points // GLL - 1):
        lines = [GLL * element + i for i in range(GLL)]
        totals = [surf_row(MASS_SUM, x) for x in lines]
        totals[0] = totals[0] + surf_row(MASS_SUM, lines[0] - 1)
        totals[-1] = totals[-1] + surf_row(MASS_SUM, lines[-1] + 1)
        scale = [1.0 / total for total in totals]
        mass = [surf_row(MASS, x) for x in lines]
        for level in range(0, levels, ROWS):
            wind = wind_tiles(wind_ref, x_points, level, lines)
            for plane in range(level, planes, levels):
                if element == 1:
                    first = average(lines[0], plane) + average(lines[0] - 1, plane)
                else:
                    first = carried[plane]
                last = average(lines[-1], plane) + average(lines[-1] + 1, plane)
                carried[plane] = last
                totals = (
                    [first] + [average(x, plane) for x in lines[1:-1]] + [last]
                )
                fields = [total * factor for total, factor in zip(totals, scale)]
                moved, _ = advance(geo, fields, wind, mass)
                if element == 1:
                    put(lines[0], plane, moved[0])
                else:
                    shared = held[plane] + moved[0]
                    put(lines[0] - 1, plane, shared)
                    put(lines[0], plane, shared)
                for i in range(1, GLL - 1):
                    put(lines[i], plane, moved[i])
                held[plane] = moved[-1]
                if lines[-1] == x_points - GLL - 1:
                    put(lines[-1], plane, moved[-1])
    packs = [jnp.zeros((ROWS, LANES), jnp.float32) for _ in range(2)]
    inner = [x for x in range(x_points) if x not in outer]
    for q, pack in enumerate(edges_of(geo, packs, out_ref, planes, inner, GLL)):
        packs_ref[ROWS * q : ROWS * (q + 1), :] = pack


def second_kernel(
    planes,
    avg_ref,
    inner_ref,
    packs_ref,
    surf_ref,
    low_ref,
    high_ref,
    wind_ref,
    rows_ref,
    ocean_ref,
    slab_out,
    sums_ref,
    final_ref,
    inverse_ref,
    flux_ref,
    edges_ref,
    semaphores,
):
    geo = Geometry()
    blocks = rows_ref.shape[0]
    left, right = neighbours_of(blocks)
    x_points = final_ref.shape[0]
    levels = wind_ref.shape[0] // (2 * x_points)
    base = low_ref.shape[0] - 2 * SURF_ARRAYS - 4

    def surf_tile(number, tile, h):
        at = 4 * ROWS * number + 2 * ROWS * tile + ROWS * h
        return surf_ref[at : at + ROWS, :]

    def beside(ref, number, tile):
        at = base + 2 * number + tile
        return spread(ref[at : at + 1, :])

    ends = []
    inverse = []
    for tile in range(2):
        total = geo.sum_x(
            surf_tile(MASS_SUM, tile, 0),
            surf_tile(MASS_SUM, tile, 1),
            beside(low_ref, MASS_SUM, tile),
            beside(high_ref, MASS_SUM, tile),
        )
        inverse.append([1.0 / value for value in total])
        summed = geo.sum_x(
            surf_tile(AVG, tile, 0),
            surf_tile(AVG, tile, 1),
            beside(low_ref, AVG, tile),
            beside(high_ref, AVG, tile),
        )
        fields = [value * scale for value, scale in zip(summed, inverse[tile])]
        moved = []
        for h in range(2):
            field = fields[h]
            moved.append(
                surf_tile(MASS, tile, h)
                * (field + relax_rate * (surf_tile(SURF, tile, h) - field))
                - surf_tile(COEF_X, tile, h) * geo.d_x(field)
                - surf_tile(COEF_Y, tile, h) * geo.d_y(field)[0]
            )
        halos = []
        for ref, field, own_coef in (
            (low_ref, spread(fields[0][:1]), deriv_table[3][3]),
            (high_ref, spread(fields[1][ROWS - 1 :]), deriv_table[0][0]),
        ):
            halos.append(
                beside(ref, MASS, tile)
                * (field + relax_rate * (beside(ref, SURF, tile) - field))
                - beside(ref, SURF_ARRAYS, tile)
                - beside(ref, COEF_X, tile) * (own_coef * field)
                - beside(ref, COEF_Y, tile) * geo.d_y(field)[0]
            )
        ends.append(geo.sum_x(moved[0], moved[1], halos[0], halos[1]))
    final = []
    for h in range(2):
        summed, _ = geo.sum_y_pair(ends[0][h], ends[1][h])
        final.append(summed * inverse[0][h])
        final_ref[ROWS * h : ROWS * (h + 1), :] = final[h]
        inverse_ref[ROWS * h : ROWS * (h + 1), :] = inverse[0][h]
    flux = [final[h] - surf_tile(SURF, 0, h) for h in range(2)]
    for group in range(blocks // ROWS):
        ids = rows_ref[ROWS * group : ROWS * (group + 1), :]
        high, low = ids >> 7, ids & (LANES - 1)
        picked = jnp.zeros((ROWS, LANES), jnp.float32)
        for x in range(2 * ROWS):
            line = spread(flux[x // ROWS][x % ROWS : x % ROWS + 1])
            picked = jnp.where(high == x, take(line, low, 1), picked)
        for c in range(ROWS):
            flux_ref[ROWS * group + c, 0:1, :] = picked[c : c + 1]

    copies = [
        pltpu.make_async_copy(flux_ref, slab_out.at[:, :HEAD], semaphores.at[0])
    ]
    copies[0].start()

    kept = outer_rows(x_points)

    def put(x, plane, value):
        at = planes * kept.index(x) + plane
        sums_ref[at : at + ROWS, :] = value

    def beyond(ref, plane, field, slope, own_coef):
        wind_at = 2 * planes + plane % levels
        return (
            beside(ref, MASS, 0) * field
            - ref[planes + plane : planes + plane + ROWS, :]
            - ref[wind_at : wind_at + ROWS, :] * (own_coef * field)
            - ref[wind_at + levels : wind_at + levels + ROWS, :] * slope
        )

    def row_of(tiles, x):
        return spread(tiles[x // ROWS][x % ROWS : x % ROWS + 1])

    masses = [surf_tile(MASS, 0, h) for h in range(2)]
    last_element = x_points // GLL - 1
    for element in (0, last_element):
        lines = [GLL * element + i for i in range(GLL)]
        scale = [row_of(inverse[0], x) for x in lines]
        mass = [row_of(masses, x) for x in lines]
        for level in range(0, levels, ROWS):
            wind = wind_tiles(wind_ref, x_points, level, lines)
            for plane in range(level, planes, levels):
                here = slice(plane, plane + ROWS)
                fields = []
                for i, x in enumerate(lines):
                    total = avg_ref[planes * x + plane : planes * x + plane + ROWS, :]
                    other = x - 1 if i == 0 else x + 1
                    if other < 0:
                        total = total + low_ref[here, :]
                    elif other == x_points:
                        total = total + high_ref[here, :]
                    elif i in (0, GLL - 1):
                        at = planes * other + plane
                        total = total + avg_ref[at : at + ROWS, :]
                    fields.append(total * scale[i])
                moved, slopes = advance(geo, fields, wind, mass)
                if element == 0:
                    before = beyond(low_ref, plane, fields[0], slopes[0], deriv_table[3][3])
                    put(lines[0], plane, before + moved[0])
                    shared = moved[-1] + inner_ref[here, :]
                    put(lines[-1], plane, shared)
                    put(lines[-1] + 1, plane, shared)
                else:
                    at = inner_ref.shape[0] - planes + plane
                    shared = moved[0] + inner_ref[at : at + ROWS, :]
                    put(lines[0] - 1, plane, shared)
                    put(lines[0], plane, shared)
                    after = beyond(
                        high_ref, plane, fields[-1], slopes[-1], deriv_table[0][0]
                    )
                    put(lines[-1], plane, moved[-1] + after)
                for i in range(1, GLL - 1):
                    put(lines[i], plane, moved[i])
    packs = [packs_ref[:ROWS, :], packs_ref[ROWS:, :]]
    packs = edges_of(geo, packs, sums_ref, planes, kept)
    to_right, to_left = split_sides(geo, packs[0], packs[1], 1)
    for i, (to, edges) in enumerate(((right, to_right), (left, to_left))):
        edges_ref[i] = edges
        copies.append(
            pltpu.make_async_copy(
                edges_ref.at[i],
                slab_out.at[to, EDGE_AT : EDGE_AT + ROWS],
                semaphores.at[1 + i],
            )
        )
        copies[-1].start()
    for copy in copies:
        copy.wait()


def last_kernel(planes, inner_ref, outer_ref, inverse_ref, out_ref):
    geo = Geometry()
    x_points = inverse_ref.shape[0]
    kept = outer_rows(x_points)
    for x in range(x_points):
        inverse = spread(inverse_ref[x : x + 1, :])
        ref, first = inner_ref, planes * (x - GLL)
        if x in kept:
            ref, first = outer_ref, planes * kept.index(x)
        for group in range(planes // ROWS):
            tile = ref[first + ROWS * group : first + ROWS * (group + 1), :]
            at = planes * x + ROWS * group
            out_ref[at : at + ROWS, :] = inverse * geo.sum_y(tile, 0.0)


def end_kernel(
    planes,
    last_ref,
    recv_ref,
    final_ref,
    inverse_ref,
    cols_ref,
    weights_ref,
    gain_ref,
    ocean_ref,
    air_out,
    ocean_out,
    air_ref,
    first_ref,
    semaphores,
):
    geo = Geometry()
    blocks = cols_ref.shape[0]
    left, right = neighbours_of(blocks)
    chunks = gain_ref.shape[0]
    x_points = inverse_ref.shape[0]
    copies = []

    def send(source, target):
        copies.append(
            pltpu.make_async_copy(source, target, semaphores.at[len(copies)])
        )
        copies[-1].start()

    send(ocean_ref.at[ROWS:], ocean_out.at[ROWS:])
    arrived = jnp.concatenate([recv_ref[c, 0:1, :] for c in range(blocks)], axis=0)
    (inflow,) = scatter_sum([weights_ref[...] * arrived], cols_ref[...], chunks)
    gain = inflow * gain_ref[...]
    first_ref[...] = ocean_ref[:ROWS, :]
    for k in range(chunks):
        at = slice(LANES * k, LANES * (k + 1))
        first_ref[0:1, at] = ocean_ref[0:1, at] + gain[k : k + 1]
    send(first_ref, ocean_out.at[:ROWS])

    joined = join_edges(
        geo,
        recv_ref[left, EDGE_AT : EDGE_AT + ROWS, :],
        recv_ref[right, EDGE_AT : EDGE_AT + ROWS, :],
    )
    for group in range(planes // ROWS):
        for x in range(x_points):
            at = planes * x + ROWS * group
            beside = spread(inverse_ref[x : x + 1, :]) * outer_edges(joined, x, group)
            air_ref[pl.ds(ROWS * group * x_points + x, ROWS, stride=x_points), :] = last_ref[
                at : at + ROWS, :
            ] + jnp.where(geo.outer_lane, beside, 0.0)
        if group == 0:
            air_ref[0:x_points, :] = final_ref[...]
        rows = slice(ROWS * group * x_points, ROWS * (group + 1) * x_points)
        send(air_ref.at[rows], air_out.at[rows])
    for copy in copies:
        copy.wait()


def gathered(ids, coefs, source, sources, groups, first=0):
    totals = [jnp.zeros((ROWS, LANES), jnp.float32) for _ in range(groups)]
    for edge in range(ids.shape[0]):
        cell = spread(ids[edge : edge + 1])
        coef = spread(coefs[edge : edge + 1])
        high, low = cell >> 7, cell & (LANES - 1)
        for s in range(sources):
            scaled = jnp.where(high == first + s, coef, 0.0)
            for group in range(groups):
                totals[group] += scaled * take(source(group, s), low, 1)
    return totals


def multiplied(ids, coefs, halves_ref, sources, groups):
    lane_at = iota((LANES, LANES), 0)
    hot = jnp.concatenate(
        [
            jnp.where(lane_at == (ids[edge : edge + 1] & (LANES - 1)), 1.0, 0.0).astype(
                jnp.bfloat16
            )
            for edge in range(2)
        ],
        axis=1,
    )
    picked = jnp.dot(
        halves_ref[...],
        jnp.concatenate([hot, hot], axis=0),
        preferred_element_type=jnp.float32,
    )
    totals = [jnp.zeros((ROWS, LANES), jnp.float32) for _ in range(groups)]
    for edge in range(2):
        high = spread(ids[edge : edge + 1]) >> 7
        coef = spread(coefs[edge : edge + 1])
        side = slice(LANES * edge, LANES * (edge + 1))
        for s in range(sources):
            scaled = jnp.where(high == s, coef, 0.0)
            for group in range(groups):
                at = ROWS * (groups * s + group)
                totals[group] += scaled * picked[at : at + ROWS, side]
    return totals


def ocean_kernel(
    levels, start, tracers_ref, coef_ref, near_ref, rate_ref, after_ref, out_ref, halves_ref
):
    chunks = tracers_ref.shape[1] // LANES
    groups = tracers_ref.shape[0] // ROWS
    row = iota((ROWS, LANES), 0)

    def source(group, s):
        return tracers_ref[
            ROWS * group : ROWS * (group + 1), LANES * s : LANES * (s + 1)
        ]

    planes = tracers_ref.shape[0]
    for s in range(chunks):
        values = tracers_ref[:, LANES * s : LANES * (s + 1)]
        upper = values.astype(jnp.bfloat16)
        at = slice(planes * s, planes * (s + 1))
        halves_ref[at, :LANES] = upper
        halves_ref[at, LANES:] = (values - upper.astype(jnp.float32)).astype(jnp.bfloat16)
    edges = near_ref.shape[0]

    def one_chunk(number, carry):
        k = number + start
        at = pl.ds(pl.multiple_of(k * LANES, LANES), LANES)
        out_at = pl.ds(pl.multiple_of(number * LANES, LANES), LANES)
        ids, coefs = near_ref[:, at], coef_ref[:, at]
        by_gather = edges - edges // 3 * 2
        totals = gathered(ids[:by_gather], coefs[:by_gather], source, chunks, groups)
        for edge in range(by_gather, edges, 2):
            more = multiplied(
                ids[edge : edge + 2], coefs[edge : edge + 2], halves_ref, chunks, groups
            )
            totals = [total + part for total, part in zip(totals, more)]
        coef_sum = spread(jnp.sum(coefs, axis=0, keepdims=True))
        rate = spread(rate_ref[pl.ds(k, 1), :])
        tiles = [tracers_ref[ROWS * g : ROWS * (g + 1), at] for g in range(groups)]
        for g in range(groups):
            tile = tiles[g]
            top = bottom = tile
            if (ROWS * g) % levels:
                top = pltpu.roll(tiles[g - 1], 1, 0)
            if (ROWS * (g + 1)) % levels:
                bottom = pltpu.roll(tiles[g + 1], ROWS - 1, 0)
            above = jnp.where(row == 0, top, pltpu.roll(tile, 1, 0))
            below = jnp.where(row == ROWS - 1, bottom, pltpu.roll(tile, ROWS - 1, 0))
            vertical = rate * ((above - tile) + (below - tile))
            out_ref[ROWS * g : ROWS * (g + 1), out_at] = (
                tile + (totals[g] - coef_sum * tile) + vertical
            )
        return carry

    count = out_ref.shape[1] // LANES
    step = 2 if count % 2 == 0 else 1

    def some_chunks(number, carry):
        for i in range(step):
            one_chunk(step * number + i, carry)
        return carry

    lax.fori_loop(0, count // step, some_chunks, 0)


def send_kernel(tracers_ref, send_ref, before_ref, after_ref, *out_refs):
    chunks = tracers_ref.shape[1] // LANES
    for part, (side_ref, out_ref) in enumerate(zip((before_ref, after_ref), out_refs)):
        base = side_ref.shape[0]
        out_ref[:base, :] = side_ref[...]
        cells = spread(send_ref[0:1, LANES * part : LANES * (part + 1)])
        high, low = cells >> 7, cells & (LANES - 1)
        for group in range(tracers_ref.shape[0] // ROWS):
            half = slice(ROWS * group, ROWS * (group + 1))
            rim = jnp.zeros((ROWS, LANES), jnp.float32)
            for k in range(chunks):
                tile = tracers_ref[half, LANES * k : LANES * (k + 1)]
                rim = jnp.where(high == k, take(tile, low, 1), rim)
            out_ref[base + ROWS * group : base + ROWS * (group + 1), :] = rim


def rim_kernel(
    starts,
    before_ref,
    after_ref,
    coef_ref,
    near_ref,
    area_ref,
    rows_ref,
    *refs,
):
    partial_refs, (out_ref, gain_ref) = refs[: len(starts)], refs[len(starts) :]
    chunks = coef_ref.shape[1] // LANES
    groups = out_ref.shape[0] // ROWS
    rim_at = before_ref.shape[0] - out_ref.shape[0]
    sides = before_ref, after_ref
    gain_ref[...] = flux_gain / area_ref[...]

    def source(group, s):
        at = rim_at + ROWS * group
        return sides[s][at : at + ROWS, :]

    for k in range(chunks):
        at = slice(LANES * k, LANES * (k + 1))
        totals = gathered(near_ref[:, at], coef_ref[:, at], source, 2, groups, chunks)
        part = max(i for i, start in enumerate(starts) if start <= k)
        place = slice(LANES * (k - starts[part]), LANES * (k - starts[part] + 1))
        for g in range(groups):
            half = slice(ROWS * g, ROWS * (g + 1))
            out_ref[half, at] = partial_refs[part][half, place] + totals[g]


VMEM_SPEC = pl.BlockSpec(memory_space=pltpu.VMEM)
ANY_SPEC = pl.BlockSpec(memory_space=pl.ANY)
HBM_SPEC = pl.BlockSpec(memory_space=pltpu.HBM)


def call(kernel, outs, specs, scratch=(), cost=0, hbm_outs=0):
    estimate = None
    if cost:
        estimate = pl.CostEstimate(flops=0, bytes_accessed=cost, transcendentals=0)
    outs = [
        out if isinstance(out, jax.ShapeDtypeStruct) else jax.ShapeDtypeStruct(out, jnp.float32)
        for out in outs
    ]
    out_specs = [VMEM_SPEC] * len(outs)
    out_specs[:hbm_outs] = [HBM_SPEC] * hbm_outs
    return pl.pallas_call(
        kernel,
        out_shape=outs,
        in_specs=specs,
        out_specs=out_specs,
        scratch_shapes=list(scratch),
        cost_estimate=estimate,
        compiler_params=pltpu.CompilerParams(vmem_limit_bytes=32 * 2**20),
        name=getattr(kernel, "func", kernel).__name__,
    )


def body(
    air_state,
    air_wind,
    jacobian,
    land_area,
    xgrid_rows,
    tracers,
    edge_coef,
    neighbours,
    vert_rate,
    ocean_area,
    send_list,
    xgrid_cols,
    xgrid_weights,
):
    field_count, levels, x_points, y_points = air_state.shape
    planes = field_count * levels
    ocean_levels, cells = tracers.shape[1:]
    ocean_planes = tracers.shape[0] * ocean_levels
    faces, blocks = lax.axis_size("face"), lax.axis_size("blk")
    air = air_state.reshape(planes * x_points, y_points)
    wind = air_wind.reshape(2 * levels * x_points, y_points)
    ocean = tracers.reshape(ocean_planes, cells)
    point_ids, cell_ids, weights = xgrid_rows[0], xgrid_cols[0], xgrid_weights[0]
    rate = vert_rate.reshape(cells // LANES, LANES)
    area = ocean_area.reshape(cells // LANES, LANES)
    first_inputs = (
        cell_ids,
        weights,
        ocean,
        point_ids,
        jacobian,
        land_area,
        wind,
        air,
        send_list,
    )
    kept = (cell_ids, weights, point_ids, send_list)
    slab, moved, to_before, to_after, cell_ids, weights, point_ids, send_list = call(
        functools.partial(start_kernel, planes),
        [(blocks, HEAD, LANES), air.shape]
        + [(SIDE_IDS + blocks, LANES)] * 2
        + [jax.ShapeDtypeStruct(array.shape, array.dtype) for array in kept],
        [HBM_SPEC] * len(first_inputs),
        [
            pltpu.VMEM(shape, jnp.float32)
            for shape in (
                (blocks, HEAD, LANES),
                (ROWS, cells),
                jacobian.shape,
                land_area.shape,
                wind.shape,
                air.shape,
            )
        ]
        + [pltpu.SemaphoreType.DMA((len(first_inputs) + 1,))],
        hbm_outs=1,
    )(*(pltpu.with_memory_space_constraint(array, pltpu.HBM) for array in first_inputs))
    recv = lax.all_to_all(slab, "blk", split_axis=0, concat_axis=0, tiled=True)

    chunks = cells // LANES
    reads_per_chunk = edge_coef.shape[0] * chunks * (ocean_planes // ROWS)
    starts = (0, chunks // 4, chunks * 3 // 4)

    def ocean_part(start, end, after):
        (result,) = call(
            functools.partial(ocean_kernel, ocean_levels, start),
            [(ocean_planes, (end - start) * LANES)],
            [VMEM_SPEC] * 4 + [ANY_SPEC],
            [pltpu.VMEM((chunks * ocean_planes, 2 * LANES), jnp.bfloat16)],
            cost=(end - start) * reads_per_chunk * ROWS * LANES * 2,
        )(ocean, edge_coef, neighbours, rate, after)
        return result

    to_before, to_after = call(
        send_kernel,
        [(SIDE_IDS + blocks + ocean_planes, LANES)] * 2,
        [VMEM_SPEC] * 4,
        cost=reads_per_chunk * ROWS * LANES,
    )(ocean, send_list, to_before, to_after)
    onward = [(i, (i + 1) % blocks) for i in range(blocks)]
    before = lax.ppermute(to_after, "blk", onward)
    after = lax.ppermute(to_before, "blk", [(to, source) for source, to in onward])
    first_part = ocean_part(starts[0], starts[1], to_before)
    side_rows = 2 * planes + 2 * levels + 2 * SURF_ARRAYS + 4
    avg, down, up, surf = call(
        functools.partial(panel_kernel, planes),
        [air.shape, (side_rows, LANES), (side_rows, LANES), (4 * ROWS * SURF_ARRAYS, LANES)],
        [VMEM_SPEC] * 9 + [ANY_SPEC],
    )(
        moved,
        recv,
        before,
        after,
        air,
        wind,
        jacobian,
        land_area,
        point_ids,
        first_part,
    )
    after_me = [(i, (i + 1) % faces) for i in range(faces)]
    low = lax.ppermute(up, "face", after_me)
    high = lax.ppermute(down, "face", [(to, source) for source, to in after_me])
    inner, packs = call(
        functools.partial(inner_kernel, planes),
        [((x_points - 2 * GLL) * planes, LANES), (2 * ROWS, LANES)],
        [VMEM_SPEC] * 6,
        cost=2 * air.size * 4,
    )(avg, moved, before, after, surf, wind)
    second_part = ocean_part(starts[1], starts[2], surf)

    slab, outer, final, inverse = call(
        functools.partial(second_kernel, planes),
        [
            (blocks, EDGE_AT + ROWS, LANES),
            (len(outer_rows(x_points)) * planes, LANES),
            (x_points, y_points),
            (x_points, y_points),
        ],
        [VMEM_SPEC] * 8 + [ANY_SPEC],
        [
            pltpu.VMEM((blocks, HEAD, LANES), jnp.float32),
            pltpu.VMEM((2, ROWS, LANES), jnp.float32),
            pltpu.SemaphoreType.DMA((3,)),
        ],
        hbm_outs=1,
    )(avg, inner, packs, surf, low, high, wind, point_ids, second_part)
    arrived = lax.all_to_all(slab, "blk", split_axis=0, concat_axis=0, tiled=True)
    (last,) = call(
        functools.partial(last_kernel, planes),
        [air.shape],
        [VMEM_SPEC] * 3,
        cost=2 * air.size * 4,
    )(inner, outer, inverse)
    third_part = ocean_part(starts[2], chunks, final)
    partial, gain = call(
        functools.partial(rim_kernel, starts),
        [ocean.shape, area.shape],
        [VMEM_SPEC] * 5 + [ANY_SPEC] + [VMEM_SPEC] * len(starts),
        cost=chunks * reads_per_chunk // 8 * ROWS * LANES * 4,
    )(
        before,
        after,
        edge_coef,
        neighbours,
        area,
        final,
        first_part,
        second_part,
        third_part,
    )
    air_final, ocean_final = call(
        functools.partial(end_kernel, planes),
        [air.shape, ocean.shape],
        [VMEM_SPEC] * 8,
        [
            pltpu.VMEM(air.shape, jnp.float32),
            pltpu.VMEM((ROWS, cells), jnp.float32),
            pltpu.SemaphoreType.DMA((2 + planes // ROWS,)),
        ],
        hbm_outs=2,
    )(last, arrived, final, inverse, cell_ids, weights, gain, partial)
    return air_final.reshape(air_state.shape), ocean_final.reshape(tracers.shape)


def solution(mesh):
    return jax.shard_map(
        body,
        mesh=mesh,
        in_specs=(
            P(None, None, "face", "blk"),
            P(None, None, "face", "blk"),
            P("face", "blk"),
            P("face", "blk"),
            P(("face", "blk"), None, None),
            P(None, None, ("face", "blk")),
            P(None, ("face", "blk")),
            P(None, ("face", "blk")),
            P(("face", "blk")),
            P(("face", "blk")),
            P(("face", "blk"), None),
            P(("face", "blk"), None, None),
            P(("face", "blk"), None, None),
        ),
        out_specs=(P(None, None, "face", "blk"), P(None, None, ("face", "blk"))),
        check_vma=False,
    )
```

```python
import functools

import jax
import jax.numpy as jnp
from jax import lax
from jax.experimental import pallas as pl
from jax.experimental.pallas import tpu as pltpu
from jax.sharding import PartitionSpec as P

GLL = 4
ROWS = 8
LANES = 128

deriv_table = [
    [-3.0, 4.045084971874737, -1.545084971874737, 0.5],
    [-0.8090169943749475, 0.0, 1.118033988749895, -0.30901699437494745],
    [0.30901699437494745, -1.118033988749895, 0.0, 0.8090169943749475],
    [-0.5, 1.545084971874737, -4.045084971874737, 3.0],
]
time_step = 0.05
relax_rate = 0.3
flux_gain = 0.2

HEAD, EDGE_AT = 8, 8
SIDE_EDGE, SIDE_STRIP, SIDE_IDS = 0, 8, 16
AVG, MASS_SUM, MASS, COEF_X, COEF_Y, SURF = range(6)
SURF_ARRAYS = 6


def iota(shape, dim):
    return lax.broadcasted_iota(jnp.int32, shape, dim)


def take(values, index, axis):
    return jnp.take_along_axis(values, index, axis=axis, mode="promise_in_bounds")


def by_position(pos, values):
    result = jnp.full(pos.shape, values[-1], jnp.float32)
    for i, value in enumerate(values[:-1]):
        result = jnp.where(pos == i, value, result)
    return result


def spread(row):
    return jnp.broadcast_to(row, (ROWS, LANES))


class Geometry:
    def __init__(self):
        shape = (ROWS, LANES)
        self.row, self.lane = iota(shape, 0), iota(shape, 1)
        x_pos, y_pos = self.row & (GLL - 1), self.lane & (GLL - 1)
        self.y_from = [self.lane - y_pos + j for j in range(GLL)]
        columns = [[line[j] for line in deriv_table] for j in range(GLL)]
        self.x_coef = {
            step: by_position(
                x_pos,
                [
                    deriv_table[i][i + step] if 0 <= i + step < GLL else 0.0
                    for i in range(GLL)
                ],
            )
            for step in range(1 - GLL, GLL)
        }
        self.y_coef = [by_position(y_pos, column) for column in columns]
        self.y_swap = (
            self.lane + jnp.where(y_pos == GLL - 1, 1, 0) - jnp.where(y_pos == 0, 1, 0)
        ) & (LANES - 1)
        self.x_edge = (x_pos == 0) | (x_pos == GLL - 1)
        self.y_edge = (y_pos == 0) | (y_pos == GLL - 1)
        self.first_row, self.last_row = self.row == 0, self.row == ROWS - 1
        self.middle_row = self.row == GLL
        self.outer_lane = (self.lane == 0) | (self.lane == LANES - 1)
        self.weight = jnp.where(self.x_edge, 1.0 / 6.0, 5.0 / 6.0) * jnp.where(
            self.y_edge, 1.0 / 6.0, 5.0 / 6.0
        )

    def d_x(self, tile):
        return sum(
            coef * (pltpu.roll(tile, -step % ROWS, 0) if step else tile)
            for step, coef in self.x_coef.items()
        )

    def d_y(self, *tiles):
        totals = [0.0] * len(tiles)
        for j in range(GLL):
            for i, tile in enumerate(tiles):
                totals[i] += self.y_coef[j] * take(tile, self.y_from[j], 1)
        return totals

    def sum_x(self, low, high, before, after):
        low_down, low_up = pltpu.roll(low, 1, 0), pltpu.roll(low, ROWS - 1, 0)
        high_down, high_up = pltpu.roll(high, 1, 0), pltpu.roll(high, ROWS - 1, 0)
        low_other = jnp.where(
            self.first_row,
            before,
            jnp.where(
                self.middle_row, low_down, jnp.where(self.last_row, high_up, low_up)
            ),
        )
        high_other = jnp.where(
            self.first_row,
            low_down,
            jnp.where(
                self.middle_row, high_down, jnp.where(self.last_row, after, high_up)
            ),
        )
        return (
            low + jnp.where(self.x_edge, low_other, 0.0),
            high + jnp.where(self.x_edge, high_other, 0.0),
        )

    def sum_y(self, tile, outer):
        other = jnp.where(self.outer_lane, outer, take(tile, self.y_swap, 1))
        return tile + jnp.where(self.y_edge, other, 0.0)

    def sum_y_pair(self, own, strip):
        own_swap, strip_swap = take(own, self.y_swap, 1), take(strip, self.y_swap, 1)
        own_other = jnp.where(self.outer_lane, strip_swap, own_swap)
        strip_other = jnp.where(self.outer_lane, own_swap, strip_swap)
        return (
            own + jnp.where(self.y_edge, own_other, 0.0),
            strip + jnp.where(self.y_edge, strip_other, 0.0),
        )


def edge_place(x, group):
    return x // ROWS, LANES // 2 * (x % 2) + ROWS * group + 2 * (x % ROWS // 2)


def edges_of(geo, packs, ref, planes, lines, first=None):
    packs = list(packs)
    for number, x in enumerate(lines):
        base = planes * (number if first is None else x - first)
        for group in range(planes // ROWS):
            q, at = edge_place(x, group)
            tile = ref[base + ROWS * group : base + ROWS * (group + 1), :]
            rolled = pltpu.roll(tile, (at + 1) % LANES, 1)
            packs[q] = jnp.where((geo.lane >> 1) == at // 2, rolled, packs[q])
    return packs


def outer_edges(joined, x, group):
    q, at = edge_place(x, group)
    return pltpu.roll(joined[q], (-(at + 1)) % LANES, 1)


def split_sides(geo, first, second, unit):
    odd = (geo.lane & unit) != 0
    return (
        jnp.where(odd, pltpu.roll(second, unit, 1), first),
        jnp.where(odd, second, pltpu.roll(first, LANES - unit, 1)),
    )


def join_sides(geo, before, after, unit):
    odd = (geo.lane & unit) != 0
    return (
        jnp.where(odd, pltpu.roll(after, unit, 1), before),
        jnp.where(odd, after, pltpu.roll(before, LANES - unit, 1)),
    )


def join_edges(geo, before, after):
    odd = (geo.lane & 1) != 0
    return (
        jnp.where(odd, pltpu.roll(before, 1, 1), after),
        jnp.where(odd, before, pltpu.roll(after, LANES - 1, 1)),
    )


def neighbours_of(blocks):
    here = lax.axis_index("blk")
    return lax.rem(here + blocks - 1, blocks), lax.rem(here + 1, blocks)


def one_hot(index, allowed=None):
    low = index & (LANES - 1)
    lane_at = iota((LANES, LANES), 0)
    if allowed is not None:
        lane_at = jnp.where(allowed(lane_at), lane_at, -1)
    return jnp.concatenate(
        [
            jnp.where(lane_at == low[c : c + 1], 1.0, 0.0).astype(jnp.bfloat16)
            for c in range(index.shape[0])
        ],
        axis=1,
    )


def scatter_sum(lines, index, bins, lanes_hot):
    split = []
    for values in lines:
        for part in range(3):
            short = values.astype(jnp.bfloat16).astype(jnp.float32)
            split.append(short)
            values = values - short
    high = index >> 7
    bin_at = iota((bins, LANES), 0)
    left = []
    for c in range(index.shape[0]):
        hit = bin_at == high[c : c + 1]
        left.append(
            jnp.concatenate(
                [jnp.where(hit, part[c : c + 1], 0.0) for part in split], axis=0
            ).astype(jnp.bfloat16)
        )
    total = lax.dot_general(
        jnp.concatenate(left, axis=1),
        lanes_hot,
        (((1,), (1,)), ((), ())),
        preferred_element_type=jnp.float32,
    )
    sums = []
    for i in range(len(lines)):
        part = total[3 * i * bins : 3 * (i + 1) * bins]
        sums.append(part[:bins] + part[bins : 2 * bins] + part[2 * bins :])
    return sums


def wind_tiles(wind_ref, x_points, level, lines):
    levels = wind_ref.shape[0] // (2 * x_points)
    return [
        [
            time_step
            * wind_ref[
                pl.ds((levels * part + level) * x_points + x, ROWS, stride=x_points), :
            ]
            for x in lines
        ]
        for part in range(2)
    ]


def start_kernel(
    planes,
    cols_in,
    weights_in,
    tracers_in,
    rows_in,
    jac_in,
    land_in,
    wind_in,
    air_in,
    send_in,
    slab_out,
    moved_ref,
    before_ref,
    after_ref,
    cols_ref,
    weights_ref,
    rows_ref,
    send_ref,
    slab_ref,
    tracers_ref,
    jac_ref,
    land_ref,
    wind_ref,
    air_ref,
    semaphores,
):
    copies = [
        pltpu.make_async_copy(source, target, semaphores.at[i])
        for i, (source, target) in enumerate(
            (
                (cols_in, cols_ref),
                (tracers_in.at[:ROWS], tracers_ref),
                (weights_in, weights_ref),
                (rows_in, rows_ref),
                (air_in, air_ref),
                (wind_in, wind_ref),
                (jac_in, jac_ref),
                (land_in, land_ref),
                (send_in, send_ref),
            )
        )
    ]
    for copy in copies:
        copy.start()
    geo = Geometry()
    blocks = cols_ref.shape[0]
    x_points = jac_ref.shape[0]
    levels = wind_ref.shape[0] // (2 * x_points)
    chunks = tracers_ref.shape[1] // LANES
    for copy in copies[:4]:
        copy.wait()

    for group in range(blocks // ROWS):
        at = slice(ROWS * group, ROWS * (group + 1))
        cells = cols_ref[at, :]
        high, low = cells >> 7, cells & (LANES - 1)
        surface = jnp.zeros((ROWS, LANES), jnp.float32)
        for k in range(chunks):
            line = spread(tracers_ref[0:1, LANES * k : LANES * (k + 1)])
            surface = jnp.where(high == k, take(line, low, 1), surface)
        area = weights_ref[at, :]
        heat = area * surface
        for c in range(ROWS):
            owner = ROWS * group + c
            for place, step in enumerate((1, 0, -1)):
                to = (owner + step) % blocks
                slab_ref[to, 2 * place : 2 * place + 1, :] = heat[c : c + 1]
                slab_ref[to, 2 * place + 1 : 2 * place + 2, :] = area[c : c + 1]

    out = pltpu.make_async_copy(slab_ref, slab_out, semaphores.at[len(copies)])
    out.start()
    ids = rows_ref[...].astype(jnp.float32)
    for side_ref in (before_ref, after_ref):
        side_ref[SIDE_IDS : SIDE_IDS + blocks, :] = ids

    for copy in copies[4:]:
        copy.wait()
    strips = []
    for h in range(2):
        half = slice(ROWS * h, ROWS * (h + 1))
        second = levels * x_points
        pack = jnp.zeros((ROWS, LANES), jnp.float32)
        for i, strip in enumerate(
            (
                air_ref[half, :],
                wind_ref[half, :],
                wind_ref[second + ROWS * h : second + ROWS * (h + 1), :],
                jac_ref[half, :],
                land_ref[half, :],
            )
        ):
            pack = jnp.where(
                (geo.lane >> 4) == i, pltpu.roll(strip, 16 * i + 8, 1), pack
            )
        strips.append(pack)
    to_right, to_left = split_sides(geo, strips[0], strips[1], ROWS)
    after_ref[SIDE_STRIP : SIDE_STRIP + ROWS, :] = to_right
    before_ref[SIDE_STRIP : SIDE_STRIP + ROWS, :] = to_left

    y_weight = jnp.where(geo.y_edge, 1.0 / 6.0, 5.0 / 6.0)
    for element in range(x_points // GLL):
        lines = [GLL * element + i for i in range(GLL)]
        mass = [
            (1.0 / 6.0 if i in (0, GLL - 1) else 5.0 / 6.0)
            * y_weight
            * spread(jac_ref[x : x + 1, :])
            for i, x in enumerate(lines)
        ]
        for level in range(0, levels, ROWS):
            wind = wind_tiles(wind_ref, x_points, level, lines)
            for plane in range(level, planes, levels):
                fields = [
                    air_ref[pl.ds(plane * x_points + x, ROWS, stride=x_points), :]
                    for x in lines
                ]
                slopes = geo.d_y(*fields)
                for i, x in enumerate(lines):
                    slope = sum(deriv_table[i][j] * fields[j] for j in range(GLL))
                    moved = mass[i] * (
                        fields[i] - (wind[0][i] * slope + wind[1][i] * slopes[i])
                    )
                    moved_ref[planes * x + plane : planes * x + plane + ROWS, :] = moved
    packs = [jnp.zeros((ROWS, LANES), jnp.float32) for _ in range(2)]
    packs = edges_of(geo, packs, moved_ref, planes, range(x_points))
    to_right, to_left = split_sides(geo, packs[0], packs[1], 1)
    after_ref[SIDE_EDGE : SIDE_EDGE + ROWS, :] = to_right
    before_ref[SIDE_EDGE : SIDE_EDGE + ROWS, :] = to_left
    out.wait()


def panel_kernel(
    planes,
    moved_ref,
    recv_ref,
    before_ref,
    after_ref,
    air_ref,
    wind_ref,
    jac_ref,
    land_ref,
    rows_ref,
    ocean_ref,
    avg_ref,
    down_ref,
    up_ref,
    surf_ref,
):
    geo = Geometry()
    blocks = rows_ref.shape[0]
    x_points = jac_ref.shape[0]
    levels = wind_ref.shape[0] // (2 * x_points)

    own_ids = rows_ref[...]
    left_ids = before_ref[SIDE_IDS : SIDE_IDS + blocks, :].astype(jnp.int32)
    right_ids = after_ref[SIDE_IDS : SIDE_IDS + blocks, :].astype(jnp.int32)
    head = [
        jnp.concatenate([recv_ref[c, i : i + 1, :] for c in range(blocks)], axis=0)
        for i in range(6)
    ]
    heat, frac = scatter_sum(head[2:4], own_ids, 2 * ROWS, one_hot(own_ids))
    from_left = scatter_sum(
        head[0:2], left_ids, 2 * ROWS, one_hot(left_ids, lambda lane: lane >= LANES - ROWS)
    )
    from_right = scatter_sum(
        head[4:6], right_ids, 2 * ROWS, one_hot(right_ids, lambda lane: lane < ROWS)
    )
    strip_heat = from_left[0] + from_right[0]
    strip_frac = from_left[1] + from_right[1]

    in_strip = (geo.lane < ROWS) | (geo.lane >= LANES - ROWS)
    packs = join_sides(
        geo,
        before_ref[SIDE_STRIP : SIDE_STRIP + ROWS, :],
        after_ref[SIDE_STRIP : SIDE_STRIP + ROWS, :],
        ROWS,
    )
    own, strip = [], []
    for h, pack in enumerate(packs):
        half = slice(ROWS * h, ROWS * (h + 1))
        strip.append(
            [
                jnp.where(
                    in_strip, pltpu.roll(pack, (-(16 * i + 8)) % LANES, 1), 1.0
                )
                for i in range(5)
            ]
        )
        own.append(
            [
                air_ref[half, :],
                wind_ref[half, :],
                wind_ref[
                    levels * x_points + ROWS * h : levels * x_points + ROWS * (h + 1), :
                ],
                jac_ref[half, :],
                land_ref[half, :],
            ]
        )
    for h in range(2):
        half = slice(ROWS * h, ROWS * (h + 1))
        pair = []
        for tile, ((field, wind_x, wind_y, jac, land), tile_heat, tile_frac) in enumerate(
            ((own[h], heat[half], frac[half]), (strip[h], strip_heat[half], strip_frac[half]))
        ):
            mass = geo.weight * jac
            if tile == 1:
                tile_heat = jnp.where(in_strip, tile_heat, 0.0)
                tile_frac = jnp.where(in_strip, tile_frac, 0.0)
            surf = (tile_heat + land * field) / (tile_frac + land)
            coef_x, coef_y = time_step * mass * wind_x, time_step * mass * wind_y
            moved = (
                mass * (field + relax_rate * (surf - field))
                - coef_x * geo.d_x(field)
                - coef_y * geo.d_y(field)[0]
            )
            pair.append((moved, mass))
            at = 2 * ROWS * tile + ROWS * h
            for number, value in (
                (MASS, mass),
                (COEF_X, coef_x),
                (COEF_Y, coef_y),
                (SURF, surf),
            ):
                surf_ref[4 * ROWS * number + at : 4 * ROWS * number + at + ROWS, :] = value
        for number, i in ((AVG, 0), (MASS_SUM, 1)):
            for tile, value in enumerate(geo.sum_y_pair(pair[0][i], pair[1][i])):
                at = 4 * ROWS * number + 2 * ROWS * tile + ROWS * h
                surf_ref[at : at + ROWS, :] = value

    joined = join_edges(
        geo,
        before_ref[SIDE_EDGE : SIDE_EDGE + ROWS, :],
        after_ref[SIDE_EDGE : SIDE_EDGE + ROWS, :],
    )
    for x in outer_rows(x_points):
        for group in range(planes // ROWS):
            at = slice(planes * x + ROWS * group, planes * x + ROWS * (group + 1))
            avg_ref[at, :] = geo.sum_y(moved_ref[at, :], outer_edges(joined, x, group))

    def line(r):
        return avg_ref[planes * r : planes * (r + 1), :]

    def surf_line(number, r):
        return surf_ref[pl.ds(4 * ROWS * number + r, 2, stride=x_points), :]

    def first_step(get, mass_at):
        return (
            [
                get(1) / mass_at(1),
                get(2) / mass_at(2),
                (get(3) + get(4)) / (mass_at(3) + mass_at(4)),
            ],
            [
                (get(11) + get(12)) / (mass_at(11) + mass_at(12)),
                get(13) / mass_at(13),
                get(14) / mass_at(14),
            ],
        )

    def own_mass_sum(r):
        return surf_ref[4 * ROWS * MASS_SUM + r : 4 * ROWS * MASS_SUM + r + 1, :]

    low_lines, high_lines = first_step(line, own_mass_sum)
    surf_low, surf_high = first_step(
        functools.partial(surf_line, AVG), functools.partial(surf_line, MASS_SUM)
    )
    for out_ref, r, lines, surf_lines, coefs in (
        (down_ref, 0, low_lines, surf_low, deriv_table[0][1:]),
        (up_ref, 15, high_lines, surf_high, deriv_table[3][:3]),
    ):
        slope = sum(coef * value for coef, value in zip(coefs, lines))
        surf_slope = sum(coef * value for coef, value in zip(coefs, surf_lines))
        mass = surf_ref[4 * ROWS * MASS + r : 4 * ROWS * MASS + r + 1, :]
        wind = time_step * mass * wind_ref[pl.ds(r, 2 * levels, stride=x_points), :]
        out_ref[0:planes, :] = line(r)
        for first in range(0, planes, levels):
            out_ref[planes + first : planes + first + levels, :] = (
                wind[:levels] * slope[first : first + levels]
            )
        base = 2 * planes
        out_ref[base : base + 2 * levels, :] = wind
        base += 2 * levels
        for number in range(SURF_ARRAYS):
            out_ref[base + 2 * number : base + 2 * number + 2, :] = surf_line(number, r)
        base += 2 * SURF_ARRAYS
        out_ref[base : base + 2, :] = surf_line(COEF_X, r) * surf_slope


def outer_rows(x_points):
    return [x for x in range(x_points) if x <= GLL or x >= x_points - GLL - 1]


def advance(geo, fields, wind, mass):
    slopes = geo.d_y(*fields)
    moved = []
    for i in range(GLL):
        slope = sum(deriv_table[i][j] * fields[j] for j in range(GLL))
        moved.append(mass[i] * (fields[i] - (wind[0][i] * slope + wind[1][i] * slopes[i])))
    return moved, slopes


def inner_kernel(
    planes, avg_ref, moved_ref, before_ref, after_ref, surf_ref, wind_ref, out_ref, packs_ref
):
    geo = Geometry()
    x_points = avg_ref.shape[0] // planes
    levels = wind_ref.shape[0] // (2 * x_points)
    joined = join_edges(
        geo,
        before_ref[SIDE_EDGE : SIDE_EDGE + ROWS, :],
        after_ref[SIDE_EDGE : SIDE_EDGE + ROWS, :],
    )
    outer = outer_rows(x_points)

    def average(x, plane):
        at = slice(planes * x + plane, planes * x + plane + ROWS)
        if x in outer:
            return avg_ref[at, :]
        return geo.sum_y(moved_ref[at, :], outer_edges(joined, x, plane // ROWS))

    def surf_row(number, x):
        at = 4 * ROWS * number + x
        return spread(surf_ref[at : at + 1, :])

    def put(x, plane, value):
        at = planes * (x - GLL) + plane
        out_ref[at : at + ROWS, :] = value

    held = {}
    carried = {}
    for element in range(1, x_points // GLL - 1):
        lines = [GLL * element + i for i in range(GLL)]
        totals = [surf_row(MASS_SUM, x) for x in lines]
        totals[0] = totals[0] + surf_row(MASS_SUM, lines[0] - 1)
        totals[-1] = totals[-1] + surf_row(MASS_SUM, lines[-1] + 1)
        scale = [1.0 / total for total in totals]
        mass = [surf_row(MASS, x) for x in lines]
        for level in range(0, levels, ROWS):
            wind = wind_tiles(wind_ref, x_points, level, lines)
            for plane in range(level, planes, levels):
                if element == 1:
                    first = average(lines[0], plane) + average(lines[0] - 1, plane)
                else:
                    first = carried[plane]
                last = average(lines[-1], plane) + average(lines[-1] + 1, plane)
                carried[plane] = last
                totals = (
                    [first] + [average(x, plane) for x in lines[1:-1]] + [last]
                )
                fields = [total * factor for total, factor in zip(totals, scale)]
                moved, _ = advance(geo, fields, wind, mass)
                if element == 1:
                    put(lines[0], plane, moved[0])
                else:
                    shared = held[plane] + moved[0]
                    put(lines[0] - 1, plane, shared)
                    put(lines[0], plane, shared)
                for i in range(1, GLL - 1):
                    put(lines[i], plane, moved[i])
                held[plane] = moved[-1]
                if lines[-1] == x_points - GLL - 1:
                    put(lines[-1], plane, moved[-1])
    packs = [jnp.zeros((ROWS, LANES), jnp.float32) for _ in range(2)]
    inner = [x for x in range(x_points) if x not in outer]
    for q, pack in enumerate(edges_of(geo, packs, out_ref, planes, inner, GLL)):
        packs_ref[ROWS * q : ROWS * (q + 1), :] = pack


def second_kernel(
    planes,
    avg_ref,
    inner_ref,
    packs_ref,
    surf_ref,
    low_ref,
    high_ref,
    wind_ref,
    rows_ref,
    ocean_ref,
    slab_out,
    sums_ref,
    final_ref,
    inverse_ref,
    flux_ref,
    edges_ref,
    semaphores,
):
    geo = Geometry()
    blocks = rows_ref.shape[0]
    left, right = neighbours_of(blocks)
    x_points = final_ref.shape[0]
    levels = wind_ref.shape[0] // (2 * x_points)
    base = low_ref.shape[0] - 2 * SURF_ARRAYS - 4

    def surf_tile(number, tile, h):
        at = 4 * ROWS * number + 2 * ROWS * tile + ROWS * h
        return surf_ref[at : at + ROWS, :]

    def beside(ref, number, tile):
        at = base + 2 * number + tile
        return spread(ref[at : at + 1, :])

    ends = []
    inverse = []
    for tile in range(2):
        total = geo.sum_x(
            surf_tile(MASS_SUM, tile, 0),
            surf_tile(MASS_SUM, tile, 1),
            beside(low_ref, MASS_SUM, tile),
            beside(high_ref, MASS_SUM, tile),
        )
        inverse.append([1.0 / value for value in total])
        summed = geo.sum_x(
            surf_tile(AVG, tile, 0),
            surf_tile(AVG, tile, 1),
            beside(low_ref, AVG, tile),
            beside(high_ref, AVG, tile),
        )
        fields = [value * scale for value, scale in zip(summed, inverse[tile])]
        moved = []
        for h in range(2):
            field = fields[h]
            moved.append(
                surf_tile(MASS, tile, h)
                * (field + relax_rate * (surf_tile(SURF, tile, h) - field))
                - surf_tile(COEF_X, tile, h) * geo.d_x(field)
                - surf_tile(COEF_Y, tile, h) * geo.d_y(field)[0]
            )
        halos = []
        for ref, field, own_coef in (
            (low_ref, spread(fields[0][:1]), deriv_table[3][3]),
            (high_ref, spread(fields[1][ROWS - 1 :]), deriv_table[0][0]),
        ):
            halos.append(
                beside(ref, MASS, tile)
                * (field + relax_rate * (beside(ref, SURF, tile) - field))
                - beside(ref, SURF_ARRAYS, tile)
                - beside(ref, COEF_X, tile) * (own_coef * field)
                - beside(ref, COEF_Y, tile) * geo.d_y(field)[0]
            )
        ends.append(geo.sum_x(moved[0], moved[1], halos[0], halos[1]))
    final = []
    for h in range(2):
        summed, _ = geo.sum_y_pair(ends[0][h], ends[1][h])
        final.append(summed * inverse[0][h])
        final_ref[ROWS * h : ROWS * (h + 1), :] = final[h]
        inverse_ref[ROWS * h : ROWS * (h + 1), :] = inverse[0][h]
    flux = [final[h] - surf_tile(SURF, 0, h) for h in range(2)]
    for group in range(blocks // ROWS):
        ids = rows_ref[ROWS * group : ROWS * (group + 1), :]
        high, low = ids >> 7, ids & (LANES - 1)
        picked = jnp.zeros((ROWS, LANES), jnp.float32)
        for x in range(2 * ROWS):
            line = spread(flux[x // ROWS][x % ROWS : x % ROWS + 1])
            picked = jnp.where(high == x, take(line, low, 1), picked)
        for c in range(ROWS):
            flux_ref[ROWS * group + c, 0:1, :] = picked[c : c + 1]

    kept = outer_rows(x_points)

    def put(x, plane, value):
        at = planes * kept.index(x) + plane
        sums_ref[at : at + ROWS, :] = value

    def beyond(ref, plane, field, slope, own_coef):
        wind_at = 2 * planes + plane % levels
        return (
            beside(ref, MASS, 0) * field
            - ref[planes + plane : planes + plane + ROWS, :]
            - ref[wind_at : wind_at + ROWS, :] * (own_coef * field)
            - ref[wind_at + levels : wind_at + levels + ROWS, :] * slope
        )

    def row_of(tiles, x):
        return spread(tiles[x // ROWS][x % ROWS : x % ROWS + 1])

    masses = [surf_tile(MASS, 0, h) for h in range(2)]
    last_element = x_points // GLL - 1
    for element in (0, last_element):
        lines = [GLL * element + i for i in range(GLL)]
        scale = [row_of(inverse[0], x) for x in lines]
        mass = [row_of(masses, x) for x in lines]
        for level in range(0, levels, ROWS):
            wind = wind_tiles(wind_ref, x_points, level, lines)
            for plane in range(level, planes, levels):
                here = slice(plane, plane + ROWS)
                fields = []
                for i, x in enumerate(lines):
                    total = avg_ref[planes * x + plane : planes * x + plane + ROWS, :]
                    other = x - 1 if i == 0 else x + 1
                    if other < 0:
                        total = total + low_ref[here, :]
                    elif other == x_points:
                        total = total + high_ref[here, :]
                    elif i in (0, GLL - 1):
                        at = planes * other + plane
                        total = total + avg_ref[at : at + ROWS, :]
                    fields.append(total * scale[i])
                moved, slopes = advance(geo, fields, wind, mass)
                if element == 0:
                    before = beyond(low_ref, plane, fields[0], slopes[0], deriv_table[3][3])
                    put(lines[0], plane, before + moved[0])
                    shared = moved[-1] + inner_ref[here, :]
                    put(lines[-1], plane, shared)
                    put(lines[-1] + 1, plane, shared)
                else:
                    at = inner_ref.shape[0] - planes + plane
                    shared = moved[0] + inner_ref[at : at + ROWS, :]
                    put(lines[0] - 1, plane, shared)
                    put(lines[0], plane, shared)
                    after = beyond(
                        high_ref, plane, fields[-1], slopes[-1], deriv_table[0][0]
                    )
                    put(lines[-1], plane, moved[-1] + after)
                for i in range(1, GLL - 1):
                    put(lines[i], plane, moved[i])
    packs = [packs_ref[:ROWS, :], packs_ref[ROWS:, :]]
    packs = edges_of(geo, packs, sums_ref, planes, kept)
    to_right, to_left = split_sides(geo, packs[0], packs[1], 1)
    edges_ref[0] = to_right
    edges_ref[1] = to_left
    copies = [
        pltpu.make_async_copy(
            edges_ref.at[i], slab_out.at[to, EDGE_AT : EDGE_AT + ROWS], semaphores.at[i]
        )
        for i, to in enumerate((right, left))
    ]
    copies.append(
        pltpu.make_async_copy(flux_ref, slab_out.at[:, :HEAD], semaphores.at[2])
    )
    for copy in copies:
        copy.start()
    for copy in copies:
        copy.wait()


def last_kernel(planes, inner_ref, outer_ref, inverse_ref, cols_ref, out_ref, hot_ref):
    geo = Geometry()
    x_points = inverse_ref.shape[0]
    kept = outer_rows(x_points)
    hot_ref[...] = one_hot(cols_ref[...])
    for x in range(x_points):
        inverse = spread(inverse_ref[x : x + 1, :])
        ref, first = inner_ref, planes * (x - GLL)
        if x in kept:
            ref, first = outer_ref, planes * kept.index(x)
        for group in range(planes // ROWS):
            tile = ref[first + ROWS * group : first + ROWS * (group + 1), :]
            at = planes * x + ROWS * group
            out_ref[at : at + ROWS, :] = inverse * geo.sum_y(tile, 0.0)


def end_kernel(
    planes,
    last_ref,
    recv_ref,
    final_ref,
    inverse_ref,
    cols_ref,
    hot_ref,
    weights_ref,
    gain_ref,
    first_ref,
    ocean_in,
    ocean_out,
    air_out,
    air_ref,
    row_ref,
    semaphores,
):
    geo = Geometry()
    blocks = cols_ref.shape[0]
    left, right = neighbours_of(blocks)
    chunks = gain_ref.shape[0]
    x_points = inverse_ref.shape[0]
    copies = []

    def send(source, target):
        copies.append(
            pltpu.make_async_copy(source, target, semaphores.at[len(copies)])
        )
        copies[-1].start()

    joined = join_edges(
        geo,
        recv_ref[left, EDGE_AT : EDGE_AT + ROWS, :],
        recv_ref[right, EDGE_AT : EDGE_AT + ROWS, :],
    )
    groups = planes // ROWS
    for group in range(groups):
        for x in range(x_points):
            at = planes * x + ROWS * group
            beside = spread(inverse_ref[x : x + 1, :]) * outer_edges(joined, x, group)
            air_ref[pl.ds(ROWS * group * x_points + x, ROWS, stride=x_points), :] = last_ref[
                at : at + ROWS, :
            ] + jnp.where(geo.outer_lane, beside, 0.0)
        if group == 0:
            air_ref[0:x_points, :] = final_ref[...]
        if group % 2:
            rows = slice(
                ROWS * (group - 1) * x_points, ROWS * (group + 1) * x_points
            )
            send(air_ref.at[rows], air_out.at[rows])
    if groups % 2:
        rows = slice(ROWS * (groups - 1) * x_points, planes * x_points)
        send(air_ref.at[rows], air_out.at[rows])

    arrived = jnp.concatenate([recv_ref[c, 0:1, :] for c in range(blocks)], axis=0)
    (inflow,) = scatter_sum(
        [weights_ref[...] * arrived], cols_ref[...], chunks, hot_ref[...]
    )
    gain = inflow * gain_ref[...]
    row_ref[...] = first_ref[...]
    for k in range(chunks):
        at = slice(LANES * k, LANES * (k + 1))
        row_ref[0:1, at] = first_ref[0:1, at] + gain[k : k + 1]
    send(row_ref, ocean_out.at[:ROWS])
    for copy in copies:
        copy.wait()


def gathered(ids, coefs, source, sources, groups, first=0):
    totals = [jnp.zeros((ROWS, LANES), jnp.float32) for _ in range(groups)]
    for edge in range(ids.shape[0]):
        cell = spread(ids[edge : edge + 1])
        coef = spread(coefs[edge : edge + 1])
        high, low = cell >> 7, cell & (LANES - 1)
        for s in range(sources):
            scaled = jnp.where(high == first + s, coef, 0.0)
            for group in range(groups):
                totals[group] += scaled * take(source(group, s), low, 1)
    return totals


def multiplied(ids, coefs, halves_ref, sources, groups):
    lane_at = iota((LANES, LANES), 0)
    hot = jnp.concatenate(
        [
            jnp.where(lane_at == (ids[edge : edge + 1] & (LANES - 1)), 1.0, 0.0).astype(
                jnp.bfloat16
            )
            for edge in range(2)
        ],
        axis=1,
    )
    picked = jnp.dot(
        halves_ref[...],
        jnp.concatenate([hot, hot], axis=0),
        preferred_element_type=jnp.float32,
    )
    totals = [jnp.zeros((ROWS, LANES), jnp.float32) for _ in range(groups)]
    for edge in range(2):
        high = spread(ids[edge : edge + 1]) >> 7
        coef = spread(coefs[edge : edge + 1])
        side = slice(LANES * edge, LANES * (edge + 1))
        for s in range(sources):
            scaled = jnp.where(high == s, coef, 0.0)
            for group in range(groups):
                at = ROWS * (groups * s + group)
                totals[group] += scaled * picked[at : at + ROWS, side]
    return totals


def ocean_kernel(
    levels, start, tracers_ref, coef_ref, near_ref, rate_ref, after_ref, out_ref, halves_ref
):
    chunks = tracers_ref.shape[1] // LANES
    groups = tracers_ref.shape[0] // ROWS
    row = iota((ROWS, LANES), 0)

    def source(group, s):
        return tracers_ref[
            ROWS * group : ROWS * (group + 1), LANES * s : LANES * (s + 1)
        ]

    planes = tracers_ref.shape[0]
    for s in range(chunks):
        values = tracers_ref[:, LANES * s : LANES * (s + 1)]
        upper = values.astype(jnp.bfloat16)
        at = slice(planes * s, planes * (s + 1))
        halves_ref[at, :LANES] = upper
        halves_ref[at, LANES:] = (values - upper.astype(jnp.float32)).astype(jnp.bfloat16)
    edges = near_ref.shape[0]

    def one_chunk(number, carry):
        k = number + start
        at = pl.ds(pl.multiple_of(k * LANES, LANES), LANES)
        out_at = pl.ds(pl.multiple_of(number * LANES, LANES), LANES)
        ids, coefs = near_ref[:, at], coef_ref[:, at]
        by_gather = edges - edges // 3 * 2
        totals = gathered(ids[:by_gather], coefs[:by_gather], source, chunks, groups)
        for edge in range(by_gather, edges, 2):
            more = multiplied(
                ids[edge : edge + 2], coefs[edge : edge + 2], halves_ref, chunks, groups
            )
            totals = [total + part for total, part in zip(totals, more)]
        coef_sum = spread(jnp.sum(coefs, axis=0, keepdims=True))
        rate = spread(rate_ref[pl.ds(k, 1), :])
        tiles = [tracers_ref[ROWS * g : ROWS * (g + 1), at] for g in range(groups)]
        for g in range(groups):
            tile = tiles[g]
            top = bottom = tile
            if (ROWS * g) % levels:
                top = pltpu.roll(tiles[g - 1], 1, 0)
            if (ROWS * (g + 1)) % levels:
                bottom = pltpu.roll(tiles[g + 1], ROWS - 1, 0)
            above = jnp.where(row == 0, top, pltpu.roll(tile, 1, 0))
            below = jnp.where(row == ROWS - 1, bottom, pltpu.roll(tile, ROWS - 1, 0))
            vertical = rate * ((above - tile) + (below - tile))
            out_ref[ROWS * g : ROWS * (g + 1), out_at] = (
                tile + (totals[g] - coef_sum * tile) + vertical
            )
        return carry

    count = out_ref.shape[1] // LANES
    step = 2 if count % 2 == 0 else 1

    def some_chunks(number, carry):
        for i in range(step):
            one_chunk(step * number + i, carry)
        return carry

    lax.fori_loop(0, count // step, some_chunks, 0)


def send_kernel(tracers_ref, send_ref, before_ref, after_ref, *out_refs):
    chunks = tracers_ref.shape[1] // LANES
    for part, (side_ref, out_ref) in enumerate(zip((before_ref, after_ref), out_refs)):
        base = side_ref.shape[0]
        out_ref[:base, :] = side_ref[...]
        cells = spread(send_ref[0:1, LANES * part : LANES * (part + 1)])
        high, low = cells >> 7, cells & (LANES - 1)
        for group in range(tracers_ref.shape[0] // ROWS):
            half = slice(ROWS * group, ROWS * (group + 1))
            rim = jnp.zeros((ROWS, LANES), jnp.float32)
            for k in range(chunks):
                tile = tracers_ref[half, LANES * k : LANES * (k + 1)]
                rim = jnp.where(high == k, take(tile, low, 1), rim)
            out_ref[base + ROWS * group : base + ROWS * (group + 1), :] = rim


def rim_kernel(
    starts,
    before_ref,
    after_ref,
    coef_ref,
    near_ref,
    area_ref,
    rows_ref,
    *refs,
):
    partial_refs, (out_ref, gain_ref, first_ref) = refs[: len(starts)], refs[len(starts) :]
    chunks = coef_ref.shape[1] // LANES
    groups = out_ref.shape[0] // ROWS
    rim_at = before_ref.shape[0] - out_ref.shape[0]
    sides = before_ref, after_ref
    gain_ref[...] = flux_gain / area_ref[...]

    def source(group, s):
        at = rim_at + ROWS * group
        return sides[s][at : at + ROWS, :]

    for k in range(chunks):
        at = slice(LANES * k, LANES * (k + 1))
        totals = gathered(near_ref[:, at], coef_ref[:, at], source, 2, groups, chunks)
        part = max(i for i, start in enumerate(starts) if start <= k)
        place = slice(LANES * (k - starts[part]), LANES * (k - starts[part] + 1))
        for g in range(groups):
            half = slice(ROWS * g, ROWS * (g + 1))
            out_ref[half, at] = partial_refs[part][half, place] + totals[g]
    first_ref[...] = out_ref[:ROWS, :]


VMEM_SPEC = pl.BlockSpec(memory_space=pltpu.VMEM)
ANY_SPEC = pl.BlockSpec(memory_space=pl.ANY)
HBM_SPEC = pl.BlockSpec(memory_space=pltpu.HBM)


def call(kernel, outs, specs, scratch=(), cost=0, hbm_outs=0, aliases=None):
    estimate = None
    if cost:
        estimate = pl.CostEstimate(flops=0, bytes_accessed=cost, transcendentals=0)
    outs = [
        out if isinstance(out, jax.ShapeDtypeStruct) else jax.ShapeDtypeStruct(out, jnp.float32)
        for out in outs
    ]
    out_specs = [VMEM_SPEC] * len(outs)
    out_specs[:hbm_outs] = [HBM_SPEC] * hbm_outs
    return pl.pallas_call(
        kernel,
        out_shape=outs,
        in_specs=specs,
        out_specs=out_specs,
        scratch_shapes=list(scratch),
        input_output_aliases=aliases or {},
        cost_estimate=estimate,
        compiler_params=pltpu.CompilerParams(vmem_limit_bytes=32 * 2**20),
        name=getattr(kernel, "func", kernel).__name__,
    )


def body(
    air_state,
    air_wind,
    jacobian,
    land_area,
    xgrid_rows,
    tracers,
    edge_coef,
    neighbours,
    vert_rate,
    ocean_area,
    send_list,
    xgrid_cols,
    xgrid_weights,
):
    field_count, levels, x_points, y_points = air_state.shape
    planes = field_count * levels
    ocean_levels, cells = tracers.shape[1:]
    ocean_planes = tracers.shape[0] * ocean_levels
    faces, blocks = lax.axis_size("face"), lax.axis_size("blk")
    air = air_state.reshape(planes * x_points, y_points)
    wind = air_wind.reshape(2 * levels * x_points, y_points)
    ocean = tracers.reshape(ocean_planes, cells)
    point_ids, cell_ids, weights = xgrid_rows[0], xgrid_cols[0], xgrid_weights[0]
    rate = vert_rate.reshape(cells // LANES, LANES)
    area = ocean_area.reshape(cells // LANES, LANES)
    first_inputs = (
        cell_ids,
        weights,
        ocean,
        point_ids,
        jacobian,
        land_area,
        wind,
        air,
        send_list,
    )
    kept = (cell_ids, weights, point_ids, send_list)
    slab, moved, to_before, to_after, cell_ids, weights, point_ids, send_list = call(
        functools.partial(start_kernel, planes),
        [(blocks, HEAD, LANES), air.shape]
        + [(SIDE_IDS + blocks, LANES)] * 2
        + [jax.ShapeDtypeStruct(array.shape, array.dtype) for array in kept],
        [HBM_SPEC] * len(first_inputs),
        [
            pltpu.VMEM(shape, jnp.float32)
            for shape in (
                (blocks, HEAD, LANES),
                (ROWS, cells),
                jacobian.shape,
                land_area.shape,
                wind.shape,
                air.shape,
            )
        ]
        + [pltpu.SemaphoreType.DMA((len(first_inputs) + 1,))],
        hbm_outs=1,
    )(*(pltpu.with_memory_space_constraint(array, pltpu.HBM) for array in first_inputs))
    recv = lax.all_to_all(slab, "blk", split_axis=0, concat_axis=0, tiled=True)

    chunks = cells // LANES
    reads_per_chunk = edge_coef.shape[0] * chunks * (ocean_planes // ROWS)
    starts = (0, chunks // 4, chunks * 3 // 4)

    def ocean_part(start, end, after):
        (result,) = call(
            functools.partial(ocean_kernel, ocean_levels, start),
            [(ocean_planes, (end - start) * LANES)],
            [VMEM_SPEC] * 4 + [ANY_SPEC],
            [pltpu.VMEM((chunks * ocean_planes, 2 * LANES), jnp.bfloat16)],
            cost=(end - start) * reads_per_chunk * ROWS * LANES * 2,
        )(ocean, edge_coef, neighbours, rate, after)
        return result

    to_before, to_after = call(
        send_kernel,
        [(SIDE_IDS + blocks + ocean_planes, LANES)] * 2,
        [VMEM_SPEC] * 4,
        cost=reads_per_chunk * ROWS * LANES,
    )(ocean, send_list, to_before, to_after)
    onward = [(i, (i + 1) % blocks) for i in range(blocks)]
    before = lax.ppermute(to_after, "blk", onward)
    after = lax.ppermute(to_before, "blk", [(to, source) for source, to in onward])
    first_part = ocean_part(starts[0], starts[1], to_before)
    side_rows = 2 * planes + 2 * levels + 2 * SURF_ARRAYS + 4
    avg, down, up, surf = call(
        functools.partial(panel_kernel, planes),
        [air.shape, (side_rows, LANES), (side_rows, LANES), (4 * ROWS * SURF_ARRAYS, LANES)],
        [VMEM_SPEC] * 9 + [ANY_SPEC],
    )(
        moved,
        recv,
        before,
        after,
        air,
        wind,
        jacobian,
        land_area,
        point_ids,
        first_part,
    )
    after_me = [(i, (i + 1) % faces) for i in range(faces)]
    low = lax.ppermute(up, "face", after_me)
    high = lax.ppermute(down, "face", [(to, source) for source, to in after_me])
    inner, packs = call(
        functools.partial(inner_kernel, planes),
        [((x_points - 2 * GLL) * planes, LANES), (2 * ROWS, LANES)],
        [VMEM_SPEC] * 6,
        cost=2 * air.size * 4,
    )(avg, moved, before, after, surf, wind)
    second_part = ocean_part(starts[1], starts[2], surf)

    slab, outer, final, inverse = call(
        functools.partial(second_kernel, planes),
        [
            (blocks, EDGE_AT + ROWS, LANES),
            (len(outer_rows(x_points)) * planes, LANES),
            (x_points, y_points),
            (x_points, y_points),
        ],
        [VMEM_SPEC] * 8 + [ANY_SPEC],
        [
            pltpu.VMEM((blocks, HEAD, LANES), jnp.float32),
            pltpu.VMEM((2, ROWS, LANES), jnp.float32),
            pltpu.SemaphoreType.DMA((3,)),
        ],
        hbm_outs=1,
    )(avg, inner, packs, surf, low, high, wind, point_ids, second_part)
    arrived = lax.all_to_all(slab, "blk", split_axis=0, concat_axis=0, tiled=True)
    last, hot = call(
        functools.partial(last_kernel, planes),
        [air.shape, jax.ShapeDtypeStruct((LANES, blocks * LANES), jnp.bfloat16)],
        [VMEM_SPEC] * 4,
        cost=2 * air.size * 4,
    )(inner, outer, inverse, cell_ids)
    third_part = ocean_part(starts[2], chunks, final)
    partial, gain, first_rows = call(
        functools.partial(rim_kernel, starts),
        [ocean.shape, area.shape, (ROWS, cells)],
        [VMEM_SPEC] * 5 + [ANY_SPEC] + [VMEM_SPEC] * len(starts),
        cost=chunks * reads_per_chunk // 8 * ROWS * LANES * 4,
    )(
        before,
        after,
        edge_coef,
        neighbours,
        area,
        final,
        first_part,
        second_part,
        third_part,
    )
    ocean_final, air_final = call(
        functools.partial(end_kernel, planes),
        [ocean.shape, air.shape],
        [VMEM_SPEC] * 9 + [HBM_SPEC],
        [
            pltpu.VMEM(air.shape, jnp.float32),
            pltpu.VMEM((ROWS, cells), jnp.float32),
            pltpu.SemaphoreType.DMA((1 + planes // ROWS,)),
        ],
        hbm_outs=2,
        aliases={9: 0},
    )(
        last,
        arrived,
        final,
        inverse,
        cell_ids,
        hot,
        weights,
        gain,
        first_rows,
        pltpu.with_memory_space_constraint(partial, pltpu.HBM),
    )
    return air_final.reshape(air_state.shape), ocean_final.reshape(tracers.shape)


def solution(mesh):
    return jax.shard_map(
        body,
        mesh=mesh,
        in_specs=(
            P(None, None, "face", "blk"),
            P(None, None, "face", "blk"),
            P("face", "blk"),
            P("face", "blk"),
            P(("face", "blk"), None, None),
            P(None, None, ("face", "blk")),
            P(None, ("face", "blk")),
            P(None, ("face", "blk")),
            P(("face", "blk")),
            P(("face", "blk")),
            P(("face", "blk"), None),
            P(("face", "blk"), None, None),
            P(("face", "blk"), None, None),
        ),
        out_specs=(P(None, None, "face", "blk"), P(None, None, ("face", "blk"))),
        check_vma=False,
    )
```

```python
import functools

import jax
import jax.numpy as jnp
from jax import lax
from jax.experimental import pallas as pl
from jax.experimental.pallas import tpu as pltpu
from jax.sharding import PartitionSpec as P

GLL = 4
ROWS = 8
LANES = 128

deriv_table = [
    [-3.0, 4.045084971874737, -1.545084971874737, 0.5],
    [-0.8090169943749475, 0.0, 1.118033988749895, -0.30901699437494745],
    [0.30901699437494745, -1.118033988749895, 0.0, 0.8090169943749475],
    [-0.5, 1.545084971874737, -4.045084971874737, 3.0],
]
time_step = 0.05
relax_rate = 0.3
flux_gain = 0.2

HEAD, EDGE_AT = 8, 8
SIDE_EDGE, SIDE_STRIP, SIDE_IDS = 0, 8, 16
AVG, MASS_SUM, MASS, COEF_X, COEF_Y, SURF = range(6)
SURF_ARRAYS = 6


def iota(shape, dim):
    return lax.broadcasted_iota(jnp.int32, shape, dim)


def take(values, index, axis):
    return jnp.take_along_axis(values, index, axis=axis, mode="promise_in_bounds")


def by_position(pos, values):
    result = jnp.full(pos.shape, values[-1], jnp.float32)
    for i, value in enumerate(values[:-1]):
        result = jnp.where(pos == i, value, result)
    return result


def spread(row):
    return jnp.broadcast_to(row, (ROWS, LANES))


class Geometry:
    def __init__(self):
        shape = (ROWS, LANES)
        self.row, self.lane = iota(shape, 0), iota(shape, 1)
        x_pos, y_pos = self.row & (GLL - 1), self.lane & (GLL - 1)
        self.y_from = [self.lane - y_pos + j for j in range(GLL)]
        columns = [[line[j] for line in deriv_table] for j in range(GLL)]
        self.x_coef = {
            step: by_position(
                x_pos,
                [
                    deriv_table[i][i + step] if 0 <= i + step < GLL else 0.0
                    for i in range(GLL)
                ],
            )
            for step in range(1 - GLL, GLL)
        }
        self.y_coef = [by_position(y_pos, column) for column in columns]
        self.y_swap = (
            self.lane + jnp.where(y_pos == GLL - 1, 1, 0) - jnp.where(y_pos == 0, 1, 0)
        ) & (LANES - 1)
        self.x_edge = (x_pos == 0) | (x_pos == GLL - 1)
        self.y_edge = (y_pos == 0) | (y_pos == GLL - 1)
        self.first_row, self.last_row = self.row == 0, self.row == ROWS - 1
        self.middle_row = self.row == GLL
        self.outer_lane = (self.lane == 0) | (self.lane == LANES - 1)
        self.weight = jnp.where(self.x_edge, 1.0 / 6.0, 5.0 / 6.0) * jnp.where(
            self.y_edge, 1.0 / 6.0, 5.0 / 6.0
        )

    def d_x(self, tile):
        return sum(
            coef * (pltpu.roll(tile, -step % ROWS, 0) if step else tile)
            for step, coef in self.x_coef.items()
        )

    def d_y(self, *tiles):
        totals = [0.0] * len(tiles)
        for j in range(GLL):
            for i, tile in enumerate(tiles):
                totals[i] += self.y_coef[j] * take(tile, self.y_from[j], 1)
        return totals

    def sum_x(self, low, high, before, after):
        low_down, low_up = pltpu.roll(low, 1, 0), pltpu.roll(low, ROWS - 1, 0)
        high_down, high_up = pltpu.roll(high, 1, 0), pltpu.roll(high, ROWS - 1, 0)
        low_other = jnp.where(
            self.first_row,
            before,
            jnp.where(
                self.middle_row, low_down, jnp.where(self.last_row, high_up, low_up)
            ),
        )
        high_other = jnp.where(
            self.first_row,
            low_down,
            jnp.where(
                self.middle_row, high_down, jnp.where(self.last_row, after, high_up)
            ),
        )
        return (
            low + jnp.where(self.x_edge, low_other, 0.0),
            high + jnp.where(self.x_edge, high_other, 0.0),
        )

    def sum_y(self, tile, outer):
        other = jnp.where(self.outer_lane, outer, take(tile, self.y_swap, 1))
        return tile + jnp.where(self.y_edge, other, 0.0)

    def sum_y_pair(self, own, strip):
        own_swap, strip_swap = take(own, self.y_swap, 1), take(strip, self.y_swap, 1)
        own_other = jnp.where(self.outer_lane, strip_swap, own_swap)
        strip_other = jnp.where(self.outer_lane, own_swap, strip_swap)
        return (
            own + jnp.where(self.y_edge, own_other, 0.0),
            strip + jnp.where(self.y_edge, strip_other, 0.0),
        )


def edge_place(x, group):
    return x // ROWS, LANES // 2 * (x % 2) + ROWS * group + 2 * (x % ROWS // 2)


def edges_of(geo, packs, ref, planes, lines, first=None):
    packs = list(packs)
    for number, x in enumerate(lines):
        base = planes * (number if first is None else x - first)
        for group in range(planes // ROWS):
            q, at = edge_place(x, group)
            tile = ref[base + ROWS * group : base + ROWS * (group + 1), :]
            rolled = pltpu.roll(tile, (at + 1) % LANES, 1)
            packs[q] = jnp.where((geo.lane >> 1) == at // 2, rolled, packs[q])
    return packs


def outer_edges(joined, x, group):
    q, at = edge_place(x, group)
    return pltpu.roll(joined[q], (-(at + 1)) % LANES, 1)


def split_sides(geo, first, second, unit):
    odd = (geo.lane & unit) != 0
    return (
        jnp.where(odd, pltpu.roll(second, unit, 1), first),
        jnp.where(odd, second, pltpu.roll(first, LANES - unit, 1)),
    )


def join_sides(geo, before, after, unit):
    odd = (geo.lane & unit) != 0
    return (
        jnp.where(odd, pltpu.roll(after, unit, 1), before),
        jnp.where(odd, after, pltpu.roll(before, LANES - unit, 1)),
    )


def join_edges(geo, before, after):
    odd = (geo.lane & 1) != 0
    return (
        jnp.where(odd, pltpu.roll(before, 1, 1), after),
        jnp.where(odd, before, pltpu.roll(after, LANES - 1, 1)),
    )


def neighbours_of(blocks):
    here = lax.axis_index("blk")
    return lax.rem(here + blocks - 1, blocks), lax.rem(here + 1, blocks)


def one_hot(index, allowed=None):
    low = index & (LANES - 1)
    lane_at = iota((LANES, LANES), 0)
    if allowed is not None:
        lane_at = jnp.where(allowed(lane_at), lane_at, -1)
    return jnp.concatenate(
        [
            jnp.where(lane_at == low[c : c + 1], 1.0, 0.0).astype(jnp.bfloat16)
            for c in range(index.shape[0])
        ],
        axis=1,
    )


def scatter_sum(lines, index, bins, lanes_hot):
    split = []
    for values in lines:
        for part in range(3):
            short = values.astype(jnp.bfloat16).astype(jnp.float32)
            split.append(short)
            values = values - short
    high = index >> 7
    bin_at = iota((bins, LANES), 0)
    left = []
    for c in range(index.shape[0]):
        hit = bin_at == high[c : c + 1]
        left.append(
            jnp.concatenate(
                [jnp.where(hit, part[c : c + 1], 0.0) for part in split], axis=0
            ).astype(jnp.bfloat16)
        )
    total = lax.dot_general(
        jnp.concatenate(left, axis=1),
        lanes_hot,
        (((1,), (1,)), ((), ())),
        preferred_element_type=jnp.float32,
    )
    sums = []
    for i in range(len(lines)):
        part = total[3 * i * bins : 3 * (i + 1) * bins]
        sums.append(part[:bins] + part[bins : 2 * bins] + part[2 * bins :])
    return sums


def wind_tiles(wind_ref, x_points, level, lines):
    levels = wind_ref.shape[0] // (2 * x_points)
    return [
        [
            time_step
            * wind_ref[
                pl.ds((levels * part + level) * x_points + x, ROWS, stride=x_points), :
            ]
            for x in lines
        ]
        for part in range(2)
    ]


def start_kernel(
    planes,
    cols_in,
    weights_in,
    tracers_in,
    rows_in,
    jac_in,
    land_in,
    wind_in,
    air_in,
    send_in,
    slab_out,
    moved_ref,
    before_ref,
    after_ref,
    cols_ref,
    weights_ref,
    rows_ref,
    send_ref,
    slab_ref,
    tracers_ref,
    jac_ref,
    land_ref,
    wind_ref,
    air_ref,
    semaphores,
):
    copies = [
        pltpu.make_async_copy(source, target, semaphores.at[i])
        for i, (source, target) in enumerate(
            (
                (cols_in, cols_ref),
                (tracers_in.at[:ROWS], tracers_ref),
                (weights_in, weights_ref),
                (rows_in, rows_ref),
                (air_in, air_ref),
                (wind_in, wind_ref),
                (jac_in, jac_ref),
                (land_in, land_ref),
                (send_in, send_ref),
            )
        )
    ]
    for copy in copies:
        copy.start()
    geo = Geometry()
    blocks = cols_ref.shape[0]
    x_points = jac_ref.shape[0]
    levels = wind_ref.shape[0] // (2 * x_points)
    chunks = tracers_ref.shape[1] // LANES
    for copy in copies[:4]:
        copy.wait()

    for group in range(blocks // ROWS):
        at = slice(ROWS * group, ROWS * (group + 1))
        cells = cols_ref[at, :]
        high, low = cells >> 7, cells & (LANES - 1)
        surface = jnp.zeros((ROWS, LANES), jnp.float32)
        for k in range(chunks):
            line = spread(tracers_ref[0:1, LANES * k : LANES * (k + 1)])
            surface = jnp.where(high == k, take(line, low, 1), surface)
        area = weights_ref[at, :]
        heat = area * surface
        for c in range(ROWS):
            owner = ROWS * group + c
            for place, step in enumerate((1, 0, -1)):
                to = (owner + step) % blocks
                slab_ref[to, 2 * place : 2 * place + 1, :] = heat[c : c + 1]
                slab_ref[to, 2 * place + 1 : 2 * place + 2, :] = area[c : c + 1]

    out = pltpu.make_async_copy(slab_ref, slab_out, semaphores.at[len(copies)])
    out.start()
    ids = rows_ref[...].astype(jnp.float32)
    for side_ref in (before_ref, after_ref):
        side_ref[SIDE_IDS : SIDE_IDS + blocks, :] = ids

    for copy in copies[4:]:
        copy.wait()
    strips = []
    for h in range(2):
        half = slice(ROWS * h, ROWS * (h + 1))
        second = levels * x_points
        pack = jnp.zeros((ROWS, LANES), jnp.float32)
        for i, strip in enumerate(
            (
                air_ref[half, :],
                wind_ref[half, :],
                wind_ref[second + ROWS * h : second + ROWS * (h + 1), :],
                jac_ref[half, :],
                land_ref[half, :],
            )
        ):
            pack = jnp.where(
                (geo.lane >> 4) == i, pltpu.roll(strip, 16 * i + 8, 1), pack
            )
        strips.append(pack)
    to_right, to_left = split_sides(geo, strips[0], strips[1], ROWS)
    after_ref[SIDE_STRIP : SIDE_STRIP + ROWS, :] = to_right
    before_ref[SIDE_STRIP : SIDE_STRIP + ROWS, :] = to_left

    y_weight = jnp.where(geo.y_edge, 1.0 / 6.0, 5.0 / 6.0)
    for element in range(x_points // GLL):
        lines = [GLL * element + i for i in range(GLL)]
        mass = [
            (1.0 / 6.0 if i in (0, GLL - 1) else 5.0 / 6.0)
            * y_weight
            * spread(jac_ref[x : x + 1, :])
            for i, x in enumerate(lines)
        ]
        for level in range(0, levels, ROWS):
            wind = wind_tiles(wind_ref, x_points, level, lines)
            for plane in range(level, planes, levels):
                fields = [
                    air_ref[pl.ds(plane * x_points + x, ROWS, stride=x_points), :]
                    for x in lines
                ]
                slopes = geo.d_y(*fields)
                for i, x in enumerate(lines):
                    slope = sum(deriv_table[i][j] * fields[j] for j in range(GLL))
                    moved = mass[i] * (
                        fields[i] - (wind[0][i] * slope + wind[1][i] * slopes[i])
                    )
                    moved_ref[planes * x + plane : planes * x + plane + ROWS, :] = moved
    packs = [jnp.zeros((ROWS, LANES), jnp.float32) for _ in range(2)]
    packs = edges_of(geo, packs, moved_ref, planes, range(x_points))
    to_right, to_left = split_sides(geo, packs[0], packs[1], 1)
    after_ref[SIDE_EDGE : SIDE_EDGE + ROWS, :] = to_right
    before_ref[SIDE_EDGE : SIDE_EDGE + ROWS, :] = to_left
    out.wait()


def panel_kernel(
    planes,
    moved_ref,
    recv_ref,
    before_ref,
    after_ref,
    air_ref,
    wind_ref,
    jac_ref,
    land_ref,
    rows_ref,
    avg_ref,
    down_ref,
    up_ref,
    surf_ref,
):
    geo = Geometry()
    blocks = rows_ref.shape[0]
    x_points = jac_ref.shape[0]
    levels = wind_ref.shape[0] // (2 * x_points)

    own_ids = rows_ref[...]
    left_ids = before_ref[SIDE_IDS : SIDE_IDS + blocks, :].astype(jnp.int32)
    right_ids = after_ref[SIDE_IDS : SIDE_IDS + blocks, :].astype(jnp.int32)
    head = [
        jnp.concatenate([recv_ref[c, i : i + 1, :] for c in range(blocks)], axis=0)
        for i in range(6)
    ]
    heat, frac = scatter_sum(head[2:4], own_ids, 2 * ROWS, one_hot(own_ids))
    from_left = scatter_sum(
        head[0:2], left_ids, 2 * ROWS, one_hot(left_ids, lambda lane: lane >= LANES - ROWS)
    )
    from_right = scatter_sum(
        head[4:6], right_ids, 2 * ROWS, one_hot(right_ids, lambda lane: lane < ROWS)
    )
    strip_heat = from_left[0] + from_right[0]
    strip_frac = from_left[1] + from_right[1]

    in_strip = (geo.lane < ROWS) | (geo.lane >= LANES - ROWS)
    packs = join_sides(
        geo,
        before_ref[SIDE_STRIP : SIDE_STRIP + ROWS, :],
        after_ref[SIDE_STRIP : SIDE_STRIP + ROWS, :],
        ROWS,
    )
    own, strip = [], []
    for h, pack in enumerate(packs):
        half = slice(ROWS * h, ROWS * (h + 1))
        strip.append(
            [
                jnp.where(
                    in_strip, pltpu.roll(pack, (-(16 * i + 8)) % LANES, 1), 1.0
                )
                for i in range(5)
            ]
        )
        own.append(
            [
                air_ref[half, :],
                wind_ref[half, :],
                wind_ref[
                    levels * x_points + ROWS * h : levels * x_points + ROWS * (h + 1), :
                ],
                jac_ref[half, :],
                land_ref[half, :],
            ]
        )
    for h in range(2):
        half = slice(ROWS * h, ROWS * (h + 1))
        pair = []
        for tile, ((field, wind_x, wind_y, jac, land), tile_heat, tile_frac) in enumerate(
            ((own[h], heat[half], frac[half]), (strip[h], strip_heat[half], strip_frac[half]))
        ):
            mass = geo.weight * jac
            if tile == 1:
                tile_heat = jnp.where(in_strip, tile_heat, 0.0)
                tile_frac = jnp.where(in_strip, tile_frac, 0.0)
            surf = (tile_heat + land * field) / (tile_frac + land)
            coef_x, coef_y = time_step * mass * wind_x, time_step * mass * wind_y
            moved = (
                mass * (field + relax_rate * (surf - field))
                - coef_x * geo.d_x(field)
                - coef_y * geo.d_y(field)[0]
            )
            pair.append((moved, mass))
            at = 2 * ROWS * tile + ROWS * h
            for number, value in (
                (MASS, mass),
                (COEF_X, coef_x),
                (COEF_Y, coef_y),
                (SURF, surf),
            ):
                surf_ref[4 * ROWS * number + at : 4 * ROWS * number + at + ROWS, :] = value
        for number, i in ((AVG, 0), (MASS_SUM, 1)):
            for tile, value in enumerate(geo.sum_y_pair(pair[0][i], pair[1][i])):
                at = 4 * ROWS * number + 2 * ROWS * tile + ROWS * h
                surf_ref[at : at + ROWS, :] = value

    joined = join_edges(
        geo,
        before_ref[SIDE_EDGE : SIDE_EDGE + ROWS, :],
        after_ref[SIDE_EDGE : SIDE_EDGE + ROWS, :],
    )
    for x in outer_rows(x_points):
        for group in range(planes // ROWS):
            at = slice(planes * x + ROWS * group, planes * x + ROWS * (group + 1))
            avg_ref[at, :] = geo.sum_y(moved_ref[at, :], outer_edges(joined, x, group))

    def line(r):
        return avg_ref[planes * r : planes * (r + 1), :]

    def surf_line(number, r):
        return surf_ref[pl.ds(4 * ROWS * number + r, 2, stride=x_points), :]

    def first_step(get, mass_at):
        return (
            [
                get(1) / mass_at(1),
                get(2) / mass_at(2),
                (get(3) + get(4)) / (mass_at(3) + mass_at(4)),
            ],
            [
                (get(11) + get(12)) / (mass_at(11) + mass_at(12)),
                get(13) / mass_at(13),
                get(14) / mass_at(14),
            ],
        )

    def own_mass_sum(r):
        return surf_ref[4 * ROWS * MASS_SUM + r : 4 * ROWS * MASS_SUM + r + 1, :]

    low_lines, high_lines = first_step(line, own_mass_sum)
    surf_low, surf_high = first_step(
        functools.partial(surf_line, AVG), functools.partial(surf_line, MASS_SUM)
    )
    for out_ref, r, lines, surf_lines, coefs in (
        (down_ref, 0, low_lines, surf_low, deriv_table[0][1:]),
        (up_ref, 15, high_lines, surf_high, deriv_table[3][:3]),
    ):
        slope = sum(coef * value for coef, value in zip(coefs, lines))
        surf_slope = sum(coef * value for coef, value in zip(coefs, surf_lines))
        mass = surf_ref[4 * ROWS * MASS + r : 4 * ROWS * MASS + r + 1, :]
        wind = time_step * mass * wind_ref[pl.ds(r, levels, stride=x_points), :]
        edge = line(r)
        columns = [edge[plane : plane + ROWS] for plane in range(0, planes, ROWS)] + [
            wind[plane % levels : plane % levels + ROWS] * slope[plane : plane + ROWS]
            for plane in range(0, planes, ROWS)
        ]
        pack = jnp.zeros((ROWS, LANES), jnp.float32)
        for i, tile in enumerate(columns):
            pack = jnp.where((geo.lane >> 1) == i, pltpu.roll(tile, 2 * i + 1, 1), pack)
        out_ref[:ROWS, :] = pack
        base = ROWS
        for number in range(SURF_ARRAYS):
            out_ref[base + 2 * number : base + 2 * number + 2, :] = surf_line(number, r)
        base += 2 * SURF_ARRAYS
        out_ref[base : base + 2, :] = surf_line(COEF_X, r) * surf_slope


def outer_rows(x_points):
    return [x for x in range(x_points) if x <= GLL or x >= x_points - GLL - 1]


def advance(geo, fields, wind, mass):
    slopes = geo.d_y(*fields)
    moved = []
    for i in range(GLL):
        slope = sum(deriv_table[i][j] * fields[j] for j in range(GLL))
        moved.append(mass[i] * (fields[i] - (wind[0][i] * slope + wind[1][i] * slopes[i])))
    return moved, slopes


def rows_kernel(planes, moved_ref, wind_ref, jac_ref, before_ref, down_ref, up_ref):
    geo = Geometry()
    x_points = jac_ref.shape[0]
    levels = wind_ref.shape[0] // (2 * x_points)
    y_weight = jnp.where(geo.y_edge, 1.0 / 6.0, 5.0 / 6.0)

    def mass_of(x):
        x_weight = 1.0 / 6.0 if x % GLL in (0, GLL - 1) else 5.0 / 6.0
        return x_weight * y_weight * spread(jac_ref[x : x + 1, :])

    for out_ref, r, inward, coefs in (
        (down_ref, 0, 1, deriv_table[0][1:]),
        (up_ref, x_points - 1, -1, deriv_table[3][2::-1]),
    ):
        lines = [r + inward * step for step in range(1, GLL + 1)]
        totals = [geo.sum_y(mass_of(x), 0.0) for x in lines]
        totals = totals[:-2] + [totals[-2] + totals[-1]]
        factors = [coef / total for coef, total in zip(coefs, totals)]
        mass = mass_of(r)
        for level in range(0, levels, ROWS):
            wind = [tiles[0] * mass for tiles in wind_tiles(wind_ref, x_points, level, [r])]
            for part, tile in enumerate(wind):
                at = 2 * planes + levels * part + level
                out_ref[at : at + ROWS, :] = tile
            for plane in range(level, planes, levels):
                sums = [
                    geo.sum_y(moved_ref[planes * x + plane : planes * x + plane + ROWS, :], 0.0)
                    for x in [r] + lines
                ]
                edge, inner = sums[0], sums[1:-2] + [sums[-2] + sums[-1]]
                slope = sum(factor * total for factor, total in zip(factors, inner))
                out_ref[plane : plane + ROWS, :] = edge
                out_ref[planes + plane : planes + plane + ROWS, :] = wind[0] * slope


def inner_kernel(
    planes,
    avg_ref,
    moved_ref,
    before_ref,
    after_ref,
    surf_ref,
    wind_ref,
    ocean_ref,
    out_ref,
    packs_ref,
):
    geo = Geometry()
    x_points = avg_ref.shape[0] // planes
    levels = wind_ref.shape[0] // (2 * x_points)
    joined = join_edges(
        geo,
        before_ref[SIDE_EDGE : SIDE_EDGE + ROWS, :],
        after_ref[SIDE_EDGE : SIDE_EDGE + ROWS, :],
    )
    outer = outer_rows(x_points)

    def average(x, plane):
        at = slice(planes * x + plane, planes * x + plane + ROWS)
        if x in outer:
            return avg_ref[at, :]
        return geo.sum_y(moved_ref[at, :], outer_edges(joined, x, plane // ROWS))

    def surf_row(number, x):
        at = 4 * ROWS * number + x
        return spread(surf_ref[at : at + 1, :])

    def put(x, plane, value):
        at = planes * (x - GLL) + plane
        out_ref[at : at + ROWS, :] = value

    held = {}
    carried = {}
    for element in range(1, x_points // GLL - 1):
        lines = [GLL * element + i for i in range(GLL)]
        totals = [surf_row(MASS_SUM, x) for x in lines]
        totals[0] = totals[0] + surf_row(MASS_SUM, lines[0] - 1)
        totals[-1] = totals[-1] + surf_row(MASS_SUM, lines[-1] + 1)
        scale = [1.0 / total for total in totals]
        mass = [surf_row(MASS, x) for x in lines]
        for level in range(0, levels, ROWS):
            wind = wind_tiles(wind_ref, x_points, level, lines)
            for plane in range(level, planes, levels):
                if element == 1:
                    first = average(lines[0], plane) + average(lines[0] - 1, plane)
                else:
                    first = carried[plane]
                last = average(lines[-1], plane) + average(lines[-1] + 1, plane)
                carried[plane] = last
                totals = (
                    [first] + [average(x, plane) for x in lines[1:-1]] + [last]
                )
                fields = [total * factor for total, factor in zip(totals, scale)]
                moved, _ = advance(geo, fields, wind, mass)
                if element == 1:
                    put(lines[0], plane, moved[0])
                else:
                    shared = held[plane] + moved[0]
                    put(lines[0] - 1, plane, shared)
                    put(lines[0], plane, shared)
                for i in range(1, GLL - 1):
                    put(lines[i], plane, moved[i])
                held[plane] = moved[-1]
                if lines[-1] == x_points - GLL - 1:
                    put(lines[-1], plane, moved[-1])
    packs = [jnp.zeros((ROWS, LANES), jnp.float32) for _ in range(2)]
    inner = [x for x in range(x_points) if x not in outer]
    for q, pack in enumerate(edges_of(geo, packs, out_ref, planes, inner, GLL)):
        packs_ref[ROWS * q : ROWS * (q + 1), :] = pack


def second_kernel(
    planes,
    avg_ref,
    inner_ref,
    packs_ref,
    surf_ref,
    early_low_ref,
    early_high_ref,
    low_ref,
    high_ref,
    wind_ref,
    rows_ref,
    slab_out,
    sums_ref,
    final_ref,
    inverse_ref,
    flux_ref,
    edges_ref,
    semaphores,
):
    geo = Geometry()
    blocks = rows_ref.shape[0]
    left, right = neighbours_of(blocks)
    x_points = final_ref.shape[0]
    levels = wind_ref.shape[0] // (2 * x_points)
    base = ROWS

    def surf_tile(number, tile, h):
        at = 4 * ROWS * number + 2 * ROWS * tile + ROWS * h
        return surf_ref[at : at + ROWS, :]

    def beside(ref, number, tile):
        at = base + 2 * number + tile
        return spread(ref[at : at + 1, :])

    ends = []
    inverse = []
    for tile in range(2):
        total = geo.sum_x(
            surf_tile(MASS_SUM, tile, 0),
            surf_tile(MASS_SUM, tile, 1),
            beside(low_ref, MASS_SUM, tile),
            beside(high_ref, MASS_SUM, tile),
        )
        inverse.append([1.0 / value for value in total])
        summed = geo.sum_x(
            surf_tile(AVG, tile, 0),
            surf_tile(AVG, tile, 1),
            beside(low_ref, AVG, tile),
            beside(high_ref, AVG, tile),
        )
        fields = [value * scale for value, scale in zip(summed, inverse[tile])]
        moved = []
        for h in range(2):
            field = fields[h]
            moved.append(
                surf_tile(MASS, tile, h)
                * (field + relax_rate * (surf_tile(SURF, tile, h) - field))
                - surf_tile(COEF_X, tile, h) * geo.d_x(field)
                - surf_tile(COEF_Y, tile, h) * geo.d_y(field)[0]
            )
        halos = []
        for ref, field, own_coef in (
            (low_ref, spread(fields[0][:1]), deriv_table[3][3]),
            (high_ref, spread(fields[1][ROWS - 1 :]), deriv_table[0][0]),
        ):
            halos.append(
                beside(ref, MASS, tile)
                * (field + relax_rate * (beside(ref, SURF, tile) - field))
                - beside(ref, SURF_ARRAYS, tile)
                - beside(ref, COEF_X, tile) * (own_coef * field)
                - beside(ref, COEF_Y, tile) * geo.d_y(field)[0]
            )
        ends.append(geo.sum_x(moved[0], moved[1], halos[0], halos[1]))
    final = []
    for h in range(2):
        summed, _ = geo.sum_y_pair(ends[0][h], ends[1][h])
        final.append(summed * inverse[0][h])
        final_ref[ROWS * h : ROWS * (h + 1), :] = final[h]
        inverse_ref[ROWS * h : ROWS * (h + 1), :] = inverse[0][h]
    flux = [final[h] - surf_tile(SURF, 0, h) for h in range(2)]
    for group in range(blocks // ROWS):
        ids = rows_ref[ROWS * group : ROWS * (group + 1), :]
        high, low = ids >> 7, ids & (LANES - 1)
        picked = jnp.zeros((ROWS, LANES), jnp.float32)
        for x in range(2 * ROWS):
            line = spread(flux[x // ROWS][x % ROWS : x % ROWS + 1])
            picked = jnp.where(high == x, take(line, low, 1), picked)
        for c in range(ROWS):
            flux_ref[ROWS * group + c, 0:1, :] = picked[c : c + 1]

    kept = outer_rows(x_points)

    def put(x, plane, value):
        at = planes * kept.index(x) + plane
        sums_ref[at : at + ROWS, :] = value

    def fixed(early_ref, ref, number):
        late = pltpu.roll(ref[:ROWS, :], (-(2 * number + 1)) % LANES, 1)
        early = early_ref[ROWS * number : ROWS * (number + 1), :]
        return jnp.where(geo.outer_lane, late, early)

    def beyond(early_ref, ref, plane, field, slope, own_coef):
        wind_at = 2 * planes + plane % levels
        return (
            beside(ref, MASS, 0) * field
            - fixed(early_ref, ref, (planes + plane) // ROWS)
            - early_ref[wind_at : wind_at + ROWS, :] * (own_coef * field)
            - early_ref[wind_at + levels : wind_at + levels + ROWS, :] * slope
        )

    def row_of(tiles, x):
        return spread(tiles[x // ROWS][x % ROWS : x % ROWS + 1])

    masses = [surf_tile(MASS, 0, h) for h in range(2)]
    last_element = x_points // GLL - 1
    for element in (0, last_element):
        lines = [GLL * element + i for i in range(GLL)]
        scale = [row_of(inverse[0], x) for x in lines]
        mass = [row_of(masses, x) for x in lines]
        for level in range(0, levels, ROWS):
            wind = wind_tiles(wind_ref, x_points, level, lines)
            for plane in range(level, planes, levels):
                here = slice(plane, plane + ROWS)
                fields = []
                for i, x in enumerate(lines):
                    total = avg_ref[planes * x + plane : planes * x + plane + ROWS, :]
                    other = x - 1 if i == 0 else x + 1
                    if other < 0:
                        total = total + fixed(early_low_ref, low_ref, plane // ROWS)
                    elif other == x_points:
                        total = total + fixed(early_high_ref, high_ref, plane // ROWS)
                    elif i in (0, GLL - 1):
                        at = planes * other + plane
                        total = total + avg_ref[at : at + ROWS, :]
                    fields.append(total * scale[i])
                moved, slopes = advance(geo, fields, wind, mass)
                if element == 0:
                    before = beyond(
                        early_low_ref, low_ref, plane, fields[0], slopes[0], deriv_table[3][3]
                    )
                    put(lines[0], plane, before + moved[0])
                    shared = moved[-1] + inner_ref[here, :]
                    put(lines[-1], plane, shared)
                    put(lines[-1] + 1, plane, shared)
                else:
                    at = inner_ref.shape[0] - planes + plane
                    shared = moved[0] + inner_ref[at : at + ROWS, :]
                    put(lines[0] - 1, plane, shared)
                    put(lines[0], plane, shared)
                    after = beyond(
                        early_high_ref, high_ref, plane, fields[-1], slopes[-1], deriv_table[0][0]
                    )
                    put(lines[-1], plane, moved[-1] + after)
                for i in range(1, GLL - 1):
                    put(lines[i], plane, moved[i])
    packs = [packs_ref[:ROWS, :], packs_ref[ROWS:, :]]
    packs = edges_of(geo, packs, sums_ref, planes, kept)
    to_right, to_left = split_sides(geo, packs[0], packs[1], 1)
    edges_ref[0] = to_right
    edges_ref[1] = to_left
    copies = [
        pltpu.make_async_copy(
            edges_ref.at[i], slab_out.at[to, EDGE_AT : EDGE_AT + ROWS], semaphores.at[i]
        )
        for i, to in enumerate((right, left))
    ]
    copies.append(
        pltpu.make_async_copy(flux_ref, slab_out.at[:, :HEAD], semaphores.at[2])
    )
    for copy in copies:
        copy.start()
    for copy in copies:
        copy.wait()


def last_kernel(planes, inner_ref, outer_ref, inverse_ref, cols_ref, out_ref, hot_ref):
    geo = Geometry()
    x_points = inverse_ref.shape[0]
    kept = outer_rows(x_points)
    hot_ref[...] = one_hot(cols_ref[...])
    for x in range(x_points):
        inverse = spread(inverse_ref[x : x + 1, :])
        ref, first = inner_ref, planes * (x - GLL)
        if x in kept:
            ref, first = outer_ref, planes * kept.index(x)
        for group in range(planes // ROWS):
            tile = ref[first + ROWS * group : first + ROWS * (group + 1), :]
            at = planes * x + ROWS * group
            out_ref[at : at + ROWS, :] = inverse * geo.sum_y(tile, 0.0)


def end_kernel(
    planes,
    last_ref,
    recv_ref,
    final_ref,
    inverse_ref,
    cols_ref,
    hot_ref,
    weights_ref,
    gain_ref,
    ocean_ref,
    air_out,
    ocean_out,
    air_ref,
    row_ref,
    semaphores,
):
    geo = Geometry()
    blocks = cols_ref.shape[0]
    left, right = neighbours_of(blocks)
    chunks = gain_ref.shape[0]
    x_points = inverse_ref.shape[0]
    copies = []

    def send(source, target):
        copies.append(
            pltpu.make_async_copy(source, target, semaphores.at[len(copies)])
        )
        copies[-1].start()

    send(ocean_ref.at[ROWS:], ocean_out.at[ROWS:])
    joined = join_edges(
        geo,
        recv_ref[left, EDGE_AT : EDGE_AT + ROWS, :],
        recv_ref[right, EDGE_AT : EDGE_AT + ROWS, :],
    )
    groups = planes // ROWS
    for group in range(groups):
        for x in range(x_points):
            at = planes * x + ROWS * group
            beside = spread(inverse_ref[x : x + 1, :]) * outer_edges(joined, x, group)
            air_ref[pl.ds(ROWS * group * x_points + x, ROWS, stride=x_points), :] = last_ref[
                at : at + ROWS, :
            ] + jnp.where(geo.outer_lane, beside, 0.0)
        if group == 0:
            air_ref[0:x_points, :] = final_ref[...]
        if group % 2:
            rows = slice(
                ROWS * (group - 1) * x_points, ROWS * (group + 1) * x_points
            )
            send(air_ref.at[rows], air_out.at[rows])
    if groups % 2:
        rows = slice(ROWS * (groups - 1) * x_points, planes * x_points)
        send(air_ref.at[rows], air_out.at[rows])

    arrived = jnp.concatenate([recv_ref[c, 0:1, :] for c in range(blocks)], axis=0)
    (inflow,) = scatter_sum(
        [weights_ref[...] * arrived], cols_ref[...], chunks, hot_ref[...]
    )
    gain = inflow * gain_ref[...]
    row_ref[...] = ocean_ref[:ROWS, :]
    for k in range(chunks):
        at = slice(LANES * k, LANES * (k + 1))
        row_ref[0:1, at] = ocean_ref[0:1, at] + gain[k : k + 1]
    send(row_ref, ocean_out.at[:ROWS])
    for copy in copies:
        copy.wait()


def gathered(ids, coefs, source, sources, groups, first=0):
    totals = [jnp.zeros((ROWS, LANES), jnp.float32) for _ in range(groups)]
    for edge in range(ids.shape[0]):
        cell = spread(ids[edge : edge + 1])
        coef = spread(coefs[edge : edge + 1])
        high, low = cell >> 7, cell & (LANES - 1)
        for s in range(sources):
            scaled = jnp.where(high == first + s, coef, 0.0)
            for group in range(groups):
                totals[group] += scaled * take(source(group, s), low, 1)
    return totals


def multiplied(ids, coefs, halves_ref, sources, groups):
    lane_at = iota((LANES, LANES), 0)
    hot = jnp.concatenate(
        [
            jnp.where(lane_at == (ids[edge : edge + 1] & (LANES - 1)), 1.0, 0.0).astype(
                jnp.bfloat16
            )
            for edge in range(2)
        ],
        axis=1,
    )
    picked = jnp.dot(
        halves_ref[...],
        jnp.concatenate([hot, hot], axis=0),
        preferred_element_type=jnp.float32,
    )
    totals = [jnp.zeros((ROWS, LANES), jnp.float32) for _ in range(groups)]
    for edge in range(2):
        high = spread(ids[edge : edge + 1]) >> 7
        coef = spread(coefs[edge : edge + 1])
        side = slice(LANES * edge, LANES * (edge + 1))
        for s in range(sources):
            scaled = jnp.where(high == s, coef, 0.0)
            for group in range(groups):
                at = ROWS * (groups * s + group)
                totals[group] += scaled * picked[at : at + ROWS, side]
    return totals


def ocean_kernel(
    levels, start, tracers_ref, coef_ref, near_ref, rate_ref, after_ref, out_ref, halves_ref
):
    chunks = tracers_ref.shape[1] // LANES
    groups = tracers_ref.shape[0] // ROWS
    row = iota((ROWS, LANES), 0)

    def source(group, s):
        return tracers_ref[
            ROWS * group : ROWS * (group + 1), LANES * s : LANES * (s + 1)
        ]

    planes = tracers_ref.shape[0]
    for s in range(chunks):
        values = tracers_ref[:, LANES * s : LANES * (s + 1)]
        upper = values.astype(jnp.bfloat16)
        at = slice(planes * s, planes * (s + 1))
        halves_ref[at, :LANES] = upper
        halves_ref[at, LANES:] = (values - upper.astype(jnp.float32)).astype(jnp.bfloat16)
    edges = near_ref.shape[0]

    def one_chunk(number, carry):
        k = number + start
        at = pl.ds(pl.multiple_of(k * LANES, LANES), LANES)
        out_at = pl.ds(pl.multiple_of(number * LANES, LANES), LANES)
        ids, coefs = near_ref[:, at], coef_ref[:, at]
        by_gather = edges - edges // 3 * 2
        totals = gathered(ids[:by_gather], coefs[:by_gather], source, chunks, groups)
        for edge in range(by_gather, edges, 2):
            more = multiplied(
                ids[edge : edge + 2], coefs[edge : edge + 2], halves_ref, chunks, groups
            )
            totals = [total + part for total, part in zip(totals, more)]
        coef_sum = spread(jnp.sum(coefs, axis=0, keepdims=True))
        rate = spread(rate_ref[pl.ds(k, 1), :])
        tiles = [tracers_ref[ROWS * g : ROWS * (g + 1), at] for g in range(groups)]
        for g in range(groups):
            tile = tiles[g]
            top = bottom = tile
            if (ROWS * g) % levels:
                top = pltpu.roll(tiles[g - 1], 1, 0)
            if (ROWS * (g + 1)) % levels:
                bottom = pltpu.roll(tiles[g + 1], ROWS - 1, 0)
            above = jnp.where(row == 0, top, pltpu.roll(tile, 1, 0))
            below = jnp.where(row == ROWS - 1, bottom, pltpu.roll(tile, ROWS - 1, 0))
            vertical = rate * ((above - tile) + (below - tile))
            out_ref[ROWS * g : ROWS * (g + 1), out_at] = (
                tile + (totals[g] - coef_sum * tile) + vertical
            )
        return carry

    count = out_ref.shape[1] // LANES
    step = 2 if count % 2 == 0 else 1

    def some_chunks(number, carry):
        for i in range(step):
            one_chunk(step * number + i, carry)
        return carry

    lax.fori_loop(0, count // step, some_chunks, 0)


def send_kernel(tracers_ref, send_ref, before_ref, after_ref, *out_refs):
    chunks = tracers_ref.shape[1] // LANES
    for part, (side_ref, out_ref) in enumerate(zip((before_ref, after_ref), out_refs)):
        base = side_ref.shape[0]
        out_ref[:base, :] = side_ref[...]
        cells = spread(send_ref[0:1, LANES * part : LANES * (part + 1)])
        high, low = cells >> 7, cells & (LANES - 1)
        for group in range(tracers_ref.shape[0] // ROWS):
            half = slice(ROWS * group, ROWS * (group + 1))
            rim = jnp.zeros((ROWS, LANES), jnp.float32)
            for k in range(chunks):
                tile = tracers_ref[half, LANES * k : LANES * (k + 1)]
                rim = jnp.where(high == k, take(tile, low, 1), rim)
            out_ref[base + ROWS * group : base + ROWS * (group + 1), :] = rim


def rim_kernel(
    starts,
    before_ref,
    after_ref,
    coef_ref,
    near_ref,
    area_ref,
    rows_ref,
    *refs,
):
    partial_refs, (out_ref, gain_ref) = refs[: len(starts)], refs[len(starts) :]
    chunks = coef_ref.shape[1] // LANES
    groups = out_ref.shape[0] // ROWS
    rim_at = before_ref.shape[0] - out_ref.shape[0]
    sides = before_ref, after_ref
    gain_ref[...] = flux_gain / area_ref[...]

    def source(group, s):
        at = rim_at + ROWS * group
        return sides[s][at : at + ROWS, :]

    for k in range(chunks):
        at = slice(LANES * k, LANES * (k + 1))
        totals = gathered(near_ref[:, at], coef_ref[:, at], source, 2, groups, chunks)
        part = max(i for i, start in enumerate(starts) if start <= k)
        place = slice(LANES * (k - starts[part]), LANES * (k - starts[part] + 1))
        for g in range(groups):
            half = slice(ROWS * g, ROWS * (g + 1))
            out_ref[half, at] = partial_refs[part][half, place] + totals[g]


VMEM_SPEC = pl.BlockSpec(memory_space=pltpu.VMEM)
ANY_SPEC = pl.BlockSpec(memory_space=pl.ANY)
HBM_SPEC = pl.BlockSpec(memory_space=pltpu.HBM)


def call(kernel, outs, specs, scratch=(), cost=0, hbm_outs=0):
    estimate = None
    if cost:
        estimate = pl.CostEstimate(flops=cost * 1000, bytes_accessed=cost, transcendentals=0)
    outs = [
        out if isinstance(out, jax.ShapeDtypeStruct) else jax.ShapeDtypeStruct(out, jnp.float32)
        for out in outs
    ]
    out_specs = [VMEM_SPEC] * len(outs)
    out_specs[:hbm_outs] = [HBM_SPEC] * hbm_outs
    return pl.pallas_call(
        kernel,
        out_shape=outs,
        in_specs=specs,
        out_specs=out_specs,
        scratch_shapes=list(scratch),
        cost_estimate=estimate,
        compiler_params=pltpu.CompilerParams(vmem_limit_bytes=32 * 2**20),
        name=getattr(kernel, "func", kernel).__name__,
    )


def body(
    air_state,
    air_wind,
    jacobian,
    land_area,
    xgrid_rows,
    tracers,
    edge_coef,
    neighbours,
    vert_rate,
    ocean_area,
    send_list,
    xgrid_cols,
    xgrid_weights,
):
    field_count, levels, x_points, y_points = air_state.shape
    planes = field_count * levels
    ocean_levels, cells = tracers.shape[1:]
    ocean_planes = tracers.shape[0] * ocean_levels
    faces, blocks = lax.axis_size("face"), lax.axis_size("blk")
    air = air_state.reshape(planes * x_points, y_points)
    wind = air_wind.reshape(2 * levels * x_points, y_points)
    ocean = tracers.reshape(ocean_planes, cells)
    point_ids, cell_ids, weights = xgrid_rows[0], xgrid_cols[0], xgrid_weights[0]
    rate = vert_rate.reshape(cells // LANES, LANES)
    area = ocean_area.reshape(cells // LANES, LANES)
    first_inputs = (
        cell_ids,
        weights,
        ocean,
        point_ids,
        jacobian,
        land_area,
        wind,
        air,
        send_list,
    )
    kept = (cell_ids, weights, point_ids, send_list)
    slab, moved, to_before, to_after, cell_ids, weights, point_ids, send_list = call(
        functools.partial(start_kernel, planes),
        [(blocks, HEAD, LANES), air.shape]
        + [(SIDE_IDS + blocks, LANES)] * 2
        + [jax.ShapeDtypeStruct(array.shape, array.dtype) for array in kept],
        [HBM_SPEC] * len(first_inputs),
        [
            pltpu.VMEM(shape, jnp.float32)
            for shape in (
                (blocks, HEAD, LANES),
                (ROWS, cells),
                jacobian.shape,
                land_area.shape,
                wind.shape,
                air.shape,
            )
        ]
        + [pltpu.SemaphoreType.DMA((len(first_inputs) + 1,))],
        hbm_outs=1,
    )(*(pltpu.with_memory_space_constraint(array, pltpu.HBM) for array in first_inputs))
    recv = lax.all_to_all(slab, "blk", split_axis=0, concat_axis=0, tiled=True)

    chunks = cells // LANES
    reads_per_chunk = edge_coef.shape[0] * chunks * (ocean_planes // ROWS)
    starts = (0, chunks * 6 // 16)

    def ocean_part(start, end, after):
        (result,) = call(
            functools.partial(ocean_kernel, ocean_levels, start),
            [(ocean_planes, (end - start) * LANES)],
            [VMEM_SPEC] * 4 + [ANY_SPEC],
            [pltpu.VMEM((chunks * ocean_planes, 2 * LANES), jnp.bfloat16)],
            cost=(end - start) * reads_per_chunk * ROWS * LANES * 2,
        )(ocean, edge_coef, neighbours, rate, after)
        return result

    to_before, to_after = call(
        send_kernel,
        [(SIDE_IDS + blocks + ocean_planes, LANES)] * 2,
        [VMEM_SPEC] * 4,
        cost=reads_per_chunk * ROWS * LANES,
    )(ocean, send_list, to_before, to_after)
    onward = [(i, (i + 1) % blocks) for i in range(blocks)]
    before = lax.ppermute(to_after, "blk", onward)
    after = lax.ppermute(to_before, "blk", [(to, source) for source, to in onward])
    down, up = call(
        functools.partial(rows_kernel, planes),
        [(2 * planes + 2 * levels, LANES)] * 2,
        [VMEM_SPEC] * 3 + [ANY_SPEC],
    )(moved, wind, jacobian, to_before)
    after_me = [(i, (i + 1) % faces) for i in range(faces)]
    before_me = [(to, source) for source, to in after_me]
    early_low = lax.ppermute(up, "face", after_me)
    early_high = lax.ppermute(down, "face", before_me)

    side_rows = ROWS + 2 * SURF_ARRAYS + 4
    avg, down, up, surf = call(
        functools.partial(panel_kernel, planes),
        [air.shape, (side_rows, LANES), (side_rows, LANES), (4 * ROWS * SURF_ARRAYS, LANES)],
        [VMEM_SPEC] * 9,
        cost=60 * air.size * 4,
    )(
        moved,
        recv,
        before,
        after,
        air,
        wind,
        jacobian,
        land_area,
        point_ids,
    )
    low = lax.ppermute(up, "face", after_me)
    high = lax.ppermute(down, "face", before_me)
    first_part = ocean_part(starts[0], starts[1], surf)
    inner, packs = call(
        functools.partial(inner_kernel, planes),
        [((x_points - 2 * GLL) * planes, LANES), (2 * ROWS, LANES)],
        [VMEM_SPEC] * 6 + [ANY_SPEC],
        cost=40 * air.size * 4,
    )(avg, moved, before, after, surf, wind, first_part)

    slab, outer, final, inverse = call(
        functools.partial(second_kernel, planes),
        [
            (blocks, EDGE_AT + ROWS, LANES),
            (len(outer_rows(x_points)) * planes, LANES),
            (x_points, y_points),
            (x_points, y_points),
        ],
        [VMEM_SPEC] * 10,
        [
            pltpu.VMEM((blocks, HEAD, LANES), jnp.float32),
            pltpu.VMEM((2, ROWS, LANES), jnp.float32),
            pltpu.SemaphoreType.DMA((3,)),
        ],
        hbm_outs=1,
    )(avg, inner, packs, surf, early_low, early_high, low, high, wind, point_ids)
    arrived = lax.all_to_all(slab, "blk", split_axis=0, concat_axis=0, tiled=True)
    last, hot = call(
        functools.partial(last_kernel, planes),
        [air.shape, jax.ShapeDtypeStruct((LANES, blocks * LANES), jnp.bfloat16)],
        [VMEM_SPEC] * 4,
        cost=2 * air.size * 4,
    )(inner, outer, inverse, cell_ids)
    second_part = ocean_part(starts[1], chunks, final)
    partial, gain = call(
        functools.partial(rim_kernel, starts),
        [ocean.shape, area.shape],
        [VMEM_SPEC] * 5 + [ANY_SPEC] + [VMEM_SPEC] * len(starts),
        cost=chunks * reads_per_chunk // 8 * ROWS * LANES * 4,
    )(
        before,
        after,
        edge_coef,
        neighbours,
        area,
        final,
        first_part,
        second_part,
    )
    air_final, ocean_final = call(
        functools.partial(end_kernel, planes),
        [air.shape, ocean.shape],
        [VMEM_SPEC] * 9,
        [
            pltpu.VMEM(air.shape, jnp.float32),
            pltpu.VMEM((ROWS, cells), jnp.float32),
            pltpu.SemaphoreType.DMA((2 + planes // ROWS,)),
        ],
        hbm_outs=2,
    )(last, arrived, final, inverse, cell_ids, hot, weights, gain, partial)
    return air_final.reshape(air_state.shape), ocean_final.reshape(tracers.shape)


def solution(mesh):
    return jax.shard_map(
        body,
        mesh=mesh,
        in_specs=(
            P(None, None, "face", "blk"),
            P(None, None, "face", "blk"),
            P("face", "blk"),
            P("face", "blk"),
            P(("face", "blk"), None, None),
            P(None, None, ("face", "blk")),
            P(None, ("face", "blk")),
            P(None, ("face", "blk")),
            P(("face", "blk")),
            P(("face", "blk")),
            P(("face", "blk"), None),
            P(("face", "blk"), None, None),
            P(("face", "blk"), None, None),
        ),
        out_specs=(P(None, None, "face", "blk"), P(None, None, ("face", "blk"))),
        check_vma=False,
    )
```

```python
import functools

import jax
import jax.numpy as jnp
from jax import lax
from jax.experimental import pallas as pl
from jax.experimental.pallas import tpu as pltpu
from jax.sharding import PartitionSpec as P

GLL = 4
ROWS = 8
LANES = 128

deriv_table = [
    [-3.0, 4.045084971874737, -1.545084971874737, 0.5],
    [-0.8090169943749475, 0.0, 1.118033988749895, -0.30901699437494745],
    [0.30901699437494745, -1.118033988749895, 0.0, 0.8090169943749475],
    [-0.5, 1.545084971874737, -4.045084971874737, 3.0],
]
time_step = 0.05
relax_rate = 0.3
flux_gain = 0.2

HEAD, EDGE_AT = 8, 8
SIDE_EDGE, SIDE_STRIP, SIDE_IDS = 0, 8, 16
AVG, MASS_SUM, MASS, COEF_X, COEF_Y, SURF = range(6)
SURF_ARRAYS = 6


def iota(shape, dim):
    return lax.broadcasted_iota(jnp.int32, shape, dim)


def take(values, index, axis):
    return jnp.take_along_axis(values, index, axis=axis, mode="promise_in_bounds")


def by_position(pos, values):
    result = jnp.full(pos.shape, values[-1], jnp.float32)
    for i, value in enumerate(values[:-1]):
        result = jnp.where(pos == i, value, result)
    return result


def spread(row):
    return jnp.broadcast_to(row, (ROWS, LANES))


class Geometry:
    def __init__(self):
        shape = (ROWS, LANES)
        self.row, self.lane = iota(shape, 0), iota(shape, 1)
        x_pos, y_pos = self.row & (GLL - 1), self.lane & (GLL - 1)
        self.y_from = [self.lane - y_pos + j for j in range(GLL)]
        columns = [[line[j] for line in deriv_table] for j in range(GLL)]
        self.x_coef = {
            step: by_position(
                x_pos,
                [
                    deriv_table[i][i + step] if 0 <= i + step < GLL else 0.0
                    for i in range(GLL)
                ],
            )
            for step in range(1 - GLL, GLL)
        }
        self.y_coef = [by_position(y_pos, column) for column in columns]
        self.y_swap = (
            self.lane + jnp.where(y_pos == GLL - 1, 1, 0) - jnp.where(y_pos == 0, 1, 0)
        ) & (LANES - 1)
        self.x_edge = (x_pos == 0) | (x_pos == GLL - 1)
        self.y_edge = (y_pos == 0) | (y_pos == GLL - 1)
        self.first_row, self.last_row = self.row == 0, self.row == ROWS - 1
        self.middle_row = self.row == GLL
        self.outer_lane = (self.lane == 0) | (self.lane == LANES - 1)
        self.weight = jnp.where(self.x_edge, 1.0 / 6.0, 5.0 / 6.0) * jnp.where(
            self.y_edge, 1.0 / 6.0, 5.0 / 6.0
        )

    def d_x(self, tile):
        return sum(
            coef * (pltpu.roll(tile, -step % ROWS, 0) if step else tile)
            for step, coef in self.x_coef.items()
        )

    def d_y(self, *tiles):
        totals = [0.0] * len(tiles)
        for j in range(GLL):
            for i, tile in enumerate(tiles):
                totals[i] += self.y_coef[j] * take(tile, self.y_from[j], 1)
        return totals

    def sum_x(self, low, high, before, after):
        low_down, low_up = pltpu.roll(low, 1, 0), pltpu.roll(low, ROWS - 1, 0)
        high_down, high_up = pltpu.roll(high, 1, 0), pltpu.roll(high, ROWS - 1, 0)
        low_other = jnp.where(
            self.first_row,
            before,
            jnp.where(
                self.middle_row, low_down, jnp.where(self.last_row, high_up, low_up)
            ),
        )
        high_other = jnp.where(
            self.first_row,
            low_down,
            jnp.where(
                self.middle_row, high_down, jnp.where(self.last_row, after, high_up)
            ),
        )
        return (
            low + jnp.where(self.x_edge, low_other, 0.0),
            high + jnp.where(self.x_edge, high_other, 0.0),
        )

    def sum_y(self, tile, outer):
        other = jnp.where(self.outer_lane, outer, take(tile, self.y_swap, 1))
        return tile + jnp.where(self.y_edge, other, 0.0)

    def sum_y_pair(self, own, strip):
        own_swap, strip_swap = take(own, self.y_swap, 1), take(strip, self.y_swap, 1)
        own_other = jnp.where(self.outer_lane, strip_swap, own_swap)
        strip_other = jnp.where(self.outer_lane, own_swap, strip_swap)
        return (
            own + jnp.where(self.y_edge, own_other, 0.0),
            strip + jnp.where(self.y_edge, strip_other, 0.0),
        )


def edge_place(x, group):
    return x // ROWS, LANES // 2 * (x % 2) + ROWS * group + 2 * (x % ROWS // 2)


def edges_of(geo, packs, ref, planes, lines, first=None):
    packs = list(packs)
    for number, x in enumerate(lines):
        base = planes * (number if first is None else x - first)
        for group in range(planes // ROWS):
            q, at = edge_place(x, group)
            tile = ref[base + ROWS * group : base + ROWS * (group + 1), :]
            rolled = pltpu.roll(tile, (at + 1) % LANES, 1)
            packs[q] = jnp.where((geo.lane >> 1) == at // 2, rolled, packs[q])
    return packs


def outer_edges(joined, x, group):
    q, at = edge_place(x, group)
    return pltpu.roll(joined[q], (-(at + 1)) % LANES, 1)


def split_sides(geo, first, second, unit):
    odd = (geo.lane & unit) != 0
    return (
        jnp.where(odd, pltpu.roll(second, unit, 1), first),
        jnp.where(odd, second, pltpu.roll(first, LANES - unit, 1)),
    )


def join_sides(geo, before, after, unit):
    odd = (geo.lane & unit) != 0
    return (
        jnp.where(odd, pltpu.roll(after, unit, 1), before),
        jnp.where(odd, after, pltpu.roll(before, LANES - unit, 1)),
    )


def join_edges(geo, before, after):
    odd = (geo.lane & 1) != 0
    return (
        jnp.where(odd, pltpu.roll(before, 1, 1), after),
        jnp.where(odd, before, pltpu.roll(after, LANES - 1, 1)),
    )


def neighbours_of(blocks):
    here = lax.axis_index("blk")
    return lax.rem(here + blocks - 1, blocks), lax.rem(here + 1, blocks)


def is_odd(axis):
    return lax.rem(lax.axis_index(axis), 2)


def sort_sides(axis, first, second):
    odd = is_odd(axis) == 1
    return jnp.where(odd, second, first), jnp.where(odd, first, second)


def one_hot(index, allowed=None):
    low = index & (LANES - 1)
    lane_at = iota((LANES, LANES), 0)
    if allowed is not None:
        lane_at = jnp.where(allowed(lane_at), lane_at, -1)
    return jnp.concatenate(
        [
            jnp.where(lane_at == low[c : c + 1], 1.0, 0.0).astype(jnp.bfloat16)
            for c in range(index.shape[0])
        ],
        axis=1,
    )


def scatter_sum(lines, index, bins, lanes_hot):
    split = []
    for values in lines:
        for part in range(3):
            short = values.astype(jnp.bfloat16).astype(jnp.float32)
            split.append(short)
            values = values - short
    high = index >> 7
    bin_at = iota((bins, LANES), 0)
    left = []
    for c in range(index.shape[0]):
        hit = bin_at == high[c : c + 1]
        left.append(
            jnp.concatenate(
                [jnp.where(hit, part[c : c + 1], 0.0) for part in split], axis=0
            ).astype(jnp.bfloat16)
        )
    total = lax.dot_general(
        jnp.concatenate(left, axis=1),
        lanes_hot,
        (((1,), (1,)), ((), ())),
        preferred_element_type=jnp.float32,
    )
    sums = []
    for i in range(len(lines)):
        part = total[3 * i * bins : 3 * (i + 1) * bins]
        sums.append(part[:bins] + part[bins : 2 * bins] + part[2 * bins :])
    return sums


def wind_tiles(wind_ref, x_points, level, lines):
    levels = wind_ref.shape[0] // (2 * x_points)
    return [
        [
            time_step
            * wind_ref[
                pl.ds((levels * part + level) * x_points + x, ROWS, stride=x_points), :
            ]
            for x in lines
        ]
        for part in range(2)
    ]


def start_kernel(
    planes,
    cols_in,
    weights_in,
    tracers_in,
    rows_in,
    jac_in,
    land_in,
    wind_in,
    air_in,
    send_in,
    slab_out,
    moved_ref,
    before_ref,
    after_ref,
    cols_ref,
    weights_ref,
    rows_ref,
    send_ref,
    slab_ref,
    tracers_ref,
    jac_ref,
    land_ref,
    wind_ref,
    air_ref,
    semaphores,
):
    copies = [
        pltpu.make_async_copy(source, target, semaphores.at[i])
        for i, (source, target) in enumerate(
            (
                (cols_in, cols_ref),
                (tracers_in.at[:ROWS], tracers_ref),
                (weights_in, weights_ref),
                (rows_in, rows_ref),
                (air_in, air_ref),
                (wind_in, wind_ref),
                (jac_in, jac_ref),
                (land_in, land_ref),
                (send_in, send_ref),
            )
        )
    ]
    for copy in copies:
        copy.start()
    geo = Geometry()
    blocks = cols_ref.shape[0]
    x_points = jac_ref.shape[0]
    levels = wind_ref.shape[0] // (2 * x_points)
    chunks = tracers_ref.shape[1] // LANES
    for copy in copies[:4]:
        copy.wait()

    for group in range(blocks // ROWS):
        at = slice(ROWS * group, ROWS * (group + 1))
        cells = cols_ref[at, :]
        high, low = cells >> 7, cells & (LANES - 1)
        surface = jnp.zeros((ROWS, LANES), jnp.float32)
        for k in range(chunks):
            line = spread(tracers_ref[0:1, LANES * k : LANES * (k + 1)])
            surface = jnp.where(high == k, take(line, low, 1), surface)
        area = weights_ref[at, :]
        heat = area * surface
        for c in range(ROWS):
            owner = ROWS * group + c
            for place, step in enumerate((1, 0, -1)):
                to = (owner + step) % blocks
                slab_ref[to, 2 * place : 2 * place + 1, :] = heat[c : c + 1]
                slab_ref[to, 2 * place + 1 : 2 * place + 2, :] = area[c : c + 1]

    out = pltpu.make_async_copy(slab_ref, slab_out, semaphores.at[len(copies)])
    out.start()
    ids = rows_ref[...].astype(jnp.float32)
    for side_ref in (before_ref, after_ref):
        side_ref[SIDE_IDS : SIDE_IDS + blocks, :] = ids

    for copy in copies[4:]:
        copy.wait()
    strips = []
    for h in range(2):
        half = slice(ROWS * h, ROWS * (h + 1))
        second = levels * x_points
        pack = jnp.zeros((ROWS, LANES), jnp.float32)
        for i, strip in enumerate(
            (
                air_ref[half, :],
                wind_ref[half, :],
                wind_ref[second + ROWS * h : second + ROWS * (h + 1), :],
                jac_ref[half, :],
                land_ref[half, :],
            )
        ):
            pack = jnp.where(
                (geo.lane >> 4) == i, pltpu.roll(strip, 16 * i + 8, 1), pack
            )
        strips.append(pack)
    to_right, to_left = split_sides(geo, strips[0], strips[1], ROWS)
    after_ref[SIDE_STRIP : SIDE_STRIP + ROWS, :] = to_right
    before_ref[SIDE_STRIP : SIDE_STRIP + ROWS, :] = to_left

    y_weight = jnp.where(geo.y_edge, 1.0 / 6.0, 5.0 / 6.0)
    for element in range(x_points // GLL):
        lines = [GLL * element + i for i in range(GLL)]
        mass = [
            (1.0 / 6.0 if i in (0, GLL - 1) else 5.0 / 6.0)
            * y_weight
            * spread(jac_ref[x : x + 1, :])
            for i, x in enumerate(lines)
        ]
        for level in range(0, levels, ROWS):
            wind = wind_tiles(wind_ref, x_points, level, lines)
            for plane in range(level, planes, levels):
                fields = [
                    air_ref[pl.ds(plane * x_points + x, ROWS, stride=x_points), :]
                    for x in lines
                ]
                slopes = geo.d_y(*fields)
                for i, x in enumerate(lines):
                    slope = sum(deriv_table[i][j] * fields[j] for j in range(GLL))
                    moved = mass[i] * (
                        fields[i] - (wind[0][i] * slope + wind[1][i] * slopes[i])
                    )
                    moved_ref[planes * x + plane : planes * x + plane + ROWS, :] = moved
    packs = [jnp.zeros((ROWS, LANES), jnp.float32) for _ in range(2)]
    packs = edges_of(geo, packs, moved_ref, planes, range(x_points))
    to_right, to_left = split_sides(geo, packs[0], packs[1], 1)
    after_ref[SIDE_EDGE : SIDE_EDGE + ROWS, :] = to_right
    before_ref[SIDE_EDGE : SIDE_EDGE + ROWS, :] = to_left
    out.wait()


def panel_kernel(
    planes,
    moved_ref,
    recv_ref,
    first_ref,
    second_ref,
    air_ref,
    wind_ref,
    jac_ref,
    land_ref,
    rows_ref,
    ocean_ref,
    avg_ref,
    face_first_ref,
    face_second_ref,
    surf_ref,
    before_ref,
    after_ref,
    held_ref,
):
    geo = Geometry()
    side = slice(0, before_ref.shape[0])
    before_ref[...], after_ref[...] = sort_sides(
        "blk", first_ref[side, :], second_ref[side, :]
    )
    odd_face = is_odd("face")
    down_ref, up_ref = held_ref.at[odd_face], held_ref.at[1 - odd_face]
    blocks = rows_ref.shape[0]
    x_points = jac_ref.shape[0]
    levels = wind_ref.shape[0] // (2 * x_points)

    own_ids = rows_ref[...]
    left_ids = before_ref[SIDE_IDS : SIDE_IDS + blocks, :].astype(jnp.int32)
    right_ids = after_ref[SIDE_IDS : SIDE_IDS + blocks, :].astype(jnp.int32)
    head = [
        jnp.concatenate([recv_ref[c, i : i + 1, :] for c in range(blocks)], axis=0)
        for i in range(6)
    ]
    heat, frac = scatter_sum(head[2:4], own_ids, 2 * ROWS, one_hot(own_ids))
    from_left = scatter_sum(
        head[0:2], left_ids, 2 * ROWS, one_hot(left_ids, lambda lane: lane >= LANES - ROWS)
    )
    from_right = scatter_sum(
        head[4:6], right_ids, 2 * ROWS, one_hot(right_ids, lambda lane: lane < ROWS)
    )
    strip_heat = from_left[0] + from_right[0]
    strip_frac = from_left[1] + from_right[1]

    in_strip = (geo.lane < ROWS) | (geo.lane >= LANES - ROWS)
    packs = join_sides(
        geo,
        before_ref[SIDE_STRIP : SIDE_STRIP + ROWS, :],
        after_ref[SIDE_STRIP : SIDE_STRIP + ROWS, :],
        ROWS,
    )
    own, strip = [], []
    for h, pack in enumerate(packs):
        half = slice(ROWS * h, ROWS * (h + 1))
        strip.append(
            [
                jnp.where(
                    in_strip, pltpu.roll(pack, (-(16 * i + 8)) % LANES, 1), 1.0
                )
                for i in range(5)
            ]
        )
        own.append(
            [
                air_ref[half, :],
                wind_ref[half, :],
                wind_ref[
                    levels * x_points + ROWS * h : levels * x_points + ROWS * (h + 1), :
                ],
                jac_ref[half, :],
                land_ref[half, :],
            ]
        )
    for h in range(2):
        half = slice(ROWS * h, ROWS * (h + 1))
        pair = []
        for tile, ((field, wind_x, wind_y, jac, land), tile_heat, tile_frac) in enumerate(
            ((own[h], heat[half], frac[half]), (strip[h], strip_heat[half], strip_frac[half]))
        ):
            mass = geo.weight * jac
            if tile == 1:
                tile_heat = jnp.where(in_strip, tile_heat, 0.0)
                tile_frac = jnp.where(in_strip, tile_frac, 0.0)
            surf = (tile_heat + land * field) / (tile_frac + land)
            coef_x, coef_y = time_step * mass * wind_x, time_step * mass * wind_y
            moved = (
                mass * (field + relax_rate * (surf - field))
                - coef_x * geo.d_x(field)
                - coef_y * geo.d_y(field)[0]
            )
            pair.append((moved, mass))
            at = 2 * ROWS * tile + ROWS * h
            for number, value in (
                (MASS, mass),
                (COEF_X, coef_x),
                (COEF_Y, coef_y),
                (SURF, surf),
            ):
                surf_ref[4 * ROWS * number + at : 4 * ROWS * number + at + ROWS, :] = value
        for number, i in ((AVG, 0), (MASS_SUM, 1)):
            for tile, value in enumerate(geo.sum_y_pair(pair[0][i], pair[1][i])):
                at = 4 * ROWS * number + 2 * ROWS * tile + ROWS * h
                surf_ref[at : at + ROWS, :] = value

    joined = join_edges(
        geo,
        before_ref[SIDE_EDGE : SIDE_EDGE + ROWS, :],
        after_ref[SIDE_EDGE : SIDE_EDGE + ROWS, :],
    )
    for x in outer_rows(x_points):
        for group in range(planes // ROWS):
            at = slice(planes * x + ROWS * group, planes * x + ROWS * (group + 1))
            avg_ref[at, :] = geo.sum_y(moved_ref[at, :], outer_edges(joined, x, group))

    def line(r):
        return avg_ref[planes * r : planes * (r + 1), :]

    def surf_line(number, r):
        return surf_ref[pl.ds(4 * ROWS * number + r, 2, stride=x_points), :]

    def first_step(get, mass_at):
        return (
            [
                get(1) / mass_at(1),
                get(2) / mass_at(2),
                (get(3) + get(4)) / (mass_at(3) + mass_at(4)),
            ],
            [
                (get(11) + get(12)) / (mass_at(11) + mass_at(12)),
                get(13) / mass_at(13),
                get(14) / mass_at(14),
            ],
        )

    def own_mass_sum(r):
        return surf_ref[4 * ROWS * MASS_SUM + r : 4 * ROWS * MASS_SUM + r + 1, :]

    low_lines, high_lines = first_step(line, own_mass_sum)
    surf_low, surf_high = first_step(
        functools.partial(surf_line, AVG), functools.partial(surf_line, MASS_SUM)
    )
    for out_ref, r, lines, surf_lines, coefs in (
        (down_ref, 0, low_lines, surf_low, deriv_table[0][1:]),
        (up_ref, 15, high_lines, surf_high, deriv_table[3][:3]),
    ):
        slope = sum(coef * value for coef, value in zip(coefs, lines))
        surf_slope = sum(coef * value for coef, value in zip(coefs, surf_lines))
        mass = surf_ref[4 * ROWS * MASS + r : 4 * ROWS * MASS + r + 1, :]
        wind = time_step * mass * wind_ref[pl.ds(r, 2 * levels, stride=x_points), :]
        out_ref[0:planes, :] = line(r)
        for first in range(0, planes, levels):
            out_ref[planes + first : planes + first + levels, :] = (
                wind[:levels] * slope[first : first + levels]
            )
        base = 2 * planes
        out_ref[base : base + 2 * levels, :] = wind
        base += 2 * levels
        for number in range(SURF_ARRAYS):
            out_ref[base + 2 * number : base + 2 * number + 2, :] = surf_line(number, r)
        base += 2 * SURF_ARRAYS
        out_ref[base : base + 2, :] = surf_line(COEF_X, r) * surf_slope
    face_first_ref[...] = held_ref[0]
    face_second_ref[...] = held_ref[1]


def outer_rows(x_points):
    return [x for x in range(x_points) if x <= GLL or x >= x_points - GLL - 1]


def advance(geo, fields, wind, mass):
    slopes = geo.d_y(*fields)
    moved = []
    for i in range(GLL):
        slope = sum(deriv_table[i][j] * fields[j] for j in range(GLL))
        moved.append(mass[i] * (fields[i] - (wind[0][i] * slope + wind[1][i] * slopes[i])))
    return moved, slopes


def inner_kernel(
    planes, avg_ref, moved_ref, first_ref, second_ref, surf_ref, wind_ref, out_ref, packs_ref
):
    geo = Geometry()
    x_points = avg_ref.shape[0] // planes
    levels = wind_ref.shape[0] // (2 * x_points)
    joined = join_edges(
        geo,
        *sort_sides(
            "blk",
            first_ref[SIDE_EDGE : SIDE_EDGE + ROWS, :],
            second_ref[SIDE_EDGE : SIDE_EDGE + ROWS, :],
        ),
    )
    outer = outer_rows(x_points)

    def average(x, plane):
        at = slice(planes * x + plane, planes * x + plane + ROWS)
        if x in outer:
            return avg_ref[at, :]
        return geo.sum_y(moved_ref[at, :], outer_edges(joined, x, plane // ROWS))

    def surf_row(number, x):
        at = 4 * ROWS * number + x
        return spread(surf_ref[at : at + 1, :])

    def put(x, plane, value):
        at = planes * (x - GLL) + plane
        out_ref[at : at + ROWS, :] = value

    held = {}
    carried = {}
    for element in range(1, x_points // GLL - 1):
        lines = [GLL * element + i for i in range(GLL)]
        totals = [surf_row(MASS_SUM, x) for x in lines]
        totals[0] = totals[0] + surf_row(MASS_SUM, lines[0] - 1)
        totals[-1] = totals[-1] + surf_row(MASS_SUM, lines[-1] + 1)
        scale = [1.0 / total for total in totals]
        mass = [surf_row(MASS, x) for x in lines]
        for level in range(0, levels, ROWS):
            wind = wind_tiles(wind_ref, x_points, level, lines)
            for plane in range(level, planes, levels):
                if element == 1:
                    first = average(lines[0], plane) + average(lines[0] - 1, plane)
                else:
                    first = carried[plane]
                last = average(lines[-1], plane) + average(lines[-1] + 1, plane)
                carried[plane] = last
                totals = (
                    [first] + [average(x, plane) for x in lines[1:-1]] + [last]
                )
                fields = [total * factor for total, factor in zip(totals, scale)]
                moved, _ = advance(geo, fields, wind, mass)
                if element == 1:
                    put(lines[0], plane, moved[0])
                else:
                    shared = held[plane] + moved[0]
                    put(lines[0] - 1, plane, shared)
                    put(lines[0], plane, shared)
                for i in range(1, GLL - 1):
                    put(lines[i], plane, moved[i])
                held[plane] = moved[-1]
                if lines[-1] == x_points - GLL - 1:
                    put(lines[-1], plane, moved[-1])
    packs = [jnp.zeros((ROWS, LANES), jnp.float32) for _ in range(2)]
    inner = [x for x in range(x_points) if x not in outer]
    for q, pack in enumerate(edges_of(geo, packs, out_ref, planes, inner, GLL)):
        packs_ref[ROWS * q : ROWS * (q + 1), :] = pack


def second_kernel(
    planes,
    avg_ref,
    inner_ref,
    packs_ref,
    surf_ref,
    first_ref,
    second_ref,
    wind_ref,
    rows_ref,
    ocean_ref,
    slab_out,
    sums_ref,
    final_ref,
    inverse_ref,
    flux_ref,
    edges_ref,
    low_ref,
    high_ref,
    semaphores,
):
    geo = Geometry()
    low_ref[...], high_ref[...] = sort_sides("face", first_ref[...], second_ref[...])
    blocks = rows_ref.shape[0]
    left, right = neighbours_of(blocks)
    x_points = final_ref.shape[0]
    levels = wind_ref.shape[0] // (2 * x_points)
    base = low_ref.shape[0] - 2 * SURF_ARRAYS - 4

    def surf_tile(number, tile, h):
        at = 4 * ROWS * number + 2 * ROWS * tile + ROWS * h
        return surf_ref[at : at + ROWS, :]

    def beside(ref, number, tile):
        at = base + 2 * number + tile
        return spread(ref[at : at + 1, :])

    ends = []
    inverse = []
    for tile in range(2):
        total = geo.sum_x(
            surf_tile(MASS_SUM, tile, 0),
            surf_tile(MASS_SUM, tile, 1),
            beside(low_ref, MASS_SUM, tile),
            beside(high_ref, MASS_SUM, tile),
        )
        inverse.append([1.0 / value for value in total])
        summed = geo.sum_x(
            surf_tile(AVG, tile, 0),
            surf_tile(AVG, tile, 1),
            beside(low_ref, AVG, tile),
            beside(high_ref, AVG, tile),
        )
        fields = [value * scale for value, scale in zip(summed, inverse[tile])]
        moved = []
        for h in range(2):
            field = fields[h]
            moved.append(
                surf_tile(MASS, tile, h)
                * (field + relax_rate * (surf_tile(SURF, tile, h) - field))
                - surf_tile(COEF_X, tile, h) * geo.d_x(field)
                - surf_tile(COEF_Y, tile, h) * geo.d_y(field)[0]
            )
        halos = []
        for ref, field, own_coef in (
            (low_ref, spread(fields[0][:1]), deriv_table[3][3]),
            (high_ref, spread(fields[1][ROWS - 1 :]), deriv_table[0][0]),
        ):
            halos.append(
                beside(ref, MASS, tile)
                * (field + relax_rate * (beside(ref, SURF, tile) - field))
                - beside(ref, SURF_ARRAYS, tile)
                - beside(ref, COEF_X, tile) * (own_coef * field)
                - beside(ref, COEF_Y, tile) * geo.d_y(field)[0]
            )
        ends.append(geo.sum_x(moved[0], moved[1], halos[0], halos[1]))
    final = []
    for h in range(2):
        summed, _ = geo.sum_y_pair(ends[0][h], ends[1][h])
        final.append(summed * inverse[0][h])
        final_ref[ROWS * h : ROWS * (h + 1), :] = final[h]
        inverse_ref[ROWS * h : ROWS * (h + 1), :] = inverse[0][h]
    flux = [final[h] - surf_tile(SURF, 0, h) for h in range(2)]
    for group in range(blocks // ROWS):
        ids = rows_ref[ROWS * group : ROWS * (group + 1), :]
        high, low = ids >> 7, ids & (LANES - 1)
        picked = jnp.zeros((ROWS, LANES), jnp.float32)
        for x in range(2 * ROWS):
            line = spread(flux[x // ROWS][x % ROWS : x % ROWS + 1])
            picked = jnp.where(high == x, take(line, low, 1), picked)
        for c in range(ROWS):
            flux_ref[ROWS * group + c, 0:1, :] = picked[c : c + 1]

    kept = outer_rows(x_points)

    def put(x, plane, value):
        at = planes * kept.index(x) + plane
        sums_ref[at : at + ROWS, :] = value

    def beyond(ref, plane, field, slope, own_coef):
        wind_at = 2 * planes + plane % levels
        return (
            beside(ref, MASS, 0) * field
            - ref[planes + plane : planes + plane + ROWS, :]
            - ref[wind_at : wind_at + ROWS, :] * (own_coef * field)
            - ref[wind_at + levels : wind_at + levels + ROWS, :] * slope
        )

    def row_of(tiles, x):
        return spread(tiles[x // ROWS][x % ROWS : x % ROWS + 1])

    masses = [surf_tile(MASS, 0, h) for h in range(2)]
    last_element = x_points // GLL - 1
    for element in (0, last_element):
        lines = [GLL * element + i for i in range(GLL)]
        scale = [row_of(inverse[0], x) for x in lines]
        mass = [row_of(masses, x) for x in lines]
        for level in range(0, levels, ROWS):
            wind = wind_tiles(wind_ref, x_points, level, lines)
            for plane in range(level, planes, levels):
                here = slice(plane, plane + ROWS)
                fields = []
                for i, x in enumerate(lines):
                    total = avg_ref[planes * x + plane : planes * x + plane + ROWS, :]
                    other = x - 1 if i == 0 else x + 1
                    if other < 0:
                        total = total + low_ref[here, :]
                    elif other == x_points:
                        total = total + high_ref[here, :]
                    elif i in (0, GLL - 1):
                        at = planes * other + plane
                        total = total + avg_ref[at : at + ROWS, :]
                    fields.append(total * scale[i])
                moved, slopes = advance(geo, fields, wind, mass)
                if element == 0:
                    before = beyond(low_ref, plane, fields[0], slopes[0], deriv_table[3][3])
                    put(lines[0], plane, before + moved[0])
                    shared = moved[-1] + inner_ref[here, :]
                    put(lines[-1], plane, shared)
                    put(lines[-1] + 1, plane, shared)
                else:
                    at = inner_ref.shape[0] - planes + plane
                    shared = moved[0] + inner_ref[at : at + ROWS, :]
                    put(lines[0] - 1, plane, shared)
                    put(lines[0], plane, shared)
                    after = beyond(
                        high_ref, plane, fields[-1], slopes[-1], deriv_table[0][0]
                    )
                    put(lines[-1], plane, moved[-1] + after)
                for i in range(1, GLL - 1):
                    put(lines[i], plane, moved[i])
    packs = [packs_ref[:ROWS, :], packs_ref[ROWS:, :]]
    packs = edges_of(geo, packs, sums_ref, planes, kept)
    to_right, to_left = split_sides(geo, packs[0], packs[1], 1)
    edges_ref[0] = to_right
    edges_ref[1] = to_left
    copies = [
        pltpu.make_async_copy(
            edges_ref.at[i], slab_out.at[to, EDGE_AT : EDGE_AT + ROWS], semaphores.at[i]
        )
        for i, to in enumerate((right, left))
    ]
    copies.append(
        pltpu.make_async_copy(flux_ref, slab_out.at[:, :HEAD], semaphores.at[2])
    )
    for copy in copies:
        copy.start()
    for copy in copies:
        copy.wait()


def last_kernel(planes, inner_ref, outer_ref, inverse_ref, cols_ref, out_ref, hot_ref):
    geo = Geometry()
    x_points = inverse_ref.shape[0]
    kept = outer_rows(x_points)
    hot_ref[...] = one_hot(cols_ref[...])
    for x in range(x_points):
        inverse = spread(inverse_ref[x : x + 1, :])
        ref, first = inner_ref, planes * (x - GLL)
        if x in kept:
            ref, first = outer_ref, planes * kept.index(x)
        for group in range(planes // ROWS):
            tile = ref[first + ROWS * group : first + ROWS * (group + 1), :]
            at = planes * x + ROWS * group
            out_ref[at : at + ROWS, :] = inverse * geo.sum_y(tile, 0.0)


def end_kernel(
    planes,
    last_ref,
    recv_ref,
    final_ref,
    inverse_ref,
    cols_ref,
    hot_ref,
    weights_ref,
    gain_ref,
    first_ref,
    ocean_in,
    ocean_out,
    air_out,
    air_ref,
    row_ref,
    semaphores,
):
    geo = Geometry()
    blocks = cols_ref.shape[0]
    left, right = neighbours_of(blocks)
    chunks = gain_ref.shape[0]
    x_points = inverse_ref.shape[0]
    copies = []

    def send(source, target):
        copies.append(
            pltpu.make_async_copy(source, target, semaphores.at[len(copies)])
        )
        copies[-1].start()

    joined = join_edges(
        geo,
        recv_ref[left, EDGE_AT : EDGE_AT + ROWS, :],
        recv_ref[right, EDGE_AT : EDGE_AT + ROWS, :],
    )
    groups = planes // ROWS
    for group in range(groups):
        for x in range(x_points):
            at = planes * x + ROWS * group
            beside = spread(inverse_ref[x : x + 1, :]) * outer_edges(joined, x, group)
            air_ref[pl.ds(ROWS * group * x_points + x, ROWS, stride=x_points), :] = last_ref[
                at : at + ROWS, :
            ] + jnp.where(geo.outer_lane, beside, 0.0)
        if group == 0:
            air_ref[0:x_points, :] = final_ref[...]
        if group % 2:
            rows = slice(
                ROWS * (group - 1) * x_points, ROWS * (group + 1) * x_points
            )
            send(air_ref.at[rows], air_out.at[rows])
    if groups % 2:
        rows = slice(ROWS * (groups - 1) * x_points, planes * x_points)
        send(air_ref.at[rows], air_out.at[rows])

    arrived = jnp.concatenate([recv_ref[c, 0:1, :] for c in range(blocks)], axis=0)
    (inflow,) = scatter_sum(
        [weights_ref[...] * arrived], cols_ref[...], chunks, hot_ref[...]
    )
    gain = inflow * gain_ref[...]
    row_ref[...] = first_ref[...]
    for k in range(chunks):
        at = slice(LANES * k, LANES * (k + 1))
        row_ref[0:1, at] = first_ref[0:1, at] + gain[k : k + 1]
    send(row_ref, ocean_out.at[:ROWS])
    for copy in copies:
        copy.wait()


def gathered(ids, coefs, source, sources, groups, first=0):
    totals = [jnp.zeros((ROWS, LANES), jnp.float32) for _ in range(groups)]
    for edge in range(ids.shape[0]):
        cell = spread(ids[edge : edge + 1])
        coef = spread(coefs[edge : edge + 1])
        high, low = cell >> 7, cell & (LANES - 1)
        for s in range(sources):
            scaled = jnp.where(high == first + s, coef, 0.0)
            for group in range(groups):
                totals[group] += scaled * take(source(group, s), low, 1)
    return totals


def multiplied(ids, coefs, halves_ref, sources, groups):
    lane_at = iota((LANES, LANES), 0)
    hot = jnp.concatenate(
        [
            jnp.where(lane_at == (ids[edge : edge + 1] & (LANES - 1)), 1.0, 0.0).astype(
                jnp.bfloat16
            )
            for edge in range(2)
        ],
        axis=1,
    )
    picked = jnp.dot(
        halves_ref[...],
        jnp.concatenate([hot, hot], axis=0),
        preferred_element_type=jnp.float32,
    )
    totals = [jnp.zeros((ROWS, LANES), jnp.float32) for _ in range(groups)]
    for edge in range(2):
        high = spread(ids[edge : edge + 1]) >> 7
        coef = spread(coefs[edge : edge + 1])
        side = slice(LANES * edge, LANES * (edge + 1))
        for s in range(sources):
            scaled = jnp.where(high == s, coef, 0.0)
            for group in range(groups):
                at = ROWS * (groups * s + group)
                totals[group] += scaled * picked[at : at + ROWS, side]
    return totals


def ocean_kernel(
    levels, start, tracers_ref, coef_ref, near_ref, rate_ref, after_ref, out_ref, halves_ref
):
    chunks = tracers_ref.shape[1] // LANES
    groups = tracers_ref.shape[0] // ROWS
    row = iota((ROWS, LANES), 0)

    def source(group, s):
        return tracers_ref[
            ROWS * group : ROWS * (group + 1), LANES * s : LANES * (s + 1)
        ]

    planes = tracers_ref.shape[0]
    for s in range(chunks):
        values = tracers_ref[:, LANES * s : LANES * (s + 1)]
        upper = values.astype(jnp.bfloat16)
        at = slice(planes * s, planes * (s + 1))
        halves_ref[at, :LANES] = upper
        halves_ref[at, LANES:] = (values - upper.astype(jnp.float32)).astype(jnp.bfloat16)
    edges = near_ref.shape[0]

    def one_chunk(number, carry):
        k = number + start
        at = pl.ds(pl.multiple_of(k * LANES, LANES), LANES)
        out_at = pl.ds(pl.multiple_of(number * LANES, LANES), LANES)
        ids, coefs = near_ref[:, at], coef_ref[:, at]
        by_gather = edges - edges // 3 * 2
        totals = gathered(ids[:by_gather], coefs[:by_gather], source, chunks, groups)
        for edge in range(by_gather, edges, 2):
            more = multiplied(
                ids[edge : edge + 2], coefs[edge : edge + 2], halves_ref, chunks, groups
            )
            totals = [total + part for total, part in zip(totals, more)]
        coef_sum = spread(jnp.sum(coefs, axis=0, keepdims=True))
        rate = spread(rate_ref[pl.ds(k, 1), :])
        tiles = [tracers_ref[ROWS * g : ROWS * (g + 1), at] for g in range(groups)]
        for g in range(groups):
            tile = tiles[g]
            top = bottom = tile
            if (ROWS * g) % levels:
                top = pltpu.roll(tiles[g - 1], 1, 0)
            if (ROWS * (g + 1)) % levels:
                bottom = pltpu.roll(tiles[g + 1], ROWS - 1, 0)
            above = jnp.where(row == 0, top, pltpu.roll(tile, 1, 0))
            below = jnp.where(row == ROWS - 1, bottom, pltpu.roll(tile, ROWS - 1, 0))
            vertical = rate * ((above - tile) + (below - tile))
            out_ref[ROWS * g : ROWS * (g + 1), out_at] = (
                tile + (totals[g] - coef_sum * tile) + vertical
            )
        return carry

    count = out_ref.shape[1] // LANES
    step = 2 if count % 2 == 0 else 1

    def some_chunks(number, carry):
        for i in range(step):
            one_chunk(step * number + i, carry)
        return carry

    lax.fori_loop(0, count // step, some_chunks, 0)


def send_kernel(
    tracers_ref, send_ref, before_ref, after_ref, first_ref, second_ref, held_ref
):
    chunks = tracers_ref.shape[1] // LANES
    odd = is_odd("blk")
    for part, side_ref in enumerate((before_ref, after_ref)):
        out_ref = held_ref.at[1 - odd if part else odd]
        base = side_ref.shape[0]
        out_ref[:base, :] = side_ref[...]
        cells = spread(send_ref[0:1, LANES * part : LANES * (part + 1)])
        high, low = cells >> 7, cells & (LANES - 1)
        for group in range(tracers_ref.shape[0] // ROWS):
            half = slice(ROWS * group, ROWS * (group + 1))
            rim = jnp.zeros((ROWS, LANES), jnp.float32)
            for k in range(chunks):
                tile = tracers_ref[half, LANES * k : LANES * (k + 1)]
                rim = jnp.where(high == k, take(tile, low, 1), rim)
            out_ref[base + ROWS * group : base + ROWS * (group + 1), :] = rim
    first_ref[...] = held_ref[0]
    second_ref[...] = held_ref[1]


def rim_kernel(
    starts,
    first_ref,
    second_ref,
    coef_ref,
    near_ref,
    area_ref,
    rows_ref,
    *refs,
):
    partial_refs, (out_ref, gain_ref, top_ref, sides_ref) = (
        refs[: len(starts)],
        refs[len(starts) :],
    )
    chunks = coef_ref.shape[1] // LANES
    groups = out_ref.shape[0] // ROWS
    rim_at = first_ref.shape[0] - out_ref.shape[0]
    sides_ref[0], sides_ref[1] = sort_sides(
        "blk", first_ref[rim_at:, :], second_ref[rim_at:, :]
    )
    gain_ref[...] = flux_gain / area_ref[...]

    def source(group, s):
        return sides_ref[s, ROWS * group : ROWS * (group + 1), :]

    for k in range(chunks):
        at = slice(LANES * k, LANES * (k + 1))
        totals = gathered(near_ref[:, at], coef_ref[:, at], source, 2, groups, chunks)
        part = max(i for i, start in enumerate(starts) if start <= k)
        place = slice(LANES * (k - starts[part]), LANES * (k - starts[part] + 1))
        for g in range(groups):
            half = slice(ROWS * g, ROWS * (g + 1))
            out_ref[half, at] = partial_refs[part][half, place] + totals[g]
    top_ref[...] = out_ref[:ROWS, :]


VMEM_SPEC = pl.BlockSpec(memory_space=pltpu.VMEM)
ANY_SPEC = pl.BlockSpec(memory_space=pl.ANY)
HBM_SPEC = pl.BlockSpec(memory_space=pltpu.HBM)


def call(kernel, outs, specs, scratch=(), cost=0, hbm_outs=0, aliases=None):
    estimate = None
    if cost:
        estimate = pl.CostEstimate(flops=0, bytes_accessed=cost, transcendentals=0)
    outs = [
        out if isinstance(out, jax.ShapeDtypeStruct) else jax.ShapeDtypeStruct(out, jnp.float32)
        for out in outs
    ]
    out_specs = [VMEM_SPEC] * len(outs)
    out_specs[:hbm_outs] = [HBM_SPEC] * hbm_outs
    return pl.pallas_call(
        kernel,
        out_shape=outs,
        in_specs=specs,
        out_specs=out_specs,
        scratch_shapes=list(scratch),
        input_output_aliases=aliases or {},
        cost_estimate=estimate,
        compiler_params=pltpu.CompilerParams(vmem_limit_bytes=32 * 2**20),
        name=getattr(kernel, "func", kernel).__name__,
    )


def swap_sides(first, second, axis):
    count = lax.axis_size(axis)

    def pairs(start):
        swaps = []
        for i in range(start, count, 2):
            swaps += [(i, (i + 1) % count), ((i + 1) % count, i)]
        return swaps

    return lax.ppermute(first, axis, pairs(1)), lax.ppermute(second, axis, pairs(0))


def body(
    air_state,
    air_wind,
    jacobian,
    land_area,
    xgrid_rows,
    tracers,
    edge_coef,
    neighbours,
    vert_rate,
    ocean_area,
    send_list,
    xgrid_cols,
    xgrid_weights,
):
    field_count, levels, x_points, y_points = air_state.shape
    planes = field_count * levels
    ocean_levels, cells = tracers.shape[1:]
    ocean_planes = tracers.shape[0] * ocean_levels
    faces, blocks = lax.axis_size("face"), lax.axis_size("blk")
    air = air_state.reshape(planes * x_points, y_points)
    wind = air_wind.reshape(2 * levels * x_points, y_points)
    ocean = tracers.reshape(ocean_planes, cells)
    point_ids, cell_ids, weights = xgrid_rows[0], xgrid_cols[0], xgrid_weights[0]
    rate = vert_rate.reshape(cells // LANES, LANES)
    area = ocean_area.reshape(cells // LANES, LANES)
    first_inputs = (
        cell_ids,
        weights,
        ocean,
        point_ids,
        jacobian,
        land_area,
        wind,
        air,
        send_list,
    )
    kept = (cell_ids, weights, point_ids, send_list)
    slab, moved, to_before, to_after, cell_ids, weights, point_ids, send_list = call(
        functools.partial(start_kernel, planes),
        [(blocks, HEAD, LANES), air.shape]
        + [(SIDE_IDS + blocks, LANES)] * 2
        + [jax.ShapeDtypeStruct(array.shape, array.dtype) for array in kept],
        [HBM_SPEC] * len(first_inputs),
        [
            pltpu.VMEM(shape, jnp.float32)
            for shape in (
                (blocks, HEAD, LANES),
                (ROWS, cells),
                jacobian.shape,
                land_area.shape,
                wind.shape,
                air.shape,
            )
        ]
        + [pltpu.SemaphoreType.DMA((len(first_inputs) + 1,))],
        hbm_outs=1,
    )(*(pltpu.with_memory_space_constraint(array, pltpu.HBM) for array in first_inputs))
    recv = lax.all_to_all(slab, "blk", split_axis=0, concat_axis=0, tiled=True)

    chunks = cells // LANES
    reads_per_chunk = edge_coef.shape[0] * chunks * (ocean_planes // ROWS)
    starts = (0, chunks // 4, chunks * 3 // 4)

    def ocean_part(start, end, after):
        (result,) = call(
            functools.partial(ocean_kernel, ocean_levels, start),
            [(ocean_planes, (end - start) * LANES)],
            [VMEM_SPEC] * 4 + [ANY_SPEC],
            [pltpu.VMEM((chunks * ocean_planes, 2 * LANES), jnp.bfloat16)],
            cost=(end - start) * reads_per_chunk * ROWS * LANES * 2,
        )(ocean, edge_coef, neighbours, rate, after)
        return result

    first, second = call(
        send_kernel,
        [(SIDE_IDS + blocks + ocean_planes, LANES)] * 2,
        [VMEM_SPEC] * 4,
        [pltpu.VMEM((2, SIDE_IDS + blocks + ocean_planes, LANES), jnp.float32)],
        cost=reads_per_chunk * ROWS * LANES,
    )(ocean, send_list, to_before, to_after)
    side_first, side_second = swap_sides(first, second, "blk")
    first_part = ocean_part(starts[0], starts[1], first)
    side_rows = 2 * planes + 2 * levels + 2 * SURF_ARRAYS + 4
    avg, first, second, surf = call(
        functools.partial(panel_kernel, planes),
        [air.shape, (side_rows, LANES), (side_rows, LANES), (4 * ROWS * SURF_ARRAYS, LANES)],
        [VMEM_SPEC] * 9 + [ANY_SPEC],
        [pltpu.VMEM((SIDE_IDS + blocks, LANES), jnp.float32) for _ in range(2)]
        + [pltpu.VMEM((2, side_rows, LANES), jnp.float32)],
    )(
        moved,
        recv,
        side_first,
        side_second,
        air,
        wind,
        jacobian,
        land_area,
        point_ids,
        first_part,
    )
    face_first, face_second = swap_sides(first, second, "face")
    inner, packs = call(
        functools.partial(inner_kernel, planes),
        [((x_points - 2 * GLL) * planes, LANES), (2 * ROWS, LANES)],
        [VMEM_SPEC] * 6,
        cost=2 * air.size * 4,
    )(avg, moved, side_first, side_second, surf, wind)
    second_part = ocean_part(starts[1], starts[2], surf)

    slab, outer, final, inverse = call(
        functools.partial(second_kernel, planes),
        [
            (blocks, EDGE_AT + ROWS, LANES),
            (len(outer_rows(x_points)) * planes, LANES),
            (x_points, y_points),
            (x_points, y_points),
        ],
        [VMEM_SPEC] * 8 + [ANY_SPEC],
        [
            pltpu.VMEM((blocks, HEAD, LANES), jnp.float32),
            pltpu.VMEM((2, ROWS, LANES), jnp.float32),
            pltpu.VMEM((side_rows, LANES), jnp.float32),
            pltpu.VMEM((side_rows, LANES), jnp.float32),
            pltpu.SemaphoreType.DMA((3,)),
        ],
        hbm_outs=1,
    )(avg, inner, packs, surf, face_first, face_second, wind, point_ids, second_part)
    arrived = lax.all_to_all(slab, "blk", split_axis=0, concat_axis=0, tiled=True)
    last, hot = call(
        functools.partial(last_kernel, planes),
        [air.shape, jax.ShapeDtypeStruct((LANES, blocks * LANES), jnp.bfloat16)],
        [VMEM_SPEC] * 4,
        cost=2 * air.size * 4,
    )(inner, outer, inverse, cell_ids)
    third_part = ocean_part(starts[2], chunks, final)
    partial, gain, first_rows = call(
        functools.partial(rim_kernel, starts),
        [ocean.shape, area.shape, (ROWS, cells)],
        [VMEM_SPEC] * 5 + [ANY_SPEC] + [VMEM_SPEC] * len(starts),
        [pltpu.VMEM((2, ocean_planes, LANES), jnp.float32)],
        cost=chunks * reads_per_chunk // 8 * ROWS * LANES * 4,
    )(
        side_first,
        side_second,
        edge_coef,
        neighbours,
        area,
        final,
        first_part,
        second_part,
        third_part,
    )
    ocean_final, air_final = call(
        functools.partial(end_kernel, planes),
        [ocean.shape, air.shape],
        [VMEM_SPEC] * 9 + [HBM_SPEC],
        [
            pltpu.VMEM(air.shape, jnp.float32),
            pltpu.VMEM((ROWS, cells), jnp.float32),
            pltpu.SemaphoreType.DMA((1 + planes // ROWS,)),
        ],
        hbm_outs=2,
        aliases={9: 0},
    )(
        last,
        arrived,
        final,
        inverse,
        cell_ids,
        hot,
        weights,
        gain,
        first_rows,
        pltpu.with_memory_space_constraint(partial, pltpu.HBM),
    )
    return air_final.reshape(air_state.shape), ocean_final.reshape(tracers.shape)


def solution(mesh):
    return jax.shard_map(
        body,
        mesh=mesh,
        in_specs=(
            P(None, None, "face", "blk"),
            P(None, None, "face", "blk"),
            P("face", "blk"),
            P("face", "blk"),
            P(("face", "blk"), None, None),
            P(None, None, ("face", "blk")),
            P(None, ("face", "blk")),
            P(None, ("face", "blk")),
            P(("face", "blk")),
            P(("face", "blk")),
            P(("face", "blk"), None),
            P(("face", "blk"), None, None),
            P(("face", "blk"), None, None),
        ),
        out_specs=(P(None, None, "face", "blk"), P(None, None, ("face", "blk"))),
        check_vma=False,
    )
```

```python
import functools

import jax
import jax.numpy as jnp
from jax import lax
from jax.experimental import pallas as pl
from jax.experimental.pallas import tpu as pltpu
from jax.sharding import PartitionSpec as P

GLL = 4
ROWS = 8
LANES = 128

deriv_table = [
    [-3.0, 4.045084971874737, -1.545084971874737, 0.5],
    [-0.8090169943749475, 0.0, 1.118033988749895, -0.30901699437494745],
    [0.30901699437494745, -1.118033988749895, 0.0, 0.8090169943749475],
    [-0.5, 1.545084971874737, -4.045084971874737, 3.0],
]
time_step = 0.05
relax_rate = 0.3
flux_gain = 0.2

HEAD, EDGE_AT = 8, 8
SIDE_EDGE, SIDE_STRIP, SIDE_IDS = 0, 8, 16
AVG, MASS_SUM, MASS, COEF_X, COEF_Y, SURF = range(6)
SURF_ARRAYS = 6


def iota(shape, dim):
    return lax.broadcasted_iota(jnp.int32, shape, dim)


def take(values, index, axis):
    return jnp.take_along_axis(values, index, axis=axis, mode="promise_in_bounds")


def by_position(pos, values):
    result = jnp.full(pos.shape, values[-1], jnp.float32)
    for i, value in enumerate(values[:-1]):
        result = jnp.where(pos == i, value, result)
    return result


def spread(row):
    return jnp.broadcast_to(row, (ROWS, LANES))


class Geometry:
    def __init__(self):
        shape = (ROWS, LANES)
        self.row, self.lane = iota(shape, 0), iota(shape, 1)
        x_pos, y_pos = self.row & (GLL - 1), self.lane & (GLL - 1)
        self.y_from = [self.lane - y_pos + j for j in range(GLL)]
        columns = [[line[j] for line in deriv_table] for j in range(GLL)]
        self.x_coef = {
            step: by_position(
                x_pos,
                [
                    deriv_table[i][i + step] if 0 <= i + step < GLL else 0.0
                    for i in range(GLL)
                ],
            )
            for step in range(1 - GLL, GLL)
        }
        self.y_coef = [by_position(y_pos, column) for column in columns]
        self.y_swap = (
            self.lane + jnp.where(y_pos == GLL - 1, 1, 0) - jnp.where(y_pos == 0, 1, 0)
        ) & (LANES - 1)
        self.x_edge = (x_pos == 0) | (x_pos == GLL - 1)
        self.y_edge = (y_pos == 0) | (y_pos == GLL - 1)
        self.first_row, self.last_row = self.row == 0, self.row == ROWS - 1
        self.middle_row = self.row == GLL
        self.outer_lane = (self.lane == 0) | (self.lane == LANES - 1)
        self.weight = jnp.where(self.x_edge, 1.0 / 6.0, 5.0 / 6.0) * jnp.where(
            self.y_edge, 1.0 / 6.0, 5.0 / 6.0
        )

    def d_x(self, tile):
        return sum(
            coef * (pltpu.roll(tile, -step % ROWS, 0) if step else tile)
            for step, coef in self.x_coef.items()
        )

    def d_y(self, *tiles):
        totals = [0.0] * len(tiles)
        for j in range(GLL):
            for i, tile in enumerate(tiles):
                totals[i] += self.y_coef[j] * take(tile, self.y_from[j], 1)
        return totals

    def sum_x(self, low, high, before, after):
        low_down, low_up = pltpu.roll(low, 1, 0), pltpu.roll(low, ROWS - 1, 0)
        high_down, high_up = pltpu.roll(high, 1, 0), pltpu.roll(high, ROWS - 1, 0)
        low_other = jnp.where(
            self.first_row,
            before,
            jnp.where(
                self.middle_row, low_down, jnp.where(self.last_row, high_up, low_up)
            ),
        )
        high_other = jnp.where(
            self.first_row,
            low_down,
            jnp.where(
                self.middle_row, high_down, jnp.where(self.last_row, after, high_up)
            ),
        )
        return (
            low + jnp.where(self.x_edge, low_other, 0.0),
            high + jnp.where(self.x_edge, high_other, 0.0),
        )

    def sum_y(self, tile, outer):
        other = jnp.where(self.outer_lane, outer, take(tile, self.y_swap, 1))
        return tile + jnp.where(self.y_edge, other, 0.0)

    def sum_y_pair(self, own, strip):
        own_swap, strip_swap = take(own, self.y_swap, 1), take(strip, self.y_swap, 1)
        own_other = jnp.where(self.outer_lane, strip_swap, own_swap)
        strip_other = jnp.where(self.outer_lane, own_swap, strip_swap)
        return (
            own + jnp.where(self.y_edge, own_other, 0.0),
            strip + jnp.where(self.y_edge, strip_other, 0.0),
        )


def edge_place(x, group):
    return x // ROWS, LANES // 2 * (x % 2) + ROWS * group + 2 * (x % ROWS // 2)


def edges_of(geo, packs, ref, planes, lines, first=None):
    packs = list(packs)
    for number, x in enumerate(lines):
        base = planes * (number if first is None else x - first)
        for group in range(planes // ROWS):
            q, at = edge_place(x, group)
            tile = ref[base + ROWS * group : base + ROWS * (group + 1), :]
            rolled = pltpu.roll(tile, (at + 1) % LANES, 1)
            packs[q] = jnp.where((geo.lane >> 1) == at // 2, rolled, packs[q])
    return packs


def outer_edges(joined, x, group):
    q, at = edge_place(x, group)
    return pltpu.roll(joined[q], (-(at + 1)) % LANES, 1)


def split_sides(geo, first, second, unit):
    odd = (geo.lane & unit) != 0
    return (
        jnp.where(odd, pltpu.roll(second, unit, 1), first),
        jnp.where(odd, second, pltpu.roll(first, LANES - unit, 1)),
    )


def join_sides(geo, before, after, unit):
    odd = (geo.lane & unit) != 0
    return (
        jnp.where(odd, pltpu.roll(after, unit, 1), before),
        jnp.where(odd, after, pltpu.roll(before, LANES - unit, 1)),
    )


def join_edges(geo, before, after):
    odd = (geo.lane & 1) != 0
    return (
        jnp.where(odd, pltpu.roll(before, 1, 1), after),
        jnp.where(odd, before, pltpu.roll(after, LANES - 1, 1)),
    )


def neighbours_of(blocks):
    here = lax.axis_index("blk")
    return lax.rem(here + blocks - 1, blocks), lax.rem(here + 1, blocks)


def one_hot(index, allowed=None):
    low = index & (LANES - 1)
    lane_at = iota((LANES, LANES), 0)
    if allowed is not None:
        lane_at = jnp.where(allowed(lane_at), lane_at, -1)
    return jnp.concatenate(
        [
            jnp.where(lane_at == low[c : c + 1], 1.0, 0.0).astype(jnp.bfloat16)
            for c in range(index.shape[0])
        ],
        axis=1,
    )


def scatter_sum(lines, index, bins, lanes_hot):
    split = []
    for values in lines:
        for part in range(3):
            short = values.astype(jnp.bfloat16).astype(jnp.float32)
            split.append(short)
            values = values - short
    high = index >> 7
    bin_at = iota((bins, LANES), 0)
    left = []
    for c in range(index.shape[0]):
        hit = bin_at == high[c : c + 1]
        left.append(
            jnp.concatenate(
                [jnp.where(hit, part[c : c + 1], 0.0) for part in split], axis=0
            ).astype(jnp.bfloat16)
        )
    total = lax.dot_general(
        jnp.concatenate(left, axis=1),
        lanes_hot,
        (((1,), (1,)), ((), ())),
        preferred_element_type=jnp.float32,
    )
    sums = []
    for i in range(len(lines)):
        part = total[3 * i * bins : 3 * (i + 1) * bins]
        sums.append(part[:bins] + part[bins : 2 * bins] + part[2 * bins :])
    return sums


def wind_tiles(wind_ref, x_points, level, lines):
    levels = wind_ref.shape[0] // (2 * x_points)
    return [
        [
            time_step
            * wind_ref[
                pl.ds((levels * part + level) * x_points + x, ROWS, stride=x_points), :
            ]
            for x in lines
        ]
        for part in range(2)
    ]


def start_kernel(
    planes,
    cols_in,
    weights_in,
    tracers_in,
    rows_in,
    jac_in,
    land_in,
    wind_in,
    air_in,
    send_in,
    slab_out,
    moved_ref,
    before_ref,
    after_ref,
    cols_ref,
    weights_ref,
    rows_ref,
    send_ref,
    slab_ref,
    tracers_ref,
    jac_ref,
    land_ref,
    wind_ref,
    air_ref,
    semaphores,
):
    copies = [
        pltpu.make_async_copy(source, target, semaphores.at[i])
        for i, (source, target) in enumerate(
            (
                (cols_in, cols_ref),
                (tracers_in.at[:ROWS], tracers_ref),
                (weights_in, weights_ref),
                (rows_in, rows_ref),
                (air_in, air_ref),
                (wind_in, wind_ref),
                (jac_in, jac_ref),
                (land_in, land_ref),
                (send_in, send_ref),
            )
        )
    ]
    for copy in copies:
        copy.start()
    geo = Geometry()
    blocks = cols_ref.shape[0]
    x_points = jac_ref.shape[0]
    levels = wind_ref.shape[0] // (2 * x_points)
    chunks = tracers_ref.shape[1] // LANES
    for copy in copies[:4]:
        copy.wait()

    for group in range(blocks // ROWS):
        at = slice(ROWS * group, ROWS * (group + 1))
        cells = cols_ref[at, :]
        high, low = cells >> 7, cells & (LANES - 1)
        surface = jnp.zeros((ROWS, LANES), jnp.float32)
        for k in range(chunks):
            line = spread(tracers_ref[0:1, LANES * k : LANES * (k + 1)])
            surface = jnp.where(high == k, take(line, low, 1), surface)
        area = weights_ref[at, :]
        heat = area * surface
        for c in range(ROWS):
            owner = ROWS * group + c
            for place, step in enumerate((1, 0, -1)):
                to = (owner + step) % blocks
                slab_ref[to, 2 * place : 2 * place + 1, :] = heat[c : c + 1]
                slab_ref[to, 2 * place + 1 : 2 * place + 2, :] = area[c : c + 1]

    out = pltpu.make_async_copy(slab_ref, slab_out, semaphores.at[len(copies)])
    out.start()
    ids = rows_ref[...].astype(jnp.float32)
    for side_ref in (before_ref, after_ref):
        side_ref[SIDE_IDS : SIDE_IDS + blocks, :] = ids

    for copy in copies[4:]:
        copy.wait()
    strips = []
    for h in range(2):
        half = slice(ROWS * h, ROWS * (h + 1))
        second = levels * x_points
        pack = jnp.zeros((ROWS, LANES), jnp.float32)
        for i, strip in enumerate(
            (
                air_ref[half, :],
                wind_ref[half, :],
                wind_ref[second + ROWS * h : second + ROWS * (h + 1), :],
                jac_ref[half, :],
                land_ref[half, :],
            )
        ):
            pack = jnp.where(
                (geo.lane >> 4) == i, pltpu.roll(strip, 16 * i + 8, 1), pack
            )
        strips.append(pack)
    to_right, to_left = split_sides(geo, strips[0], strips[1], ROWS)
    after_ref[SIDE_STRIP : SIDE_STRIP + ROWS, :] = to_right
    before_ref[SIDE_STRIP : SIDE_STRIP + ROWS, :] = to_left

    y_weight = jnp.where(geo.y_edge, 1.0 / 6.0, 5.0 / 6.0)
    for element in range(x_points // GLL):
        lines = [GLL * element + i for i in range(GLL)]
        mass = [
            (1.0 / 6.0 if i in (0, GLL - 1) else 5.0 / 6.0)
            * y_weight
            * spread(jac_ref[x : x + 1, :])
            for i, x in enumerate(lines)
        ]
        for level in range(0, levels, ROWS):
            wind = wind_tiles(wind_ref, x_points, level, lines)
            for plane in range(level, planes, levels):
                fields = [
                    air_ref[pl.ds(plane * x_points + x, ROWS, stride=x_points), :]
                    for x in lines
                ]
                slopes = geo.d_y(*fields)
                for i, x in enumerate(lines):
                    slope = sum(deriv_table[i][j] * fields[j] for j in range(GLL))
                    moved = mass[i] * (
                        fields[i] - (wind[0][i] * slope + wind[1][i] * slopes[i])
                    )
                    moved_ref[planes * x + plane : planes * x + plane + ROWS, :] = moved
    packs = [jnp.zeros((ROWS, LANES), jnp.float32) for _ in range(2)]
    packs = edges_of(geo, packs, moved_ref, planes, range(x_points))
    to_right, to_left = split_sides(geo, packs[0], packs[1], 1)
    after_ref[SIDE_EDGE : SIDE_EDGE + ROWS, :] = to_right
    before_ref[SIDE_EDGE : SIDE_EDGE + ROWS, :] = to_left
    out.wait()


def panel_kernel(
    planes,
    moved_ref,
    recv_ref,
    before_ref,
    after_ref,
    air_ref,
    wind_ref,
    jac_ref,
    land_ref,
    rows_ref,
    ocean_ref,
    avg_ref,
    down_ref,
    up_ref,
    down_again_ref,
    up_again_ref,
    surf_ref,
):
    geo = Geometry()
    blocks = rows_ref.shape[0]
    x_points = jac_ref.shape[0]
    levels = wind_ref.shape[0] // (2 * x_points)

    own_ids = rows_ref[...]
    left_ids = before_ref[SIDE_IDS : SIDE_IDS + blocks, :].astype(jnp.int32)
    right_ids = after_ref[SIDE_IDS : SIDE_IDS + blocks, :].astype(jnp.int32)
    head = [
        jnp.concatenate([recv_ref[c, i : i + 1, :] for c in range(blocks)], axis=0)
        for i in range(6)
    ]
    heat, frac = scatter_sum(head[2:4], own_ids, 2 * ROWS, one_hot(own_ids))
    from_left = scatter_sum(
        head[0:2], left_ids, 2 * ROWS, one_hot(left_ids, lambda lane: lane >= LANES - ROWS)
    )
    from_right = scatter_sum(
        head[4:6], right_ids, 2 * ROWS, one_hot(right_ids, lambda lane: lane < ROWS)
    )
    strip_heat = from_left[0] + from_right[0]
    strip_frac = from_left[1] + from_right[1]

    in_strip = (geo.lane < ROWS) | (geo.lane >= LANES - ROWS)
    packs = join_sides(
        geo,
        before_ref[SIDE_STRIP : SIDE_STRIP + ROWS, :],
        after_ref[SIDE_STRIP : SIDE_STRIP + ROWS, :],
        ROWS,
    )
    own, strip = [], []
    for h, pack in enumerate(packs):
        half = slice(ROWS * h, ROWS * (h + 1))
        strip.append(
            [
                jnp.where(
                    in_strip, pltpu.roll(pack, (-(16 * i + 8)) % LANES, 1), 1.0
                )
                for i in range(5)
            ]
        )
        own.append(
            [
                air_ref[half, :],
                wind_ref[half, :],
                wind_ref[
                    levels * x_points + ROWS * h : levels * x_points + ROWS * (h + 1), :
                ],
                jac_ref[half, :],
                land_ref[half, :],
            ]
        )
    for h in range(2):
        half = slice(ROWS * h, ROWS * (h + 1))
        pair = []
        for tile, ((field, wind_x, wind_y, jac, land), tile_heat, tile_frac) in enumerate(
            ((own[h], heat[half], frac[half]), (strip[h], strip_heat[half], strip_frac[half]))
        ):
            mass = geo.weight * jac
            if tile == 1:
                tile_heat = jnp.where(in_strip, tile_heat, 0.0)
                tile_frac = jnp.where(in_strip, tile_frac, 0.0)
            surf = (tile_heat + land * field) / (tile_frac + land)
            coef_x, coef_y = time_step * mass * wind_x, time_step * mass * wind_y
            moved = (
                mass * (field + relax_rate * (surf - field))
                - coef_x * geo.d_x(field)
                - coef_y * geo.d_y(field)[0]
            )
            pair.append((moved, mass))
            at = 2 * ROWS * tile + ROWS * h
            for number, value in (
                (MASS, mass),
                (COEF_X, coef_x),
                (COEF_Y, coef_y),
                (SURF, surf),
            ):
                surf_ref[4 * ROWS * number + at : 4 * ROWS * number + at + ROWS, :] = value
        for number, i in ((AVG, 0), (MASS_SUM, 1)):
            for tile, value in enumerate(geo.sum_y_pair(pair[0][i], pair[1][i])):
                at = 4 * ROWS * number + 2 * ROWS * tile + ROWS * h
                surf_ref[at : at + ROWS, :] = value

    joined = join_edges(
        geo,
        before_ref[SIDE_EDGE : SIDE_EDGE + ROWS, :],
        after_ref[SIDE_EDGE : SIDE_EDGE + ROWS, :],
    )
    for x in outer_rows(x_points):
        for group in range(planes // ROWS):
            at = slice(planes * x + ROWS * group, planes * x + ROWS * (group + 1))
            avg_ref[at, :] = geo.sum_y(moved_ref[at, :], outer_edges(joined, x, group))

    def line(r):
        return avg_ref[planes * r : planes * (r + 1), :]

    def surf_line(number, r):
        return surf_ref[pl.ds(4 * ROWS * number + r, 2, stride=x_points), :]

    def first_step(get, mass_at):
        return (
            [
                get(1) / mass_at(1),
                get(2) / mass_at(2),
                (get(3) + get(4)) / (mass_at(3) + mass_at(4)),
            ],
            [
                (get(11) + get(12)) / (mass_at(11) + mass_at(12)),
                get(13) / mass_at(13),
                get(14) / mass_at(14),
            ],
        )

    def own_mass_sum(r):
        return surf_ref[4 * ROWS * MASS_SUM + r : 4 * ROWS * MASS_SUM + r + 1, :]

    low_lines, high_lines = first_step(line, own_mass_sum)
    surf_low, surf_high = first_step(
        functools.partial(surf_line, AVG), functools.partial(surf_line, MASS_SUM)
    )
    for out_ref, r, lines, surf_lines, coefs in (
        (down_ref, 0, low_lines, surf_low, deriv_table[0][1:]),
        (up_ref, 15, high_lines, surf_high, deriv_table[3][:3]),
    ):
        slope = sum(coef * value for coef, value in zip(coefs, lines))
        surf_slope = sum(coef * value for coef, value in zip(coefs, surf_lines))
        mass = surf_ref[4 * ROWS * MASS + r : 4 * ROWS * MASS + r + 1, :]
        wind = time_step * mass * wind_ref[pl.ds(r, 2 * levels, stride=x_points), :]
        out_ref[0:planes, :] = line(r)
        for first in range(0, planes, levels):
            out_ref[planes + first : planes + first + levels, :] = (
                wind[:levels] * slope[first : first + levels]
            )
        base = 2 * planes
        out_ref[base : base + 2 * levels, :] = wind
        base += 2 * levels
        for number in range(SURF_ARRAYS):
            out_ref[base + 2 * number : base + 2 * number + 2, :] = surf_line(number, r)
        base += 2 * SURF_ARRAYS
        out_ref[base : base + 2, :] = surf_line(COEF_X, r) * surf_slope
    down_again_ref[...] = down_ref[...]
    up_again_ref[...] = up_ref[...]


def outer_rows(x_points):
    return [x for x in range(x_points) if x <= GLL or x >= x_points - GLL - 1]


def advance(geo, fields, wind, mass):
    slopes = geo.d_y(*fields)
    moved = []
    for i in range(GLL):
        slope = sum(deriv_table[i][j] * fields[j] for j in range(GLL))
        moved.append(mass[i] * (fields[i] - (wind[0][i] * slope + wind[1][i] * slopes[i])))
    return moved, slopes


def inner_kernel(
    planes, avg_ref, moved_ref, before_ref, after_ref, surf_ref, wind_ref, out_ref, packs_ref
):
    geo = Geometry()
    x_points = avg_ref.shape[0] // planes
    levels = wind_ref.shape[0] // (2 * x_points)
    joined = join_edges(
        geo,
        before_ref[SIDE_EDGE : SIDE_EDGE + ROWS, :],
        after_ref[SIDE_EDGE : SIDE_EDGE + ROWS, :],
    )
    outer = outer_rows(x_points)

    def average(x, plane):
        at = slice(planes * x + plane, planes * x + plane + ROWS)
        if x in outer:
            return avg_ref[at, :]
        return geo.sum_y(moved_ref[at, :], outer_edges(joined, x, plane // ROWS))

    def surf_row(number, x):
        at = 4 * ROWS * number + x
        return spread(surf_ref[at : at + 1, :])

    def put(x, plane, value):
        at = planes * (x - GLL) + plane
        out_ref[at : at + ROWS, :] = value

    held = {}
    carried = {}
    for element in range(1, x_points // GLL - 1):
        lines = [GLL * element + i for i in range(GLL)]
        totals = [surf_row(MASS_SUM, x) for x in lines]
        totals[0] = totals[0] + surf_row(MASS_SUM, lines[0] - 1)
        totals[-1] = totals[-1] + surf_row(MASS_SUM, lines[-1] + 1)
        scale = [1.0 / total for total in totals]
        mass = [surf_row(MASS, x) for x in lines]
        for level in range(0, levels, ROWS):
            wind = wind_tiles(wind_ref, x_points, level, lines)
            for plane in range(level, planes, levels):
                if element == 1:
                    first = average(lines[0], plane) + average(lines[0] - 1, plane)
                else:
                    first = carried[plane]
                last = average(lines[-1], plane) + average(lines[-1] + 1, plane)
                carried[plane] = last
                totals = (
                    [first] + [average(x, plane) for x in lines[1:-1]] + [last]
                )
                fields = [total * factor for total, factor in zip(totals, scale)]
                moved, _ = advance(geo, fields, wind, mass)
                if element == 1:
                    put(lines[0], plane, moved[0])
                else:
                    shared = held[plane] + moved[0]
                    put(lines[0] - 1, plane, shared)
                    put(lines[0], plane, shared)
                for i in range(1, GLL - 1):
                    put(lines[i], plane, moved[i])
                held[plane] = moved[-1]
                if lines[-1] == x_points - GLL - 1:
                    put(lines[-1], plane, moved[-1])
    packs = [jnp.zeros((ROWS, LANES), jnp.float32) for _ in range(2)]
    inner = [x for x in range(x_points) if x not in outer]
    for q, pack in enumerate(edges_of(geo, packs, out_ref, planes, inner, GLL)):
        packs_ref[ROWS * q : ROWS * (q + 1), :] = pack


def second_kernel(
    planes,
    avg_ref,
    inner_ref,
    packs_ref,
    surf_ref,
    high_odd_ref,
    low_odd_ref,
    low_even_ref,
    high_even_ref,
    wind_ref,
    rows_ref,
    slab_out,
    sums_ref,
    final_ref,
    inverse_ref,
    flux_ref,
    edges_ref,
    low_ref,
    high_ref,
    semaphores,
):
    geo = Geometry()
    odd = lax.rem(lax.axis_index("face"), 2) == 1
    low_ref[...] = jnp.where(odd, low_even_ref[...], low_odd_ref[...])
    high_ref[...] = jnp.where(odd, high_even_ref[...], high_odd_ref[...])
    blocks = rows_ref.shape[0]
    left, right = neighbours_of(blocks)
    x_points = final_ref.shape[0]
    levels = wind_ref.shape[0] // (2 * x_points)
    base = low_ref.shape[0] - 2 * SURF_ARRAYS - 4

    def surf_tile(number, tile, h):
        at = 4 * ROWS * number + 2 * ROWS * tile + ROWS * h
        return surf_ref[at : at + ROWS, :]

    def beside(ref, number, tile):
        at = base + 2 * number + tile
        return spread(ref[at : at + 1, :])

    ends = []
    inverse = []
    for tile in range(2):
        total = geo.sum_x(
            surf_tile(MASS_SUM, tile, 0),
            surf_tile(MASS_SUM, tile, 1),
            beside(low_ref, MASS_SUM, tile),
            beside(high_ref, MASS_SUM, tile),
        )
        inverse.append([1.0 / value for value in total])
        summed = geo.sum_x(
            surf_tile(AVG, tile, 0),
            surf_tile(AVG, tile, 1),
            beside(low_ref, AVG, tile),
            beside(high_ref, AVG, tile),
        )
        fields = [value * scale for value, scale in zip(summed, inverse[tile])]
        moved = []
        for h in range(2):
            field = fields[h]
            moved.append(
                surf_tile(MASS, tile, h)
                * (field + relax_rate * (surf_tile(SURF, tile, h) - field))
                - surf_tile(COEF_X, tile, h) * geo.d_x(field)
                - surf_tile(COEF_Y, tile, h) * geo.d_y(field)[0]
            )
        halos = []
        for ref, field, own_coef in (
            (low_ref, spread(fields[0][:1]), deriv_table[3][3]),
            (high_ref, spread(fields[1][ROWS - 1 :]), deriv_table[0][0]),
        ):
            halos.append(
                beside(ref, MASS, tile)
                * (field + relax_rate * (beside(ref, SURF, tile) - field))
                - beside(ref, SURF_ARRAYS, tile)
                - beside(ref, COEF_X, tile) * (own_coef * field)
                - beside(ref, COEF_Y, tile) * geo.d_y(field)[0]
            )
        ends.append(geo.sum_x(moved[0], moved[1], halos[0], halos[1]))
    final = []
    for h in range(2):
        summed, _ = geo.sum_y_pair(ends[0][h], ends[1][h])
        final.append(summed * inverse[0][h])
        final_ref[ROWS * h : ROWS * (h + 1), :] = final[h]
        inverse_ref[ROWS * h : ROWS * (h + 1), :] = inverse[0][h]
    flux = [final[h] - surf_tile(SURF, 0, h) for h in range(2)]
    for group in range(blocks // ROWS):
        ids = rows_ref[ROWS * group : ROWS * (group + 1), :]
        high, low = ids >> 7, ids & (LANES - 1)
        picked = jnp.zeros((ROWS, LANES), jnp.float32)
        for x in range(2 * ROWS):
            line = spread(flux[x // ROWS][x % ROWS : x % ROWS + 1])
            picked = jnp.where(high == x, take(line, low, 1), picked)
        for c in range(ROWS):
            flux_ref[ROWS * group + c, 0:1, :] = picked[c : c + 1]

    kept = outer_rows(x_points)

    def put(x, plane, value):
        at = planes * kept.index(x) + plane
        sums_ref[at : at + ROWS, :] = value

    def beyond(ref, plane, field, slope, own_coef):
        wind_at = 2 * planes + plane % levels
        return (
            beside(ref, MASS, 0) * field
            - ref[planes + plane : planes + plane + ROWS, :]
            - ref[wind_at : wind_at + ROWS, :] * (own_coef * field)
            - ref[wind_at + levels : wind_at + levels + ROWS, :] * slope
        )

    def row_of(tiles, x):
        return spread(tiles[x // ROWS][x % ROWS : x % ROWS + 1])

    masses = [surf_tile(MASS, 0, h) for h in range(2)]
    last_element = x_points // GLL - 1
    for element in (0, last_element):
        lines = [GLL * element + i for i in range(GLL)]
        scale = [row_of(inverse[0], x) for x in lines]
        mass = [row_of(masses, x) for x in lines]
        for level in range(0, levels, ROWS):
            wind = wind_tiles(wind_ref, x_points, level, lines)
            for plane in range(level, planes, levels):
                here = slice(plane, plane + ROWS)
                fields = []
                for i, x in enumerate(lines):
                    total = avg_ref[planes * x + plane : planes * x + plane + ROWS, :]
                    other = x - 1 if i == 0 else x + 1
                    if other < 0:
                        total = total + low_ref[here, :]
                    elif other == x_points:
                        total = total + high_ref[here, :]
                    elif i in (0, GLL - 1):
                        at = planes * other + plane
                        total = total + avg_ref[at : at + ROWS, :]
                    fields.append(total * scale[i])
                moved, slopes = advance(geo, fields, wind, mass)
                if element == 0:
                    before = beyond(low_ref, plane, fields[0], slopes[0], deriv_table[3][3])
                    put(lines[0], plane, before + moved[0])
                    shared = moved[-1] + inner_ref[here, :]
                    put(lines[-1], plane, shared)
                    put(lines[-1] + 1, plane, shared)
                else:
                    at = inner_ref.shape[0] - planes + plane
                    shared = moved[0] + inner_ref[at : at + ROWS, :]
                    put(lines[0] - 1, plane, shared)
                    put(lines[0], plane, shared)
                    after = beyond(
                        high_ref, plane, fields[-1], slopes[-1], deriv_table[0][0]
                    )
                    put(lines[-1], plane, moved[-1] + after)
                for i in range(1, GLL - 1):
                    put(lines[i], plane, moved[i])
    packs = [packs_ref[:ROWS, :], packs_ref[ROWS:, :]]
    packs = edges_of(geo, packs, sums_ref, planes, kept)
    to_right, to_left = split_sides(geo, packs[0], packs[1], 1)
    edges_ref[0] = to_right
    edges_ref[1] = to_left
    copies = [
        pltpu.make_async_copy(
            edges_ref.at[i], slab_out.at[to, EDGE_AT : EDGE_AT + ROWS], semaphores.at[i]
        )
        for i, to in enumerate((right, left))
    ]
    copies.append(
        pltpu.make_async_copy(flux_ref, slab_out.at[:, :HEAD], semaphores.at[2])
    )
    for copy in copies:
        copy.start()
    for copy in copies:
        copy.wait()


def last_kernel(planes, inner_ref, outer_ref, inverse_ref, cols_ref, out_ref, hot_ref):
    geo = Geometry()
    x_points = inverse_ref.shape[0]
    kept = outer_rows(x_points)
    hot_ref[...] = one_hot(cols_ref[...])
    for x in range(x_points):
        inverse = spread(inverse_ref[x : x + 1, :])
        ref, first = inner_ref, planes * (x - GLL)
        if x in kept:
            ref, first = outer_ref, planes * kept.index(x)
        for group in range(planes // ROWS):
            tile = ref[first + ROWS * group : first + ROWS * (group + 1), :]
            at = planes * x + ROWS * group
            out_ref[at : at + ROWS, :] = inverse * geo.sum_y(tile, 0.0)


def end_kernel(
    planes,
    last_ref,
    recv_ref,
    final_ref,
    inverse_ref,
    cols_ref,
    hot_ref,
    weights_ref,
    gain_ref,
    first_ref,
    ocean_in,
    ocean_out,
    air_out,
    air_ref,
    row_ref,
    semaphores,
):
    geo = Geometry()
    blocks = cols_ref.shape[0]
    left, right = neighbours_of(blocks)
    chunks = gain_ref.shape[0]
    x_points = inverse_ref.shape[0]
    copies = []

    def send(source, target):
        copies.append(
            pltpu.make_async_copy(source, target, semaphores.at[len(copies)])
        )
        copies[-1].start()

    joined = join_edges(
        geo,
        recv_ref[left, EDGE_AT : EDGE_AT + ROWS, :],
        recv_ref[right, EDGE_AT : EDGE_AT + ROWS, :],
    )
    groups = planes // ROWS
    for group in range(groups):
        for x in range(x_points):
            at = planes * x + ROWS * group
            beside = spread(inverse_ref[x : x + 1, :]) * outer_edges(joined, x, group)
            air_ref[pl.ds(ROWS * group * x_points + x, ROWS, stride=x_points), :] = last_ref[
                at : at + ROWS, :
            ] + jnp.where(geo.outer_lane, beside, 0.0)
        if group == 0:
            air_ref[0:x_points, :] = final_ref[...]
        if group % 2:
            rows = slice(
                ROWS * (group - 1) * x_points, ROWS * (group + 1) * x_points
            )
            send(air_ref.at[rows], air_out.at[rows])
    if groups % 2:
        rows = slice(ROWS * (groups - 1) * x_points, planes * x_points)
        send(air_ref.at[rows], air_out.at[rows])

    arrived = jnp.concatenate([recv_ref[c, 0:1, :] for c in range(blocks)], axis=0)
    (inflow,) = scatter_sum(
        [weights_ref[...] * arrived], cols_ref[...], chunks, hot_ref[...]
    )
    gain = inflow * gain_ref[...]
    row_ref[...] = first_ref[...]
    for k in range(chunks):
        at = slice(LANES * k, LANES * (k + 1))
        row_ref[0:1, at] = first_ref[0:1, at] + gain[k : k + 1]
    send(row_ref, ocean_out.at[:ROWS])
    for copy in copies:
        copy.wait()


def gathered(ids, coefs, source, sources, groups, first=0):
    totals = [jnp.zeros((ROWS, LANES), jnp.float32) for _ in range(groups)]
    for edge in range(ids.shape[0]):
        cell = spread(ids[edge : edge + 1])
        coef = spread(coefs[edge : edge + 1])
        high, low = cell >> 7, cell & (LANES - 1)
        for s in range(sources):
            scaled = jnp.where(high == first + s, coef, 0.0)
            for group in range(groups):
                totals[group] += scaled * take(source(group, s), low, 1)
    return totals


def multiplied(ids, coefs, halves_ref, sources, groups):
    lane_at = iota((LANES, LANES), 0)
    hot = jnp.concatenate(
        [
            jnp.where(lane_at == (ids[edge : edge + 1] & (LANES - 1)), 1.0, 0.0).astype(
                jnp.bfloat16
            )
            for edge in range(2)
        ],
        axis=1,
    )
    picked = jnp.dot(
        halves_ref[...],
        jnp.concatenate([hot, hot], axis=0),
        preferred_element_type=jnp.float32,
    )
    totals = [jnp.zeros((ROWS, LANES), jnp.float32) for _ in range(groups)]
    for edge in range(2):
        high = spread(ids[edge : edge + 1]) >> 7
        coef = spread(coefs[edge : edge + 1])
        side = slice(LANES * edge, LANES * (edge + 1))
        for s in range(sources):
            scaled = jnp.where(high == s, coef, 0.0)
            for group in range(groups):
                at = ROWS * (groups * s + group)
                totals[group] += scaled * picked[at : at + ROWS, side]
    return totals


def ocean_kernel(
    levels, start, tracers_ref, coef_ref, near_ref, rate_ref, after_ref, out_ref, halves_ref
):
    chunks = tracers_ref.shape[1] // LANES
    groups = tracers_ref.shape[0] // ROWS
    row = iota((ROWS, LANES), 0)

    def source(group, s):
        return tracers_ref[
            ROWS * group : ROWS * (group + 1), LANES * s : LANES * (s + 1)
        ]

    planes = tracers_ref.shape[0]
    for s in range(chunks):
        values = tracers_ref[:, LANES * s : LANES * (s + 1)]
        upper = values.astype(jnp.bfloat16)
        at = slice(planes * s, planes * (s + 1))
        halves_ref[at, :LANES] = upper
        halves_ref[at, LANES:] = (values - upper.astype(jnp.float32)).astype(jnp.bfloat16)
    edges = near_ref.shape[0]

    def one_chunk(number, carry):
        k = number + start
        at = pl.ds(pl.multiple_of(k * LANES, LANES), LANES)
        out_at = pl.ds(pl.multiple_of(number * LANES, LANES), LANES)
        ids, coefs = near_ref[:, at], coef_ref[:, at]
        by_gather = edges - edges // 3 * 2
        totals = gathered(ids[:by_gather], coefs[:by_gather], source, chunks, groups)
        for edge in range(by_gather, edges, 2):
            more = multiplied(
                ids[edge : edge + 2], coefs[edge : edge + 2], halves_ref, chunks, groups
            )
            totals = [total + part for total, part in zip(totals, more)]
        coef_sum = spread(jnp.sum(coefs, axis=0, keepdims=True))
        rate = spread(rate_ref[pl.ds(k, 1), :])
        tiles = [tracers_ref[ROWS * g : ROWS * (g + 1), at] for g in range(groups)]
        for g in range(groups):
            tile = tiles[g]
            top = bottom = tile
            if (ROWS * g) % levels:
                top = pltpu.roll(tiles[g - 1], 1, 0)
            if (ROWS * (g + 1)) % levels:
                bottom = pltpu.roll(tiles[g + 1], ROWS - 1, 0)
            above = jnp.where(row == 0, top, pltpu.roll(tile, 1, 0))
            below = jnp.where(row == ROWS - 1, bottom, pltpu.roll(tile, ROWS - 1, 0))
            vertical = rate * ((above - tile) + (below - tile))
            out_ref[ROWS * g : ROWS * (g + 1), out_at] = (
                tile + (totals[g] - coef_sum * tile) + vertical
            )
        return carry

    count = out_ref.shape[1] // LANES
    step = 2 if count % 2 == 0 else 1

    def some_chunks(number, carry):
        for i in range(step):
            one_chunk(step * number + i, carry)
        return carry

    lax.fori_loop(0, count // step, some_chunks, 0)


def send_kernel(tracers_ref, send_ref, before_ref, after_ref, *out_refs):
    chunks = tracers_ref.shape[1] // LANES
    for part, (side_ref, out_ref) in enumerate(zip((before_ref, after_ref), out_refs)):
        base = side_ref.shape[0]
        out_ref[:base, :] = side_ref[...]
        cells = spread(send_ref[0:1, LANES * part : LANES * (part + 1)])
        high, low = cells >> 7, cells & (LANES - 1)
        for group in range(tracers_ref.shape[0] // ROWS):
            half = slice(ROWS * group, ROWS * (group + 1))
            rim = jnp.zeros((ROWS, LANES), jnp.float32)
            for k in range(chunks):
                tile = tracers_ref[half, LANES * k : LANES * (k + 1)]
                rim = jnp.where(high == k, take(tile, low, 1), rim)
            out_ref[base + ROWS * group : base + ROWS * (group + 1), :] = rim


def rim_kernel(
    starts,
    before_ref,
    after_ref,
    coef_ref,
    near_ref,
    area_ref,
    rows_ref,
    *refs,
):
    partial_refs, (out_ref, gain_ref, first_ref) = refs[: len(starts)], refs[len(starts) :]
    chunks = coef_ref.shape[1] // LANES
    groups = out_ref.shape[0] // ROWS
    rim_at = before_ref.shape[0] - out_ref.shape[0]
    sides = before_ref, after_ref
    gain_ref[...] = flux_gain / area_ref[...]

    def source(group, s):
        at = rim_at + ROWS * group
        return sides[s][at : at + ROWS, :]

    for k in range(chunks):
        at = slice(LANES * k, LANES * (k + 1))
        totals = gathered(near_ref[:, at], coef_ref[:, at], source, 2, groups, chunks)
        part = max(i for i, start in enumerate(starts) if start <= k)
        place = slice(LANES * (k - starts[part]), LANES * (k - starts[part] + 1))
        for g in range(groups):
            half = slice(ROWS * g, ROWS * (g + 1))
            out_ref[half, at] = partial_refs[part][half, place] + totals[g]
    first_ref[...] = out_ref[:ROWS, :]


VMEM_SPEC = pl.BlockSpec(memory_space=pltpu.VMEM)
ANY_SPEC = pl.BlockSpec(memory_space=pl.ANY)
HBM_SPEC = pl.BlockSpec(memory_space=pltpu.HBM)


def call(kernel, outs, specs, scratch=(), cost=0, hbm_outs=0, aliases=None):
    estimate = None
    if cost:
        estimate = pl.CostEstimate(flops=0, bytes_accessed=cost, transcendentals=0)
    outs = [
        out if isinstance(out, jax.ShapeDtypeStruct) else jax.ShapeDtypeStruct(out, jnp.float32)
        for out in outs
    ]
    out_specs = [VMEM_SPEC] * len(outs)
    out_specs[:hbm_outs] = [HBM_SPEC] * hbm_outs
    return pl.pallas_call(
        kernel,
        out_shape=outs,
        in_specs=specs,
        out_specs=out_specs,
        scratch_shapes=list(scratch),
        input_output_aliases=aliases or {},
        cost_estimate=estimate,
        compiler_params=pltpu.CompilerParams(vmem_limit_bytes=32 * 2**20),
        name=getattr(kernel, "func", kernel).__name__,
    )


def body(
    air_state,
    air_wind,
    jacobian,
    land_area,
    xgrid_rows,
    tracers,
    edge_coef,
    neighbours,
    vert_rate,
    ocean_area,
    send_list,
    xgrid_cols,
    xgrid_weights,
):
    field_count, levels, x_points, y_points = air_state.shape
    planes = field_count * levels
    ocean_levels, cells = tracers.shape[1:]
    ocean_planes = tracers.shape[0] * ocean_levels
    faces, blocks = lax.axis_size("face"), lax.axis_size("blk")
    air = air_state.reshape(planes * x_points, y_points)
    wind = air_wind.reshape(2 * levels * x_points, y_points)
    ocean = tracers.reshape(ocean_planes, cells)
    point_ids, cell_ids, weights = xgrid_rows[0], xgrid_cols[0], xgrid_weights[0]
    rate = vert_rate.reshape(cells // LANES, LANES)
    area = ocean_area.reshape(cells // LANES, LANES)
    first_inputs = (
        cell_ids,
        weights,
        ocean,
        point_ids,
        jacobian,
        land_area,
        wind,
        air,
        send_list,
    )
    kept = (cell_ids, weights, point_ids, send_list)
    slab, moved, to_before, to_after, cell_ids, weights, point_ids, send_list = call(
        functools.partial(start_kernel, planes),
        [(blocks, HEAD, LANES), air.shape]
        + [(SIDE_IDS + blocks, LANES)] * 2
        + [jax.ShapeDtypeStruct(array.shape, array.dtype) for array in kept],
        [HBM_SPEC] * len(first_inputs),
        [
            pltpu.VMEM(shape, jnp.float32)
            for shape in (
                (blocks, HEAD, LANES),
                (ROWS, cells),
                jacobian.shape,
                land_area.shape,
                wind.shape,
                air.shape,
            )
        ]
        + [pltpu.SemaphoreType.DMA((len(first_inputs) + 1,))],
        hbm_outs=1,
    )(*(pltpu.with_memory_space_constraint(array, pltpu.HBM) for array in first_inputs))
    recv = lax.all_to_all(slab, "blk", split_axis=0, concat_axis=0, tiled=True)

    chunks = cells // LANES
    reads_per_chunk = edge_coef.shape[0] * chunks * (ocean_planes // ROWS)
    starts = (0, chunks * 6 // 16)

    def ocean_part(start, end, after):
        (result,) = call(
            functools.partial(ocean_kernel, ocean_levels, start),
            [(ocean_planes, (end - start) * LANES)],
            [VMEM_SPEC] * 4 + [ANY_SPEC],
            [pltpu.VMEM((chunks * ocean_planes, 2 * LANES), jnp.bfloat16)],
            cost=(end - start) * reads_per_chunk * ROWS * LANES * 2,
        )(ocean, edge_coef, neighbours, rate, after)
        return result

    to_before, to_after = call(
        send_kernel,
        [(SIDE_IDS + blocks + ocean_planes, LANES)] * 2,
        [VMEM_SPEC] * 4,
        cost=reads_per_chunk * ROWS * LANES,
    )(ocean, send_list, to_before, to_after)
    onward = [(i, (i + 1) % blocks) for i in range(blocks)]
    before = lax.ppermute(to_after, "blk", onward)
    after = lax.ppermute(to_before, "blk", [(to, source) for source, to in onward])
    first_part = ocean_part(starts[0], starts[1], to_before)
    side_rows = 2 * planes + 2 * levels + 2 * SURF_ARRAYS + 4
    avg, down, up, down_again, up_again, surf = call(
        functools.partial(panel_kernel, planes),
        [air.shape] + [(side_rows, LANES)] * 4 + [(4 * ROWS * SURF_ARRAYS, LANES)],
        [VMEM_SPEC] * 9 + [ANY_SPEC],
    )(
        moved,
        recv,
        before,
        after,
        air,
        wind,
        jacobian,
        land_area,
        point_ids,
        first_part,
    )
    odd_faces, even_faces = range(1, faces, 2), range(0, faces, 2)
    high_odd = lax.ppermute(down, "face", [(i, (i - 1) % faces) for i in odd_faces])
    low_odd = lax.ppermute(up, "face", [(i, (i + 1) % faces) for i in odd_faces])
    low_even = lax.ppermute(up_again, "face", [(i, (i + 1) % faces) for i in even_faces])
    high_even = lax.ppermute(down_again, "face", [(i, (i - 1) % faces) for i in even_faces])
    inner, packs = call(
        functools.partial(inner_kernel, planes),
        [((x_points - 2 * GLL) * planes, LANES), (2 * ROWS, LANES)],
        [VMEM_SPEC] * 6,
        cost=2 * air.size * 4,
    )(avg, moved, before, after, surf, wind)
    slab, outer, final, inverse = call(
        functools.partial(second_kernel, planes),
        [
            (blocks, EDGE_AT + ROWS, LANES),
            (len(outer_rows(x_points)) * planes, LANES),
            (x_points, y_points),
            (x_points, y_points),
        ],
        [VMEM_SPEC] * 10,
        [
            pltpu.VMEM((blocks, HEAD, LANES), jnp.float32),
            pltpu.VMEM((2, ROWS, LANES), jnp.float32),
            pltpu.VMEM((side_rows, LANES), jnp.float32),
            pltpu.VMEM((side_rows, LANES), jnp.float32),
            pltpu.SemaphoreType.DMA((3,)),
        ],
        hbm_outs=1,
    )(
        avg,
        inner,
        packs,
        surf,
        high_odd,
        low_odd,
        low_even,
        high_even,
        wind,
        point_ids,
    )
    arrived = lax.all_to_all(slab, "blk", split_axis=0, concat_axis=0, tiled=True)
    last, hot = call(
        functools.partial(last_kernel, planes),
        [air.shape, jax.ShapeDtypeStruct((LANES, blocks * LANES), jnp.bfloat16)],
        [VMEM_SPEC] * 4,
        cost=2 * air.size * 4,
    )(inner, outer, inverse, cell_ids)
    second_part = ocean_part(starts[1], chunks, final)
    partial, gain, first_rows = call(
        functools.partial(rim_kernel, starts),
        [ocean.shape, area.shape, (ROWS, cells)],
        [VMEM_SPEC] * 5 + [ANY_SPEC] + [VMEM_SPEC] * len(starts),
        cost=chunks * reads_per_chunk // 8 * ROWS * LANES * 4,
    )(
        before,
        after,
        edge_coef,
        neighbours,
        area,
        final,
        first_part,
        second_part,
    )
    ocean_final, air_final = call(
        functools.partial(end_kernel, planes),
        [ocean.shape, air.shape],
        [VMEM_SPEC] * 9 + [HBM_SPEC],
        [
            pltpu.VMEM(air.shape, jnp.float32),
            pltpu.VMEM((ROWS, cells), jnp.float32),
            pltpu.SemaphoreType.DMA((1 + planes // ROWS,)),
        ],
        hbm_outs=2,
        aliases={9: 0},
    )(
        last,
        arrived,
        final,
        inverse,
        cell_ids,
        hot,
        weights,
        gain,
        first_rows,
        pltpu.with_memory_space_constraint(partial, pltpu.HBM),
    )
    return air_final.reshape(air_state.shape), ocean_final.reshape(tracers.shape)


def solution(mesh):
    return jax.shard_map(
        body,
        mesh=mesh,
        in_specs=(
            P(None, None, "face", "blk"),
            P(None, None, "face", "blk"),
            P("face", "blk"),
            P("face", "blk"),
            P(("face", "blk"), None, None),
            P(None, None, ("face", "blk")),
            P(None, ("face", "blk")),
            P(None, ("face", "blk")),
            P(("face", "blk")),
            P(("face", "blk")),
            P(("face", "blk"), None),
            P(("face", "blk"), None, None),
            P(("face", "blk"), None, None),
        ),
        out_specs=(P(None, None, "face", "blk"), P(None, None, ("face", "blk"))),
        check_vma=False,
    )
```

```python
import functools

import jax
import jax.numpy as jnp
from jax import lax
from jax.experimental import pallas as pl
from jax.experimental.pallas import tpu as pltpu
from jax.sharding import PartitionSpec as P

GLL = 4
ROWS = 8
LANES = 128

deriv_table = [
    [-3.0, 4.045084971874737, -1.545084971874737, 0.5],
    [-0.8090169943749475, 0.0, 1.118033988749895, -0.30901699437494745],
    [0.30901699437494745, -1.118033988749895, 0.0, 0.8090169943749475],
    [-0.5, 1.545084971874737, -4.045084971874737, 3.0],
]
time_step = 0.05
relax_rate = 0.3
flux_gain = 0.2

HEAD = 8
SIDE_EDGE, SIDE_STRIP, SIDE_IDS = 0, 8, 16
AVG, MASS_SUM, MASS, COEF_X, COEF_Y, SURF = range(6)
SURF_ARRAYS = 6


def iota(shape, dim):
    return lax.broadcasted_iota(jnp.int32, shape, dim)


def take(values, index, axis):
    return jnp.take_along_axis(values, index, axis=axis, mode="promise_in_bounds")


def by_position(pos, values):
    result = jnp.full(pos.shape, values[-1], jnp.float32)
    for i, value in enumerate(values[:-1]):
        result = jnp.where(pos == i, value, result)
    return result


def spread(row):
    return jnp.broadcast_to(row, (ROWS, LANES))


class Geometry:
    def __init__(self):
        shape = (ROWS, LANES)
        self.row, self.lane = iota(shape, 0), iota(shape, 1)
        x_pos, y_pos = self.row & (GLL - 1), self.lane & (GLL - 1)
        self.y_from = [self.lane - y_pos + j for j in range(GLL)]
        columns = [[line[j] for line in deriv_table] for j in range(GLL)]
        self.x_coef = {
            step: by_position(
                x_pos,
                [
                    deriv_table[i][i + step] if 0 <= i + step < GLL else 0.0
                    for i in range(GLL)
                ],
            )
            for step in range(1 - GLL, GLL)
        }
        self.y_coef = [by_position(y_pos, column) for column in columns]
        self.y_swap = (
            self.lane + jnp.where(y_pos == GLL - 1, 1, 0) - jnp.where(y_pos == 0, 1, 0)
        ) & (LANES - 1)
        self.x_edge = (x_pos == 0) | (x_pos == GLL - 1)
        self.y_edge = (y_pos == 0) | (y_pos == GLL - 1)
        self.first_row, self.last_row = self.row == 0, self.row == ROWS - 1
        self.middle_row = self.row == GLL
        self.outer_lane = (self.lane == 0) | (self.lane == LANES - 1)
        self.weight = jnp.where(self.x_edge, 1.0 / 6.0, 5.0 / 6.0) * jnp.where(
            self.y_edge, 1.0 / 6.0, 5.0 / 6.0
        )

    def d_x(self, tile):
        return sum(
            coef * (pltpu.roll(tile, -step % ROWS, 0) if step else tile)
            for step, coef in self.x_coef.items()
        )

    def d_y(self, *tiles):
        totals = [0.0] * len(tiles)
        for j in range(GLL):
            for i, tile in enumerate(tiles):
                totals[i] += self.y_coef[j] * take(tile, self.y_from[j], 1)
        return totals

    def sum_x(self, low, high, before, after):
        low_down, low_up = pltpu.roll(low, 1, 0), pltpu.roll(low, ROWS - 1, 0)
        high_down, high_up = pltpu.roll(high, 1, 0), pltpu.roll(high, ROWS - 1, 0)
        low_other = jnp.where(
            self.first_row,
            before,
            jnp.where(
                self.middle_row, low_down, jnp.where(self.last_row, high_up, low_up)
            ),
        )
        high_other = jnp.where(
            self.first_row,
            low_down,
            jnp.where(
                self.middle_row, high_down, jnp.where(self.last_row, after, high_up)
            ),
        )
        return (
            low + jnp.where(self.x_edge, low_other, 0.0),
            high + jnp.where(self.x_edge, high_other, 0.0),
        )

    def sum_y(self, tile, outer):
        other = jnp.where(self.outer_lane, outer, take(tile, self.y_swap, 1))
        return tile + jnp.where(self.y_edge, other, 0.0)

    def sum_y_pair(self, own, strip):
        own_swap, strip_swap = take(own, self.y_swap, 1), take(strip, self.y_swap, 1)
        own_other = jnp.where(self.outer_lane, strip_swap, own_swap)
        strip_other = jnp.where(self.outer_lane, own_swap, strip_swap)
        return (
            own + jnp.where(self.y_edge, own_other, 0.0),
            strip + jnp.where(self.y_edge, strip_other, 0.0),
        )


def edge_place(x, group):
    return x // ROWS, LANES // 2 * (x % 2) + ROWS * group + 2 * (x % ROWS // 2)


def edges_of(geo, packs, ref, planes, lines, first=None):
    packs = list(packs)
    for number, x in enumerate(lines):
        base = planes * (number if first is None else x - first)
        for group in range(planes // ROWS):
            q, at = edge_place(x, group)
            tile = ref[base + ROWS * group : base + ROWS * (group + 1), :]
            rolled = pltpu.roll(tile, (at + 1) % LANES, 1)
            packs[q] = jnp.where((geo.lane >> 1) == at // 2, rolled, packs[q])
    return packs


def outer_edges(joined, x, group):
    q, at = edge_place(x, group)
    return pltpu.roll(joined[q], (-(at + 1)) % LANES, 1)


def split_sides(geo, first, second, unit):
    odd = (geo.lane & unit) != 0
    return (
        jnp.where(odd, pltpu.roll(second, unit, 1), first),
        jnp.where(odd, second, pltpu.roll(first, LANES - unit, 1)),
    )


def join_sides(geo, before, after, unit):
    odd = (geo.lane & unit) != 0
    return (
        jnp.where(odd, pltpu.roll(after, unit, 1), before),
        jnp.where(odd, after, pltpu.roll(before, LANES - unit, 1)),
    )


def join_edges(geo, before, after):
    odd = (geo.lane & 1) != 0
    return (
        jnp.where(odd, pltpu.roll(before, 1, 1), after),
        jnp.where(odd, before, pltpu.roll(after, LANES - 1, 1)),
    )


def neighbours_of(blocks):
    here = lax.axis_index("blk")
    return lax.rem(here + blocks - 1, blocks), lax.rem(here + 1, blocks)


def one_hot(index, allowed=None):
    low = index & (LANES - 1)
    lane_at = iota((LANES, LANES), 0)
    if allowed is not None:
        lane_at = jnp.where(allowed(lane_at), lane_at, -1)
    return jnp.concatenate(
        [
            jnp.where(lane_at == low[c : c + 1], 1.0, 0.0).astype(jnp.bfloat16)
            for c in range(index.shape[0])
        ],
        axis=1,
    )


def scatter_sum(lines, index, bins, lanes_hot):
    split = []
    for values in lines:
        for part in range(3):
            short = values.astype(jnp.bfloat16).astype(jnp.float32)
            split.append(short)
            values = values - short
    high = index >> 7
    bin_at = iota((bins, LANES), 0)
    left = []
    for c in range(index.shape[0]):
        hit = bin_at == high[c : c + 1]
        left.append(
            jnp.concatenate(
                [jnp.where(hit, part[c : c + 1], 0.0) for part in split], axis=0
            ).astype(jnp.bfloat16)
        )
    total = lax.dot_general(
        jnp.concatenate(left, axis=1),
        lanes_hot,
        (((1,), (1,)), ((), ())),
        preferred_element_type=jnp.float32,
    )
    sums = []
    for i in range(len(lines)):
        part = total[3 * i * bins : 3 * (i + 1) * bins]
        sums.append(part[:bins] + part[bins : 2 * bins] + part[2 * bins :])
    return sums


def wind_tiles(wind_ref, x_points, level, lines):
    levels = wind_ref.shape[0] // (2 * x_points)
    return [
        [
            time_step
            * wind_ref[
                pl.ds((levels * part + level) * x_points + x, ROWS, stride=x_points), :
            ]
            for x in lines
        ]
        for part in range(2)
    ]


def start_kernel(
    planes,
    cols_in,
    weights_in,
    tracers_in,
    rows_in,
    jac_in,
    land_in,
    wind_in,
    air_in,
    send_in,
    slab_out,
    moved_ref,
    before_ref,
    after_ref,
    cols_ref,
    weights_ref,
    rows_ref,
    send_ref,
    slab_ref,
    tracers_ref,
    jac_ref,
    land_ref,
    wind_ref,
    air_ref,
    semaphores,
):
    copies = [
        pltpu.make_async_copy(source, target, semaphores.at[i])
        for i, (source, target) in enumerate(
            (
                (cols_in, cols_ref),
                (tracers_in.at[:ROWS], tracers_ref),
                (weights_in, weights_ref),
                (rows_in, rows_ref),
                (air_in, air_ref),
                (wind_in, wind_ref),
                (jac_in, jac_ref),
                (land_in, land_ref),
                (send_in, send_ref),
            )
        )
    ]
    for copy in copies:
        copy.start()
    geo = Geometry()
    blocks = cols_ref.shape[0]
    x_points = jac_ref.shape[0]
    levels = wind_ref.shape[0] // (2 * x_points)
    chunks = tracers_ref.shape[1] // LANES
    for copy in copies[:4]:
        copy.wait()

    for group in range(blocks // ROWS):
        at = slice(ROWS * group, ROWS * (group + 1))
        cells = cols_ref[at, :]
        high, low = cells >> 7, cells & (LANES - 1)
        surface = jnp.zeros((ROWS, LANES), jnp.float32)
        for k in range(chunks):
            line = spread(tracers_ref[0:1, LANES * k : LANES * (k + 1)])
            surface = jnp.where(high == k, take(line, low, 1), surface)
        area = weights_ref[at, :]
        heat = area * surface
        for c in range(ROWS):
            owner = ROWS * group + c
            for place, step in enumerate((1, 0, -1)):
                to = (owner + step) % blocks
                slab_ref[to, 2 * place : 2 * place + 1, :] = heat[c : c + 1]
                slab_ref[to, 2 * place + 1 : 2 * place + 2, :] = area[c : c + 1]

    out = pltpu.make_async_copy(slab_ref, slab_out, semaphores.at[len(copies)])
    out.start()
    ids = rows_ref[...].astype(jnp.float32)
    for side_ref in (before_ref, after_ref):
        side_ref[SIDE_IDS : SIDE_IDS + blocks, :] = ids

    for copy in copies[4:]:
        copy.wait()
    strips = []
    for h in range(2):
        half = slice(ROWS * h, ROWS * (h + 1))
        second = levels * x_points
        pack = jnp.zeros((ROWS, LANES), jnp.float32)
        for i, strip in enumerate(
            (
                air_ref[half, :],
                wind_ref[half, :],
                wind_ref[second + ROWS * h : second + ROWS * (h + 1), :],
                jac_ref[half, :],
                land_ref[half, :],
            )
        ):
            pack = jnp.where(
                (geo.lane >> 4) == i, pltpu.roll(strip, 16 * i + 8, 1), pack
            )
        strips.append(pack)
    to_right, to_left = split_sides(geo, strips[0], strips[1], ROWS)
    after_ref[SIDE_STRIP : SIDE_STRIP + ROWS, :] = to_right
    before_ref[SIDE_STRIP : SIDE_STRIP + ROWS, :] = to_left

    y_weight = jnp.where(geo.y_edge, 1.0 / 6.0, 5.0 / 6.0)
    for element in range(x_points // GLL):
        lines = [GLL * element + i for i in range(GLL)]
        mass = [
            (1.0 / 6.0 if i in (0, GLL - 1) else 5.0 / 6.0)
            * y_weight
            * spread(jac_ref[x : x + 1, :])
            for i, x in enumerate(lines)
        ]
        for level in range(0, levels, ROWS):
            wind = wind_tiles(wind_ref, x_points, level, lines)
            for plane in range(level, planes, levels):
                fields = [
                    air_ref[pl.ds(plane * x_points + x, ROWS, stride=x_points), :]
                    for x in lines
                ]
                slopes = geo.d_y(*fields)
                for i, x in enumerate(lines):
                    slope = sum(deriv_table[i][j] * fields[j] for j in range(GLL))
                    moved = mass[i] * (
                        fields[i] - (wind[0][i] * slope + wind[1][i] * slopes[i])
                    )
                    moved_ref[planes * x + plane : planes * x + plane + ROWS, :] = moved
    packs = [jnp.zeros((ROWS, LANES), jnp.float32) for _ in range(2)]
    packs = edges_of(geo, packs, moved_ref, planes, range(x_points))
    to_right, to_left = split_sides(geo, packs[0], packs[1], 1)
    after_ref[SIDE_EDGE : SIDE_EDGE + ROWS, :] = to_right
    before_ref[SIDE_EDGE : SIDE_EDGE + ROWS, :] = to_left
    out.wait()


def panel_kernel(
    planes,
    moved_ref,
    recv_ref,
    before_ref,
    after_ref,
    air_ref,
    wind_ref,
    jac_ref,
    land_ref,
    rows_ref,
    ocean_ref,
    avg_ref,
    down_ref,
    up_ref,
    surf_ref,
):
    geo = Geometry()
    blocks = rows_ref.shape[0]
    x_points = jac_ref.shape[0]
    levels = wind_ref.shape[0] // (2 * x_points)

    own_ids = rows_ref[...]
    left_ids = before_ref[SIDE_IDS : SIDE_IDS + blocks, :].astype(jnp.int32)
    right_ids = after_ref[SIDE_IDS : SIDE_IDS + blocks, :].astype(jnp.int32)
    head = [
        jnp.concatenate([recv_ref[c, i : i + 1, :] for c in range(blocks)], axis=0)
        for i in range(6)
    ]
    heat, frac = scatter_sum(head[2:4], own_ids, 2 * ROWS, one_hot(own_ids))
    from_left = scatter_sum(
        head[0:2], left_ids, 2 * ROWS, one_hot(left_ids, lambda lane: lane >= LANES - ROWS)
    )
    from_right = scatter_sum(
        head[4:6], right_ids, 2 * ROWS, one_hot(right_ids, lambda lane: lane < ROWS)
    )
    strip_heat = from_left[0] + from_right[0]
    strip_frac = from_left[1] + from_right[1]

    in_strip = (geo.lane < ROWS) | (geo.lane >= LANES - ROWS)
    packs = join_sides(
        geo,
        before_ref[SIDE_STRIP : SIDE_STRIP + ROWS, :],
        after_ref[SIDE_STRIP : SIDE_STRIP + ROWS, :],
        ROWS,
    )
    own, strip = [], []
    for h, pack in enumerate(packs):
        half = slice(ROWS * h, ROWS * (h + 1))
        strip.append(
            [
                jnp.where(
                    in_strip, pltpu.roll(pack, (-(16 * i + 8)) % LANES, 1), 1.0
                )
                for i in range(5)
            ]
        )
        own.append(
            [
                air_ref[half, :],
                wind_ref[half, :],
                wind_ref[
                    levels * x_points + ROWS * h : levels * x_points + ROWS * (h + 1), :
                ],
                jac_ref[half, :],
                land_ref[half, :],
            ]
        )
    for h in range(2):
        half = slice(ROWS * h, ROWS * (h + 1))
        pair = []
        for tile, ((field, wind_x, wind_y, jac, land), tile_heat, tile_frac) in enumerate(
            ((own[h], heat[half], frac[half]), (strip[h], strip_heat[half], strip_frac[half]))
        ):
            mass = geo.weight * jac
            if tile == 1:
                tile_heat = jnp.where(in_strip, tile_heat, 0.0)
                tile_frac = jnp.where(in_strip, tile_frac, 0.0)
            surf = (tile_heat + land * field) / (tile_frac + land)
            coef_x, coef_y = time_step * mass * wind_x, time_step * mass * wind_y
            moved = (
                mass * (field + relax_rate * (surf - field))
                - coef_x * geo.d_x(field)
                - coef_y * geo.d_y(field)[0]
            )
            pair.append((moved, mass))
            at = 2 * ROWS * tile + ROWS * h
            for number, value in (
                (MASS, mass),
                (COEF_X, coef_x),
                (COEF_Y, coef_y),
                (SURF, surf),
            ):
                surf_ref[4 * ROWS * number + at : 4 * ROWS * number + at + ROWS, :] = value
        for number, i in ((AVG, 0), (MASS_SUM, 1)):
            for tile, value in enumerate(geo.sum_y_pair(pair[0][i], pair[1][i])):
                at = 4 * ROWS * number + 2 * ROWS * tile + ROWS * h
                surf_ref[at : at + ROWS, :] = value

    joined = join_edges(
        geo,
        before_ref[SIDE_EDGE : SIDE_EDGE + ROWS, :],
        after_ref[SIDE_EDGE : SIDE_EDGE + ROWS, :],
    )
    for x in outer_rows(x_points):
        for group in range(planes // ROWS):
            at = slice(planes * x + ROWS * group, planes * x + ROWS * (group + 1))
            avg_ref[at, :] = geo.sum_y(moved_ref[at, :], outer_edges(joined, x, group))

    def line(r):
        return avg_ref[planes * r : planes * (r + 1), :]

    def surf_line(number, r):
        return surf_ref[pl.ds(4 * ROWS * number + r, 2, stride=x_points), :]

    def first_step(get, mass_at):
        return (
            [
                get(1) / mass_at(1),
                get(2) / mass_at(2),
                (get(3) + get(4)) / (mass_at(3) + mass_at(4)),
            ],
            [
                (get(11) + get(12)) / (mass_at(11) + mass_at(12)),
                get(13) / mass_at(13),
                get(14) / mass_at(14),
            ],
        )

    def own_mass_sum(r):
        return surf_ref[4 * ROWS * MASS_SUM + r : 4 * ROWS * MASS_SUM + r + 1, :]

    low_lines, high_lines = first_step(line, own_mass_sum)
    surf_low, surf_high = first_step(
        functools.partial(surf_line, AVG), functools.partial(surf_line, MASS_SUM)
    )
    for out_ref, r, lines, surf_lines, coefs in (
        (down_ref, 0, low_lines, surf_low, deriv_table[0][1:]),
        (up_ref, 15, high_lines, surf_high, deriv_table[3][:3]),
    ):
        slope = sum(coef * value for coef, value in zip(coefs, lines))
        surf_slope = sum(coef * value for coef, value in zip(coefs, surf_lines))
        mass = surf_ref[4 * ROWS * MASS + r : 4 * ROWS * MASS + r + 1, :]
        wind = time_step * mass * wind_ref[pl.ds(r, 2 * levels, stride=x_points), :]
        out_ref[0:planes, :] = line(r)
        for first in range(0, planes, levels):
            out_ref[planes + first : planes + first + levels, :] = (
                wind[:levels] * slope[first : first + levels]
            )
        base = 2 * planes
        out_ref[base : base + 2 * levels, :] = wind
        base += 2 * levels
        for number in range(SURF_ARRAYS):
            out_ref[base + 2 * number : base + 2 * number + 2, :] = surf_line(number, r)
        base += 2 * SURF_ARRAYS
        out_ref[base : base + 2, :] = surf_line(COEF_X, r) * surf_slope


def outer_rows(x_points):
    return [x for x in range(x_points) if x <= GLL or x >= x_points - GLL - 1]


def advance(geo, fields, wind, mass):
    slopes = geo.d_y(*fields)
    moved = []
    for i in range(GLL):
        slope = sum(deriv_table[i][j] * fields[j] for j in range(GLL))
        moved.append(mass[i] * (fields[i] - (wind[0][i] * slope + wind[1][i] * slopes[i])))
    return moved, slopes


def inner_kernel(
    planes, avg_ref, moved_ref, before_ref, after_ref, surf_ref, wind_ref, out_ref, packs_ref
):
    geo = Geometry()
    x_points = avg_ref.shape[0] // planes
    levels = wind_ref.shape[0] // (2 * x_points)
    joined = join_edges(
        geo,
        before_ref[SIDE_EDGE : SIDE_EDGE + ROWS, :],
        after_ref[SIDE_EDGE : SIDE_EDGE + ROWS, :],
    )
    outer = outer_rows(x_points)

    def average(x, plane):
        at = slice(planes * x + plane, planes * x + plane + ROWS)
        if x in outer:
            return avg_ref[at, :]
        return geo.sum_y(moved_ref[at, :], outer_edges(joined, x, plane // ROWS))

    def surf_row(number, x):
        at = 4 * ROWS * number + x
        return spread(surf_ref[at : at + 1, :])

    def put(x, plane, value):
        at = planes * (x - GLL) + plane
        out_ref[at : at + ROWS, :] = value

    held = {}
    carried = {}
    for element in range(1, x_points // GLL - 1):
        lines = [GLL * element + i for i in range(GLL)]
        totals = [surf_row(MASS_SUM, x) for x in lines]
        totals[0] = totals[0] + surf_row(MASS_SUM, lines[0] - 1)
        totals[-1] = totals[-1] + surf_row(MASS_SUM, lines[-1] + 1)
        scale = [1.0 / total for total in totals]
        mass = [surf_row(MASS, x) for x in lines]
        for level in range(0, levels, ROWS):
            wind = wind_tiles(wind_ref, x_points, level, lines)
            for plane in range(level, planes, levels):
                if element == 1:
                    first = average(lines[0], plane) + average(lines[0] - 1, plane)
                else:
                    first = carried[plane]
                last = average(lines[-1], plane) + average(lines[-1] + 1, plane)
                carried[plane] = last
                totals = (
                    [first] + [average(x, plane) for x in lines[1:-1]] + [last]
                )
                fields = [total * factor for total, factor in zip(totals, scale)]
                moved, _ = advance(geo, fields, wind, mass)
                if element == 1:
                    put(lines[0], plane, moved[0])
                else:
                    shared = held[plane] + moved[0]
                    put(lines[0] - 1, plane, shared)
                    put(lines[0], plane, shared)
                for i in range(1, GLL - 1):
                    put(lines[i], plane, moved[i])
                held[plane] = moved[-1]
                if lines[-1] == x_points - GLL - 1:
                    put(lines[-1], plane, moved[-1])
    packs = [jnp.zeros((ROWS, LANES), jnp.float32) for _ in range(2)]
    inner = [x for x in range(x_points) if x not in outer]
    for q, pack in enumerate(edges_of(geo, packs, out_ref, planes, inner, GLL)):
        packs_ref[ROWS * q : ROWS * (q + 1), :] = pack


def second_kernel(
    planes,
    avg_ref,
    inner_ref,
    packs_ref,
    surf_ref,
    low_ref,
    high_ref,
    wind_ref,
    rows_ref,
    ocean_ref,
    slab_out,
    sums_ref,
    final_ref,
    inverse_ref,
    edges_ref,
    flux_ref,
    semaphore,
):
    geo = Geometry()
    blocks = rows_ref.shape[0]
    x_points = final_ref.shape[0]
    levels = wind_ref.shape[0] // (2 * x_points)
    base = low_ref.shape[0] - 2 * SURF_ARRAYS - 4

    def surf_tile(number, tile, h):
        at = 4 * ROWS * number + 2 * ROWS * tile + ROWS * h
        return surf_ref[at : at + ROWS, :]

    def beside(ref, number, tile):
        at = base + 2 * number + tile
        return spread(ref[at : at + 1, :])

    ends = []
    inverse = []
    for tile in range(2):
        total = geo.sum_x(
            surf_tile(MASS_SUM, tile, 0),
            surf_tile(MASS_SUM, tile, 1),
            beside(low_ref, MASS_SUM, tile),
            beside(high_ref, MASS_SUM, tile),
        )
        inverse.append([1.0 / value for value in total])
        summed = geo.sum_x(
            surf_tile(AVG, tile, 0),
            surf_tile(AVG, tile, 1),
            beside(low_ref, AVG, tile),
            beside(high_ref, AVG, tile),
        )
        fields = [value * scale for value, scale in zip(summed, inverse[tile])]
        moved = []
        for h in range(2):
            field = fields[h]
            moved.append(
                surf_tile(MASS, tile, h)
                * (field + relax_rate * (surf_tile(SURF, tile, h) - field))
                - surf_tile(COEF_X, tile, h) * geo.d_x(field)
                - surf_tile(COEF_Y, tile, h) * geo.d_y(field)[0]
            )
        halos = []
        for ref, field, own_coef in (
            (low_ref, spread(fields[0][:1]), deriv_table[3][3]),
            (high_ref, spread(fields[1][ROWS - 1 :]), deriv_table[0][0]),
        ):
            halos.append(
                beside(ref, MASS, tile)
                * (field + relax_rate * (beside(ref, SURF, tile) - field))
                - beside(ref, SURF_ARRAYS, tile)
                - beside(ref, COEF_X, tile) * (own_coef * field)
                - beside(ref, COEF_Y, tile) * geo.d_y(field)[0]
            )
        ends.append(geo.sum_x(moved[0], moved[1], halos[0], halos[1]))
    final = []
    for h in range(2):
        summed, _ = geo.sum_y_pair(ends[0][h], ends[1][h])
        final.append(summed * inverse[0][h])
        final_ref[ROWS * h : ROWS * (h + 1), :] = final[h]
        inverse_ref[ROWS * h : ROWS * (h + 1), :] = inverse[0][h]
    flux = [final[h] - surf_tile(SURF, 0, h) for h in range(2)]
    for group in range(blocks // ROWS):
        ids = rows_ref[ROWS * group : ROWS * (group + 1), :]
        high, low = ids >> 7, ids & (LANES - 1)
        picked = jnp.zeros((ROWS, LANES), jnp.float32)
        for x in range(2 * ROWS):
            line = spread(flux[x // ROWS][x % ROWS : x % ROWS + 1])
            picked = jnp.where(high == x, take(line, low, 1), picked)
        for c in range(ROWS):
            flux_ref[ROWS * group + c, 0:1, :] = picked[c : c + 1]

    out = pltpu.make_async_copy(flux_ref, slab_out, semaphore)
    out.start()

    kept = outer_rows(x_points)

    def put(x, plane, value):
        at = planes * kept.index(x) + plane
        sums_ref[at : at + ROWS, :] = value

    def beyond(ref, plane, field, slope, own_coef):
        wind_at = 2 * planes + plane % levels
        return (
            beside(ref, MASS, 0) * field
            - ref[planes + plane : planes + plane + ROWS, :]
            - ref[wind_at : wind_at + ROWS, :] * (own_coef * field)
            - ref[wind_at + levels : wind_at + levels + ROWS, :] * slope
        )

    def row_of(tiles, x):
        return spread(tiles[x // ROWS][x % ROWS : x % ROWS + 1])

    masses = [surf_tile(MASS, 0, h) for h in range(2)]
    last_element = x_points // GLL - 1
    for element in (0, last_element):
        lines = [GLL * element + i for i in range(GLL)]
        scale = [row_of(inverse[0], x) for x in lines]
        mass = [row_of(masses, x) for x in lines]
        for level in range(0, levels, ROWS):
            wind = wind_tiles(wind_ref, x_points, level, lines)
            for plane in range(level, planes, levels):
                here = slice(plane, plane + ROWS)
                fields = []
                for i, x in enumerate(lines):
                    total = avg_ref[planes * x + plane : planes * x + plane + ROWS, :]
                    other = x - 1 if i == 0 else x + 1
                    if other < 0:
                        total = total + low_ref[here, :]
                    elif other == x_points:
                        total = total + high_ref[here, :]
                    elif i in (0, GLL - 1):
                        at = planes * other + plane
                        total = total + avg_ref[at : at + ROWS, :]
                    fields.append(total * scale[i])
                moved, slopes = advance(geo, fields, wind, mass)
                if element == 0:
                    before = beyond(low_ref, plane, fields[0], slopes[0], deriv_table[3][3])
                    put(lines[0], plane, before + moved[0])
                    shared = moved[-1] + inner_ref[here, :]
                    put(lines[-1], plane, shared)
                    put(lines[-1] + 1, plane, shared)
                else:
                    at = inner_ref.shape[0] - planes + plane
                    shared = moved[0] + inner_ref[at : at + ROWS, :]
                    put(lines[0] - 1, plane, shared)
                    put(lines[0], plane, shared)
                    after = beyond(
                        high_ref, plane, fields[-1], slopes[-1], deriv_table[0][0]
                    )
                    put(lines[-1], plane, moved[-1] + after)
                for i in range(1, GLL - 1):
                    put(lines[i], plane, moved[i])
    packs = [packs_ref[:ROWS, :], packs_ref[ROWS:, :]]
    packs = edges_of(geo, packs, sums_ref, planes, kept)
    for q, pack in enumerate(packs):
        edges_ref[ROWS * q : ROWS * (q + 1), :] = pack
    out.wait()


def last_kernel(
    planes,
    inner_ref,
    outer_ref,
    inverse_ref,
    edges_ref,
    cols_ref,
    out_ref,
    hot_ref,
    before_ref,
    after_ref,
):
    geo = Geometry()
    x_points = inverse_ref.shape[0]
    kept = outer_rows(x_points)
    hot_ref[...] = one_hot(cols_ref[...])
    after_ref[...], before_ref[...] = split_sides(
        geo, edges_ref[:ROWS, :], edges_ref[ROWS:, :], 1
    )
    for x in range(x_points):
        inverse = spread(inverse_ref[x : x + 1, :])
        ref, first = inner_ref, planes * (x - GLL)
        if x in kept:
            ref, first = outer_ref, planes * kept.index(x)
        for group in range(planes // ROWS):
            tile = ref[first + ROWS * group : first + ROWS * (group + 1), :]
            at = planes * x + ROWS * group
            out_ref[at : at + ROWS, :] = inverse * geo.sum_y(tile, 0.0)


def end_kernel(
    planes,
    last_ref,
    before_ref,
    after_ref,
    recv_ref,
    final_ref,
    inverse_ref,
    cols_ref,
    hot_ref,
    weights_ref,
    gain_ref,
    ocean_ref,
    air_out,
    ocean_out,
    air_ref,
    row_ref,
    semaphores,
):
    geo = Geometry()
    blocks = cols_ref.shape[0]
    chunks = gain_ref.shape[0]
    x_points = inverse_ref.shape[0]
    copies = []

    def send(source, target):
        copies.append(
            pltpu.make_async_copy(source, target, semaphores.at[len(copies)])
        )
        copies[-1].start()

    send(ocean_ref.at[ROWS:], ocean_out.at[ROWS:])
    joined = join_edges(geo, before_ref[...], after_ref[...])
    groups = planes // ROWS
    for group in range(groups):
        for x in range(x_points):
            at = planes * x + ROWS * group
            beside = spread(inverse_ref[x : x + 1, :]) * outer_edges(joined, x, group)
            air_ref[pl.ds(ROWS * group * x_points + x, ROWS, stride=x_points), :] = last_ref[
                at : at + ROWS, :
            ] + jnp.where(geo.outer_lane, beside, 0.0)
        if group == 0:
            air_ref[0:x_points, :] = final_ref[...]
        if group % 2:
            rows = slice(
                ROWS * (group - 1) * x_points, ROWS * (group + 1) * x_points
            )
            send(air_ref.at[rows], air_out.at[rows])
    if groups % 2:
        rows = slice(ROWS * (groups - 1) * x_points, planes * x_points)
        send(air_ref.at[rows], air_out.at[rows])

    arrived = jnp.concatenate([recv_ref[c, 0:1, :] for c in range(blocks)], axis=0)
    (inflow,) = scatter_sum(
        [weights_ref[...] * arrived], cols_ref[...], chunks, hot_ref[...]
    )
    gain = inflow * gain_ref[...]
    row_ref[...] = ocean_ref[:ROWS, :]
    for k in range(chunks):
        at = slice(LANES * k, LANES * (k + 1))
        row_ref[0:1, at] = ocean_ref[0:1, at] + gain[k : k + 1]
    send(row_ref, ocean_out.at[:ROWS])
    for copy in copies:
        copy.wait()


def gathered(ids, coefs, source, sources, groups, first=0):
    totals = [jnp.zeros((ROWS, LANES), jnp.float32) for _ in range(groups)]
    for edge in range(ids.shape[0]):
        cell = spread(ids[edge : edge + 1])
        coef = spread(coefs[edge : edge + 1])
        high, low = cell >> 7, cell & (LANES - 1)
        for s in range(sources):
            scaled = jnp.where(high == first + s, coef, 0.0)
            for group in range(groups):
                totals[group] += scaled * take(source(group, s), low, 1)
    return totals


def multiplied(ids, coefs, halves_ref, sources, groups):
    lane_at = iota((LANES, LANES), 0)
    hot = jnp.concatenate(
        [
            jnp.where(lane_at == (ids[edge : edge + 1] & (LANES - 1)), 1.0, 0.0).astype(
                jnp.bfloat16
            )
            for edge in range(2)
        ],
        axis=1,
    )
    picked = jnp.dot(
        halves_ref[...],
        jnp.concatenate([hot, hot], axis=0),
        preferred_element_type=jnp.float32,
    )
    totals = [jnp.zeros((ROWS, LANES), jnp.float32) for _ in range(groups)]
    for edge in range(2):
        high = spread(ids[edge : edge + 1]) >> 7
        coef = spread(coefs[edge : edge + 1])
        side = slice(LANES * edge, LANES * (edge + 1))
        for s in range(sources):
            scaled = jnp.where(high == s, coef, 0.0)
            for group in range(groups):
                at = ROWS * (groups * s + group)
                totals[group] += scaled * picked[at : at + ROWS, side]
    return totals


def ocean_kernel(
    levels, start, tracers_ref, coef_ref, near_ref, rate_ref, after_ref, out_ref, halves_ref
):
    chunks = tracers_ref.shape[1] // LANES
    groups = tracers_ref.shape[0] // ROWS
    row = iota((ROWS, LANES), 0)

    def source(group, s):
        return tracers_ref[
            ROWS * group : ROWS * (group + 1), LANES * s : LANES * (s + 1)
        ]

    planes = tracers_ref.shape[0]
    for s in range(chunks):
        values = tracers_ref[:, LANES * s : LANES * (s + 1)]
        upper = values.astype(jnp.bfloat16)
        at = slice(planes * s, planes * (s + 1))
        halves_ref[at, :LANES] = upper
        halves_ref[at, LANES:] = (values - upper.astype(jnp.float32)).astype(jnp.bfloat16)
    edges = near_ref.shape[0]

    def one_chunk(number, carry):
        k = number + start
        at = pl.ds(pl.multiple_of(k * LANES, LANES), LANES)
        out_at = pl.ds(pl.multiple_of(number * LANES, LANES), LANES)
        ids, coefs = near_ref[:, at], coef_ref[:, at]
        by_gather = edges - edges // 3 * 2
        totals = gathered(ids[:by_gather], coefs[:by_gather], source, chunks, groups)
        for edge in range(by_gather, edges, 2):
            more = multiplied(
                ids[edge : edge + 2], coefs[edge : edge + 2], halves_ref, chunks, groups
            )
            totals = [total + part for total, part in zip(totals, more)]
        coef_sum = spread(jnp.sum(coefs, axis=0, keepdims=True))
        rate = spread(rate_ref[pl.ds(k, 1), :])
        tiles = [tracers_ref[ROWS * g : ROWS * (g + 1), at] for g in range(groups)]
        for g in range(groups):
            tile = tiles[g]
            top = bottom = tile
            if (ROWS * g) % levels:
                top = pltpu.roll(tiles[g - 1], 1, 0)
            if (ROWS * (g + 1)) % levels:
                bottom = pltpu.roll(tiles[g + 1], ROWS - 1, 0)
            above = jnp.where(row == 0, top, pltpu.roll(tile, 1, 0))
            below = jnp.where(row == ROWS - 1, bottom, pltpu.roll(tile, ROWS - 1, 0))
            vertical = rate * ((above - tile) + (below - tile))
            out_ref[ROWS * g : ROWS * (g + 1), out_at] = (
                tile + (totals[g] - coef_sum * tile) + vertical
            )
        return carry

    count = out_ref.shape[1] // LANES
    step = 2 if count % 2 == 0 else 1

    def some_chunks(number, carry):
        for i in range(step):
            one_chunk(step * number + i, carry)
        return carry

    lax.fori_loop(0, count // step, some_chunks, 0)


def send_kernel(tracers_ref, send_ref, before_ref, after_ref, *out_refs):
    chunks = tracers_ref.shape[1] // LANES
    for part, (side_ref, out_ref) in enumerate(zip((before_ref, after_ref), out_refs)):
        base = side_ref.shape[0]
        out_ref[:base, :] = side_ref[...]
        cells = spread(send_ref[0:1, LANES * part : LANES * (part + 1)])
        high, low = cells >> 7, cells & (LANES - 1)
        for group in range(tracers_ref.shape[0] // ROWS):
            half = slice(ROWS * group, ROWS * (group + 1))
            rim = jnp.zeros((ROWS, LANES), jnp.float32)
            for k in range(chunks):
                tile = tracers_ref[half, LANES * k : LANES * (k + 1)]
                rim = jnp.where(high == k, take(tile, low, 1), rim)
            out_ref[base + ROWS * group : base + ROWS * (group + 1), :] = rim


def rim_kernel(
    starts,
    before_ref,
    after_ref,
    coef_ref,
    near_ref,
    area_ref,
    rows_ref,
    *refs,
):
    partial_refs, (out_ref, gain_ref) = refs[: len(starts)], refs[len(starts) :]
    chunks = coef_ref.shape[1] // LANES
    groups = out_ref.shape[0] // ROWS
    rim_at = before_ref.shape[0] - out_ref.shape[0]
    sides = before_ref, after_ref
    gain_ref[...] = flux_gain / area_ref[...]

    def source(group, s):
        at = rim_at + ROWS * group
        return sides[s][at : at + ROWS, :]

    for k in range(chunks):
        at = slice(LANES * k, LANES * (k + 1))
        totals = gathered(near_ref[:, at], coef_ref[:, at], source, 2, groups, chunks)
        part = max(i for i, start in enumerate(starts) if start <= k)
        place = slice(LANES * (k - starts[part]), LANES * (k - starts[part] + 1))
        for g in range(groups):
            half = slice(ROWS * g, ROWS * (g + 1))
            out_ref[half, at] = partial_refs[part][half, place] + totals[g]


VMEM_SPEC = pl.BlockSpec(memory_space=pltpu.VMEM)
ANY_SPEC = pl.BlockSpec(memory_space=pl.ANY)
HBM_SPEC = pl.BlockSpec(memory_space=pltpu.HBM)


def call(kernel, outs, specs, scratch=(), cost=0, hbm_outs=0):
    estimate = None
    if cost:
        estimate = pl.CostEstimate(flops=0, bytes_accessed=cost, transcendentals=0)
    outs = [
        out if isinstance(out, jax.ShapeDtypeStruct) else jax.ShapeDtypeStruct(out, jnp.float32)
        for out in outs
    ]
    out_specs = [VMEM_SPEC] * len(outs)
    out_specs[:hbm_outs] = [HBM_SPEC] * hbm_outs
    return pl.pallas_call(
        kernel,
        out_shape=outs,
        in_specs=specs,
        out_specs=out_specs,
        scratch_shapes=list(scratch),
        cost_estimate=estimate,
        compiler_params=pltpu.CompilerParams(vmem_limit_bytes=32 * 2**20),
        name=getattr(kernel, "func", kernel).__name__,
    )


def body(
    air_state,
    air_wind,
    jacobian,
    land_area,
    xgrid_rows,
    tracers,
    edge_coef,
    neighbours,
    vert_rate,
    ocean_area,
    send_list,
    xgrid_cols,
    xgrid_weights,
):
    field_count, levels, x_points, y_points = air_state.shape
    planes = field_count * levels
    ocean_levels, cells = tracers.shape[1:]
    ocean_planes = tracers.shape[0] * ocean_levels
    faces, blocks = lax.axis_size("face"), lax.axis_size("blk")
    air = air_state.reshape(planes * x_points, y_points)
    wind = air_wind.reshape(2 * levels * x_points, y_points)
    ocean = tracers.reshape(ocean_planes, cells)
    point_ids, cell_ids, weights = xgrid_rows[0], xgrid_cols[0], xgrid_weights[0]
    rate = vert_rate.reshape(cells // LANES, LANES)
    area = ocean_area.reshape(cells // LANES, LANES)
    first_inputs = (
        cell_ids,
        weights,
        ocean,
        point_ids,
        jacobian,
        land_area,
        wind,
        air,
        send_list,
    )
    kept = (cell_ids, weights, point_ids, send_list)
    slab, moved, to_before, to_after, cell_ids, weights, point_ids, send_list = call(
        functools.partial(start_kernel, planes),
        [(blocks, HEAD, LANES), air.shape]
        + [(SIDE_IDS + blocks, LANES)] * 2
        + [jax.ShapeDtypeStruct(array.shape, array.dtype) for array in kept],
        [HBM_SPEC] * len(first_inputs),
        [
            pltpu.VMEM(shape, jnp.float32)
            for shape in (
                (blocks, HEAD, LANES),
                (ROWS, cells),
                jacobian.shape,
                land_area.shape,
                wind.shape,
                air.shape,
            )
        ]
        + [pltpu.SemaphoreType.DMA((len(first_inputs) + 1,))],
        hbm_outs=1,
    )(*(pltpu.with_memory_space_constraint(array, pltpu.HBM) for array in first_inputs))
    recv = lax.all_to_all(slab, "blk", split_axis=0, concat_axis=0, tiled=True)

    chunks = cells // LANES
    reads_per_chunk = edge_coef.shape[0] * chunks * (ocean_planes // ROWS)
    starts = (0, chunks * 6 // 16)

    def ocean_part(start, end, after):
        (result,) = call(
            functools.partial(ocean_kernel, ocean_levels, start),
            [(ocean_planes, (end - start) * LANES)],
            [VMEM_SPEC] * 4 + [ANY_SPEC],
            [pltpu.VMEM((chunks * ocean_planes, 2 * LANES), jnp.bfloat16)],
            cost=(end - start) * reads_per_chunk * ROWS * LANES * 2,
        )(ocean, edge_coef, neighbours, rate, after)
        return result

    to_before, to_after = call(
        send_kernel,
        [(SIDE_IDS + blocks + ocean_planes, LANES)] * 2,
        [VMEM_SPEC] * 4,
        cost=reads_per_chunk * ROWS * LANES,
    )(ocean, send_list, to_before, to_after)
    onward = [(i, (i + 1) % blocks) for i in range(blocks)]
    before = lax.ppermute(to_after, "blk", onward)
    after = lax.ppermute(to_before, "blk", [(to, source) for source, to in onward])
    first_part = ocean_part(starts[0], starts[1], to_before)
    side_rows = 2 * planes + 2 * levels + 2 * SURF_ARRAYS + 4
    avg, down, up, surf = call(
        functools.partial(panel_kernel, planes),
        [air.shape, (side_rows, LANES), (side_rows, LANES), (4 * ROWS * SURF_ARRAYS, LANES)],
        [VMEM_SPEC] * 9 + [ANY_SPEC],
    )(
        moved,
        recv,
        before,
        after,
        air,
        wind,
        jacobian,
        land_area,
        point_ids,
        first_part,
    )
    after_me = [(i, (i + 1) % faces) for i in range(faces)]
    low = lax.ppermute(up, "face", after_me)
    high = lax.ppermute(down, "face", [(to, source) for source, to in after_me])
    inner, packs = call(
        functools.partial(inner_kernel, planes),
        [((x_points - 2 * GLL) * planes, LANES), (2 * ROWS, LANES)],
        [VMEM_SPEC] * 6,
        cost=2 * air.size * 4,
    )(avg, moved, before, after, surf, wind)
    second_part = ocean_part(starts[1], chunks, surf)

    slab, outer, final, inverse, edges = call(
        functools.partial(second_kernel, planes),
        [
            (blocks, HEAD, LANES),
            (len(outer_rows(x_points)) * planes, LANES),
            (x_points, y_points),
            (x_points, y_points),
            (2 * ROWS, LANES),
        ],
        [VMEM_SPEC] * 8 + [ANY_SPEC],
        [pltpu.VMEM((blocks, HEAD, LANES), jnp.float32), pltpu.SemaphoreType.DMA(())],
        hbm_outs=1,
    )(avg, inner, packs, surf, low, high, wind, point_ids, second_part)
    arrived = lax.all_to_all(slab, "blk", split_axis=0, concat_axis=0, tiled=True)
    last, hot, to_before, to_after = call(
        functools.partial(last_kernel, planes),
        [air.shape, jax.ShapeDtypeStruct((LANES, blocks * LANES), jnp.bfloat16)]
        + [(ROWS, LANES)] * 2,
        [VMEM_SPEC] * 5,
        cost=2 * air.size * 4,
    )(inner, outer, inverse, edges, cell_ids)
    edge_before = lax.ppermute(to_after, "blk", onward)
    edge_after = lax.ppermute(to_before, "blk", [(to, source) for source, to in onward])
    partial, gain = call(
        functools.partial(rim_kernel, starts),
        [ocean.shape, area.shape],
        [VMEM_SPEC] * 5 + [ANY_SPEC] + [VMEM_SPEC] * len(starts),
        cost=chunks * reads_per_chunk // 8 * ROWS * LANES * 4,
    )(
        before,
        after,
        edge_coef,
        neighbours,
        area,
        to_before,
        first_part,
        second_part,
    )
    air_final, ocean_final = call(
        functools.partial(end_kernel, planes),
        [air.shape, ocean.shape],
        [VMEM_SPEC] * 11,
        [
            pltpu.VMEM(air.shape, jnp.float32),
            pltpu.VMEM((ROWS, cells), jnp.float32),
            pltpu.SemaphoreType.DMA((2 + planes // ROWS,)),
        ],
        hbm_outs=2,
    )(
        last,
        edge_before,
        edge_after,
        arrived,
        final,
        inverse,
        cell_ids,
        hot,
        weights,
        gain,
        partial,
    )
    return air_final.reshape(air_state.shape), ocean_final.reshape(tracers.shape)


def solution(mesh):
    return jax.shard_map(
        body,
        mesh=mesh,
        in_specs=(
            P(None, None, "face", "blk"),
            P(None, None, "face", "blk"),
            P("face", "blk"),
            P("face", "blk"),
            P(("face", "blk"), None, None),
            P(None, None, ("face", "blk")),
            P(None, ("face", "blk")),
            P(None, ("face", "blk")),
            P(("face", "blk")),
            P(("face", "blk")),
            P(("face", "blk"), None),
            P(("face", "blk"), None, None),
            P(("face", "blk"), None, None),
        ),
        out_specs=(P(None, None, "face", "blk"), P(None, None, ("face", "blk"))),
        check_vma=False,
    )
```

```python
import functools

import jax
import jax.numpy as jnp
from jax import lax
from jax.experimental import pallas as pl
from jax.experimental.pallas import tpu as pltpu
from jax.sharding import PartitionSpec as P

GLL = 4
ROWS = 8
LANES = 128

deriv_table = [
    [-3.0, 4.045084971874737, -1.545084971874737, 0.5],
    [-0.8090169943749475, 0.0, 1.118033988749895, -0.30901699437494745],
    [0.30901699437494745, -1.118033988749895, 0.0, 0.8090169943749475],
    [-0.5, 1.545084971874737, -4.045084971874737, 3.0],
]
time_step = 0.05
relax_rate = 0.3
flux_gain = 0.2

HEAD = 8
SIDE_EDGE, SIDE_STRIP, SIDE_IDS = 0, 8, 16
AVG, MASS_SUM, MASS, COEF_X, COEF_Y, SURF = range(6)
SURF_ARRAYS = 6


def iota(shape, dim):
    return lax.broadcasted_iota(jnp.int32, shape, dim)


def take(values, index, axis):
    return jnp.take_along_axis(values, index, axis=axis, mode="promise_in_bounds")


def by_position(pos, values):
    result = jnp.full(pos.shape, values[-1], jnp.float32)
    for i, value in enumerate(values[:-1]):
        result = jnp.where(pos == i, value, result)
    return result


def spread(row):
    return jnp.broadcast_to(row, (ROWS, LANES))


class Geometry:
    def __init__(self):
        shape = (ROWS, LANES)
        self.row, self.lane = iota(shape, 0), iota(shape, 1)
        x_pos, y_pos = self.row & (GLL - 1), self.lane & (GLL - 1)
        self.y_from = [self.lane - y_pos + j for j in range(GLL)]
        columns = [[line[j] for line in deriv_table] for j in range(GLL)]
        self.x_coef = {
            step: by_position(
                x_pos,
                [
                    deriv_table[i][i + step] if 0 <= i + step < GLL else 0.0
                    for i in range(GLL)
                ],
            )
            for step in range(1 - GLL, GLL)
        }
        self.y_coef = [by_position(y_pos, column) for column in columns]
        self.y_swap = (
            self.lane + jnp.where(y_pos == GLL - 1, 1, 0) - jnp.where(y_pos == 0, 1, 0)
        ) & (LANES - 1)
        self.x_edge = (x_pos == 0) | (x_pos == GLL - 1)
        self.y_edge = (y_pos == 0) | (y_pos == GLL - 1)
        self.first_row, self.last_row = self.row == 0, self.row == ROWS - 1
        self.middle_row = self.row == GLL
        self.outer_lane = (self.lane == 0) | (self.lane == LANES - 1)
        self.weight = jnp.where(self.x_edge, 1.0 / 6.0, 5.0 / 6.0) * jnp.where(
            self.y_edge, 1.0 / 6.0, 5.0 / 6.0
        )

    def d_x(self, tile):
        return sum(
            coef * (pltpu.roll(tile, -step % ROWS, 0) if step else tile)
            for step, coef in self.x_coef.items()
        )

    def d_y(self, *tiles):
        totals = [0.0] * len(tiles)
        for j in range(GLL):
            for i, tile in enumerate(tiles):
                totals[i] += self.y_coef[j] * take(tile, self.y_from[j], 1)
        return totals

    def sum_x(self, low, high, before, after):
        low_down, low_up = pltpu.roll(low, 1, 0), pltpu.roll(low, ROWS - 1, 0)
        high_down, high_up = pltpu.roll(high, 1, 0), pltpu.roll(high, ROWS - 1, 0)
        low_other = jnp.where(
            self.first_row,
            before,
            jnp.where(
                self.middle_row, low_down, jnp.where(self.last_row, high_up, low_up)
            ),
        )
        high_other = jnp.where(
            self.first_row,
            low_down,
            jnp.where(
                self.middle_row, high_down, jnp.where(self.last_row, after, high_up)
            ),
        )
        return (
            low + jnp.where(self.x_edge, low_other, 0.0),
            high + jnp.where(self.x_edge, high_other, 0.0),
        )

    def sum_y(self, tile, outer):
        other = jnp.where(self.outer_lane, outer, take(tile, self.y_swap, 1))
        return tile + jnp.where(self.y_edge, other, 0.0)

    def sum_y_pair(self, own, strip):
        own_swap, strip_swap = take(own, self.y_swap, 1), take(strip, self.y_swap, 1)
        own_other = jnp.where(self.outer_lane, strip_swap, own_swap)
        strip_other = jnp.where(self.outer_lane, own_swap, strip_swap)
        return (
            own + jnp.where(self.y_edge, own_other, 0.0),
            strip + jnp.where(self.y_edge, strip_other, 0.0),
        )


def edge_place(x, group):
    return x // ROWS, LANES // 2 * (x % 2) + ROWS * group + 2 * (x % ROWS // 2)


def edges_of(geo, packs, ref, planes, lines, first=None):
    packs = list(packs)
    for number, x in enumerate(lines):
        base = planes * (number if first is None else x - first)
        for group in range(planes // ROWS):
            q, at = edge_place(x, group)
            tile = ref[base + ROWS * group : base + ROWS * (group + 1), :]
            rolled = pltpu.roll(tile, (at + 1) % LANES, 1)
            packs[q] = jnp.where((geo.lane >> 1) == at // 2, rolled, packs[q])
    return packs


def outer_edges(joined, x, group):
    q, at = edge_place(x, group)
    return pltpu.roll(joined[q], (-(at + 1)) % LANES, 1)


def split_sides(geo, first, second, unit):
    odd = (geo.lane & unit) != 0
    return (
        jnp.where(odd, pltpu.roll(second, unit, 1), first),
        jnp.where(odd, second, pltpu.roll(first, LANES - unit, 1)),
    )


def join_sides(geo, before, after, unit):
    odd = (geo.lane & unit) != 0
    return (
        jnp.where(odd, pltpu.roll(after, unit, 1), before),
        jnp.where(odd, after, pltpu.roll(before, LANES - unit, 1)),
    )


def join_edges(geo, before, after):
    odd = (geo.lane & 1) != 0
    return (
        jnp.where(odd, pltpu.roll(before, 1, 1), after),
        jnp.where(odd, before, pltpu.roll(after, LANES - 1, 1)),
    )


def neighbours_of(blocks):
    here = lax.axis_index("blk")
    return lax.rem(here + blocks - 1, blocks), lax.rem(here + 1, blocks)


def one_hot(index, allowed=None):
    low = index & (LANES - 1)
    lane_at = iota((LANES, LANES), 0)
    if allowed is not None:
        lane_at = jnp.where(allowed(lane_at), lane_at, -1)
    return jnp.concatenate(
        [
            jnp.where(lane_at == low[c : c + 1], 1.0, 0.0).astype(jnp.bfloat16)
            for c in range(index.shape[0])
        ],
        axis=1,
    )


def scatter_sum(lines, index, bins, lanes_hot):
    split = []
    for values in lines:
        for part in range(3):
            short = values.astype(jnp.bfloat16).astype(jnp.float32)
            split.append(short)
            values = values - short
    high = index >> 7
    bin_at = iota((bins, LANES), 0)
    left = []
    for c in range(index.shape[0]):
        hit = bin_at == high[c : c + 1]
        left.append(
            jnp.concatenate(
                [jnp.where(hit, part[c : c + 1], 0.0) for part in split], axis=0
            ).astype(jnp.bfloat16)
        )
    total = lax.dot_general(
        jnp.concatenate(left, axis=1),
        lanes_hot,
        (((1,), (1,)), ((), ())),
        preferred_element_type=jnp.float32,
    )
    sums = []
    for i in range(len(lines)):
        part = total[3 * i * bins : 3 * (i + 1) * bins]
        sums.append(part[:bins] + part[bins : 2 * bins] + part[2 * bins :])
    return sums


def wind_tiles(wind_ref, x_points, level, lines):
    levels = wind_ref.shape[0] // (2 * x_points)
    return [
        [
            time_step
            * wind_ref[
                pl.ds((levels * part + level) * x_points + x, ROWS, stride=x_points), :
            ]
            for x in lines
        ]
        for part in range(2)
    ]


def start_kernel(
    planes,
    cols_in,
    weights_in,
    tracers_in,
    rows_in,
    jac_in,
    land_in,
    wind_in,
    air_in,
    send_in,
    slab_out,
    moved_ref,
    before_ref,
    after_ref,
    cols_ref,
    weights_ref,
    rows_ref,
    send_ref,
    slab_ref,
    tracers_ref,
    jac_ref,
    land_ref,
    wind_ref,
    air_ref,
    semaphores,
):
    copies = [
        pltpu.make_async_copy(source, target, semaphores.at[i])
        for i, (source, target) in enumerate(
            (
                (cols_in, cols_ref),
                (tracers_in.at[:ROWS], tracers_ref),
                (weights_in, weights_ref),
                (rows_in, rows_ref),
                (air_in, air_ref),
                (wind_in, wind_ref),
                (jac_in, jac_ref),
                (land_in, land_ref),
                (send_in, send_ref),
            )
        )
    ]
    for copy in copies:
        copy.start()
    geo = Geometry()
    blocks = cols_ref.shape[0]
    x_points = jac_ref.shape[0]
    levels = wind_ref.shape[0] // (2 * x_points)
    chunks = tracers_ref.shape[1] // LANES
    for copy in copies[:4]:
        copy.wait()

    for group in range(blocks // ROWS):
        at = slice(ROWS * group, ROWS * (group + 1))
        cells = cols_ref[at, :]
        high, low = cells >> 7, cells & (LANES - 1)
        surface = jnp.zeros((ROWS, LANES), jnp.float32)
        for k in range(chunks):
            line = spread(tracers_ref[0:1, LANES * k : LANES * (k + 1)])
            surface = jnp.where(high == k, take(line, low, 1), surface)
        area = weights_ref[at, :]
        heat = area * surface
        for c in range(ROWS):
            owner = ROWS * group + c
            for place, step in enumerate((1, 0, -1)):
                to = (owner + step) % blocks
                slab_ref[to, 2 * place : 2 * place + 1, :] = heat[c : c + 1]
                slab_ref[to, 2 * place + 1 : 2 * place + 2, :] = area[c : c + 1]

    out = pltpu.make_async_copy(slab_ref, slab_out, semaphores.at[len(copies)])
    out.start()
    ids = rows_ref[...].astype(jnp.float32)
    for side_ref in (before_ref, after_ref):
        side_ref[SIDE_IDS : SIDE_IDS + blocks, :] = ids

    for copy in copies[4:]:
        copy.wait()
    strips = []
    for h in range(2):
        half = slice(ROWS * h, ROWS * (h + 1))
        second = levels * x_points
        pack = jnp.zeros((ROWS, LANES), jnp.float32)
        for i, strip in enumerate(
            (
                air_ref[half, :],
                wind_ref[half, :],
                wind_ref[second + ROWS * h : second + ROWS * (h + 1), :],
                jac_ref[half, :],
                land_ref[half, :],
            )
        ):
            pack = jnp.where(
                (geo.lane >> 4) == i, pltpu.roll(strip, 16 * i + 8, 1), pack
            )
        strips.append(pack)
    to_right, to_left = split_sides(geo, strips[0], strips[1], ROWS)
    after_ref[SIDE_STRIP : SIDE_STRIP + ROWS, :] = to_right
    before_ref[SIDE_STRIP : SIDE_STRIP + ROWS, :] = to_left

    y_weight = jnp.where(geo.y_edge, 1.0 / 6.0, 5.0 / 6.0)
    for element in range(x_points // GLL):
        lines = [GLL * element + i for i in range(GLL)]
        mass = [
            (1.0 / 6.0 if i in (0, GLL - 1) else 5.0 / 6.0)
            * y_weight
            * spread(jac_ref[x : x + 1, :])
            for i, x in enumerate(lines)
        ]
        for level in range(0, levels, ROWS):
            wind = wind_tiles(wind_ref, x_points, level, lines)
            for plane in range(level, planes, levels):
                fields = [
                    air_ref[pl.ds(plane * x_points + x, ROWS, stride=x_points), :]
                    for x in lines
                ]
                slopes = geo.d_y(*fields)
                for i, x in enumerate(lines):
                    slope = sum(deriv_table[i][j] * fields[j] for j in range(GLL))
                    moved = mass[i] * (
                        fields[i] - (wind[0][i] * slope + wind[1][i] * slopes[i])
                    )
                    moved_ref[planes * x + plane : planes * x + plane + ROWS, :] = moved
    packs = [jnp.zeros((ROWS, LANES), jnp.float32) for _ in range(2)]
    packs = edges_of(geo, packs, moved_ref, planes, range(x_points))
    to_right, to_left = split_sides(geo, packs[0], packs[1], 1)
    after_ref[SIDE_EDGE : SIDE_EDGE + ROWS, :] = to_right
    before_ref[SIDE_EDGE : SIDE_EDGE + ROWS, :] = to_left
    out.wait()


def panel_kernel(
    planes,
    moved_ref,
    recv_ref,
    before_ref,
    after_ref,
    air_ref,
    wind_ref,
    jac_ref,
    land_ref,
    rows_ref,
    ocean_ref,
    avg_ref,
    down_ref,
    up_ref,
    surf_ref,
):
    geo = Geometry()
    blocks = rows_ref.shape[0]
    x_points = jac_ref.shape[0]
    levels = wind_ref.shape[0] // (2 * x_points)

    own_ids = rows_ref[...]
    left_ids = before_ref[SIDE_IDS : SIDE_IDS + blocks, :].astype(jnp.int32)
    right_ids = after_ref[SIDE_IDS : SIDE_IDS + blocks, :].astype(jnp.int32)
    head = [
        jnp.concatenate([recv_ref[c, i : i + 1, :] for c in range(blocks)], axis=0)
        for i in range(6)
    ]
    heat, frac = scatter_sum(head[2:4], own_ids, 2 * ROWS, one_hot(own_ids))
    from_left = scatter_sum(
        head[0:2], left_ids, 2 * ROWS, one_hot(left_ids, lambda lane: lane >= LANES - ROWS)
    )
    from_right = scatter_sum(
        head[4:6], right_ids, 2 * ROWS, one_hot(right_ids, lambda lane: lane < ROWS)
    )
    strip_heat = from_left[0] + from_right[0]
    strip_frac = from_left[1] + from_right[1]

    in_strip = (geo.lane < ROWS) | (geo.lane >= LANES - ROWS)
    packs = join_sides(
        geo,
        before_ref[SIDE_STRIP : SIDE_STRIP + ROWS, :],
        after_ref[SIDE_STRIP : SIDE_STRIP + ROWS, :],
        ROWS,
    )
    own, strip = [], []
    for h, pack in enumerate(packs):
        half = slice(ROWS * h, ROWS * (h + 1))
        strip.append(
            [
                jnp.where(
                    in_strip, pltpu.roll(pack, (-(16 * i + 8)) % LANES, 1), 1.0
                )
                for i in range(5)
            ]
        )
        own.append(
            [
                air_ref[half, :],
                wind_ref[half, :],
                wind_ref[
                    levels * x_points + ROWS * h : levels * x_points + ROWS * (h + 1), :
                ],
                jac_ref[half, :],
                land_ref[half, :],
            ]
        )
    for h in range(2):
        half = slice(ROWS * h, ROWS * (h + 1))
        pair = []
        for tile, ((field, wind_x, wind_y, jac, land), tile_heat, tile_frac) in enumerate(
            ((own[h], heat[half], frac[half]), (strip[h], strip_heat[half], strip_frac[half]))
        ):
            mass = geo.weight * jac
            if tile == 1:
                tile_heat = jnp.where(in_strip, tile_heat, 0.0)
                tile_frac = jnp.where(in_strip, tile_frac, 0.0)
            surf = (tile_heat + land * field) / (tile_frac + land)
            coef_x, coef_y = time_step * mass * wind_x, time_step * mass * wind_y
            moved = (
                mass * (field + relax_rate * (surf - field))
                - coef_x * geo.d_x(field)
                - coef_y * geo.d_y(field)[0]
            )
            pair.append((moved, mass))
            at = 2 * ROWS * tile + ROWS * h
            for number, value in (
                (MASS, mass),
                (COEF_X, coef_x),
                (COEF_Y, coef_y),
                (SURF, surf),
            ):
                surf_ref[4 * ROWS * number + at : 4 * ROWS * number + at + ROWS, :] = value
        for number, i in ((AVG, 0), (MASS_SUM, 1)):
            for tile, value in enumerate(geo.sum_y_pair(pair[0][i], pair[1][i])):
                at = 4 * ROWS * number + 2 * ROWS * tile + ROWS * h
                surf_ref[at : at + ROWS, :] = value

    joined = join_edges(
        geo,
        before_ref[SIDE_EDGE : SIDE_EDGE + ROWS, :],
        after_ref[SIDE_EDGE : SIDE_EDGE + ROWS, :],
    )
    for x in outer_rows(x_points):
        for group in range(planes // ROWS):
            at = slice(planes * x + ROWS * group, planes * x + ROWS * (group + 1))
            avg_ref[at, :] = geo.sum_y(moved_ref[at, :], outer_edges(joined, x, group))

    def line(r):
        return avg_ref[planes * r : planes * (r + 1), :]

    def surf_line(number, r):
        return surf_ref[pl.ds(4 * ROWS * number + r, 2, stride=x_points), :]

    def first_step(get, mass_at):
        return (
            [
                get(1) / mass_at(1),
                get(2) / mass_at(2),
                (get(3) + get(4)) / (mass_at(3) + mass_at(4)),
            ],
            [
                (get(11) + get(12)) / (mass_at(11) + mass_at(12)),
                get(13) / mass_at(13),
                get(14) / mass_at(14),
            ],
        )

    def own_mass_sum(r):
        return surf_ref[4 * ROWS * MASS_SUM + r : 4 * ROWS * MASS_SUM + r + 1, :]

    low_lines, high_lines = first_step(line, own_mass_sum)
    surf_low, surf_high = first_step(
        functools.partial(surf_line, AVG), functools.partial(surf_line, MASS_SUM)
    )
    for out_ref, r, lines, surf_lines, coefs in (
        (down_ref, 0, low_lines, surf_low, deriv_table[0][1:]),
        (up_ref, 15, high_lines, surf_high, deriv_table[3][:3]),
    ):
        slope = sum(coef * value for coef, value in zip(coefs, lines))
        surf_slope = sum(coef * value for coef, value in zip(coefs, surf_lines))
        mass = surf_ref[4 * ROWS * MASS + r : 4 * ROWS * MASS + r + 1, :]
        wind = time_step * mass * wind_ref[pl.ds(r, 2 * levels, stride=x_points), :]
        out_ref[0:planes, :] = line(r)
        for first in range(0, planes, levels):
            out_ref[planes + first : planes + first + levels, :] = (
                wind[:levels] * slope[first : first + levels]
            )
        base = 2 * planes
        out_ref[base : base + 2 * levels, :] = wind
        base += 2 * levels
        pairs = [surf_line(number, r) for number in range(SURF_ARRAYS)]
        pairs.append(surf_line(COEF_X, r) * surf_slope)
        pack = jnp.zeros((ROWS, LANES), jnp.float32)
        for i, pair in enumerate(pairs):
            out_ref[base + i : base + i + 1, :] = pair[:1]
            pack = jnp.where(
                (geo.lane >> 4) == i, pltpu.roll(spread(pair[1:]), 16 * i + 8, 1), pack
            )
        base += len(pairs)
        out_ref[base : base + 1, :] = pack[:1]


def outer_rows(x_points):
    return [x for x in range(x_points) if x <= GLL or x >= x_points - GLL - 1]


def advance(geo, fields, wind, mass):
    slopes = geo.d_y(*fields)
    moved = []
    for i in range(GLL):
        slope = sum(deriv_table[i][j] * fields[j] for j in range(GLL))
        moved.append(mass[i] * (fields[i] - (wind[0][i] * slope + wind[1][i] * slopes[i])))
    return moved, slopes


def inner_kernel(
    planes, avg_ref, moved_ref, before_ref, after_ref, surf_ref, wind_ref, out_ref, packs_ref
):
    geo = Geometry()
    x_points = avg_ref.shape[0] // planes
    levels = wind_ref.shape[0] // (2 * x_points)
    joined = join_edges(
        geo,
        before_ref[SIDE_EDGE : SIDE_EDGE + ROWS, :],
        after_ref[SIDE_EDGE : SIDE_EDGE + ROWS, :],
    )
    outer = outer_rows(x_points)

    def average(x, plane):
        at = slice(planes * x + plane, planes * x + plane + ROWS)
        if x in outer:
            return avg_ref[at, :]
        return geo.sum_y(moved_ref[at, :], outer_edges(joined, x, plane // ROWS))

    def surf_row(number, x):
        at = 4 * ROWS * number + x
        return spread(surf_ref[at : at + 1, :])

    def put(x, plane, value):
        at = planes * (x - GLL) + plane
        out_ref[at : at + ROWS, :] = value

    held = {}
    carried = {}
    for element in range(1, x_points // GLL - 1):
        lines = [GLL * element + i for i in range(GLL)]
        totals = [surf_row(MASS_SUM, x) for x in lines]
        totals[0] = totals[0] + surf_row(MASS_SUM, lines[0] - 1)
        totals[-1] = totals[-1] + surf_row(MASS_SUM, lines[-1] + 1)
        scale = [1.0 / total for total in totals]
        mass = [surf_row(MASS, x) for x in lines]
        for level in range(0, levels, ROWS):
            wind = wind_tiles(wind_ref, x_points, level, lines)
            for plane in range(level, planes, levels):
                if element == 1:
                    first = average(lines[0], plane) + average(lines[0] - 1, plane)
                else:
                    first = carried[plane]
                last = average(lines[-1], plane) + average(lines[-1] + 1, plane)
                carried[plane] = last
                totals = (
                    [first] + [average(x, plane) for x in lines[1:-1]] + [last]
                )
                fields = [total * factor for total, factor in zip(totals, scale)]
                moved, _ = advance(geo, fields, wind, mass)
                if element == 1:
                    put(lines[0], plane, moved[0])
                else:
                    shared = held[plane] + moved[0]
                    put(lines[0] - 1, plane, shared)
                    put(lines[0], plane, shared)
                for i in range(1, GLL - 1):
                    put(lines[i], plane, moved[i])
                held[plane] = moved[-1]
                if lines[-1] == x_points - GLL - 1:
                    put(lines[-1], plane, moved[-1])
    packs = [jnp.zeros((ROWS, LANES), jnp.float32) for _ in range(2)]
    inner = [x for x in range(x_points) if x not in outer]
    for q, pack in enumerate(edges_of(geo, packs, out_ref, planes, inner, GLL)):
        packs_ref[ROWS * q : ROWS * (q + 1), :] = pack


def second_kernel(
    planes,
    avg_ref,
    inner_ref,
    packs_ref,
    surf_ref,
    low_ref,
    high_ref,
    wind_ref,
    rows_ref,
    ocean_ref,
    slab_out,
    sums_ref,
    final_ref,
    inverse_ref,
    edges_ref,
    flux_ref,
    semaphore,
):
    geo = Geometry()
    blocks = rows_ref.shape[0]
    x_points = final_ref.shape[0]
    levels = wind_ref.shape[0] // (2 * x_points)
    base = low_ref.shape[0] - SURF_ARRAYS - 2

    def surf_tile(number, tile, h):
        at = 4 * ROWS * number + 2 * ROWS * tile + ROWS * h
        return surf_ref[at : at + ROWS, :]

    in_strip = (geo.lane < ROWS) | (geo.lane >= LANES - ROWS)

    def beside(ref, number, tile):
        if tile == 0:
            return spread(ref[base + number : base + number + 1, :])
        at = base + SURF_ARRAYS + 1
        strips = spread(ref[at : at + 1, :])
        return jnp.where(
            in_strip, pltpu.roll(strips, (-(16 * number + 8)) % LANES, 1), 1.0
        )

    ends = []
    inverse = []
    for tile in range(2):
        total = geo.sum_x(
            surf_tile(MASS_SUM, tile, 0),
            surf_tile(MASS_SUM, tile, 1),
            beside(low_ref, MASS_SUM, tile),
            beside(high_ref, MASS_SUM, tile),
        )
        inverse.append([1.0 / value for value in total])
        summed = geo.sum_x(
            surf_tile(AVG, tile, 0),
            surf_tile(AVG, tile, 1),
            beside(low_ref, AVG, tile),
            beside(high_ref, AVG, tile),
        )
        fields = [value * scale for value, scale in zip(summed, inverse[tile])]
        moved = []
        for h in range(2):
            field = fields[h]
            moved.append(
                surf_tile(MASS, tile, h)
                * (field + relax_rate * (surf_tile(SURF, tile, h) - field))
                - surf_tile(COEF_X, tile, h) * geo.d_x(field)
                - surf_tile(COEF_Y, tile, h) * geo.d_y(field)[0]
            )
        halos = []
        for ref, field, own_coef in (
            (low_ref, spread(fields[0][:1]), deriv_table[3][3]),
            (high_ref, spread(fields[1][ROWS - 1 :]), deriv_table[0][0]),
        ):
            halos.append(
                beside(ref, MASS, tile)
                * (field + relax_rate * (beside(ref, SURF, tile) - field))
                - beside(ref, SURF_ARRAYS, tile)
                - beside(ref, COEF_X, tile) * (own_coef * field)
                - beside(ref, COEF_Y, tile) * geo.d_y(field)[0]
            )
        ends.append(geo.sum_x(moved[0], moved[1], halos[0], halos[1]))
    final = []
    for h in range(2):
        summed, _ = geo.sum_y_pair(ends[0][h], ends[1][h])
        final.append(summed * inverse[0][h])
        final_ref[ROWS * h : ROWS * (h + 1), :] = final[h]
        inverse_ref[ROWS * h : ROWS * (h + 1), :] = inverse[0][h]
    flux = [final[h] - surf_tile(SURF, 0, h) for h in range(2)]
    for group in range(blocks // ROWS):
        ids = rows_ref[ROWS * group : ROWS * (group + 1), :]
        high, low = ids >> 7, ids & (LANES - 1)
        picked = jnp.zeros((ROWS, LANES), jnp.float32)
        for x in range(2 * ROWS):
            line = spread(flux[x // ROWS][x % ROWS : x % ROWS + 1])
            picked = jnp.where(high == x, take(line, low, 1), picked)
        for c in range(ROWS):
            flux_ref[ROWS * group + c, 0:1, :] = picked[c : c + 1]

    out = pltpu.make_async_copy(flux_ref, slab_out, semaphore)
    out.start()

    kept = outer_rows(x_points)

    def put(x, plane, value):
        at = planes * kept.index(x) + plane
        sums_ref[at : at + ROWS, :] = value

    def beyond(ref, plane, field, slope, own_coef):
        wind_at = 2 * planes + plane % levels
        return (
            beside(ref, MASS, 0) * field
            - ref[planes + plane : planes + plane + ROWS, :]
            - ref[wind_at : wind_at + ROWS, :] * (own_coef * field)
            - ref[wind_at + levels : wind_at + levels + ROWS, :] * slope
        )

    def row_of(tiles, x):
        return spread(tiles[x // ROWS][x % ROWS : x % ROWS + 1])

    masses = [surf_tile(MASS, 0, h) for h in range(2)]
    last_element = x_points // GLL - 1
    for element in (0, last_element):
        lines = [GLL * element + i for i in range(GLL)]
        scale = [row_of(inverse[0], x) for x in lines]
        mass = [row_of(masses, x) for x in lines]
        for level in range(0, levels, ROWS):
            wind = wind_tiles(wind_ref, x_points, level, lines)
            for plane in range(level, planes, levels):
                here = slice(plane, plane + ROWS)
                fields = []
                for i, x in enumerate(lines):
                    total = avg_ref[planes * x + plane : planes * x + plane + ROWS, :]
                    other = x - 1 if i == 0 else x + 1
                    if other < 0:
                        total = total + low_ref[here, :]
                    elif other == x_points:
                        total = total + high_ref[here, :]
                    elif i in (0, GLL - 1):
                        at = planes * other + plane
                        total = total + avg_ref[at : at + ROWS, :]
                    fields.append(total * scale[i])
                moved, slopes = advance(geo, fields, wind, mass)
                if element == 0:
                    before = beyond(low_ref, plane, fields[0], slopes[0], deriv_table[3][3])
                    put(lines[0], plane, before + moved[0])
                    shared = moved[-1] + inner_ref[here, :]
                    put(lines[-1], plane, shared)
                    put(lines[-1] + 1, plane, shared)
                else:
                    at = inner_ref.shape[0] - planes + plane
                    shared = moved[0] + inner_ref[at : at + ROWS, :]
                    put(lines[0] - 1, plane, shared)
                    put(lines[0], plane, shared)
                    after = beyond(
                        high_ref, plane, fields[-1], slopes[-1], deriv_table[0][0]
                    )
                    put(lines[-1], plane, moved[-1] + after)
                for i in range(1, GLL - 1):
                    put(lines[i], plane, moved[i])
    packs = [packs_ref[:ROWS, :], packs_ref[ROWS:, :]]
    packs = edges_of(geo, packs, sums_ref, planes, kept)
    for q, pack in enumerate(packs):
        edges_ref[ROWS * q : ROWS * (q + 1), :] = pack
    out.wait()


def last_kernel(
    planes,
    inner_ref,
    outer_ref,
    inverse_ref,
    edges_ref,
    cols_ref,
    out_ref,
    hot_ref,
    before_ref,
    after_ref,
):
    geo = Geometry()
    x_points = inverse_ref.shape[0]
    kept = outer_rows(x_points)
    hot_ref[...] = one_hot(cols_ref[...])
    after_ref[...], before_ref[...] = split_sides(
        geo, edges_ref[:ROWS, :], edges_ref[ROWS:, :], 1
    )
    for x in range(x_points):
        inverse = spread(inverse_ref[x : x + 1, :])
        ref, first = inner_ref, planes * (x - GLL)
        if x in kept:
            ref, first = outer_ref, planes * kept.index(x)
        for group in range(planes // ROWS):
            tile = ref[first + ROWS * group : first + ROWS * (group + 1), :]
            at = planes * x + ROWS * group
            out_ref[at : at + ROWS, :] = inverse * geo.sum_y(tile, 0.0)


def end_kernel(
    planes,
    last_ref,
    before_ref,
    after_ref,
    recv_ref,
    final_ref,
    inverse_ref,
    cols_ref,
    hot_ref,
    weights_ref,
    gain_ref,
    ocean_ref,
    air_out,
    ocean_out,
    air_ref,
    row_ref,
    semaphores,
):
    geo = Geometry()
    blocks = cols_ref.shape[0]
    chunks = gain_ref.shape[0]
    x_points = inverse_ref.shape[0]
    copies = []

    def send(source, target):
        copies.append(
            pltpu.make_async_copy(source, target, semaphores.at[len(copies)])
        )
        copies[-1].start()

    send(ocean_ref.at[ROWS:], ocean_out.at[ROWS:])
    joined = join_edges(geo, before_ref[...], after_ref[...])
    groups = planes // ROWS
    for group in range(groups):
        for x in range(x_points):
            at = planes * x + ROWS * group
            beside = spread(inverse_ref[x : x + 1, :]) * outer_edges(joined, x, group)
            air_ref[pl.ds(ROWS * group * x_points + x, ROWS, stride=x_points), :] = last_ref[
                at : at + ROWS, :
            ] + jnp.where(geo.outer_lane, beside, 0.0)
        if group == 0:
            air_ref[0:x_points, :] = final_ref[...]
        if group % 2:
            rows = slice(
                ROWS * (group - 1) * x_points, ROWS * (group + 1) * x_points
            )
            send(air_ref.at[rows], air_out.at[rows])
    if groups % 2:
        rows = slice(ROWS * (groups - 1) * x_points, planes * x_points)
        send(air_ref.at[rows], air_out.at[rows])

    arrived = jnp.concatenate([recv_ref[c, 0:1, :] for c in range(blocks)], axis=0)
    (inflow,) = scatter_sum(
        [weights_ref[...] * arrived], cols_ref[...], chunks, hot_ref[...]
    )
    gain = inflow * gain_ref[...]
    row_ref[...] = ocean_ref[:ROWS, :]
    for k in range(chunks):
        at = slice(LANES * k, LANES * (k + 1))
        row_ref[0:1, at] = ocean_ref[0:1, at] + gain[k : k + 1]
    send(row_ref, ocean_out.at[:ROWS])
    for copy in copies:
        copy.wait()


def gathered(ids, coefs, source, sources, groups, first=0):
    totals = [jnp.zeros((ROWS, LANES), jnp.float32) for _ in range(groups)]
    for edge in range(ids.shape[0]):
        cell = spread(ids[edge : edge + 1])
        coef = spread(coefs[edge : edge + 1])
        high, low = cell >> 7, cell & (LANES - 1)
        for s in range(sources):
            scaled = jnp.where(high == first + s, coef, 0.0)
            for group in range(groups):
                totals[group] += scaled * take(source(group, s), low, 1)
    return totals


def multiplied(ids, coefs, halves_ref, sources, groups):
    lane_at = iota((LANES, LANES), 0)
    hot = jnp.concatenate(
        [
            jnp.where(lane_at == (ids[edge : edge + 1] & (LANES - 1)), 1.0, 0.0).astype(
                jnp.bfloat16
            )
            for edge in range(2)
        ],
        axis=1,
    )
    picked = jnp.dot(
        halves_ref[...],
        jnp.concatenate([hot, hot], axis=0),
        preferred_element_type=jnp.float32,
    )
    totals = [jnp.zeros((ROWS, LANES), jnp.float32) for _ in range(groups)]
    for edge in range(2):
        high = spread(ids[edge : edge + 1]) >> 7
        coef = spread(coefs[edge : edge + 1])
        side = slice(LANES * edge, LANES * (edge + 1))
        for s in range(sources):
            scaled = jnp.where(high == s, coef, 0.0)
            for group in range(groups):
                at = ROWS * (groups * s + group)
                totals[group] += scaled * picked[at : at + ROWS, side]
    return totals


def ocean_kernel(
    levels, start, tracers_ref, coef_ref, near_ref, rate_ref, after_ref, out_ref, halves_ref
):
    chunks = tracers_ref.shape[1] // LANES
    groups = tracers_ref.shape[0] // ROWS
    row = iota((ROWS, LANES), 0)

    def source(group, s):
        return tracers_ref[
            ROWS * group : ROWS * (group + 1), LANES * s : LANES * (s + 1)
        ]

    planes = tracers_ref.shape[0]
    for s in range(chunks):
        values = tracers_ref[:, LANES * s : LANES * (s + 1)]
        upper = values.astype(jnp.bfloat16)
        at = slice(planes * s, planes * (s + 1))
        halves_ref[at, :LANES] = upper
        halves_ref[at, LANES:] = (values - upper.astype(jnp.float32)).astype(jnp.bfloat16)
    edges = near_ref.shape[0]

    def one_chunk(number, carry):
        k = number + start
        at = pl.ds(pl.multiple_of(k * LANES, LANES), LANES)
        out_at = pl.ds(pl.multiple_of(number * LANES, LANES), LANES)
        ids, coefs = near_ref[:, at], coef_ref[:, at]
        by_gather = edges - edges // 3 * 2
        totals = gathered(ids[:by_gather], coefs[:by_gather], source, chunks, groups)
        for edge in range(by_gather, edges, 2):
            more = multiplied(
                ids[edge : edge + 2], coefs[edge : edge + 2], halves_ref, chunks, groups
            )
            totals = [total + part for total, part in zip(totals, more)]
        coef_sum = spread(jnp.sum(coefs, axis=0, keepdims=True))
        rate = spread(rate_ref[pl.ds(k, 1), :])
        tiles = [tracers_ref[ROWS * g : ROWS * (g + 1), at] for g in range(groups)]
        for g in range(groups):
            tile = tiles[g]
            top = bottom = tile
            if (ROWS * g) % levels:
                top = pltpu.roll(tiles[g - 1], 1, 0)
            if (ROWS * (g + 1)) % levels:
                bottom = pltpu.roll(tiles[g + 1], ROWS - 1, 0)
            above = jnp.where(row == 0, top, pltpu.roll(tile, 1, 0))
            below = jnp.where(row == ROWS - 1, bottom, pltpu.roll(tile, ROWS - 1, 0))
            vertical = rate * ((above - tile) + (below - tile))
            out_ref[ROWS * g : ROWS * (g + 1), out_at] = (
                tile + (totals[g] - coef_sum * tile) + vertical
            )
        return carry

    count = out_ref.shape[1] // LANES
    step = 2 if count % 2 == 0 else 1

    def some_chunks(number, carry):
        for i in range(step):
            one_chunk(step * number + i, carry)
        return carry

    lax.fori_loop(0, count // step, some_chunks, 0)


def send_kernel(tracers_ref, send_ref, before_ref, after_ref, *out_refs):
    chunks = tracers_ref.shape[1] // LANES
    for part, (side_ref, out_ref) in enumerate(zip((before_ref, after_ref), out_refs)):
        base = side_ref.shape[0]
        out_ref[:base, :] = side_ref[...]
        cells = spread(send_ref[0:1, LANES * part : LANES * (part + 1)])
        high, low = cells >> 7, cells & (LANES - 1)
        for group in range(tracers_ref.shape[0] // ROWS):
            half = slice(ROWS * group, ROWS * (group + 1))
            rim = jnp.zeros((ROWS, LANES), jnp.float32)
            for k in range(chunks):
                tile = tracers_ref[half, LANES * k : LANES * (k + 1)]
                rim = jnp.where(high == k, take(tile, low, 1), rim)
            out_ref[base + ROWS * group : base + ROWS * (group + 1), :] = rim


def rim_kernel(
    starts,
    before_ref,
    after_ref,
    coef_ref,
    near_ref,
    area_ref,
    rows_ref,
    *refs,
):
    partial_refs, (out_ref, gain_ref) = refs[: len(starts)], refs[len(starts) :]
    chunks = coef_ref.shape[1] // LANES
    groups = out_ref.shape[0] // ROWS
    rim_at = before_ref.shape[0] - out_ref.shape[0]
    sides = before_ref, after_ref
    gain_ref[...] = flux_gain / area_ref[...]

    def source(group, s):
        at = rim_at + ROWS * group
        return sides[s][at : at + ROWS, :]

    for k in range(chunks):
        at = slice(LANES * k, LANES * (k + 1))
        totals = gathered(near_ref[:, at], coef_ref[:, at], source, 2, groups, chunks)
        part = max(i for i, start in enumerate(starts) if start <= k)
        place = slice(LANES * (k - starts[part]), LANES * (k - starts[part] + 1))
        for g in range(groups):
            half = slice(ROWS * g, ROWS * (g + 1))
            out_ref[half, at] = partial_refs[part][half, place] + totals[g]


VMEM_SPEC = pl.BlockSpec(memory_space=pltpu.VMEM)
ANY_SPEC = pl.BlockSpec(memory_space=pl.ANY)
HBM_SPEC = pl.BlockSpec(memory_space=pltpu.HBM)


def call(kernel, outs, specs, scratch=(), cost=0, hbm_outs=0):
    estimate = None
    if cost:
        estimate = pl.CostEstimate(flops=0, bytes_accessed=cost, transcendentals=0)
    outs = [
        out if isinstance(out, jax.ShapeDtypeStruct) else jax.ShapeDtypeStruct(out, jnp.float32)
        for out in outs
    ]
    out_specs = [VMEM_SPEC] * len(outs)
    out_specs[:hbm_outs] = [HBM_SPEC] * hbm_outs
    return pl.pallas_call(
        kernel,
        out_shape=outs,
        in_specs=specs,
        out_specs=out_specs,
        scratch_shapes=list(scratch),
        cost_estimate=estimate,
        compiler_params=pltpu.CompilerParams(vmem_limit_bytes=32 * 2**20),
        name=getattr(kernel, "func", kernel).__name__,
    )


def body(
    air_state,
    air_wind,
    jacobian,
    land_area,
    xgrid_rows,
    tracers,
    edge_coef,
    neighbours,
    vert_rate,
    ocean_area,
    send_list,
    xgrid_cols,
    xgrid_weights,
):
    field_count, levels, x_points, y_points = air_state.shape
    planes = field_count * levels
    ocean_levels, cells = tracers.shape[1:]
    ocean_planes = tracers.shape[0] * ocean_levels
    faces, blocks = lax.axis_size("face"), lax.axis_size("blk")
    air = air_state.reshape(planes * x_points, y_points)
    wind = air_wind.reshape(2 * levels * x_points, y_points)
    ocean = tracers.reshape(ocean_planes, cells)
    point_ids, cell_ids, weights = xgrid_rows[0], xgrid_cols[0], xgrid_weights[0]
    rate = vert_rate.reshape(cells // LANES, LANES)
    area = ocean_area.reshape(cells // LANES, LANES)
    first_inputs = (
        cell_ids,
        weights,
        ocean,
        point_ids,
        jacobian,
        land_area,
        wind,
        air,
        send_list,
    )
    kept = (cell_ids, weights, point_ids, send_list)
    slab, moved, to_before, to_after, cell_ids, weights, point_ids, send_list = call(
        functools.partial(start_kernel, planes),
        [(blocks, HEAD, LANES), air.shape]
        + [(SIDE_IDS + blocks, LANES)] * 2
        + [jax.ShapeDtypeStruct(array.shape, array.dtype) for array in kept],
        [HBM_SPEC] * len(first_inputs),
        [
            pltpu.VMEM(shape, jnp.float32)
            for shape in (
                (blocks, HEAD, LANES),
                (ROWS, cells),
                jacobian.shape,
                land_area.shape,
                wind.shape,
                air.shape,
            )
        ]
        + [pltpu.SemaphoreType.DMA((len(first_inputs) + 1,))],
        hbm_outs=1,
    )(*(pltpu.with_memory_space_constraint(array, pltpu.HBM) for array in first_inputs))
    recv = lax.all_to_all(slab, "blk", split_axis=0, concat_axis=0, tiled=True)

    chunks = cells // LANES
    reads_per_chunk = edge_coef.shape[0] * chunks * (ocean_planes // ROWS)
    starts = (0, chunks * 6 // 16, chunks * 14 // 16)

    def ocean_part(start, end, after):
        (result,) = call(
            functools.partial(ocean_kernel, ocean_levels, start),
            [(ocean_planes, (end - start) * LANES)],
            [VMEM_SPEC] * 4 + [ANY_SPEC],
            [pltpu.VMEM((chunks * ocean_planes, 2 * LANES), jnp.bfloat16)],
            cost=(end - start) * reads_per_chunk * ROWS * LANES * 2,
        )(ocean, edge_coef, neighbours, rate, after)
        return result

    to_before, to_after = call(
        send_kernel,
        [(SIDE_IDS + blocks + ocean_planes, LANES)] * 2,
        [VMEM_SPEC] * 4,
        cost=reads_per_chunk * ROWS * LANES,
    )(ocean, send_list, to_before, to_after)
    onward = [(i, (i + 1) % blocks) for i in range(blocks)]
    before = lax.ppermute(to_after, "blk", onward)
    after = lax.ppermute(to_before, "blk", [(to, source) for source, to in onward])
    first_part = ocean_part(starts[0], starts[1], to_before)
    side_rows = 2 * planes + 2 * levels + SURF_ARRAYS + 2
    avg, down, up, surf = call(
        functools.partial(panel_kernel, planes),
        [air.shape, (side_rows, LANES), (side_rows, LANES), (4 * ROWS * SURF_ARRAYS, LANES)],
        [VMEM_SPEC] * 9 + [ANY_SPEC],
    )(
        moved,
        recv,
        before,
        after,
        air,
        wind,
        jacobian,
        land_area,
        point_ids,
        first_part,
    )
    after_me = [(i, (i + 1) % faces) for i in range(faces)]
    low = lax.ppermute(up, "face", after_me)
    high = lax.ppermute(down, "face", [(to, source) for source, to in after_me])
    inner, packs = call(
        functools.partial(inner_kernel, planes),
        [((x_points - 2 * GLL) * planes, LANES), (2 * ROWS, LANES)],
        [VMEM_SPEC] * 6,
        cost=2 * air.size * 4,
    )(avg, moved, before, after, surf, wind)
    second_part = ocean_part(starts[1], starts[2], surf)

    slab, outer, final, inverse, edges = call(
        functools.partial(second_kernel, planes),
        [
            (blocks, HEAD, LANES),
            (len(outer_rows(x_points)) * planes, LANES),
            (x_points, y_points),
            (x_points, y_points),
            (2 * ROWS, LANES),
        ],
        [VMEM_SPEC] * 8 + [ANY_SPEC],
        [pltpu.VMEM((blocks, HEAD, LANES), jnp.float32), pltpu.SemaphoreType.DMA(())],
        hbm_outs=1,
    )(avg, inner, packs, surf, low, high, wind, point_ids, second_part)
    arrived = lax.all_to_all(slab, "blk", split_axis=0, concat_axis=0, tiled=True)
    last, hot, to_before, to_after = call(
        functools.partial(last_kernel, planes),
        [air.shape, jax.ShapeDtypeStruct((LANES, blocks * LANES), jnp.bfloat16)]
        + [(ROWS, LANES)] * 2,
        [VMEM_SPEC] * 5,
        cost=2 * air.size * 4,
    )(inner, outer, inverse, edges, cell_ids)
    edge_before = lax.ppermute(to_after, "blk", onward)
    edge_after = lax.ppermute(to_before, "blk", [(to, source) for source, to in onward])
    third_part = ocean_part(starts[2], chunks, to_before)
    partial, gain = call(
        functools.partial(rim_kernel, starts),
        [ocean.shape, area.shape],
        [VMEM_SPEC] * 5 + [ANY_SPEC] + [VMEM_SPEC] * len(starts),
        cost=chunks * reads_per_chunk // 8 * ROWS * LANES * 4,
    )(
        before,
        after,
        edge_coef,
        neighbours,
        area,
        to_before,
        first_part,
        second_part,
        third_part,
    )
    air_final, ocean_final = call(
        functools.partial(end_kernel, planes),
        [air.shape, ocean.shape],
        [VMEM_SPEC] * 11,
        [
            pltpu.VMEM(air.shape, jnp.float32),
            pltpu.VMEM((ROWS, cells), jnp.float32),
            pltpu.SemaphoreType.DMA((2 + planes // ROWS,)),
        ],
        hbm_outs=2,
    )(
        last,
        edge_before,
        edge_after,
        arrived,
        final,
        inverse,
        cell_ids,
        hot,
        weights,
        gain,
        partial,
    )
    return air_final.reshape(air_state.shape), ocean_final.reshape(tracers.shape)


def solution(mesh):
    return jax.shard_map(
        body,
        mesh=mesh,
        in_specs=(
            P(None, None, "face", "blk"),
            P(None, None, "face", "blk"),
            P("face", "blk"),
            P("face", "blk"),
            P(("face", "blk"), None, None),
            P(None, None, ("face", "blk")),
            P(None, ("face", "blk")),
            P(None, ("face", "blk")),
            P(("face", "blk")),
            P(("face", "blk")),
            P(("face", "blk"), None),
            P(("face", "blk"), None, None),
            P(("face", "blk"), None, None),
        ),
        out_specs=(P(None, None, "face", "blk"), P(None, None, ("face", "blk"))),
        check_vma=False,
    )
```

```python
import functools

import jax
import jax.numpy as jnp
from jax import lax
from jax.experimental import pallas as pl
from jax.experimental.pallas import tpu as pltpu
from jax.sharding import PartitionSpec as P

GLL = 4
ROWS = 8
LANES = 128

deriv_table = [
    [-3.0, 4.045084971874737, -1.545084971874737, 0.5],
    [-0.8090169943749475, 0.0, 1.118033988749895, -0.30901699437494745],
    [0.30901699437494745, -1.118033988749895, 0.0, 0.8090169943749475],
    [-0.5, 1.545084971874737, -4.045084971874737, 3.0],
]
time_step = 0.05
relax_rate = 0.3
flux_gain = 0.2

HEAD = 8
SIDE_EDGE, SIDE_STRIP, SIDE_IDS = 0, 8, 16
AVG, MASS_SUM, MASS, COEF_X, COEF_Y, SURF = range(6)
SURF_ARRAYS = 6


def iota(shape, dim):
    return lax.broadcasted_iota(jnp.int32, shape, dim)


def take(values, index, axis):
    return jnp.take_along_axis(values, index, axis=axis, mode="promise_in_bounds")


def by_position(pos, values):
    result = jnp.full(pos.shape, values[-1], jnp.float32)
    for i, value in enumerate(values[:-1]):
        result = jnp.where(pos == i, value, result)
    return result


def spread(row):
    return jnp.broadcast_to(row, (ROWS, LANES))


class Geometry:
    def __init__(self):
        shape = (ROWS, LANES)
        self.row, self.lane = iota(shape, 0), iota(shape, 1)
        x_pos, y_pos = self.row & (GLL - 1), self.lane & (GLL - 1)
        self.y_from = [self.lane - y_pos + j for j in range(GLL)]
        columns = [[line[j] for line in deriv_table] for j in range(GLL)]
        self.x_coef = {
            step: by_position(
                x_pos,
                [
                    deriv_table[i][i + step] if 0 <= i + step < GLL else 0.0
                    for i in range(GLL)
                ],
            )
            for step in range(1 - GLL, GLL)
        }
        self.y_coef = [by_position(y_pos, column) for column in columns]
        self.y_swap = (
            self.lane + jnp.where(y_pos == GLL - 1, 1, 0) - jnp.where(y_pos == 0, 1, 0)
        ) & (LANES - 1)
        self.x_edge = (x_pos == 0) | (x_pos == GLL - 1)
        self.y_edge = (y_pos == 0) | (y_pos == GLL - 1)
        self.first_row, self.last_row = self.row == 0, self.row == ROWS - 1
        self.middle_row = self.row == GLL
        self.outer_lane = (self.lane == 0) | (self.lane == LANES - 1)
        self.weight = jnp.where(self.x_edge, 1.0 / 6.0, 5.0 / 6.0) * jnp.where(
            self.y_edge, 1.0 / 6.0, 5.0 / 6.0
        )

    def d_x(self, tile):
        return sum(
            coef * (pltpu.roll(tile, -step % ROWS, 0) if step else tile)
            for step, coef in self.x_coef.items()
        )

    def d_y(self, *tiles):
        totals = [0.0] * len(tiles)
        for j in range(GLL):
            for i, tile in enumerate(tiles):
                totals[i] += self.y_coef[j] * take(tile, self.y_from[j], 1)
        return totals

    def sum_x(self, low, high, before, after):
        low_down, low_up = pltpu.roll(low, 1, 0), pltpu.roll(low, ROWS - 1, 0)
        high_down, high_up = pltpu.roll(high, 1, 0), pltpu.roll(high, ROWS - 1, 0)
        low_other = jnp.where(
            self.first_row,
            before,
            jnp.where(
                self.middle_row, low_down, jnp.where(self.last_row, high_up, low_up)
            ),
        )
        high_other = jnp.where(
            self.first_row,
            low_down,
            jnp.where(
                self.middle_row, high_down, jnp.where(self.last_row, after, high_up)
            ),
        )
        return (
            low + jnp.where(self.x_edge, low_other, 0.0),
            high + jnp.where(self.x_edge, high_other, 0.0),
        )

    def sum_y(self, tile, outer):
        other = jnp.where(self.outer_lane, outer, take(tile, self.y_swap, 1))
        return tile + jnp.where(self.y_edge, other, 0.0)

    def sum_y_pair(self, own, strip):
        own_swap, strip_swap = take(own, self.y_swap, 1), take(strip, self.y_swap, 1)
        own_other = jnp.where(self.outer_lane, strip_swap, own_swap)
        strip_other = jnp.where(self.outer_lane, own_swap, strip_swap)
        return (
            own + jnp.where(self.y_edge, own_other, 0.0),
            strip + jnp.where(self.y_edge, strip_other, 0.0),
        )


def edge_place(x, group):
    return x // ROWS, LANES // 2 * (x % 2) + ROWS * group + 2 * (x % ROWS // 2)


def edges_of(geo, packs, ref, planes, lines, first=None):
    packs = list(packs)
    for number, x in enumerate(lines):
        base = planes * (number if first is None else x - first)
        for group in range(planes // ROWS):
            q, at = edge_place(x, group)
            tile = ref[base + ROWS * group : base + ROWS * (group + 1), :]
            rolled = pltpu.roll(tile, (at + 1) % LANES, 1)
            packs[q] = jnp.where((geo.lane >> 1) == at // 2, rolled, packs[q])
    return packs


def outer_edges(joined, x, group):
    q, at = edge_place(x, group)
    return pltpu.roll(joined[q], (-(at + 1)) % LANES, 1)


def split_sides(geo, first, second, unit):
    odd = (geo.lane & unit) != 0
    return (
        jnp.where(odd, pltpu.roll(second, unit, 1), first),
        jnp.where(odd, second, pltpu.roll(first, LANES - unit, 1)),
    )


def join_sides(geo, before, after, unit):
    odd = (geo.lane & unit) != 0
    return (
        jnp.where(odd, pltpu.roll(after, unit, 1), before),
        jnp.where(odd, after, pltpu.roll(before, LANES - unit, 1)),
    )


def join_edges(geo, before, after):
    odd = (geo.lane & 1) != 0
    return (
        jnp.where(odd, pltpu.roll(before, 1, 1), after),
        jnp.where(odd, before, pltpu.roll(after, LANES - 1, 1)),
    )


def neighbours_of(blocks):
    here = lax.axis_index("blk")
    return lax.rem(here + blocks - 1, blocks), lax.rem(here + 1, blocks)


def one_hot(index, allowed=None):
    low = index & (LANES - 1)
    lane_at = iota((LANES, LANES), 0)
    if allowed is not None:
        lane_at = jnp.where(allowed(lane_at), lane_at, -1)
    return jnp.concatenate(
        [
            jnp.where(lane_at == low[c : c + 1], 1.0, 0.0).astype(jnp.bfloat16)
            for c in range(index.shape[0])
        ],
        axis=1,
    )


def scatter_sum(lines, index, bins, lanes_hot):
    split = []
    for values in lines:
        for part in range(3):
            short = values.astype(jnp.bfloat16).astype(jnp.float32)
            split.append(short)
            values = values - short
    high = index >> 7
    bin_at = iota((bins, LANES), 0)
    left = []
    for c in range(index.shape[0]):
        hit = bin_at == high[c : c + 1]
        left.append(
            jnp.concatenate(
                [jnp.where(hit, part[c : c + 1], 0.0) for part in split], axis=0
            ).astype(jnp.bfloat16)
        )
    total = lax.dot_general(
        jnp.concatenate(left, axis=1),
        lanes_hot,
        (((1,), (1,)), ((), ())),
        preferred_element_type=jnp.float32,
    )
    sums = []
    for i in range(len(lines)):
        part = total[3 * i * bins : 3 * (i + 1) * bins]
        sums.append(part[:bins] + part[bins : 2 * bins] + part[2 * bins :])
    return sums


def wind_tiles(wind_ref, x_points, level, lines):
    levels = wind_ref.shape[0] // (2 * x_points)
    return [
        [
            time_step
            * wind_ref[
                pl.ds((levels * part + level) * x_points + x, ROWS, stride=x_points), :
            ]
            for x in lines
        ]
        for part in range(2)
    ]


def start_kernel(
    planes,
    cols_in,
    weights_in,
    tracers_in,
    rows_in,
    jac_in,
    land_in,
    wind_in,
    air_in,
    send_in,
    slab_out,
    moved_ref,
    before_ref,
    after_ref,
    cols_ref,
    weights_ref,
    rows_ref,
    send_ref,
    slab_ref,
    tracers_ref,
    jac_ref,
    land_ref,
    wind_ref,
    air_ref,
    semaphores,
):
    copies = [
        pltpu.make_async_copy(source, target, semaphores.at[i])
        for i, (source, target) in enumerate(
            (
                (cols_in, cols_ref),
                (tracers_in.at[:ROWS], tracers_ref),
                (weights_in, weights_ref),
                (rows_in, rows_ref),
                (air_in, air_ref),
                (wind_in, wind_ref),
                (jac_in, jac_ref),
                (land_in, land_ref),
                (send_in, send_ref),
            )
        )
    ]
    for copy in copies:
        copy.start()
    geo = Geometry()
    blocks = cols_ref.shape[0]
    x_points = jac_ref.shape[0]
    levels = wind_ref.shape[0] // (2 * x_points)
    chunks = tracers_ref.shape[1] // LANES
    for copy in copies[:4]:
        copy.wait()

    for group in range(blocks // ROWS):
        at = slice(ROWS * group, ROWS * (group + 1))
        cells = cols_ref[at, :]
        high, low = cells >> 7, cells & (LANES - 1)
        surface = jnp.zeros((ROWS, LANES), jnp.float32)
        for k in range(chunks):
            line = spread(tracers_ref[0:1, LANES * k : LANES * (k + 1)])
            surface = jnp.where(high == k, take(line, low, 1), surface)
        area = weights_ref[at, :]
        heat = area * surface
        for c in range(ROWS):
            owner = ROWS * group + c
            for place, step in enumerate((1, 0, -1)):
                to = (owner + step) % blocks
                slab_ref[to, 2 * place : 2 * place + 1, :] = heat[c : c + 1]
                slab_ref[to, 2 * place + 1 : 2 * place + 2, :] = area[c : c + 1]

    out = pltpu.make_async_copy(slab_ref, slab_out, semaphores.at[len(copies)])
    out.start()
    ids = rows_ref[...].astype(jnp.float32)
    for side_ref in (before_ref, after_ref):
        side_ref[SIDE_IDS : SIDE_IDS + blocks, :] = ids

    for copy in copies[4:]:
        copy.wait()
    strips = []
    for h in range(2):
        half = slice(ROWS * h, ROWS * (h + 1))
        second = levels * x_points
        pack = jnp.zeros((ROWS, LANES), jnp.float32)
        for i, strip in enumerate(
            (
                air_ref[half, :],
                wind_ref[half, :],
                wind_ref[second + ROWS * h : second + ROWS * (h + 1), :],
                jac_ref[half, :],
                land_ref[half, :],
            )
        ):
            pack = jnp.where(
                (geo.lane >> 4) == i, pltpu.roll(strip, 16 * i + 8, 1), pack
            )
        strips.append(pack)
    to_right, to_left = split_sides(geo, strips[0], strips[1], ROWS)
    after_ref[SIDE_STRIP : SIDE_STRIP + ROWS, :] = to_right
    before_ref[SIDE_STRIP : SIDE_STRIP + ROWS, :] = to_left

    y_weight = jnp.where(geo.y_edge, 1.0 / 6.0, 5.0 / 6.0)
    for element in range(x_points // GLL):
        lines = [GLL * element + i for i in range(GLL)]
        mass = [
            (1.0 / 6.0 if i in (0, GLL - 1) else 5.0 / 6.0)
            * y_weight
            * spread(jac_ref[x : x + 1, :])
            for i, x in enumerate(lines)
        ]
        for level in range(0, levels, ROWS):
            wind = wind_tiles(wind_ref, x_points, level, lines)
            for plane in range(level, planes, levels):
                fields = [
                    air_ref[pl.ds(plane * x_points + x, ROWS, stride=x_points), :]
                    for x in lines
                ]
                slopes = geo.d_y(*fields)
                for i, x in enumerate(lines):
                    slope = sum(deriv_table[i][j] * fields[j] for j in range(GLL))
                    moved = mass[i] * (
                        fields[i] - (wind[0][i] * slope + wind[1][i] * slopes[i])
                    )
                    moved_ref[planes * x + plane : planes * x + plane + ROWS, :] = moved
    packs = [jnp.zeros((ROWS, LANES), jnp.float32) for _ in range(2)]
    packs = edges_of(geo, packs, moved_ref, planes, range(x_points))
    to_right, to_left = split_sides(geo, packs[0], packs[1], 1)
    after_ref[SIDE_EDGE : SIDE_EDGE + ROWS, :] = to_right
    before_ref[SIDE_EDGE : SIDE_EDGE + ROWS, :] = to_left
    out.wait()


def panel_kernel(
    planes,
    moved_ref,
    recv_ref,
    before_ref,
    after_ref,
    air_ref,
    wind_ref,
    jac_ref,
    land_ref,
    rows_ref,
    ocean_ref,
    avg_ref,
    down_ref,
    up_ref,
    surf_ref,
):
    geo = Geometry()
    blocks = rows_ref.shape[0]
    x_points = jac_ref.shape[0]
    levels = wind_ref.shape[0] // (2 * x_points)

    own_ids = rows_ref[...]
    left_ids = before_ref[SIDE_IDS : SIDE_IDS + blocks, :].astype(jnp.int32)
    right_ids = after_ref[SIDE_IDS : SIDE_IDS + blocks, :].astype(jnp.int32)
    head = [
        jnp.concatenate([recv_ref[c, i : i + 1, :] for c in range(blocks)], axis=0)
        for i in range(6)
    ]
    heat, frac = scatter_sum(head[2:4], own_ids, x_points, one_hot(own_ids))
    from_left = scatter_sum(
        head[0:2], left_ids, x_points, one_hot(left_ids, lambda lane: lane >= LANES - ROWS)
    )
    from_right = scatter_sum(
        head[4:6], right_ids, x_points, one_hot(right_ids, lambda lane: lane < ROWS)
    )
    strip_heat = from_left[0] + from_right[0]
    strip_frac = from_left[1] + from_right[1]

    in_strip = (geo.lane < ROWS) | (geo.lane >= LANES - ROWS)
    packs = join_sides(
        geo,
        before_ref[SIDE_STRIP : SIDE_STRIP + ROWS, :],
        after_ref[SIDE_STRIP : SIDE_STRIP + ROWS, :],
        ROWS,
    )
    own, strip = [], []
    for h, pack in enumerate(packs):
        half = slice(ROWS * h, ROWS * (h + 1))
        strip.append(
            [
                jnp.where(
                    in_strip, pltpu.roll(pack, (-(16 * i + 8)) % LANES, 1), 1.0
                )
                for i in range(5)
            ]
        )
        own.append(
            [
                air_ref[half, :],
                wind_ref[half, :],
                wind_ref[
                    levels * x_points + ROWS * h : levels * x_points + ROWS * (h + 1), :
                ],
                jac_ref[half, :],
                land_ref[half, :],
            ]
        )
    for h in range(2):
        half = slice(ROWS * h, ROWS * (h + 1))
        pair = []
        for tile, ((field, wind_x, wind_y, jac, land), tile_heat, tile_frac) in enumerate(
            ((own[h], heat[half], frac[half]), (strip[h], strip_heat[half], strip_frac[half]))
        ):
            mass = geo.weight * jac
            if tile == 1:
                tile_heat = jnp.where(in_strip, tile_heat, 0.0)
                tile_frac = jnp.where(in_strip, tile_frac, 0.0)
            surf = (tile_heat + land * field) / (tile_frac + land)
            coef_x, coef_y = time_step * mass * wind_x, time_step * mass * wind_y
            moved = (
                mass * (field + relax_rate * (surf - field))
                - coef_x * geo.d_x(field)
                - coef_y * geo.d_y(field)[0]
            )
            pair.append((moved, mass))
            at = x_points * tile + ROWS * h
            for number, value in (
                (MASS, mass),
                (COEF_X, coef_x),
                (COEF_Y, coef_y),
                (SURF, surf),
            ):
                surf_ref[2 * x_points * number + at : 2 * x_points * number + at + ROWS, :] = value
        for number, i in ((AVG, 0), (MASS_SUM, 1)):
            for tile, value in enumerate(geo.sum_y_pair(pair[0][i], pair[1][i])):
                at = 2 * x_points * number + x_points * tile + ROWS * h
                surf_ref[at : at + ROWS, :] = value

    joined = join_edges(
        geo,
        before_ref[SIDE_EDGE : SIDE_EDGE + ROWS, :],
        after_ref[SIDE_EDGE : SIDE_EDGE + ROWS, :],
    )
    for x in outer_rows(x_points):
        for group in range(planes // ROWS):
            at = slice(planes * x + ROWS * group, planes * x + ROWS * (group + 1))
            avg_ref[at, :] = geo.sum_y(moved_ref[at, :], outer_edges(joined, x, group))

    def line(r):
        return avg_ref[planes * r : planes * (r + 1), :]

    def surf_line(number, r):
        return surf_ref[pl.ds(2 * x_points * number + r, 2, stride=x_points), :]

    def first_step(get, mass_at):
        top = x_points - 1
        return (
            [
                get(1) / mass_at(1),
                get(2) / mass_at(2),
                (get(3) + get(GLL)) / (mass_at(3) + mass_at(GLL)),
            ],
            [
                (get(top - 4) + get(top - 3)) / (mass_at(top - 4) + mass_at(top - 3)),
                get(top - 2) / mass_at(top - 2),
                get(top - 1) / mass_at(top - 1),
            ],
        )

    def own_mass_sum(r):
        return surf_ref[2 * x_points * MASS_SUM + r : 2 * x_points * MASS_SUM + r + 1, :]

    low_lines, high_lines = first_step(line, own_mass_sum)
    surf_low, surf_high = first_step(
        functools.partial(surf_line, AVG), functools.partial(surf_line, MASS_SUM)
    )
    for out_ref, r, lines, surf_lines, coefs in (
        (down_ref, 0, low_lines, surf_low, deriv_table[0][1:]),
        (up_ref, x_points - 1, high_lines, surf_high, deriv_table[3][:3]),
    ):
        slope = sum(coef * value for coef, value in zip(coefs, lines))
        surf_slope = sum(coef * value for coef, value in zip(coefs, surf_lines))
        mass = surf_ref[2 * x_points * MASS + r : 2 * x_points * MASS + r + 1, :]
        wind = time_step * mass * wind_ref[pl.ds(r, 2 * levels, stride=x_points), :]
        out_ref[0:planes, :] = line(r)
        for first in range(0, planes, levels):
            out_ref[planes + first : planes + first + levels, :] = (
                wind[:levels] * slope[first : first + levels]
            )
        base = 2 * planes
        out_ref[base : base + 2 * levels, :] = wind
        base += 2 * levels
        pairs = [surf_line(number, r) for number in range(SURF_ARRAYS)]
        pairs.append(surf_line(COEF_X, r) * surf_slope)
        pack = jnp.zeros((ROWS, LANES), jnp.float32)
        for i, pair in enumerate(pairs):
            out_ref[base + i : base + i + 1, :] = pair[:1]
            pack = jnp.where(
                (geo.lane >> 4) == i, pltpu.roll(spread(pair[1:]), 16 * i + 8, 1), pack
            )
        base += len(pairs)
        out_ref[base : base + 1, :] = pack[:1]


def outer_rows(x_points):
    return [x for x in range(x_points) if x <= GLL or x >= x_points - GLL - 1]


def advance(geo, fields, wind, mass):
    slopes = geo.d_y(*fields)
    moved = []
    for i in range(GLL):
        slope = sum(deriv_table[i][j] * fields[j] for j in range(GLL))
        moved.append(mass[i] * (fields[i] - (wind[0][i] * slope + wind[1][i] * slopes[i])))
    return moved, slopes


def inner_kernel(
    planes, avg_ref, moved_ref, before_ref, after_ref, surf_ref, wind_ref, out_ref, packs_ref
):
    geo = Geometry()
    x_points = avg_ref.shape[0] // planes
    levels = wind_ref.shape[0] // (2 * x_points)
    joined = join_edges(
        geo,
        before_ref[SIDE_EDGE : SIDE_EDGE + ROWS, :],
        after_ref[SIDE_EDGE : SIDE_EDGE + ROWS, :],
    )
    outer = outer_rows(x_points)

    def average(x, plane):
        at = slice(planes * x + plane, planes * x + plane + ROWS)
        if x in outer:
            return avg_ref[at, :]
        return geo.sum_y(moved_ref[at, :], outer_edges(joined, x, plane // ROWS))

    def surf_row(number, x):
        at = 2 * x_points * number + x
        return spread(surf_ref[at : at + 1, :])

    def put(x, plane, value):
        at = planes * (x - GLL) + plane
        out_ref[at : at + ROWS, :] = value

    held = {}
    carried = {}
    for element in range(1, x_points // GLL - 1):
        lines = [GLL * element + i for i in range(GLL)]
        totals = [surf_row(MASS_SUM, x) for x in lines]
        totals[0] = totals[0] + surf_row(MASS_SUM, lines[0] - 1)
        totals[-1] = totals[-1] + surf_row(MASS_SUM, lines[-1] + 1)
        scale = [1.0 / total for total in totals]
        mass = [surf_row(MASS, x) for x in lines]
        for level in range(0, levels, ROWS):
            wind = wind_tiles(wind_ref, x_points, level, lines)
            for plane in range(level, planes, levels):
                if element == 1:
                    first = average(lines[0], plane) + average(lines[0] - 1, plane)
                else:
                    first = carried[plane]
                last = average(lines[-1], plane) + average(lines[-1] + 1, plane)
                carried[plane] = last
                totals = (
                    [first] + [average(x, plane) for x in lines[1:-1]] + [last]
                )
                fields = [total * factor for total, factor in zip(totals, scale)]
                moved, _ = advance(geo, fields, wind, mass)
                if element == 1:
                    put(lines[0], plane, moved[0])
                else:
                    shared = held[plane] + moved[0]
                    put(lines[0] - 1, plane, shared)
                    put(lines[0], plane, shared)
                for i in range(1, GLL - 1):
                    put(lines[i], plane, moved[i])
                held[plane] = moved[-1]
                if lines[-1] == x_points - GLL - 1:
                    put(lines[-1], plane, moved[-1])
    packs = [jnp.zeros((ROWS, LANES), jnp.float32) for _ in range(2)]
    inner = [x for x in range(x_points) if x not in outer]
    for q, pack in enumerate(edges_of(geo, packs, out_ref, planes, inner, GLL)):
        packs_ref[ROWS * q : ROWS * (q + 1), :] = pack


def second_kernel(
    planes,
    avg_ref,
    inner_ref,
    packs_ref,
    surf_ref,
    low_ref,
    high_ref,
    wind_ref,
    rows_ref,
    ocean_ref,
    slab_out,
    sums_ref,
    final_ref,
    inverse_ref,
    edges_ref,
    flux_ref,
    semaphore,
):
    geo = Geometry()
    blocks = rows_ref.shape[0]
    x_points = final_ref.shape[0]
    levels = wind_ref.shape[0] // (2 * x_points)
    base = low_ref.shape[0] - SURF_ARRAYS - 2

    def surf_tile(number, tile, h):
        at = 2 * x_points * number + x_points * tile + ROWS * h
        return surf_ref[at : at + ROWS, :]

    in_strip = (geo.lane < ROWS) | (geo.lane >= LANES - ROWS)

    def beside(ref, number, tile):
        if tile == 0:
            return spread(ref[base + number : base + number + 1, :])
        at = base + SURF_ARRAYS + 1
        strips = spread(ref[at : at + 1, :])
        return jnp.where(
            in_strip, pltpu.roll(strips, (-(16 * number + 8)) % LANES, 1), 1.0
        )

    ends = []
    inverse = []
    for tile in range(2):
        total = geo.sum_x(
            surf_tile(MASS_SUM, tile, 0),
            surf_tile(MASS_SUM, tile, 1),
            beside(low_ref, MASS_SUM, tile),
            beside(high_ref, MASS_SUM, tile),
        )
        inverse.append([1.0 / value for value in total])
        summed = geo.sum_x(
            surf_tile(AVG, tile, 0),
            surf_tile(AVG, tile, 1),
            beside(low_ref, AVG, tile),
            beside(high_ref, AVG, tile),
        )
        fields = [value * scale for value, scale in zip(summed, inverse[tile])]
        moved = []
        for h in range(2):
            field = fields[h]
            moved.append(
                surf_tile(MASS, tile, h)
                * (field + relax_rate * (surf_tile(SURF, tile, h) - field))
                - surf_tile(COEF_X, tile, h) * geo.d_x(field)
                - surf_tile(COEF_Y, tile, h) * geo.d_y(field)[0]
            )
        halos = []
        for ref, field, own_coef in (
            (low_ref, spread(fields[0][:1]), deriv_table[3][3]),
            (high_ref, spread(fields[1][ROWS - 1 :]), deriv_table[0][0]),
        ):
            halos.append(
                beside(ref, MASS, tile)
                * (field + relax_rate * (beside(ref, SURF, tile) - field))
                - beside(ref, SURF_ARRAYS, tile)
                - beside(ref, COEF_X, tile) * (own_coef * field)
                - beside(ref, COEF_Y, tile) * geo.d_y(field)[0]
            )
        ends.append(geo.sum_x(moved[0], moved[1], halos[0], halos[1]))
    final = []
    for h in range(2):
        summed, _ = geo.sum_y_pair(ends[0][h], ends[1][h])
        final.append(summed * inverse[0][h])
        final_ref[ROWS * h : ROWS * (h + 1), :] = final[h]
        inverse_ref[ROWS * h : ROWS * (h + 1), :] = inverse[0][h]
    flux = [final[h] - surf_tile(SURF, 0, h) for h in range(2)]
    for group in range(blocks // ROWS):
        ids = rows_ref[ROWS * group : ROWS * (group + 1), :]
        high, low = ids >> 7, ids & (LANES - 1)
        picked = jnp.zeros((ROWS, LANES), jnp.float32)
        for x in range(x_points):
            line = spread(flux[x // ROWS][x % ROWS : x % ROWS + 1])
            picked = jnp.where(high == x, take(line, low, 1), picked)
        for c in range(ROWS):
            flux_ref[ROWS * group + c, 0:1, :] = picked[c : c + 1]

    out = pltpu.make_async_copy(flux_ref, slab_out, semaphore)
    out.start()

    kept = outer_rows(x_points)

    def put(x, plane, value):
        at = planes * kept.index(x) + plane
        sums_ref[at : at + ROWS, :] = value

    def beyond(ref, plane, field, slope, own_coef):
        wind_at = 2 * planes + plane % levels
        return (
            beside(ref, MASS, 0) * field
            - ref[planes + plane : planes + plane + ROWS, :]
            - ref[wind_at : wind_at + ROWS, :] * (own_coef * field)
            - ref[wind_at + levels : wind_at + levels + ROWS, :] * slope
        )

    def row_of(tiles, x):
        return spread(tiles[x // ROWS][x % ROWS : x % ROWS + 1])

    masses = [surf_tile(MASS, 0, h) for h in range(2)]
    last_element = x_points // GLL - 1
    for element in (0, last_element):
        lines = [GLL * element + i for i in range(GLL)]
        scale = [row_of(inverse[0], x) for x in lines]
        mass = [row_of(masses, x) for x in lines]
        for level in range(0, levels, ROWS):
            wind = wind_tiles(wind_ref, x_points, level, lines)
            for plane in range(level, planes, levels):
                here = slice(plane, plane + ROWS)
                fields = []
                for i, x in enumerate(lines):
                    total = avg_ref[planes * x + plane : planes * x + plane + ROWS, :]
                    other = x - 1 if i == 0 else x + 1
                    if other < 0:
                        total = total + low_ref[here, :]
                    elif other == x_points:
                        total = total + high_ref[here, :]
                    elif i in (0, GLL - 1):
                        at = planes * other + plane
                        total = total + avg_ref[at : at + ROWS, :]
                    fields.append(total * scale[i])
                moved, slopes = advance(geo, fields, wind, mass)
                if element == 0:
                    before = beyond(low_ref, plane, fields[0], slopes[0], deriv_table[3][3])
                    put(lines[0], plane, before + moved[0])
                    shared = moved[-1] + inner_ref[here, :]
                    put(lines[-1], plane, shared)
                    put(lines[-1] + 1, plane, shared)
                else:
                    at = inner_ref.shape[0] - planes + plane
                    shared = moved[0] + inner_ref[at : at + ROWS, :]
                    put(lines[0] - 1, plane, shared)
                    put(lines[0], plane, shared)
                    after = beyond(
                        high_ref, plane, fields[-1], slopes[-1], deriv_table[0][0]
                    )
                    put(lines[-1], plane, moved[-1] + after)
                for i in range(1, GLL - 1):
                    put(lines[i], plane, moved[i])
    packs = [packs_ref[:ROWS, :], packs_ref[ROWS:, :]]
    packs = edges_of(geo, packs, sums_ref, planes, kept)
    for q, pack in enumerate(packs):
        edges_ref[ROWS * q : ROWS * (q + 1), :] = pack
    out.wait()


def last_kernel(
    planes,
    inner_ref,
    outer_ref,
    inverse_ref,
    edges_ref,
    cols_ref,
    out_ref,
    hot_ref,
    before_ref,
    after_ref,
):
    geo = Geometry()
    x_points = inverse_ref.shape[0]
    kept = outer_rows(x_points)
    hot_ref[...] = one_hot(cols_ref[...])
    after_ref[...], before_ref[...] = split_sides(
        geo, edges_ref[:ROWS, :], edges_ref[ROWS:, :], 1
    )
    for x in range(x_points):
        inverse = spread(inverse_ref[x : x + 1, :])
        ref, first = inner_ref, planes * (x - GLL)
        if x in kept:
            ref, first = outer_ref, planes * kept.index(x)
        for group in range(planes // ROWS):
            tile = ref[first + ROWS * group : first + ROWS * (group + 1), :]
            at = planes * x + ROWS * group
            out_ref[at : at + ROWS, :] = inverse * geo.sum_y(tile, 0.0)


def end_kernel(
    planes,
    last_ref,
    before_ref,
    after_ref,
    recv_ref,
    final_ref,
    inverse_ref,
    cols_ref,
    hot_ref,
    weights_ref,
    gain_ref,
    ocean_ref,
    air_out,
    ocean_out,
    air_ref,
    row_ref,
    semaphores,
):
    geo = Geometry()
    blocks = cols_ref.shape[0]
    chunks = gain_ref.shape[0]
    x_points = inverse_ref.shape[0]
    copies = []

    def send(source, target):
        copies.append(
            pltpu.make_async_copy(source, target, semaphores.at[len(copies)])
        )
        copies[-1].start()

    send(ocean_ref.at[ROWS:], ocean_out.at[ROWS:])
    joined = join_edges(geo, before_ref[...], after_ref[...])
    groups = planes // ROWS
    for group in range(groups):
        for x in range(x_points):
            at = planes * x + ROWS * group
            beside = spread(inverse_ref[x : x + 1, :]) * outer_edges(joined, x, group)
            air_ref[pl.ds(ROWS * group * x_points + x, ROWS, stride=x_points), :] = last_ref[
                at : at + ROWS, :
            ] + jnp.where(geo.outer_lane, beside, 0.0)
        if group == 0:
            air_ref[0:x_points, :] = final_ref[...]
        if group % 2:
            rows = slice(
                ROWS * (group - 1) * x_points, ROWS * (group + 1) * x_points
            )
            send(air_ref.at[rows], air_out.at[rows])
    if groups % 2:
        rows = slice(ROWS * (groups - 1) * x_points, planes * x_points)
        send(air_ref.at[rows], air_out.at[rows])

    arrived = jnp.concatenate([recv_ref[c, 0:1, :] for c in range(blocks)], axis=0)
    (inflow,) = scatter_sum(
        [weights_ref[...] * arrived], cols_ref[...], chunks, hot_ref[...]
    )
    gain = inflow * gain_ref[...]
    row_ref[...] = ocean_ref[:ROWS, :]
    for k in range(chunks):
        at = slice(LANES * k, LANES * (k + 1))
        row_ref[0:1, at] = ocean_ref[0:1, at] + gain[k : k + 1]
    send(row_ref, ocean_out.at[:ROWS])
    for copy in copies:
        copy.wait()


def gathered(ids, coefs, source, sources, groups, first=0):
    totals = [jnp.zeros((ROWS, LANES), jnp.float32) for _ in range(groups)]
    for edge in range(ids.shape[0]):
        cell = spread(ids[edge : edge + 1])
        coef = spread(coefs[edge : edge + 1])
        high, low = cell >> 7, cell & (LANES - 1)
        for s in range(sources):
            scaled = jnp.where(high == first + s, coef, 0.0)
            for group in range(groups):
                totals[group] += scaled * take(source(group, s), low, 1)
    return totals


def multiplied(ids, coefs, halves_ref, sources, groups):
    lane_at = iota((LANES, LANES), 0)
    hot = jnp.concatenate(
        [
            jnp.where(lane_at == (ids[edge : edge + 1] & (LANES - 1)), 1.0, 0.0).astype(
                jnp.bfloat16
            )
            for edge in range(2)
        ],
        axis=1,
    )
    picked = jnp.dot(
        halves_ref[...],
        jnp.concatenate([hot, hot], axis=0),
        preferred_element_type=jnp.float32,
    )
    totals = [jnp.zeros((ROWS, LANES), jnp.float32) for _ in range(groups)]
    for edge in range(2):
        high = spread(ids[edge : edge + 1]) >> 7
        coef = spread(coefs[edge : edge + 1])
        side = slice(LANES * edge, LANES * (edge + 1))
        for s in range(sources):
            scaled = jnp.where(high == s, coef, 0.0)
            for group in range(groups):
                at = ROWS * (groups * s + group)
                totals[group] += scaled * picked[at : at + ROWS, side]
    return totals


def ocean_kernel(
    levels, start, tracers_ref, coef_ref, near_ref, rate_ref, after_ref, out_ref, halves_ref
):
    chunks = tracers_ref.shape[1] // LANES
    groups = tracers_ref.shape[0] // ROWS
    row = iota((ROWS, LANES), 0)

    def source(group, s):
        return tracers_ref[
            ROWS * group : ROWS * (group + 1), LANES * s : LANES * (s + 1)
        ]

    planes = tracers_ref.shape[0]
    for s in range(chunks):
        values = tracers_ref[:, LANES * s : LANES * (s + 1)]
        upper = values.astype(jnp.bfloat16)
        at = slice(planes * s, planes * (s + 1))
        halves_ref[at, :LANES] = upper
        halves_ref[at, LANES:] = (values - upper.astype(jnp.float32)).astype(jnp.bfloat16)
    edges = near_ref.shape[0]

    def one_chunk(number, carry):
        k = number + start
        at = pl.ds(pl.multiple_of(k * LANES, LANES), LANES)
        out_at = pl.ds(pl.multiple_of(number * LANES, LANES), LANES)
        ids, coefs = near_ref[:, at], coef_ref[:, at]
        by_gather = edges - edges // 3 * 2
        totals = gathered(ids[:by_gather], coefs[:by_gather], source, chunks, groups)
        for edge in range(by_gather, edges, 2):
            more = multiplied(
                ids[edge : edge + 2], coefs[edge : edge + 2], halves_ref, chunks, groups
            )
            totals = [total + part for total, part in zip(totals, more)]
        coef_sum = spread(jnp.sum(coefs, axis=0, keepdims=True))
        rate = spread(rate_ref[pl.ds(k, 1), :])
        tiles = [tracers_ref[ROWS * g : ROWS * (g + 1), at] for g in range(groups)]
        for g in range(groups):
            tile = tiles[g]
            top = bottom = tile
            if (ROWS * g) % levels:
                top = pltpu.roll(tiles[g - 1], 1, 0)
            if (ROWS * (g + 1)) % levels:
                bottom = pltpu.roll(tiles[g + 1], ROWS - 1, 0)
            above = jnp.where(row == 0, top, pltpu.roll(tile, 1, 0))
            below = jnp.where(row == ROWS - 1, bottom, pltpu.roll(tile, ROWS - 1, 0))
            vertical = rate * ((above - tile) + (below - tile))
            out_ref[ROWS * g : ROWS * (g + 1), out_at] = (
                tile + (totals[g] - coef_sum * tile) + vertical
            )
        return carry

    count = out_ref.shape[1] // LANES
    step = 2 if count % 2 == 0 else 1

    def some_chunks(number, carry):
        for i in range(step):
            one_chunk(step * number + i, carry)
        return carry

    lax.fori_loop(0, count // step, some_chunks, 0)


def send_kernel(tracers_ref, send_ref, before_ref, after_ref, *out_refs):
    chunks = tracers_ref.shape[1] // LANES
    for part, (side_ref, out_ref) in enumerate(zip((before_ref, after_ref), out_refs)):
        base = side_ref.shape[0]
        out_ref[:base, :] = side_ref[...]
        cells = spread(send_ref[0:1, LANES * part : LANES * (part + 1)])
        high, low = cells >> 7, cells & (LANES - 1)
        for group in range(tracers_ref.shape[0] // ROWS):
            half = slice(ROWS * group, ROWS * (group + 1))
            rim = jnp.zeros((ROWS, LANES), jnp.float32)
            for k in range(chunks):
                tile = tracers_ref[half, LANES * k : LANES * (k + 1)]
                rim = jnp.where(high == k, take(tile, low, 1), rim)
            out_ref[base + ROWS * group : base + ROWS * (group + 1), :] = rim


def rim_kernel(
    starts,
    before_ref,
    after_ref,
    coef_ref,
    near_ref,
    area_ref,
    rows_ref,
    *refs,
):
    partial_refs, (out_ref, gain_ref) = refs[: len(starts)], refs[len(starts) :]
    chunks = coef_ref.shape[1] // LANES
    groups = out_ref.shape[0] // ROWS
    rim_at = before_ref.shape[0] - out_ref.shape[0]
    sides = before_ref, after_ref
    gain_ref[...] = flux_gain / area_ref[...]

    def source(group, s):
        at = rim_at + ROWS * group
        return sides[s][at : at + ROWS, :]

    for k in range(chunks):
        at = slice(LANES * k, LANES * (k + 1))
        totals = gathered(near_ref[:, at], coef_ref[:, at], source, 2, groups, chunks)
        part = max(i for i, start in enumerate(starts) if start <= k)
        place = slice(LANES * (k - starts[part]), LANES * (k - starts[part] + 1))
        for g in range(groups):
            half = slice(ROWS * g, ROWS * (g + 1))
            out_ref[half, at] = partial_refs[part][half, place] + totals[g]


VMEM_SPEC = pl.BlockSpec(memory_space=pltpu.VMEM)
ANY_SPEC = pl.BlockSpec(memory_space=pl.ANY)
HBM_SPEC = pl.BlockSpec(memory_space=pltpu.HBM)


def call(kernel, outs, specs, scratch=(), cost=0, hbm_outs=0):
    estimate = None
    if cost:
        estimate = pl.CostEstimate(flops=0, bytes_accessed=cost, transcendentals=0)
    outs = [
        out if isinstance(out, jax.ShapeDtypeStruct) else jax.ShapeDtypeStruct(out, jnp.float32)
        for out in outs
    ]
    out_specs = [VMEM_SPEC] * len(outs)
    out_specs[:hbm_outs] = [HBM_SPEC] * hbm_outs
    return pl.pallas_call(
        kernel,
        out_shape=outs,
        in_specs=specs,
        out_specs=out_specs,
        scratch_shapes=list(scratch),
        cost_estimate=estimate,
        compiler_params=pltpu.CompilerParams(vmem_limit_bytes=32 * 2**20),
        name=getattr(kernel, "func", kernel).__name__,
    )


def body(
    air_state,
    air_wind,
    jacobian,
    land_area,
    xgrid_rows,
    tracers,
    edge_coef,
    neighbours,
    vert_rate,
    ocean_area,
    send_list,
    xgrid_cols,
    xgrid_weights,
):
    field_count, levels, x_points, y_points = air_state.shape
    assert (x_points, y_points) == (2 * ROWS, LANES), air_state.shape
    assert xgrid_rows.shape[2] == send_list.shape[1] // 2 == LANES, xgrid_rows.shape
    planes = field_count * levels
    ocean_levels, cells = tracers.shape[1:]
    ocean_planes = tracers.shape[0] * ocean_levels
    faces, blocks = lax.axis_size("face"), lax.axis_size("blk")
    air = air_state.reshape(planes * x_points, y_points)
    wind = air_wind.reshape(2 * levels * x_points, y_points)
    ocean = tracers.reshape(ocean_planes, cells)
    point_ids, cell_ids, weights = xgrid_rows[0], xgrid_cols[0], xgrid_weights[0]
    rate = vert_rate.reshape(cells // LANES, LANES)
    area = ocean_area.reshape(cells // LANES, LANES)
    first_inputs = (
        cell_ids,
        weights,
        ocean,
        point_ids,
        jacobian,
        land_area,
        wind,
        air,
        send_list,
    )
    kept = (cell_ids, weights, point_ids, send_list)
    slab, moved, to_before, to_after, cell_ids, weights, point_ids, send_list = call(
        functools.partial(start_kernel, planes),
        [(blocks, HEAD, LANES), air.shape]
        + [(SIDE_IDS + blocks, LANES)] * 2
        + [jax.ShapeDtypeStruct(array.shape, array.dtype) for array in kept],
        [HBM_SPEC] * len(first_inputs),
        [
            pltpu.VMEM(shape, jnp.float32)
            for shape in (
                (blocks, HEAD, LANES),
                (ROWS, cells),
                jacobian.shape,
                land_area.shape,
                wind.shape,
                air.shape,
            )
        ]
        + [pltpu.SemaphoreType.DMA((len(first_inputs) + 1,))],
        hbm_outs=1,
    )(*(pltpu.with_memory_space_constraint(array, pltpu.HBM) for array in first_inputs))
    recv = lax.all_to_all(slab, "blk", split_axis=0, concat_axis=0, tiled=True)

    chunks = cells // LANES
    reads_per_chunk = edge_coef.shape[0] * chunks * (ocean_planes // ROWS)
    starts = (0, chunks * 6 // 16, chunks * 14 // 16)

    def ocean_part(start, end, after):
        (result,) = call(
            functools.partial(ocean_kernel, ocean_levels, start),
            [(ocean_planes, (end - start) * LANES)],
            [VMEM_SPEC] * 4 + [ANY_SPEC],
            [pltpu.VMEM((chunks * ocean_planes, 2 * LANES), jnp.bfloat16)],
            cost=(end - start) * reads_per_chunk * ROWS * LANES * 2,
        )(ocean, edge_coef, neighbours, rate, after)
        return result

    to_before, to_after = call(
        send_kernel,
        [(SIDE_IDS + blocks + ocean_planes, LANES)] * 2,
        [VMEM_SPEC] * 4,
        cost=reads_per_chunk * ROWS * LANES,
    )(ocean, send_list, to_before, to_after)
    onward = [(i, (i + 1) % blocks) for i in range(blocks)]
    before = lax.ppermute(to_after, "blk", onward)
    after = lax.ppermute(to_before, "blk", [(to, source) for source, to in onward])
    first_part = ocean_part(starts[0], starts[1], to_before)
    side_rows = 2 * planes + 2 * levels + SURF_ARRAYS + 2
    avg, down, up, surf = call(
        functools.partial(panel_kernel, planes),
        [air.shape, (side_rows, LANES), (side_rows, LANES), (2 * x_points * SURF_ARRAYS, LANES)],
        [VMEM_SPEC] * 9 + [ANY_SPEC],
    )(
        moved,
        recv,
        before,
        after,
        air,
        wind,
        jacobian,
        land_area,
        point_ids,
        first_part,
    )
    after_me = [(i, (i + 1) % faces) for i in range(faces)]
    low = lax.ppermute(up, "face", after_me)
    high = lax.ppermute(down, "face", [(to, source) for source, to in after_me])
    inner, packs = call(
        functools.partial(inner_kernel, planes),
        [((x_points - 2 * GLL) * planes, LANES), (2 * ROWS, LANES)],
        [VMEM_SPEC] * 6,
        cost=2 * air.size * 4,
    )(avg, moved, before, after, surf, wind)
    second_part = ocean_part(starts[1], starts[2], surf)

    slab, outer, final, inverse, edges = call(
        functools.partial(second_kernel, planes),
        [
            (blocks, HEAD, LANES),
            (len(outer_rows(x_points)) * planes, LANES),
            (x_points, y_points),
            (x_points, y_points),
            (2 * ROWS, LANES),
        ],
        [VMEM_SPEC] * 8 + [ANY_SPEC],
        [pltpu.VMEM((blocks, HEAD, LANES), jnp.float32), pltpu.SemaphoreType.DMA(())],
        hbm_outs=1,
    )(avg, inner, packs, surf, low, high, wind, point_ids, second_part)
    arrived = lax.all_to_all(slab, "blk", split_axis=0, concat_axis=0, tiled=True)
    last, hot, to_before, to_after = call(
        functools.partial(last_kernel, planes),
        [air.shape, jax.ShapeDtypeStruct((LANES, blocks * LANES), jnp.bfloat16)]
        + [(ROWS, LANES)] * 2,
        [VMEM_SPEC] * 5,
        cost=2 * air.size * 4,
    )(inner, outer, inverse, edges, cell_ids)
    edge_before = lax.ppermute(to_after, "blk", onward)
    edge_after = lax.ppermute(to_before, "blk", [(to, source) for source, to in onward])
    third_part = ocean_part(starts[2], chunks, to_before)
    partial, gain = call(
        functools.partial(rim_kernel, starts),
        [ocean.shape, area.shape],
        [VMEM_SPEC] * 5 + [ANY_SPEC] + [VMEM_SPEC] * len(starts),
        cost=chunks * reads_per_chunk // 8 * ROWS * LANES * 4,
    )(
        before,
        after,
        edge_coef,
        neighbours,
        area,
        to_before,
        first_part,
        second_part,
        third_part,
    )
    air_final, ocean_final = call(
        functools.partial(end_kernel, planes),
        [air.shape, ocean.shape],
        [VMEM_SPEC] * 11,
        [
            pltpu.VMEM(air.shape, jnp.float32),
            pltpu.VMEM((ROWS, cells), jnp.float32),
            pltpu.SemaphoreType.DMA((2 + planes // ROWS,)),
        ],
        hbm_outs=2,
    )(
        last,
        edge_before,
        edge_after,
        arrived,
        final,
        inverse,
        cell_ids,
        hot,
        weights,
        gain,
        partial,
    )
    return air_final.reshape(air_state.shape), ocean_final.reshape(tracers.shape)


def solution(mesh):
    return jax.shard_map(
        body,
        mesh=mesh,
        in_specs=(
            P(None, None, "face", "blk"),
            P(None, None, "face", "blk"),
            P("face", "blk"),
            P("face", "blk"),
            P(("face", "blk"), None, None),
            P(None, None, ("face", "blk")),
            P(None, ("face", "blk")),
            P(None, ("face", "blk")),
            P(("face", "blk")),
            P(("face", "blk")),
            P(("face", "blk"), None),
            P(("face", "blk"), None, None),
            P(("face", "blk"), None, None),
        ),
        out_specs=(P(None, None, "face", "blk"), P(None, None, ("face", "blk"))),
        check_vma=False,
    )
```

```python
import functools

import jax
import jax.numpy as jnp
from jax import lax
from jax.experimental import pallas as pl
from jax.experimental.pallas import tpu as pltpu
from jax.sharding import PartitionSpec as P

GLL = 4
ROWS = 8
LANES = 128

deriv_table = [
    [-3.0, 4.045084971874737, -1.545084971874737, 0.5],
    [-0.8090169943749475, 0.0, 1.118033988749895, -0.30901699437494745],
    [0.30901699437494745, -1.118033988749895, 0.0, 0.8090169943749475],
    [-0.5, 1.545084971874737, -4.045084971874737, 3.0],
]
time_step = 0.05
relax_rate = 0.3
flux_gain = 0.2

HEAD = 8
SIDE_EDGE, SIDE_STRIP, SIDE_IDS = 0, 8, 16
AVG, MASS_SUM, MASS, COEF_X, COEF_Y, SURF = range(6)
SURF_ARRAYS = 6


def iota(shape, dim):
    return lax.broadcasted_iota(jnp.int32, shape, dim)


def take(values, index, axis):
    return jnp.take_along_axis(values, index, axis=axis, mode="promise_in_bounds")


def by_position(pos, values):
    result = jnp.full(pos.shape, values[-1], jnp.float32)
    for i, value in enumerate(values[:-1]):
        result = jnp.where(pos == i, value, result)
    return result


def spread(row):
    return jnp.broadcast_to(row, (ROWS, LANES))


class Geometry:
    def __init__(self):
        shape = (ROWS, LANES)
        self.row, self.lane = iota(shape, 0), iota(shape, 1)
        x_pos, y_pos = self.row & (GLL - 1), self.lane & (GLL - 1)
        self.y_from = [self.lane - y_pos + j for j in range(GLL)]
        columns = [[line[j] for line in deriv_table] for j in range(GLL)]
        self.x_coef = {
            step: by_position(
                x_pos,
                [
                    deriv_table[i][i + step] if 0 <= i + step < GLL else 0.0
                    for i in range(GLL)
                ],
            )
            for step in range(1 - GLL, GLL)
        }
        self.y_coef = [by_position(y_pos, column) for column in columns]
        self.y_swap = (
            self.lane + jnp.where(y_pos == GLL - 1, 1, 0) - jnp.where(y_pos == 0, 1, 0)
        ) & (LANES - 1)
        self.x_edge = (x_pos == 0) | (x_pos == GLL - 1)
        self.y_edge = (y_pos == 0) | (y_pos == GLL - 1)
        self.first_row, self.last_row = self.row == 0, self.row == ROWS - 1
        self.middle_row = self.row == GLL
        self.outer_lane = (self.lane == 0) | (self.lane == LANES - 1)
        self.weight = jnp.where(self.x_edge, 1.0 / 6.0, 5.0 / 6.0) * jnp.where(
            self.y_edge, 1.0 / 6.0, 5.0 / 6.0
        )

    def d_x(self, tile):
        return sum(
            coef * (pltpu.roll(tile, -step % ROWS, 0) if step else tile)
            for step, coef in self.x_coef.items()
        )

    def d_y(self, *tiles):
        totals = [0.0] * len(tiles)
        for j in range(GLL):
            for i, tile in enumerate(tiles):
                totals[i] += self.y_coef[j] * take(tile, self.y_from[j], 1)
        return totals

    def sum_x(self, low, high, before, after):
        low_down, low_up = pltpu.roll(low, 1, 0), pltpu.roll(low, ROWS - 1, 0)
        high_down, high_up = pltpu.roll(high, 1, 0), pltpu.roll(high, ROWS - 1, 0)
        low_other = jnp.where(
            self.first_row,
            before,
            jnp.where(
                self.middle_row, low_down, jnp.where(self.last_row, high_up, low_up)
            ),
        )
        high_other = jnp.where(
            self.first_row,
            low_down,
            jnp.where(
                self.middle_row, high_down, jnp.where(self.last_row, after, high_up)
            ),
        )
        return (
            low + jnp.where(self.x_edge, low_other, 0.0),
            high + jnp.where(self.x_edge, high_other, 0.0),
        )

    def sum_y(self, tile, outer):
        other = jnp.where(self.outer_lane, outer, take(tile, self.y_swap, 1))
        return tile + jnp.where(self.y_edge, other, 0.0)

    def sum_y_pair(self, own, strip):
        own_swap, strip_swap = take(own, self.y_swap, 1), take(strip, self.y_swap, 1)
        own_other = jnp.where(self.outer_lane, strip_swap, own_swap)
        strip_other = jnp.where(self.outer_lane, own_swap, strip_swap)
        return (
            own + jnp.where(self.y_edge, own_other, 0.0),
            strip + jnp.where(self.y_edge, strip_other, 0.0),
        )


def edge_place(x, group):
    return x // ROWS, LANES // 2 * (x % 2) + ROWS * group + 2 * (x % ROWS // 2)


def edges_of(geo, packs, ref, planes, lines, first=None):
    packs = list(packs)
    for number, x in enumerate(lines):
        base = planes * (number if first is None else x - first)
        for group in range(planes // ROWS):
            q, at = edge_place(x, group)
            tile = ref[base + ROWS * group : base + ROWS * (group + 1), :]
            rolled = pltpu.roll(tile, (at + 1) % LANES, 1)
            packs[q] = jnp.where((geo.lane >> 1) == at // 2, rolled, packs[q])
    return packs


def outer_edges(joined, x, group):
    q, at = edge_place(x, group)
    return pltpu.roll(joined[q], (-(at + 1)) % LANES, 1)


def split_sides(geo, first, second, unit):
    odd = (geo.lane & unit) != 0
    return (
        jnp.where(odd, pltpu.roll(second, unit, 1), first),
        jnp.where(odd, second, pltpu.roll(first, LANES - unit, 1)),
    )


def join_sides(geo, before, after, unit):
    odd = (geo.lane & unit) != 0
    return (
        jnp.where(odd, pltpu.roll(after, unit, 1), before),
        jnp.where(odd, after, pltpu.roll(before, LANES - unit, 1)),
    )


def join_edges(geo, before, after):
    odd = (geo.lane & 1) != 0
    return (
        jnp.where(odd, pltpu.roll(before, 1, 1), after),
        jnp.where(odd, before, pltpu.roll(after, LANES - 1, 1)),
    )


def neighbours_of(blocks):
    here = lax.axis_index("blk")
    return lax.rem(here + blocks - 1, blocks), lax.rem(here + 1, blocks)


def one_hot(index, allowed=None):
    low = index & (LANES - 1)
    lane_at = iota((LANES, LANES), 0)
    if allowed is not None:
        lane_at = jnp.where(allowed(lane_at), lane_at, -1)
    return jnp.concatenate(
        [
            jnp.where(lane_at == low[c : c + 1], 1.0, 0.0).astype(jnp.bfloat16)
            for c in range(index.shape[0])
        ],
        axis=1,
    )


def scatter_sum(lines, index, bins, lanes_hot):
    split = []
    for values in lines:
        for part in range(3):
            short = values.astype(jnp.bfloat16).astype(jnp.float32)
            split.append(short)
            values = values - short
    high = index >> 7
    bin_at = iota((bins, LANES), 0)
    left = []
    for c in range(index.shape[0]):
        hit = bin_at == high[c : c + 1]
        left.append(
            jnp.concatenate(
                [jnp.where(hit, part[c : c + 1], 0.0) for part in split], axis=0
            ).astype(jnp.bfloat16)
        )
    total = lax.dot_general(
        jnp.concatenate(left, axis=1),
        lanes_hot,
        (((1,), (1,)), ((), ())),
        preferred_element_type=jnp.float32,
    )
    sums = []
    for i in range(len(lines)):
        part = total[3 * i * bins : 3 * (i + 1) * bins]
        sums.append(part[:bins] + part[bins : 2 * bins] + part[2 * bins :])
    return sums


def wind_tiles(wind_ref, x_points, level, lines):
    levels = wind_ref.shape[0] // (2 * x_points)
    return [
        [
            time_step
            * wind_ref[
                pl.ds((levels * part + level) * x_points + x, ROWS, stride=x_points), :
            ]
            for x in lines
        ]
        for part in range(2)
    ]


def start_kernel(
    planes,
    cols_in,
    weights_in,
    tracers_in,
    rows_in,
    jac_in,
    land_in,
    wind_in,
    air_in,
    send_in,
    slab_out,
    moved_ref,
    before_ref,
    after_ref,
    cols_ref,
    weights_ref,
    rows_ref,
    send_ref,
    slab_ref,
    tracers_ref,
    jac_ref,
    land_ref,
    wind_ref,
    air_ref,
    semaphores,
):
    pairs = []
    for source, target in ((wind_in, wind_ref), (air_in, air_ref)):
        middle = target.shape[0] // 2
        for part in (slice(0, middle), slice(middle, target.shape[0])):
            pairs.append((source.at[part], target.at[part]))
    large = len(pairs)
    pairs += [
        (cols_in, cols_ref),
        (tracers_in.at[:ROWS], tracers_ref),
        (weights_in, weights_ref),
        (rows_in, rows_ref),
        (jac_in, jac_ref),
        (land_in, land_ref),
        (send_in, send_ref),
    ]
    copies = [
        pltpu.make_async_copy(source, target, semaphores.at[i])
        for i, (source, target) in enumerate(pairs)
    ]
    for copy in copies:
        copy.start()
    geo = Geometry()
    blocks = cols_ref.shape[0]
    x_points = jac_ref.shape[0]
    levels = wind_ref.shape[0] // (2 * x_points)
    chunks = tracers_ref.shape[1] // LANES
    for copy in copies[large : large + 4]:
        copy.wait()

    for group in range(blocks // ROWS):
        at = slice(ROWS * group, ROWS * (group + 1))
        cells = cols_ref[at, :]
        high, low = cells >> 7, cells & (LANES - 1)
        surface = jnp.zeros((ROWS, LANES), jnp.float32)
        for k in range(chunks):
            line = spread(tracers_ref[0:1, LANES * k : LANES * (k + 1)])
            surface = jnp.where(high == k, take(line, low, 1), surface)
        area = weights_ref[at, :]
        heat = area * surface
        for c in range(ROWS):
            owner = ROWS * group + c
            for place, step in enumerate((1, 0, -1)):
                to = (owner + step) % blocks
                slab_ref[to, 2 * place : 2 * place + 1, :] = heat[c : c + 1]
                slab_ref[to, 2 * place + 1 : 2 * place + 2, :] = area[c : c + 1]

    out = pltpu.make_async_copy(slab_ref, slab_out, semaphores.at[len(copies)])
    out.start()
    ids = rows_ref[...].astype(jnp.float32)
    for side_ref in (before_ref, after_ref):
        side_ref[SIDE_IDS : SIDE_IDS + blocks, :] = ids

    for copy in copies[:large] + copies[large + 4 :]:
        copy.wait()
    strips = []
    for h in range(2):
        half = slice(ROWS * h, ROWS * (h + 1))
        second = levels * x_points
        pack = jnp.zeros((ROWS, LANES), jnp.float32)
        for i, strip in enumerate(
            (
                air_ref[half, :],
                wind_ref[half, :],
                wind_ref[second + ROWS * h : second + ROWS * (h + 1), :],
                jac_ref[half, :],
                land_ref[half, :],
            )
        ):
            pack = jnp.where(
                (geo.lane >> 4) == i, pltpu.roll(strip, 16 * i + 8, 1), pack
            )
        strips.append(pack)
    to_right, to_left = split_sides(geo, strips[0], strips[1], ROWS)
    after_ref[SIDE_STRIP : SIDE_STRIP + ROWS, :] = to_right
    before_ref[SIDE_STRIP : SIDE_STRIP + ROWS, :] = to_left

    y_weight = jnp.where(geo.y_edge, 1.0 / 6.0, 5.0 / 6.0)
    for element in range(x_points // GLL):
        lines = [GLL * element + i for i in range(GLL)]
        mass = [
            (1.0 / 6.0 if i in (0, GLL - 1) else 5.0 / 6.0)
            * y_weight
            * spread(jac_ref[x : x + 1, :])
            for i, x in enumerate(lines)
        ]
        for level in range(0, levels, ROWS):
            wind = wind_tiles(wind_ref, x_points, level, lines)
            for plane in range(level, planes, levels):
                fields = [
                    air_ref[pl.ds(plane * x_points + x, ROWS, stride=x_points), :]
                    for x in lines
                ]
                slopes = geo.d_y(*fields)
                for i, x in enumerate(lines):
                    slope = sum(deriv_table[i][j] * fields[j] for j in range(GLL))
                    moved = mass[i] * (
                        fields[i] - (wind[0][i] * slope + wind[1][i] * slopes[i])
                    )
                    moved_ref[planes * x + plane : planes * x + plane + ROWS, :] = moved
    packs = [jnp.zeros((ROWS, LANES), jnp.float32) for _ in range(2)]
    packs = edges_of(geo, packs, moved_ref, planes, range(x_points))
    to_right, to_left = split_sides(geo, packs[0], packs[1], 1)
    after_ref[SIDE_EDGE : SIDE_EDGE + ROWS, :] = to_right
    before_ref[SIDE_EDGE : SIDE_EDGE + ROWS, :] = to_left
    out.wait()


def panel_kernel(
    planes,
    moved_ref,
    recv_ref,
    before_ref,
    after_ref,
    air_ref,
    wind_ref,
    jac_ref,
    land_ref,
    rows_ref,
    ocean_ref,
    avg_ref,
    down_ref,
    up_ref,
    surf_ref,
):
    geo = Geometry()
    blocks = rows_ref.shape[0]
    x_points = jac_ref.shape[0]
    levels = wind_ref.shape[0] // (2 * x_points)

    own_ids = rows_ref[...]
    left_ids = before_ref[SIDE_IDS : SIDE_IDS + blocks, :].astype(jnp.int32)
    right_ids = after_ref[SIDE_IDS : SIDE_IDS + blocks, :].astype(jnp.int32)
    head = [
        jnp.concatenate([recv_ref[c, i : i + 1, :] for c in range(blocks)], axis=0)
        for i in range(6)
    ]
    heat, frac = scatter_sum(head[2:4], own_ids, x_points, one_hot(own_ids))
    from_left = scatter_sum(
        head[0:2], left_ids, x_points, one_hot(left_ids, lambda lane: lane >= LANES - ROWS)
    )
    from_right = scatter_sum(
        head[4:6], right_ids, x_points, one_hot(right_ids, lambda lane: lane < ROWS)
    )
    strip_heat = from_left[0] + from_right[0]
    strip_frac = from_left[1] + from_right[1]

    in_strip = (geo.lane < ROWS) | (geo.lane >= LANES - ROWS)
    packs = join_sides(
        geo,
        before_ref[SIDE_STRIP : SIDE_STRIP + ROWS, :],
        after_ref[SIDE_STRIP : SIDE_STRIP + ROWS, :],
        ROWS,
    )
    own, strip = [], []
    for h, pack in enumerate(packs):
        half = slice(ROWS * h, ROWS * (h + 1))
        strip.append(
            [
                jnp.where(
                    in_strip, pltpu.roll(pack, (-(16 * i + 8)) % LANES, 1), 1.0
                )
                for i in range(5)
            ]
        )
        own.append(
            [
                air_ref[half, :],
                wind_ref[half, :],
                wind_ref[
                    levels * x_points + ROWS * h : levels * x_points + ROWS * (h + 1), :
                ],
                jac_ref[half, :],
                land_ref[half, :],
            ]
        )
    for h in range(2):
        half = slice(ROWS * h, ROWS * (h + 1))
        pair = []
        for tile, ((field, wind_x, wind_y, jac, land), tile_heat, tile_frac) in enumerate(
            ((own[h], heat[half], frac[half]), (strip[h], strip_heat[half], strip_frac[half]))
        ):
            mass = geo.weight * jac
            if tile == 1:
                tile_heat = jnp.where(in_strip, tile_heat, 0.0)
                tile_frac = jnp.where(in_strip, tile_frac, 0.0)
            surf = (tile_heat + land * field) / (tile_frac + land)
            coef_x, coef_y = time_step * mass * wind_x, time_step * mass * wind_y
            moved = (
                mass * (field + relax_rate * (surf - field))
                - coef_x * geo.d_x(field)
                - coef_y * geo.d_y(field)[0]
            )
            pair.append((moved, mass))
            at = x_points * tile + ROWS * h
            for number, value in (
                (MASS, mass),
                (COEF_X, coef_x),
                (COEF_Y, coef_y),
                (SURF, surf),
            ):
                surf_ref[2 * x_points * number + at : 2 * x_points * number + at + ROWS, :] = value
        for number, i in ((AVG, 0), (MASS_SUM, 1)):
            for tile, value in enumerate(geo.sum_y_pair(pair[0][i], pair[1][i])):
                at = 2 * x_points * number + x_points * tile + ROWS * h
                surf_ref[at : at + ROWS, :] = value

    joined = join_edges(
        geo,
        before_ref[SIDE_EDGE : SIDE_EDGE + ROWS, :],
        after_ref[SIDE_EDGE : SIDE_EDGE + ROWS, :],
    )
    for x in outer_rows(x_points):
        for group in range(planes // ROWS):
            at = slice(planes * x + ROWS * group, planes * x + ROWS * (group + 1))
            avg_ref[at, :] = geo.sum_y(moved_ref[at, :], outer_edges(joined, x, group))

    def line(r):
        return avg_ref[planes * r : planes * (r + 1), :]

    def surf_line(number, r):
        return surf_ref[pl.ds(2 * x_points * number + r, 2, stride=x_points), :]

    def first_step(get, mass_at):
        top = x_points - 1
        return (
            [
                get(1) / mass_at(1),
                get(2) / mass_at(2),
                (get(3) + get(GLL)) / (mass_at(3) + mass_at(GLL)),
            ],
            [
                (get(top - 4) + get(top - 3)) / (mass_at(top - 4) + mass_at(top - 3)),
                get(top - 2) / mass_at(top - 2),
                get(top - 1) / mass_at(top - 1),
            ],
        )

    def own_mass_sum(r):
        return surf_ref[2 * x_points * MASS_SUM + r : 2 * x_points * MASS_SUM + r + 1, :]

    low_lines, high_lines = first_step(line, own_mass_sum)
    surf_low, surf_high = first_step(
        functools.partial(surf_line, AVG), functools.partial(surf_line, MASS_SUM)
    )
    for out_ref, r, lines, surf_lines, coefs in (
        (down_ref, 0, low_lines, surf_low, deriv_table[0][1:]),
        (up_ref, x_points - 1, high_lines, surf_high, deriv_table[3][:3]),
    ):
        slope = sum(coef * value for coef, value in zip(coefs, lines))
        surf_slope = sum(coef * value for coef, value in zip(coefs, surf_lines))
        mass = surf_ref[2 * x_points * MASS + r : 2 * x_points * MASS + r + 1, :]
        wind = time_step * mass * wind_ref[pl.ds(r, 2 * levels, stride=x_points), :]
        out_ref[0:planes, :] = line(r)
        for first in range(0, planes, levels):
            out_ref[planes + first : planes + first + levels, :] = (
                wind[:levels] * slope[first : first + levels]
            )
        base = 2 * planes
        out_ref[base : base + 2 * levels, :] = wind
        base += 2 * levels
        pairs = [surf_line(number, r) for number in range(SURF_ARRAYS)]
        pairs.append(surf_line(COEF_X, r) * surf_slope)
        pack = jnp.zeros((ROWS, LANES), jnp.float32)
        for i, pair in enumerate(pairs):
            out_ref[base + i : base + i + 1, :] = pair[:1]
            pack = jnp.where(
                (geo.lane >> 4) == i, pltpu.roll(spread(pair[1:]), 16 * i + 8, 1), pack
            )
        base += len(pairs)
        out_ref[base : base + 1, :] = pack[:1]


def outer_rows(x_points):
    return [x for x in range(x_points) if x <= GLL or x >= x_points - GLL - 1]


def advance(geo, fields, wind, mass):
    slopes = geo.d_y(*fields)
    moved = []
    for i in range(GLL):
        slope = sum(deriv_table[i][j] * fields[j] for j in range(GLL))
        moved.append(mass[i] * (fields[i] - (wind[0][i] * slope + wind[1][i] * slopes[i])))
    return moved, slopes


def inner_kernel(
    planes, avg_ref, moved_ref, before_ref, after_ref, surf_ref, wind_ref, out_ref, packs_ref
):
    geo = Geometry()
    x_points = avg_ref.shape[0] // planes
    levels = wind_ref.shape[0] // (2 * x_points)
    joined = join_edges(
        geo,
        before_ref[SIDE_EDGE : SIDE_EDGE + ROWS, :],
        after_ref[SIDE_EDGE : SIDE_EDGE + ROWS, :],
    )
    outer = outer_rows(x_points)

    def average(x, plane):
        at = slice(planes * x + plane, planes * x + plane + ROWS)
        if x in outer:
            return avg_ref[at, :]
        return geo.sum_y(moved_ref[at, :], outer_edges(joined, x, plane // ROWS))

    def surf_row(number, x):
        at = 2 * x_points * number + x
        return spread(surf_ref[at : at + 1, :])

    def put(x, plane, value):
        at = planes * (x - GLL) + plane
        out_ref[at : at + ROWS, :] = value

    held = {}
    carried = {}
    for element in range(1, x_points // GLL - 1):
        lines = [GLL * element + i for i in range(GLL)]
        totals = [surf_row(MASS_SUM, x) for x in lines]
        totals[0] = totals[0] + surf_row(MASS_SUM, lines[0] - 1)
        totals[-1] = totals[-1] + surf_row(MASS_SUM, lines[-1] + 1)
        scale = [1.0 / total for total in totals]
        mass = [surf_row(MASS, x) for x in lines]
        for level in range(0, levels, ROWS):
            wind = wind_tiles(wind_ref, x_points, level, lines)
            for plane in range(level, planes, levels):
                if element == 1:
                    first = average(lines[0], plane) + average(lines[0] - 1, plane)
                else:
                    first = carried[plane]
                last = average(lines[-1], plane) + average(lines[-1] + 1, plane)
                carried[plane] = last
                totals = (
                    [first] + [average(x, plane) for x in lines[1:-1]] + [last]
                )
                fields = [total * factor for total, factor in zip(totals, scale)]
                moved, _ = advance(geo, fields, wind, mass)
                if element == 1:
                    put(lines[0], plane, moved[0])
                else:
                    shared = held[plane] + moved[0]
                    put(lines[0] - 1, plane, shared)
                    put(lines[0], plane, shared)
                for i in range(1, GLL - 1):
                    put(lines[i], plane, moved[i])
                held[plane] = moved[-1]
                if lines[-1] == x_points - GLL - 1:
                    put(lines[-1], plane, moved[-1])
    packs = [jnp.zeros((ROWS, LANES), jnp.float32) for _ in range(2)]
    inner = [x for x in range(x_points) if x not in outer]
    for q, pack in enumerate(edges_of(geo, packs, out_ref, planes, inner, GLL)):
        packs_ref[ROWS * q : ROWS * (q + 1), :] = pack


def second_kernel(
    planes,
    avg_ref,
    inner_ref,
    packs_ref,
    surf_ref,
    low_ref,
    high_ref,
    wind_ref,
    rows_ref,
    ocean_ref,
    slab_out,
    sums_ref,
    final_ref,
    inverse_ref,
    edges_ref,
    flux_ref,
    semaphore,
):
    geo = Geometry()
    blocks = rows_ref.shape[0]
    x_points = final_ref.shape[0]
    levels = wind_ref.shape[0] // (2 * x_points)
    base = low_ref.shape[0] - SURF_ARRAYS - 2

    def surf_tile(number, tile, h):
        at = 2 * x_points * number + x_points * tile + ROWS * h
        return surf_ref[at : at + ROWS, :]

    in_strip = (geo.lane < ROWS) | (geo.lane >= LANES - ROWS)

    def beside(ref, number, tile):
        if tile == 0:
            return spread(ref[base + number : base + number + 1, :])
        at = base + SURF_ARRAYS + 1
        strips = spread(ref[at : at + 1, :])
        return jnp.where(
            in_strip, pltpu.roll(strips, (-(16 * number + 8)) % LANES, 1), 1.0
        )

    ends = []
    inverse = []
    for tile in range(2):
        total = geo.sum_x(
            surf_tile(MASS_SUM, tile, 0),
            surf_tile(MASS_SUM, tile, 1),
            beside(low_ref, MASS_SUM, tile),
            beside(high_ref, MASS_SUM, tile),
        )
        inverse.append([1.0 / value for value in total])
        summed = geo.sum_x(
            surf_tile(AVG, tile, 0),
            surf_tile(AVG, tile, 1),
            beside(low_ref, AVG, tile),
            beside(high_ref, AVG, tile),
        )
        fields = [value * scale for value, scale in zip(summed, inverse[tile])]
        moved = []
        for h in range(2):
            field = fields[h]
            moved.append(
                surf_tile(MASS, tile, h)
                * (field + relax_rate * (surf_tile(SURF, tile, h) - field))
                - surf_tile(COEF_X, tile, h) * geo.d_x(field)
                - surf_tile(COEF_Y, tile, h) * geo.d_y(field)[0]
            )
        halos = []
        for ref, field, own_coef in (
            (low_ref, spread(fields[0][:1]), deriv_table[3][3]),
            (high_ref, spread(fields[1][ROWS - 1 :]), deriv_table[0][0]),
        ):
            halos.append(
                beside(ref, MASS, tile)
                * (field + relax_rate * (beside(ref, SURF, tile) - field))
                - beside(ref, SURF_ARRAYS, tile)
                - beside(ref, COEF_X, tile) * (own_coef * field)
                - beside(ref, COEF_Y, tile) * geo.d_y(field)[0]
            )
        ends.append(geo.sum_x(moved[0], moved[1], halos[0], halos[1]))
    final = []
    for h in range(2):
        summed, _ = geo.sum_y_pair(ends[0][h], ends[1][h])
        final.append(summed * inverse[0][h])
        final_ref[ROWS * h : ROWS * (h + 1), :] = final[h]
        inverse_ref[ROWS * h : ROWS * (h + 1), :] = inverse[0][h]
    flux = [final[h] - surf_tile(SURF, 0, h) for h in range(2)]
    for group in range(blocks // ROWS):
        ids = rows_ref[ROWS * group : ROWS * (group + 1), :]
        high, low = ids >> 7, ids & (LANES - 1)
        picked = jnp.zeros((ROWS, LANES), jnp.float32)
        for x in range(x_points):
            line = spread(flux[x // ROWS][x % ROWS : x % ROWS + 1])
            picked = jnp.where(high == x, take(line, low, 1), picked)
        for c in range(ROWS):
            flux_ref[ROWS * group + c, 0:1, :] = picked[c : c + 1]

    out = pltpu.make_async_copy(flux_ref, slab_out, semaphore)
    out.start()

    kept = outer_rows(x_points)

    def put(x, plane, value):
        at = planes * kept.index(x) + plane
        sums_ref[at : at + ROWS, :] = value

    def beyond(ref, plane, field, slope, own_coef):
        wind_at = 2 * planes + plane % levels
        return (
            beside(ref, MASS, 0) * field
            - ref[planes + plane : planes + plane + ROWS, :]
            - ref[wind_at : wind_at + ROWS, :] * (own_coef * field)
            - ref[wind_at + levels : wind_at + levels + ROWS, :] * slope
        )

    def row_of(tiles, x):
        return spread(tiles[x // ROWS][x % ROWS : x % ROWS + 1])

    masses = [surf_tile(MASS, 0, h) for h in range(2)]
    last_element = x_points // GLL - 1
    for element in (0, last_element):
        lines = [GLL * element + i for i in range(GLL)]
        scale = [row_of(inverse[0], x) for x in lines]
        mass = [row_of(masses, x) for x in lines]
        for level in range(0, levels, ROWS):
            wind = wind_tiles(wind_ref, x_points, level, lines)
            for plane in range(level, planes, levels):
                here = slice(plane, plane + ROWS)
                fields = []
                for i, x in enumerate(lines):
                    total = avg_ref[planes * x + plane : planes * x + plane + ROWS, :]
                    other = x - 1 if i == 0 else x + 1
                    if other < 0:
                        total = total + low_ref[here, :]
                    elif other == x_points:
                        total = total + high_ref[here, :]
                    elif i in (0, GLL - 1):
                        at = planes * other + plane
                        total = total + avg_ref[at : at + ROWS, :]
                    fields.append(total * scale[i])
                moved, slopes = advance(geo, fields, wind, mass)
                if element == 0:
                    before = beyond(low_ref, plane, fields[0], slopes[0], deriv_table[3][3])
                    put(lines[0], plane, before + moved[0])
                    shared = moved[-1] + inner_ref[here, :]
                    put(lines[-1], plane, shared)
                    put(lines[-1] + 1, plane, shared)
                else:
                    at = inner_ref.shape[0] - planes + plane
                    shared = moved[0] + inner_ref[at : at + ROWS, :]
                    put(lines[0] - 1, plane, shared)
                    put(lines[0], plane, shared)
                    after = beyond(
                        high_ref, plane, fields[-1], slopes[-1], deriv_table[0][0]
                    )
                    put(lines[-1], plane, moved[-1] + after)
                for i in range(1, GLL - 1):
                    put(lines[i], plane, moved[i])
    packs = [packs_ref[:ROWS, :], packs_ref[ROWS:, :]]
    packs = edges_of(geo, packs, sums_ref, planes, kept)
    for q, pack in enumerate(packs):
        edges_ref[ROWS * q : ROWS * (q + 1), :] = pack
    out.wait()


def last_kernel(
    planes,
    inner_ref,
    outer_ref,
    inverse_ref,
    edges_ref,
    cols_ref,
    out_ref,
    hot_ref,
    before_ref,
    after_ref,
):
    geo = Geometry()
    x_points = inverse_ref.shape[0]
    kept = outer_rows(x_points)
    hot_ref[...] = one_hot(cols_ref[...])
    after_ref[...], before_ref[...] = split_sides(
        geo, edges_ref[:ROWS, :], edges_ref[ROWS:, :], 1
    )
    for x in range(x_points):
        inverse = spread(inverse_ref[x : x + 1, :])
        ref, first = inner_ref, planes * (x - GLL)
        if x in kept:
            ref, first = outer_ref, planes * kept.index(x)
        for group in range(planes // ROWS):
            tile = ref[first + ROWS * group : first + ROWS * (group + 1), :]
            at = planes * x + ROWS * group
            out_ref[at : at + ROWS, :] = inverse * geo.sum_y(tile, 0.0)


def end_kernel(
    planes,
    last_ref,
    before_ref,
    after_ref,
    recv_ref,
    final_ref,
    inverse_ref,
    cols_ref,
    hot_ref,
    weights_ref,
    gain_ref,
    ocean_ref,
    air_out,
    ocean_out,
    air_ref,
    row_ref,
    semaphores,
):
    geo = Geometry()
    blocks = cols_ref.shape[0]
    chunks = gain_ref.shape[0]
    x_points = inverse_ref.shape[0]
    copies = []

    def send(source, target):
        copies.append(
            pltpu.make_async_copy(source, target, semaphores.at[len(copies)])
        )
        copies[-1].start()

    send(ocean_ref.at[ROWS:], ocean_out.at[ROWS:])
    joined = join_edges(geo, before_ref[...], after_ref[...])
    groups = planes // ROWS
    for group in range(groups):
        for x in range(x_points):
            at = planes * x + ROWS * group
            beside = spread(inverse_ref[x : x + 1, :]) * outer_edges(joined, x, group)
            air_ref[pl.ds(ROWS * group * x_points + x, ROWS, stride=x_points), :] = last_ref[
                at : at + ROWS, :
            ] + jnp.where(geo.outer_lane, beside, 0.0)
        if group == 0:
            air_ref[0:x_points, :] = final_ref[...]
        if group % 2:
            rows = slice(
                ROWS * (group - 1) * x_points, ROWS * (group + 1) * x_points
            )
            send(air_ref.at[rows], air_out.at[rows])
    if groups % 2:
        rows = slice(ROWS * (groups - 1) * x_points, planes * x_points)
        send(air_ref.at[rows], air_out.at[rows])

    arrived = jnp.concatenate([recv_ref[c, 0:1, :] for c in range(blocks)], axis=0)
    (inflow,) = scatter_sum(
        [weights_ref[...] * arrived], cols_ref[...], chunks, hot_ref[...]
    )
    gain = inflow * gain_ref[...]
    row_ref[...] = ocean_ref[:ROWS, :]
    for k in range(chunks):
        at = slice(LANES * k, LANES * (k + 1))
        row_ref[0:1, at] = ocean_ref[0:1, at] + gain[k : k + 1]
    send(row_ref, ocean_out.at[:ROWS])
    for copy in copies:
        copy.wait()


def gathered(ids, coefs, source, sources, groups, first=0):
    totals = [jnp.zeros((ROWS, LANES), jnp.float32) for _ in range(groups)]
    for edge in range(ids.shape[0]):
        cell = spread(ids[edge : edge + 1])
        coef = spread(coefs[edge : edge + 1])
        high, low = cell >> 7, cell & (LANES - 1)
        for s in range(sources):
            scaled = jnp.where(high == first + s, coef, 0.0)
            for group in range(groups):
                totals[group] += scaled * take(source(group, s), low, 1)
    return totals


def multiplied(ids, coefs, halves_ref, sources, groups):
    lane_at = iota((LANES, LANES), 0)
    hot = jnp.concatenate(
        [
            jnp.where(lane_at == (ids[edge : edge + 1] & (LANES - 1)), 1.0, 0.0).astype(
                jnp.bfloat16
            )
            for edge in range(2)
        ],
        axis=1,
    )
    picked = jnp.dot(
        halves_ref[...],
        jnp.concatenate([hot, hot], axis=0),
        preferred_element_type=jnp.float32,
    )
    totals = [jnp.zeros((ROWS, LANES), jnp.float32) for _ in range(groups)]
    for edge in range(2):
        high = spread(ids[edge : edge + 1]) >> 7
        coef = spread(coefs[edge : edge + 1])
        side = slice(LANES * edge, LANES * (edge + 1))
        for s in range(sources):
            scaled = jnp.where(high == s, coef, 0.0)
            for group in range(groups):
                at = ROWS * (groups * s + group)
                totals[group] += scaled * picked[at : at + ROWS, side]
    return totals


def ocean_kernel(
    levels, start, tracers_ref, coef_ref, near_ref, rate_ref, after_ref, out_ref, halves_ref
):
    chunks = tracers_ref.shape[1] // LANES
    groups = tracers_ref.shape[0] // ROWS
    row = iota((ROWS, LANES), 0)

    def source(group, s):
        return tracers_ref[
            ROWS * group : ROWS * (group + 1), LANES * s : LANES * (s + 1)
        ]

    planes = tracers_ref.shape[0]
    for s in range(chunks):
        values = tracers_ref[:, LANES * s : LANES * (s + 1)]
        upper = values.astype(jnp.bfloat16)
        at = slice(planes * s, planes * (s + 1))
        halves_ref[at, :LANES] = upper
        halves_ref[at, LANES:] = (values - upper.astype(jnp.float32)).astype(jnp.bfloat16)
    edges = near_ref.shape[0]

    def one_chunk(number, carry):
        k = number + start
        at = pl.ds(pl.multiple_of(k * LANES, LANES), LANES)
        out_at = pl.ds(pl.multiple_of(number * LANES, LANES), LANES)
        ids, coefs = near_ref[:, at], coef_ref[:, at]
        by_gather = edges - edges // 3 * 2
        totals = gathered(ids[:by_gather], coefs[:by_gather], source, chunks, groups)
        for edge in range(by_gather, edges, 2):
            more = multiplied(
                ids[edge : edge + 2], coefs[edge : edge + 2], halves_ref, chunks, groups
            )
            totals = [total + part for total, part in zip(totals, more)]
        coef_sum = spread(jnp.sum(coefs, axis=0, keepdims=True))
        rate = spread(rate_ref[pl.ds(k, 1), :])
        tiles = [tracers_ref[ROWS * g : ROWS * (g + 1), at] for g in range(groups)]
        for g in range(groups):
            tile = tiles[g]
            top = bottom = tile
            if (ROWS * g) % levels:
                top = pltpu.roll(tiles[g - 1], 1, 0)
            if (ROWS * (g + 1)) % levels:
                bottom = pltpu.roll(tiles[g + 1], ROWS - 1, 0)
            above = jnp.where(row == 0, top, pltpu.roll(tile, 1, 0))
            below = jnp.where(row == ROWS - 1, bottom, pltpu.roll(tile, ROWS - 1, 0))
            vertical = rate * ((above - tile) + (below - tile))
            out_ref[ROWS * g : ROWS * (g + 1), out_at] = (
                tile + (totals[g] - coef_sum * tile) + vertical
            )
        return carry

    count = out_ref.shape[1] // LANES
    step = 2 if count % 2 == 0 else 1

    def some_chunks(number, carry):
        for i in range(step):
            one_chunk(step * number + i, carry)
        return carry

    lax.fori_loop(0, count // step, some_chunks, 0)


def send_kernel(tracers_ref, send_ref, before_ref, after_ref, *out_refs):
    chunks = tracers_ref.shape[1] // LANES
    for part, (side_ref, out_ref) in enumerate(zip((before_ref, after_ref), out_refs)):
        base = side_ref.shape[0]
        out_ref[:base, :] = side_ref[...]
        cells = spread(send_ref[0:1, LANES * part : LANES * (part + 1)])
        high, low = cells >> 7, cells & (LANES - 1)
        for group in range(tracers_ref.shape[0] // ROWS):
            half = slice(ROWS * group, ROWS * (group + 1))
            rim = jnp.zeros((ROWS, LANES), jnp.float32)
            for k in range(chunks):
                tile = tracers_ref[half, LANES * k : LANES * (k + 1)]
                rim = jnp.where(high == k, take(tile, low, 1), rim)
            out_ref[base + ROWS * group : base + ROWS * (group + 1), :] = rim


def rim_kernel(
    starts,
    before_ref,
    after_ref,
    coef_ref,
    near_ref,
    area_ref,
    rows_ref,
    *refs,
):
    partial_refs, (out_ref, gain_ref) = refs[: len(starts)], refs[len(starts) :]
    chunks = coef_ref.shape[1] // LANES
    groups = out_ref.shape[0] // ROWS
    rim_at = before_ref.shape[0] - out_ref.shape[0]
    sides = before_ref, after_ref
    gain_ref[...] = flux_gain / area_ref[...]

    def source(group, s):
        at = rim_at + ROWS * group
        return sides[s][at : at + ROWS, :]

    for k in range(chunks):
        at = slice(LANES * k, LANES * (k + 1))
        totals = gathered(near_ref[:, at], coef_ref[:, at], source, 2, groups, chunks)
        part = max(i for i, start in enumerate(starts) if start <= k)
        place = slice(LANES * (k - starts[part]), LANES * (k - starts[part] + 1))
        for g in range(groups):
            half = slice(ROWS * g, ROWS * (g + 1))
            out_ref[half, at] = partial_refs[part][half, place] + totals[g]


VMEM_SPEC = pl.BlockSpec(memory_space=pltpu.VMEM)
ANY_SPEC = pl.BlockSpec(memory_space=pl.ANY)
HBM_SPEC = pl.BlockSpec(memory_space=pltpu.HBM)


def call(kernel, outs, specs, scratch=(), cost=0, hbm_outs=0):
    estimate = None
    if cost:
        estimate = pl.CostEstimate(flops=0, bytes_accessed=cost, transcendentals=0)
    outs = [
        out if isinstance(out, jax.ShapeDtypeStruct) else jax.ShapeDtypeStruct(out, jnp.float32)
        for out in outs
    ]
    out_specs = [VMEM_SPEC] * len(outs)
    out_specs[:hbm_outs] = [HBM_SPEC] * hbm_outs
    return pl.pallas_call(
        kernel,
        out_shape=outs,
        in_specs=specs,
        out_specs=out_specs,
        scratch_shapes=list(scratch),
        cost_estimate=estimate,
        compiler_params=pltpu.CompilerParams(vmem_limit_bytes=32 * 2**20),
        name=getattr(kernel, "func", kernel).__name__,
    )


def body(
    air_state,
    air_wind,
    jacobian,
    land_area,
    xgrid_rows,
    tracers,
    edge_coef,
    neighbours,
    vert_rate,
    ocean_area,
    send_list,
    xgrid_cols,
    xgrid_weights,
):
    field_count, levels, x_points, y_points = air_state.shape
    assert (x_points, y_points) == (2 * ROWS, LANES), air_state.shape
    assert xgrid_rows.shape[2] == send_list.shape[1] // 2 == LANES, xgrid_rows.shape
    planes = field_count * levels
    ocean_levels, cells = tracers.shape[1:]
    ocean_planes = tracers.shape[0] * ocean_levels
    faces, blocks = lax.axis_size("face"), lax.axis_size("blk")
    air = air_state.reshape(planes * x_points, y_points)
    wind = air_wind.reshape(2 * levels * x_points, y_points)
    ocean = tracers.reshape(ocean_planes, cells)
    point_ids, cell_ids, weights = xgrid_rows[0], xgrid_cols[0], xgrid_weights[0]
    rate = vert_rate.reshape(cells // LANES, LANES)
    area = ocean_area.reshape(cells // LANES, LANES)
    first_inputs = (
        cell_ids,
        weights,
        ocean,
        point_ids,
        jacobian,
        land_area,
        wind,
        air,
        send_list,
    )
    kept = (cell_ids, weights, point_ids, send_list)
    slab, moved, to_before, to_after, cell_ids, weights, point_ids, send_list = call(
        functools.partial(start_kernel, planes),
        [(blocks, HEAD, LANES), air.shape]
        + [(SIDE_IDS + blocks, LANES)] * 2
        + [jax.ShapeDtypeStruct(array.shape, array.dtype) for array in kept],
        [HBM_SPEC] * len(first_inputs),
        [
            pltpu.VMEM(shape, jnp.float32)
            for shape in (
                (blocks, HEAD, LANES),
                (ROWS, cells),
                jacobian.shape,
                land_area.shape,
                wind.shape,
                air.shape,
            )
        ]
        + [pltpu.SemaphoreType.DMA((len(first_inputs) + 3,))],
        hbm_outs=1,
    )(*(pltpu.with_memory_space_constraint(array, pltpu.HBM) for array in first_inputs))
    recv = lax.all_to_all(slab, "blk", split_axis=0, concat_axis=0, tiled=True)

    chunks = cells // LANES
    reads_per_chunk = edge_coef.shape[0] * chunks * (ocean_planes // ROWS)
    starts = (0, chunks * 6 // 16, chunks * 14 // 16)

    def ocean_part(start, end, after):
        (result,) = call(
            functools.partial(ocean_kernel, ocean_levels, start),
            [(ocean_planes, (end - start) * LANES)],
            [VMEM_SPEC] * 4 + [ANY_SPEC],
            [pltpu.VMEM((chunks * ocean_planes, 2 * LANES), jnp.bfloat16)],
            cost=(end - start) * reads_per_chunk * ROWS * LANES * 2,
        )(ocean, edge_coef, neighbours, rate, after)
        return result

    to_before, to_after = call(
        send_kernel,
        [(SIDE_IDS + blocks + ocean_planes, LANES)] * 2,
        [VMEM_SPEC] * 4,
        cost=reads_per_chunk * ROWS * LANES,
    )(ocean, send_list, to_before, to_after)
    onward = [(i, (i + 1) % blocks) for i in range(blocks)]
    before = lax.ppermute(to_after, "blk", onward)
    after = lax.ppermute(to_before, "blk", [(to, source) for source, to in onward])
    first_part = ocean_part(starts[0], starts[1], to_before)
    side_rows = 2 * planes + 2 * levels + SURF_ARRAYS + 2
    avg, down, up, surf = call(
        functools.partial(panel_kernel, planes),
        [air.shape, (side_rows, LANES), (side_rows, LANES), (2 * x_points * SURF_ARRAYS, LANES)],
        [VMEM_SPEC] * 9 + [ANY_SPEC],
    )(
        moved,
        recv,
        before,
        after,
        air,
        wind,
        jacobian,
        land_area,
        point_ids,
        first_part,
    )
    after_me = [(i, (i + 1) % faces) for i in range(faces)]
    low = lax.ppermute(up, "face", after_me)
    high = lax.ppermute(down, "face", [(to, source) for source, to in after_me])
    inner, packs = call(
        functools.partial(inner_kernel, planes),
        [((x_points - 2 * GLL) * planes, LANES), (2 * ROWS, LANES)],
        [VMEM_SPEC] * 6,
        cost=2 * air.size * 4,
    )(avg, moved, before, after, surf, wind)
    second_part = ocean_part(starts[1], starts[2], surf)

    slab, outer, final, inverse, edges = call(
        functools.partial(second_kernel, planes),
        [
            (blocks, HEAD, LANES),
            (len(outer_rows(x_points)) * planes, LANES),
            (x_points, y_points),
            (x_points, y_points),
            (2 * ROWS, LANES),
        ],
        [VMEM_SPEC] * 8 + [ANY_SPEC],
        [pltpu.VMEM((blocks, HEAD, LANES), jnp.float32), pltpu.SemaphoreType.DMA(())],
        hbm_outs=1,
    )(avg, inner, packs, surf, low, high, wind, point_ids, second_part)
    arrived = lax.all_to_all(slab, "blk", split_axis=0, concat_axis=0, tiled=True)
    last, hot, to_before, to_after = call(
        functools.partial(last_kernel, planes),
        [air.shape, jax.ShapeDtypeStruct((LANES, blocks * LANES), jnp.bfloat16)]
        + [(ROWS, LANES)] * 2,
        [VMEM_SPEC] * 5,
        cost=2 * air.size * 4,
    )(inner, outer, inverse, edges, cell_ids)
    edge_before = lax.ppermute(to_after, "blk", onward)
    edge_after = lax.ppermute(to_before, "blk", [(to, source) for source, to in onward])
    third_part = ocean_part(starts[2], chunks, to_before)
    partial, gain = call(
        functools.partial(rim_kernel, starts),
        [ocean.shape, area.shape],
        [VMEM_SPEC] * 5 + [ANY_SPEC] + [VMEM_SPEC] * len(starts),
        cost=chunks * reads_per_chunk // 8 * ROWS * LANES * 4,
    )(
        before,
        after,
        edge_coef,
        neighbours,
        area,
        to_before,
        first_part,
        second_part,
        third_part,
    )
    air_final, ocean_final = call(
        functools.partial(end_kernel, planes),
        [air.shape, ocean.shape],
        [VMEM_SPEC] * 11,
        [
            pltpu.VMEM(air.shape, jnp.float32),
            pltpu.VMEM((ROWS, cells), jnp.float32),
            pltpu.SemaphoreType.DMA((2 + planes // ROWS,)),
        ],
        hbm_outs=2,
    )(
        last,
        edge_before,
        edge_after,
        arrived,
        final,
        inverse,
        cell_ids,
        hot,
        weights,
        gain,
        partial,
    )
    return air_final.reshape(air_state.shape), ocean_final.reshape(tracers.shape)


def solution(mesh):
    return jax.shard_map(
        body,
        mesh=mesh,
        in_specs=(
            P(None, None, "face", "blk"),
            P(None, None, "face", "blk"),
            P("face", "blk"),
            P("face", "blk"),
            P(("face", "blk"), None, None),
            P(None, None, ("face", "blk")),
            P(None, ("face", "blk")),
            P(None, ("face", "blk")),
            P(("face", "blk")),
            P(("face", "blk")),
            P(("face", "blk"), None),
            P(("face", "blk"), None, None),
            P(("face", "blk"), None, None),
        ),
        out_specs=(P(None, None, "face", "blk"), P(None, None, ("face", "blk"))),
        check_vma=False,
    )
```
